32 devices in a mesh: seq: 8 (over y, x, core), tp: 4 (over z).
Axes of the slice: x: 2, y: 2, z: 4, core: 2. Of those that a mesh axis runs over, the one named last changes fastest.
Arguments:
- tokens: bfloat16 [2, 2048, 2048], P(None, 'seq'), may hold values from -6 to 6
- seq_lengths: int32 [2], replicated, may hold values from 512 to 2048, as said below
- norm_gain: float32 [2048], replicated, may hold values from 0.5 to 1.5
- w_query: bfloat16 [2048, 2048], P(None, 'tp'), may hold values from -0.125 to 0.125
- w_key: bfloat16 [2048, 2048], P(None, 'tp'), may hold values from -0.125 to 0.125
- w_value: bfloat16 [2048, 2048], P(None, 'tp'), may hold values from -0.125 to 0.125
- w_gate: bfloat16 [2048, 2048], P(None, 'tp'), may hold values from -0.125 to 0.125
- w_beta: bfloat16 [2048, 16], P(None, 'tp'), may hold values from -0.125 to 0.125
- beta_bias: float32 [16], P('tp'), may hold values from -3.5 to -2.5
- conv_weight: float32 [3, 4, 2048], P(None, None, 'tp'), may hold values from -3 to 3
- out_gain: float32 [128], replicated, may hold values from 0.5 to 1.5
- w_out: bfloat16 [2048, 2048], P('tp'), may hold values from -0.125 to 0.125
- ffn_gain: float32 [2048], replicated, may hold values from 0.5 to 1.5
- w_ffn_gate: bfloat16 [2048, 5632], P(None, 'tp'), may hold values from -0.125 to 0.125
- w_ffn_up: bfloat16 [2048, 5632], P(None, 'tp'), may hold values from -0.125 to 0.125
- w_ffn_down: bfloat16 [5632, 2048], P('tp'), may hold values from -0.078125 to 0.078125
- cotangent: bfloat16 [2, 2048, 2048], P(None, 'seq'), may hold values from -6 to 6
Outputs:
- out_tokens: bfloat16 [2, 2048, 2048], P(None, 'seq', 'tp')
- tokens_grad: float32 [2, 2048, 2048], P(None, 'seq', 'tp')
- norm_gain_grad: float32 [2048], replicated
- w_query_grad: float32 [2048, 2048], P('seq', 'tp')
- w_key_grad: float32 [2048, 2048], P('seq', 'tp')
- w_value_grad: float32 [2048, 2048], P('seq', 'tp')
- w_gate_grad: float32 [2048, 2048], P('seq', 'tp')
- w_beta_grad: float32 [2048, 16], P('seq', 'tp')
- beta_bias_grad: float32 [16], P('tp')
- conv_weight_grad: float32 [3, 4, 2048], P(None, None, 'tp')
- out_gain_grad: float32 [128], replicated
- w_out_grad: float32 [2048, 2048], P('tp', 'seq')
- ffn_gain_grad: float32 [2048], replicated
- w_ffn_gate_grad: float32 [2048, 5632], P('seq', 'tp')
- w_ffn_up_grad: float32 [2048, 5632], P('seq', 'tp')
- w_ffn_down_grad: float32 [5632, 2048], P('tp', 'seq')
- state_norm: float32 [], replicated
The draws below stay inside these ranges and needn't reach their ends.
Inputs may be any that keep to these rules, and one draw needn't show every extreme that they name: `seq_lengths`: at least one sequence has all 2048 tokens live; tokens at or past a sequence's length are padding.
All inputs are finite; a program needn't handle non-finite values.
Results may differ from the reference program's by a relative error of at most 0.028.
Values may be sent and summed in bfloat16 or wider, within the bound.
A program may use at most 192 MiB of HBM per device.

```python
import jax
import jax.numpy as jnp
from jax import lax

D = 2048
HEADS = 16
HEAD = 128
FF = 5632
GROUP = 64
CONV = 4
SEQS = 2
LENGTH = 2048


def draw_seq_lengths(key, part):
    key = jax.random.fold_in(key, 11)
    first, second = jax.random.split(key)
    lengths = jax.random.randint(first, (SEQS,), LENGTH // 4, LENGTH + 1)
    longest = jax.random.randint(second, (), 0, SEQS)
    return jnp.where(jnp.arange(SEQS) == longest, LENGTH, lengths).astype(jnp.int32)


def shard_levels(stream_key, dims, pieces, least, top_value):
    level = 1.0
    for axis_at, parts in pieces:
        steps = jax.random.uniform(jax.random.fold_in(jax.random.fold_in(stream_key, 6), axis_at), (parts,), jnp.float32, least / len(pieces), top_value / len(pieces))
        level = level * jnp.repeat(jnp.exp(steps), dims[axis_at] // parts).reshape((-1,) + (1,) * (len(dims) - 1 - axis_at))
    return level


def scatter_about(key, extent, width, bound, cuts=(), held_as=jnp.bfloat16):
    values = jax.random.normal(key, extent, jnp.float32) * width
    if len(cuts) > 0:
        values = shard_levels(key, extent, cuts, -0.22, 0.18) * values
    return jnp.clip(values, min=-bound, max=bound).astype(held_as)


def setup_inputs(seed: int = 0) -> dict:
    splits = jax.random.split(jax.random.key(seed), 18)
    return {
        "tokens": scatter_about(splits[0], (SEQS, LENGTH, D), 1.0, 6.0, ((1, 8),)),
        "seq_lengths": draw_seq_lengths(jax.random.fold_in(splits[17], 71), 0),
        "norm_gain": jnp.clip(1.0 + 0.1 * jax.random.normal(splits[2], (D,), jnp.float32), 0.5, 1.5),
        "w_query": scatter_about(splits[3], (D, D), D ** -0.5, 0.125, ((1, 4),)),
        "w_key": scatter_about(splits[4], (D, D), D ** -0.5, 0.125, ((1, 4),)),
        "w_value": scatter_about(splits[5], (D, D), D ** -0.5, 0.125, ((1, 4),)),
        "w_gate": scatter_about(splits[6], (D, D), D ** -0.5, 0.125, ((1, 4),)),
        "w_beta": scatter_about(splits[7], (D, HEADS), D ** -0.5, 0.125, ((1, 4),)),
        "beta_bias": jnp.clip(-3.5 + 1.0 * jax.random.uniform(splits[8], (HEADS,), jnp.float32) ** shard_levels(splits[8], (HEADS,), ((0, 4),), -0.2, 0.2), -3.5, -2.5),
        "conv_weight": scatter_about(splits[9], (3, CONV, D), CONV ** -0.5, 3.0, ((2, 4),), jnp.float32),
        "out_gain": jnp.clip(1.0 + 0.1 * jax.random.normal(splits[10], (HEAD,), jnp.float32), 0.5, 1.5),
        "w_out": scatter_about(splits[11], (D, D), D ** -0.5, 0.125, ((0, 4),)),
        "ffn_gain": jnp.clip(1.0 + 0.1 * jax.random.normal(splits[12], (D,), jnp.float32), 0.5, 1.5),
        "w_ffn_gate": scatter_about(splits[13], (D, FF), D ** -0.5, 0.125, ((1, 4),)),
        "w_ffn_up": scatter_about(splits[14], (D, FF), D ** -0.5, 0.125, ((1, 4),)),
        "w_ffn_down": scatter_about(splits[15], (FF, D), FF ** -0.5, 0.078125, ((0, 4),)),
        "cotangent": scatter_about(splits[16], (SEQS, LENGTH, D), 1.0, 6.0, ((1, 8),)),
    }


@jax.custom_vjp
def low(v):
    return lax.optimization_barrier(v.astype(jnp.bfloat16)).astype(jnp.float32)

@jax.custom_vjp
def low_back(v):
    return v

def low_keep(v):
    return (low(v), None)

def low_pass(kept, grad):
    return (grad,)

def back_keep(v):
    return (v, None)

def back_low(kept, grad):
    return (low(grad),)
low.defvjp(low_keep, low_pass)
low_back.defvjp(back_keep, back_low)
norm_eps = 1e-06
highest = lax.Precision.HIGHEST

def product(left, right):
    return jnp.dot(left, right, precision=highest)

def rms_scaled(value, gain):
    return value * lax.rsqrt(lax.optimization_barrier(jnp.mean(value * value, axis=-1, keepdims=True)) + norm_eps) * gain

def unit_norm(value):
    return value * lax.rsqrt(lax.optimization_barrier(jnp.sum(value * value, axis=-1, keepdims=True)) + norm_eps)

def group_weights(key_rows, value_rows, beta_rows):
    key_inner = jnp.einsum('...ck,...dk->...cd', key_rows, key_rows, precision=highest)
    group_len = key_rows.shape[-2]
    triangle = jnp.tril(beta_rows[..., :, None] * key_inner, -1) + jnp.eye(group_len, dtype=key_rows.dtype)
    targets = beta_rows[..., :, None] * jnp.concatenate([key_rows, value_rows], axis=-1)
    solved = jax.scipy.linalg.solve_triangular(triangle, targets, lower=True)
    head_size = key_rows.shape[-1]
    return (solved[..., :head_size], solved[..., head_size:])

def delta_group(state_now, block):
    query_rows, key_rows, value_rows, beta_rows = block
    erase_rows, write_rows = group_weights(key_rows, value_rows, beta_rows)
    fresh_rows = write_rows - jnp.einsum('...ck,...kv->...cv', erase_rows, state_now, precision=highest)
    scores = jnp.tril(jnp.einsum('...ck,...dk->...cd', query_rows, key_rows, precision=highest))
    output = jnp.einsum('...ck,...kv->...cv', query_rows, state_now, precision=highest)
    output = output + jnp.einsum('...cd,...dv->...cv', scores, fresh_rows, precision=highest)
    state_next = state_now + jnp.einsum('...ck,...cv->...kv', key_rows, fresh_rows, precision=highest)
    return (state_next, output)

def layer(inputs, live_rows, norm_gain, w_query, w_key, w_value, w_gate, w_beta, beta_bias, conv_weight, out_gain, w_out, ffn_gain, w_ffn_gate, w_ffn_up, w_ffn_down):
    length = inputs.shape[0]
    group_count = length // GROUP
    normed_one = low(rms_scaled(inputs, norm_gain))
    projected = low_back(low(product(normed_one, jnp.concatenate([w_query, w_key, w_value], axis=1))))
    gate_pre = low_back(product(normed_one, w_gate))
    beta_pre = low_back(product(normed_one, w_beta) + beta_bias)
    beta_val = live_rows[:, None] * jax.nn.sigmoid(beta_pre)
    kernel = conv_weight.shape[1]
    conv_flat = jnp.transpose(conv_weight, (1, 0, 2)).reshape(kernel, 3 * D)
    padded = jnp.pad(projected, ((kernel - 1, 0), (0, 0)))
    summed = conv_flat[0] * padded[0:length]
    for tap_index in range(1, kernel):
        summed = summed + conv_flat[tap_index] * padded[tap_index:tap_index + length]
    active = jax.nn.silu(summed).reshape(length, 3, HEADS, HEAD)
    query_all = low(unit_norm(active[:, 0]))
    key_all = low(unit_norm(active[:, 1]))
    value_all = low(active[:, 2])

    def to_groups(value):
        return jnp.transpose(value.reshape(group_count, GROUP, HEADS, HEAD), (0, 2, 1, 3))
    beta_groups = jnp.transpose(beta_val.reshape(group_count, GROUP, HEADS), (0, 2, 1))
    start_state = jnp.zeros((HEADS, HEAD, HEAD), jnp.float32)
    state_end, outputs = lax.scan(jax.checkpoint(delta_group), start_state, (to_groups(query_all), to_groups(key_all), to_groups(value_all), beta_groups))
    mixed = jnp.transpose(outputs, (0, 2, 1, 3)).reshape(length, HEADS, HEAD)
    gate_heads = jax.nn.silu(gate_pre.reshape(length, HEADS, HEAD))
    normed_heads = mixed * lax.rsqrt(lax.optimization_barrier(jnp.mean(mixed * mixed, axis=-1, keepdims=True)) + norm_eps) * out_gain * gate_heads
    heads_out = low(normed_heads.reshape(length, D))
    hidden_one = inputs + live_rows[:, None] * low_back(product(heads_out, w_out))
    normed_two = low(rms_scaled(hidden_one, ffn_gain))
    ffn_gate_pre = low_back(product(normed_two, w_ffn_gate))
    ffn_up_pre = low_back(product(normed_two, w_ffn_up))
    ffn_hidden = low(jax.nn.silu(ffn_gate_pre) * ffn_up_pre)
    result = hidden_one + low_back(product(ffn_hidden, w_ffn_down))
    norms = jnp.sqrt(lax.optimization_barrier(jnp.sum(state_end * state_end, axis=(1, 2))))
    return (result, norms)

def reference(tokens, seq_lengths, norm_gain, w_query, w_key, w_value, w_gate, w_beta, beta_bias, conv_weight, out_gain, w_out, ffn_gain, w_ffn_gate, w_ffn_up, w_ffn_down, cotangent):
    weights = tuple((item.astype(jnp.float32) for item in (norm_gain, w_query, w_key, w_value, w_gate, w_beta, beta_bias, conv_weight, out_gain, w_out, ffn_gain, w_ffn_gate, w_ffn_up, w_ffn_down)))
    positions = jnp.arange(LENGTH, dtype=jnp.int32)

    def per_sequence(totals, item):
        inputs, length_now, grad_out = item
        live_rows = (positions < length_now).astype(jnp.float32)

        def forward(inputs_in, *params):
            return layer(inputs_in, live_rows, *params)
        result, pull_back, norms = jax.vjp(forward, inputs.astype(jnp.float32), *weights, has_aux=True)
        grads = pull_back(grad_out.astype(jnp.float32))
        totals = tuple((left + right for left, right in zip(totals, grads[1:])))
        return (totals, (result.astype(jnp.bfloat16), grads[0], norms))
    start = tuple((jnp.zeros_like(item) for item in weights))
    totals, emitted = lax.scan(per_sequence, start, (tokens, seq_lengths, cotangent))
    out_tokens, tokens_grad, norms = emitted
    state_norm = jnp.mean(norms)
    return (out_tokens, tokens_grad, totals[0], totals[1], totals[2], totals[3], totals[4], totals[5], totals[6], totals[7], totals[8], totals[9], totals[10], totals[11], totals[12], totals[13], state_norm)
```

```python
import functools

import jax
import jax.numpy as jnp
from jax import lax
from jax.experimental import pallas as pl
from jax.experimental.pallas import tpu as pltpu
from jax.sharding import PartitionSpec as P

HEADS = 16
HEAD = 128

norm_eps = 1e-06
f32 = jnp.float32
bf16 = jnp.bfloat16
MESH = pl.DeviceIdType.MESH
VM = pltpu.VMEM


def mm(left, right, contract_left=1, contract_right=0):
    return lax.dot_general(
        left.astype(bf16),
        right.astype(bf16),
        (((contract_left,), (contract_right,)), ((), ())),
        preferred_element_type=f32,
    )


def from_behind(block, axis, distance):
    devices = range(lax.axis_size(axis))
    route = [(i - distance, i) for i in devices if i - distance in devices]
    return lax.ppermute(block, axis, route)


def sigmoid(value):
    return 1.0 / (1.0 + jnp.exp(-value))


def silu_grad(value):
    sigmoid_val = sigmoid(value)
    return sigmoid_val * (1.0 + value * (1.0 - sigmoid_val))


def dot_left(left, right):
    return mm(left, right, 0, 0)


def dot_right(left, right):
    return mm(left, right, 1, 1)


def strict_lower(size):
    rows = lax.broadcasted_iota(jnp.int32, (size, size), 0)
    cols = lax.broadcasted_iota(jnp.int32, (size, size), 1)
    return rows > cols, rows >= cols, rows ^ cols


def unit_lower_inverse(low, apart):
    size = low.shape[0]
    inverse = jnp.where(apart == 0, 1.0, 0.0) - jnp.where(apart == 1, low, 0.0)
    step = 2
    while step < size:
        between = jnp.where((apart >= step) & (apart < 2 * step), low, 0.0)
        inner = inverse.astype(bf16)
        inverse = inverse - mm(inner, mm(between, inner))
        step *= 2
    return inverse


def conv_silu(ext_ref, col, conv_ref, part, lane, length, taps, pad):
    summed = None
    for tap in range(taps):
        term = conv_ref[part, tap : tap + 1, lane] * ext_ref[pl.ds(pad - taps + 1 + tap, length), col]
        summed = term if summed is None else summed + term
    return summed


def delta_local_kernel(heads, taps, proj_ref, halo_ref, conv_ref, beta_ref, tri_ref, keep_ref, move_ref, offset_ref, ext_ref):
    length = proj_ref.shape[1]
    width = heads * HEAD
    pad = halo_ref.shape[1]
    ext_ref[0:pad, :] = halo_ref[0].astype(f32)
    ext_ref[pad : pad + length, :] = proj_ref[0].astype(f32)
    below, upto, apart = strict_lower(length)
    for h in range(heads):
        lane = slice(h * HEAD, (h + 1) * HEAD)

        def act(part):
            col = slice(part * width + h * HEAD, part * width + (h + 1) * HEAD)
            summed = conv_silu(ext_ref, col, conv_ref, part, lane, length, taps, pad)
            return summed * sigmoid(summed)

        def unit(value):
            return value * lax.rsqrt(jnp.sum(value * value, axis=-1, keepdims=True) + norm_eps)

        query = unit(act(0)).astype(bf16)
        key = unit(act(1)).astype(bf16)
        value = act(2).astype(bf16)
        beta = beta_ref[0, :, h : h + 1]
        low = jnp.where(below, beta * mm(key, key, 1, 1), 0.0)
        inverse = unit_lower_inverse(low, apart).astype(bf16)
        targets = jnp.concatenate([beta * key.astype(f32), beta * value.astype(f32)], axis=1)
        solved = mm(inverse, targets)
        solved_low = solved.astype(bf16)
        scores = jnp.where(upto, mm(query, key, 1, 1), 0.0).astype(bf16)
        passed = mm(scores, solved_low)
        moved = mm(key, solved_low, 0, 0)
        tri_ref[0, h] = inverse
        keep_ref[0, h, :, 0:HEAD] = (query.astype(f32) - passed[:, :HEAD]).astype(bf16)
        keep_ref[0, h, :, HEAD : 2 * HEAD] = passed[:, HEAD:].astype(bf16)
        keep_ref[0, h, :, 2 * HEAD :] = solved_low
        move_ref[0, h] = (-moved[:, :HEAD]).astype(bf16)
        offset_ref[0, h] = moved[:, HEAD:].astype(bf16)


def delta_local(proj, halo, conv_weight, beta):
    seqs, length, width3 = proj.shape
    heads = beta.shape[2]
    taps = conv_weight.shape[1]
    pad = halo.shape[1]

    def whole(shape):
        return pl.BlockSpec((1,) + shape, lambda s: (s,) + (0,) * len(shape))

    return pl.pallas_call(
        functools.partial(delta_local_kernel, heads, taps),
        grid=(seqs,),
        in_specs=[
            whole((length, width3)),
            whole((pad, width3)),
            pl.BlockSpec(conv_weight.shape, lambda s: (0, 0, 0)),
            whole((length, heads)),
        ],
        out_specs=[
            whole((heads, length, length)),
            whole((heads, length, 4 * HEAD)),
            whole((heads, HEAD, HEAD)),
            whole((heads, HEAD, HEAD)),
        ],
        out_shape=[
            jax.ShapeDtypeStruct((seqs, heads, length, length), bf16),
            jax.ShapeDtypeStruct((seqs, heads, length, 4 * HEAD), bf16),
            jax.ShapeDtypeStruct((seqs, heads, HEAD, HEAD), bf16),
            jax.ShapeDtypeStruct((seqs, heads, HEAD, HEAD), bf16),
        ],
        scratch_shapes=[pltpu.VMEM((pad + length, width3), f32)],
        compiler_params=pltpu.CompilerParams(vmem_limit_bytes=40 << 20),
        name="delta_local",
    )(proj, halo, conv_weight, beta)


def exchange_kernel(devices, chains, backward, *refs):
    if backward:
        move_all, offset_in, state_out, offset_all, states, send_one, recv_one, send_two, recv_two = refs
    else:
        (move_in, offset_in, state_out, move_all, norm_out, offset_all, states,
         send_zero, recv_zero, send_one, recv_one, send_two, recv_two) = refs
    me = lax.axis_index("seq")
    barrier = pltpu.get_barrier_semaphore()
    for turn in range(1, devices):
        pl.semaphore_signal(
            barrier, inc=1, device_id={"seq": lax.rem(me + turn, devices)}, device_id_type=MESH
        )
    pl.semaphore_wait(barrier, devices - 1)

    def remote(src, dst, send, recv, device):
        return pltpu.make_async_remote_copy(
            src_ref=src, dst_ref=dst, send_sem=send, recv_sem=recv,
            device_id={"seq": device}, device_id_type=MESH,
        )

    def send_maps(chain):
        if not backward:
            remote(move_in.at[chain], move_all.at[me], send_zero.at[chain], recv_zero.at[me], chain).start()
        remote(offset_in.at[chain], offset_all.at[me], send_one.at[chain], recv_one.at[me], chain).start()

    for chain in range(chains):
        @pl.when(me != chain)
        def _():
            send_maps(chain)

        @pl.when(me == chain)
        def _():
            if not backward:
                move_all[chain] = move_in[chain]
            offset_all[chain] = offset_in[chain]

    order = range(devices - 1, -1, -1) if backward else range(devices)

    @pl.when(me < chains)
    def _():
        state = jnp.zeros((HEAD, HEAD), f32)
        for at in order:
            states[at] = state.astype(bf16)

            @pl.when(me != at)
            def _():
                remote(states.at[at], state_out.at[me], send_two.at[at], recv_two.at[me], at).start()

            @pl.when(me == at)
            def _():
                state_out[me] = states[at]

            @pl.when(me != at)
            def _():
                if not backward:
                    remote(move_in.at[0], move_all.at[at], send_zero.at[0], recv_zero.at[at], at).wait_recv()
                remote(offset_in.at[0], offset_all.at[at], send_one.at[0], recv_one.at[at], at).wait_recv()

            state = state + mm(move_all[at], state, 0 if backward else 1, 0) + offset_all[at].astype(f32)
        if not backward:
            norm_out[...] = jnp.zeros_like(norm_out) + jnp.sqrt(jnp.sum(state * state, keepdims=True))
        for at in range(devices):
            @pl.when(me != at)
            def _():
                remote(states.at[at], state_out.at[0], send_two.at[at], recv_two.at[0], at).wait_send()

    if not backward:
        @pl.when(me >= chains)
        def _():
            norm_out[...] = jnp.zeros_like(norm_out)

    for chain in range(chains):
        @pl.when(me != chain)
        def _():
            if not backward:
                remote(move_in.at[chain], move_all.at[0], send_zero.at[chain], recv_zero.at[0], chain).wait_send()
            remote(offset_in.at[chain], offset_all.at[0], send_one.at[chain], recv_one.at[0], chain).wait_send()
            remote(states.at[0], state_out.at[chain], send_two.at[0], recv_two.at[chain], chain).wait_recv()


def exchange(devices, moves, offsets, backward):
    chains = offsets.shape[0]
    square = (HEAD, HEAD)
    dma = pltpu.SemaphoreType.DMA
    vmem = pl.BlockSpec(memory_space=pltpu.VMEM)
    scratch = [
        pltpu.VMEM((devices,) + square, bf16),
        pltpu.VMEM((devices,) + square, bf16),
    ]
    if not backward:
        scratch += [dma((chains,)), dma((devices,))]
    scratch += [dma((chains,)), dma((devices,)), dma((devices,)), dma((chains,))]
    out_shape = [jax.ShapeDtypeStruct((chains,) + square, bf16)]
    if not backward:
        out_shape += [
            jax.ShapeDtypeStruct((devices,) + square, bf16),
            jax.ShapeDtypeStruct((8, HEAD), f32),
        ]
    return pl.pallas_call(
        functools.partial(exchange_kernel, devices, chains, backward),
        in_specs=[vmem, vmem],
        out_specs=[vmem] * len(out_shape),
        out_shape=out_shape,
        scratch_shapes=scratch,
        compiler_params=pltpu.CompilerParams(
            collective_id=2 if backward else 1, has_side_effects=True, vmem_limit_bytes=24 << 20
        ),
        name="states_back" if backward else "states_forward",
    )(moves, offsets)


def delta_out_kernel(heads, keep_ref, state_ref, gate_ref, gain_ref, out_ref, fresh_ref, heads_ref):
    for h in range(heads):
        lane = slice(h * HEAD, (h + 1) * HEAD)
        state = state_ref[0, h]
        mixed = keep_ref[0, h, :, HEAD : 2 * HEAD].astype(f32) + mm(keep_ref[0, h, :, 0:HEAD], state)
        fresh = keep_ref[0, h, :, 3 * HEAD :].astype(f32) - mm(keep_ref[0, h, :, 2 * HEAD : 3 * HEAD], state)
        rstd = lax.rsqrt(jnp.mean(mixed * mixed, axis=-1, keepdims=True) + norm_eps)
        gate = gate_ref[0, :, lane]
        out_ref[0, :, lane] = mixed
        fresh_ref[0, :, lane] = fresh.astype(bf16)
        heads_ref[0, :, lane] = (mixed * rstd * gain_ref[...] * (gate * sigmoid(gate))).astype(bf16)


def delta_out(keep, state, gate_pre, out_gain):
    seqs, heads, length, _ = keep.shape
    width = heads * HEAD

    def whole(shape):
        return pl.BlockSpec((1,) + shape, lambda s: (s,) + (0,) * len(shape))

    return pl.pallas_call(
        functools.partial(delta_out_kernel, heads),
        grid=(seqs,),
        in_specs=[
            whole((heads, length, 4 * HEAD)),
            whole((heads, HEAD, HEAD)),
            whole((length, width)),
            pl.BlockSpec((1, HEAD), lambda s: (0, 0)),
        ],
        out_specs=[whole((length, width))] * 3,
        out_shape=[
            jax.ShapeDtypeStruct((seqs, length, width), f32),
            jax.ShapeDtypeStruct((seqs, length, width), bf16),
            jax.ShapeDtypeStruct((seqs, length, width), bf16),
        ],
        compiler_params=pltpu.CompilerParams(vmem_limit_bytes=32 << 20),
        name="delta_out",
    )(keep, state, gate_pre, out_gain.reshape(1, HEAD))


def head_back_kernel(heads, dheads_ref, mixed_ref, gate_ref, gain_ref, keep_ref, dmixed_ref, dgate_ref, dstate_ref, dgain_ref):
    gain = gain_ref[...]
    total = jnp.zeros((8, HEAD), f32)
    for h in range(heads):
        lane = slice(h * HEAD, (h + 1) * HEAD)
        dheads = dheads_ref[0, :, lane]
        mixed = mixed_ref[0, :, lane]
        gate = gate_ref[0, :, lane]
        sig = sigmoid(gate)
        act = gate * sig
        rstd = lax.rsqrt(jnp.mean(mixed * mixed, axis=-1, keepdims=True) + norm_eps)
        unit_out = mixed * rstd
        pulled = dheads * unit_out
        total = total + jnp.sum((pulled * act).reshape(-1, 8, HEAD), axis=0)
        dgate_ref[0, :, lane] = (pulled * gain * (sig * (1.0 + gate * (1.0 - sig)))).astype(bf16)
        dunit = dheads * gain * act
        dmixed = rstd * (dunit - unit_out * jnp.mean(dunit * unit_out, axis=-1, keepdims=True))
        dmixed_low = dmixed.astype(bf16)
        dmixed_ref[0, :, lane] = dmixed_low
        dstate_ref[0, h] = mm(keep_ref[0, h, :, 0:HEAD], dmixed_low, 0, 0).astype(bf16)
    dgain_ref[0] = total


def head_back(dheads, mixed, gate_pre, out_gain, keep):
    seqs, heads, length, _ = keep.shape
    width = heads * HEAD

    def whole(shape):
        return pl.BlockSpec((1,) + shape, lambda s: (s,) + (0,) * len(shape))

    return pl.pallas_call(
        functools.partial(head_back_kernel, heads),
        grid=(seqs,),
        in_specs=[
            whole((length, width)),
            whole((length, width)),
            whole((length, width)),
            pl.BlockSpec((1, HEAD), lambda s: (0, 0)),
            whole((heads, length, 4 * HEAD)),
        ],
        out_specs=[
            whole((length, width)),
            whole((length, width)),
            whole((heads, HEAD, HEAD)),
            whole((8, HEAD)),
        ],
        out_shape=[
            jax.ShapeDtypeStruct((seqs, length, width), bf16),
            jax.ShapeDtypeStruct((seqs, length, width), bf16),
            jax.ShapeDtypeStruct((seqs, heads, HEAD, HEAD), bf16),
            jax.ShapeDtypeStruct((seqs, 8, HEAD), f32),
        ],
        compiler_params=pltpu.CompilerParams(vmem_limit_bytes=32 << 20),
        name="head_back",
    )(dheads, mixed, gate_pre, out_gain.reshape(1, HEAD), keep)


def delta_back_kernel(
    heads, taps, proj_ref, halo_ref, conv_ref, beta_ref, slope_ref, tri_ref, fresh_ref, state_ref, grad_ref, dmixed_ref,
    dproj_ref, edge_ref, dconv_ref, dbeta_ref, ext_ref, dext_ref,
):
    length = proj_ref.shape[1]
    width = heads * HEAD
    pad = halo_ref.shape[1]
    ext_ref[0:pad, :] = halo_ref[0].astype(f32)
    ext_ref[pad : pad + length, :] = proj_ref[0].astype(f32)
    dext_ref[0:pad, :] = jnp.zeros((pad, 3 * width), f32)
    dext_ref[pad + length :, :] = jnp.zeros((pad, 3 * width), f32)
    below, upto, apart = strict_lower(length)
    dbeta_cols = []
    for h in range(heads):
        lane = slice(h * HEAD, (h + 1) * HEAD)

        def conv(part):
            col = slice(part * width + h * HEAD, part * width + (h + 1) * HEAD)
            return conv_silu(ext_ref, col, conv_ref, part, lane, length, taps, pad)

        pre_q, pre_k, pre_v = conv(0), conv(1), conv(2)
        sig_q, sig_k, sig_v = sigmoid(pre_q), sigmoid(pre_k), sigmoid(pre_v)
        act_q, act_k, act_v = pre_q * sig_q, pre_k * sig_k, pre_v * sig_v
        inv_q = lax.rsqrt(jnp.sum(act_q * act_q, axis=-1, keepdims=True) + norm_eps)
        inv_k = lax.rsqrt(jnp.sum(act_k * act_k, axis=-1, keepdims=True) + norm_eps)
        query_float, key_float = act_q * inv_q, act_k * inv_k
        query, key = query_float.astype(bf16), key_float.astype(bf16)
        value = act_v.astype(bf16)
        beta = beta_ref[0, :, h : h + 1]
        state = state_ref[0, h]
        grad = grad_ref[0, h]
        dmixed = dmixed_ref[0, :, lane]
        fresh = fresh_ref[0, :, lane]
        inner = mm(key, key, 1, 1)
        scores = jnp.where(upto, mm(query, key, 1, 1), 0.0)
        dfresh = mm(scores, dmixed, 0, 0) + mm(key, grad)
        pulled = mm(tri_ref[0, h], dfresh, 0, 0)
        dscores = jnp.where(upto, mm(dmixed, fresh, 1, 1), 0.0).astype(bf16)
        dquery = mm(dmixed, state, 1, 1) + mm(dscores, key)
        dvalue = beta * pulled
        dtri = jnp.where(below, -mm(pulled, fresh, 1, 1), 0.0)
        dinner = (beta * dtri).astype(bf16)
        dkey = (
            mm(dscores, query, 0, 0)
            + mm(fresh, grad, 1, 1)
            - mm(dvalue, state, 1, 1)
            + mm(dinner, key)
            + mm(dinner, key, 0, 0)
        )
        missing = value.astype(f32) - mm(key, state)
        dbeta_cols.append(
            jnp.sum(pulled * missing, axis=-1, keepdims=True) + jnp.sum(dtri * inner, axis=-1, keepdims=True)
        )
        dact_q = inv_q * (dquery - query_float * jnp.sum(dquery * query_float, axis=-1, keepdims=True))
        dact_k = inv_k * (dkey - key_float * jnp.sum(dkey * key_float, axis=-1, keepdims=True))
        for part, dact, sig, pre in ((0, dact_q, sig_q, pre_q), (1, dact_k, sig_k, pre_k), (2, dvalue, sig_v, pre_v)):
            col = slice(part * width + h * HEAD, part * width + (h + 1) * HEAD)
            dconv = dact * (sig * (1.0 + pre * (1.0 - sig)))
            dext_ref[pad : pad + length, col] = dconv
            for tap in range(taps):
                shifted = ext_ref[pl.ds(pad - taps + 1 + tap, length), col]
                dconv_ref[0, part, tap : tap + 1, lane] = jnp.sum(dconv * shifted, axis=0, keepdims=True)
    for part in range(3):
        for h in range(heads):
            lane = slice(h * HEAD, (h + 1) * HEAD)
            col = slice(part * width + h * HEAD, part * width + (h + 1) * HEAD)
            summed, edge = None, None
            for tap in range(taps):
                weight = conv_ref[part, tap : tap + 1, lane]
                term = weight * dext_ref[pl.ds(pad + taps - 1 - tap, length), col]
                before = weight * dext_ref[pl.ds(taps - 1 - tap, pad), col]
                summed = term if summed is None else summed + term
                edge = before if edge is None else edge + before
            dproj_ref[0, :, col] = summed.astype(bf16)
            edge_ref[0, 0:pad, col] = edge
            edge_ref[0, pad:, col] = summed[length - pad :, :]
    dbeta = jnp.concatenate(dbeta_cols, axis=1)
    dbeta_ref[0] = (dbeta * slope_ref[0]).astype(bf16)


def delta_back(proj, halo, conv_weight, beta, slope, tri, fresh, state, grad, dmixed):
    seqs, length, width3 = proj.shape
    heads = beta.shape[2]
    taps = conv_weight.shape[1]
    pad = halo.shape[1]
    width = width3 // 3

    def whole(shape):
        return pl.BlockSpec((1,) + shape, lambda s: (s,) + (0,) * len(shape))

    return pl.pallas_call(
        functools.partial(delta_back_kernel, heads, taps),
        grid=(seqs,),
        in_specs=[
            whole((length, width3)),
            whole((pad, width3)),
            pl.BlockSpec(conv_weight.shape, lambda s: (0, 0, 0)),
            whole((length, heads)),
            whole((length, heads)),
            whole((heads, length, length)),
            whole((length, width)),
            whole((heads, HEAD, HEAD)),
            whole((heads, HEAD, HEAD)),
            whole((length, width)),
        ],
        out_specs=[
            whole((length, width3)),
            whole((2 * pad, width3)),
            whole((3, taps, width)),
            whole((length, heads)),
        ],
        out_shape=[
            jax.ShapeDtypeStruct((seqs, length, width3), bf16),
            jax.ShapeDtypeStruct((seqs, 2 * pad, width3), f32),
            jax.ShapeDtypeStruct((seqs, 3, taps, width), f32),
            jax.ShapeDtypeStruct((seqs, length, heads), bf16),
        ],
        scratch_shapes=[
            pltpu.VMEM((pad + length, width3), f32),
            pltpu.VMEM((2 * pad + length, width3), f32),
        ],
        compiler_params=pltpu.CompilerParams(vmem_limit_bytes=40 << 20),
        name="delta_back",
    )(proj, halo, conv_weight, beta, slope, tri, fresh, state, grad, dmixed)


def on_device(
    tokens,
    seq_lengths,
    norm_gain,
    w_query,
    w_key,
    w_value,
    w_gate,
    w_beta,
    beta_bias,
    conv_weight,
    out_gain,
    w_out,
    ffn_gain,
    w_ffn_gate,
    w_ffn_up,
    w_ffn_down,
    cotangent,
):
    seqs_here, local_len, model_dim = tokens.shape
    row_count = seqs_here * local_len
    heads_here = w_beta.shape[1]
    local_width = w_query.shape[1]
    halo_pad = 8
    seq_index = lax.axis_index("seq")
    seq_devices = lax.axis_size("seq")
    tp_index = lax.axis_index("tp")
    slice_width = model_dim // lax.axis_size("tp")
    positions = seq_index * local_len + jnp.arange(local_len, dtype=jnp.int32)
    live_rows = (positions[None, :] < seq_lengths[:, None]).astype(f32).reshape(row_count, 1)
    inputs = tokens.reshape(row_count, model_dim).astype(f32)
    rstd_one = lax.rsqrt(jnp.mean(inputs * inputs, axis=-1, keepdims=True) + norm_eps)
    normed_one = (inputs * rstd_one * norm_gain).astype(bf16)
    w_proj = jnp.concatenate([w_query, w_key, w_value], axis=1)
    proj_low = jnp.dot(normed_one, w_proj, preferred_element_type=f32).astype(bf16)
    gate_pre = jnp.dot(normed_one, w_gate, preferred_element_type=f32)
    beta_pre = jnp.dot(normed_one, w_beta, preferred_element_type=f32) + beta_bias
    beta_sig = jax.nn.sigmoid(beta_pre)
    beta_val = live_rows * beta_sig
    proj_seq = proj_low.reshape(seqs_here, local_len, 3 * local_width)
    halo_rows = from_behind(proj_seq[:, local_len - halo_pad :, :], "seq", 1)
    beta_seq = beta_val.reshape(seqs_here, local_len, heads_here)
    gate_seq = gate_pre.reshape(seqs_here, local_len, local_width)

    tri, keep, move, offset = delta_local(proj_seq, halo_rows, conv_weight, beta_seq)
    chains = seqs_here * heads_here
    flat = (chains, HEAD, HEAD)
    deep = (seqs_here, heads_here, HEAD, HEAD)
    state_in, moves, norms = exchange(seq_devices, move.reshape(flat), offset.reshape(flat), False)
    state_in = state_in.reshape(deep)
    mixed, fresh, heads_seq = delta_out(keep, state_in, gate_seq, out_gain)
    heads_out = heads_seq.reshape(row_count, local_width)

    attn_sum = lax.psum(
        jnp.dot(heads_out, w_out, preferred_element_type=f32).astype(bf16), "tp"
    ).astype(f32)
    hidden_one = inputs + live_rows * attn_sum
    rstd_two = lax.rsqrt(jnp.mean(hidden_one * hidden_one, axis=-1, keepdims=True) + norm_eps)
    normed_two = (hidden_one * rstd_two * ffn_gain).astype(bf16)
    ffn_gate_pre = jnp.dot(normed_two, w_ffn_gate, preferred_element_type=f32)
    ffn_up_pre = jnp.dot(normed_two, w_ffn_up, preferred_element_type=f32)
    ffn_silu = jax.nn.silu(ffn_gate_pre)
    ffn_hidden = (ffn_silu * ffn_up_pre).astype(bf16)
    ffn_slice = lax.psum_scatter(
        jnp.dot(ffn_hidden, w_ffn_down, preferred_element_type=f32).astype(bf16),
        "tp",
        scatter_dimension=1,
        tiled=True,
    ).astype(f32)
    resid_slice = lax.dynamic_slice_in_dim(hidden_one, tp_index * slice_width, slice_width, 1)
    out_tokens = (resid_slice + ffn_slice).astype(bf16).reshape(seqs_here, local_len, slice_width)
    grad_low = cotangent.reshape(row_count, model_dim)
    grad_two = grad_low.astype(f32)
    dffn_hidden = dot_right(grad_low, w_ffn_down)
    dw_down = dot_left(ffn_hidden, grad_low)
    dffn_gate = (dffn_hidden * ffn_up_pre * silu_grad(ffn_gate_pre)).astype(bf16)
    dffn_up = (dffn_hidden * ffn_silu).astype(bf16)
    dnormed_two = lax.psum(
        (dot_right(dffn_gate, w_ffn_gate) + dot_right(dffn_up, w_ffn_up)).astype(bf16), "tp"
    ).astype(f32)
    dw_ffn_gate = dot_left(normed_two, dffn_gate)
    dw_ffn_up = dot_left(normed_two, dffn_up)
    scaled_two = dnormed_two * ffn_gain
    grad_one = (
        grad_two
        + rstd_two * scaled_two
        - hidden_one * rstd_two**3 * jnp.mean(scaled_two * hidden_one, axis=-1, keepdims=True)
    )
    dffn_gain = jnp.sum(dnormed_two * hidden_one * rstd_two, axis=0)
    dattn = (live_rows * grad_one).astype(bf16)
    dheads = dot_right(dattn, w_out).reshape(seqs_here, local_len, local_width)
    dw_out = dot_left(heads_out, dattn)

    dmixed, dgate_seq, dstate, dgain_parts = head_back(dheads, mixed, gate_seq, out_gain, keep)
    dout_gain = jnp.sum(dgain_parts, axis=(0, 1))
    dgate_pre = dgate_seq.reshape(row_count, local_width)
    (state_grad,) = exchange(seq_devices, moves, dstate.reshape(flat), True)
    slope = (live_rows * beta_sig * (1.0 - beta_sig)).reshape(seqs_here, local_len, heads_here)
    dproj_seq, edges, dconv_parts, dbeta_seq = delta_back(
        proj_seq, halo_rows, conv_weight, beta_seq, slope, tri, fresh, state_in, state_grad.reshape(deep), dmixed
    )
    dbeta_pre = dbeta_seq.reshape(row_count, heads_here)
    dbias = jnp.sum(dbeta_pre.astype(f32), axis=0)
    halo_grad = from_behind(edges[:, :halo_pad], "seq", -1)
    last_rows = (edges[:, halo_pad:] + halo_grad).astype(bf16)
    dproj_low = jnp.concatenate([dproj_seq[:, : local_len - halo_pad], last_rows], axis=1)
    dproj_low = dproj_low.reshape(row_count, 3 * local_width)
    dconv = jnp.sum(dconv_parts, axis=0)

    dnormed_part = (
        dot_right(dproj_low, w_proj) + dot_right(dgate_pre, w_gate) + dot_right(dbeta_pre, w_beta)
    )
    dw_proj = dot_left(normed_one, dproj_low)
    dw_gate = dot_left(normed_one, dgate_pre)
    dw_beta = dot_left(normed_one, dbeta_pre)
    own_cols = jnp.arange(model_dim, dtype=jnp.int32) // slice_width == tp_index
    dnormed_one = lax.psum(dnormed_part.astype(bf16), "tp").astype(f32)
    scaled_one = dnormed_one * norm_gain
    grad_in = (
        grad_one
        + rstd_one * scaled_one
        - inputs * rstd_one**3 * jnp.mean(scaled_one * inputs, axis=-1, keepdims=True)
    )
    gain_term = jnp.where(own_cols, jnp.sum(dnormed_one * inputs * rstd_one, axis=0), 0.0)
    tokens_grad = lax.dynamic_slice_in_dim(grad_in, tp_index * slice_width, slice_width, 1).reshape(
        seqs_here, local_len, slice_width
    )

    def scattered(grad, dim):
        return lax.psum_scatter(grad.astype(bf16), "seq", scatter_dimension=dim, tiled=True).astype(f32)

    small_sums = lax.psum((dffn_gain, dbias, dconv), "seq")
    head_sums = lax.psum((dout_gain, norms[0, 0], gain_term), ("seq", "tp"))
    state_norm = head_sums[1] / (seqs_here * HEADS)
    return (
        out_tokens,
        tokens_grad,
        head_sums[2],
        scattered(dw_proj[:, :local_width], 0),
        scattered(dw_proj[:, local_width : 2 * local_width], 0),
        scattered(dw_proj[:, 2 * local_width :], 0),
        scattered(dw_gate, 0),
        scattered(dw_beta, 0),
        small_sums[1],
        small_sums[2],
        head_sums[0],
        scattered(dw_out, 1),
        small_sums[0],
        scattered(dw_ffn_gate, 0),
        scattered(dw_ffn_up, 0),
        scattered(dw_down, 1),
        state_norm,
    )


def solution(mesh):
    in_specs = (
        P(None, "seq", None),
        P(),
        P(),
        P(None, "tp"),
        P(None, "tp"),
        P(None, "tp"),
        P(None, "tp"),
        P(None, "tp"),
        P("tp"),
        P(None, None, "tp"),
        P(),
        P("tp", None),
        P(),
        P(None, "tp"),
        P(None, "tp"),
        P("tp", None),
        P(None, "seq", None),
    )
    out_specs = (
        P(None, "seq", "tp"),
        P(None, "seq", "tp"),
        P(),
        P("seq", "tp"),
        P("seq", "tp"),
        P("seq", "tp"),
        P("seq", "tp"),
        P("seq", "tp"),
        P("tp"),
        P(None, None, "tp"),
        P(),
        P("tp", "seq"),
        P(),
        P("seq", "tp"),
        P("seq", "tp"),
        P("tp", "seq"),
        P(),
    )
    return jax.shard_map(
        on_device, mesh=mesh, in_specs=in_specs, out_specs=out_specs, check_vma=False
    )
```

```python
import functools

import jax
import jax.numpy as jnp
from jax import lax
from jax.experimental import pallas as pl
from jax.experimental.pallas import tpu as pltpu
from jax.sharding import PartitionSpec as P

HEADS = 16
HEAD = 128

norm_eps = 1e-06
f32 = jnp.float32
bf16 = jnp.bfloat16
MESH = pl.DeviceIdType.MESH
VM = pltpu.VMEM


def mm(left, right, contract_left=1, contract_right=0):
    return lax.dot_general(
        left.astype(bf16),
        right.astype(bf16),
        (((contract_left,), (contract_right,)), ((), ())),
        preferred_element_type=f32,
    )


def from_behind(block, axis, distance):
    devices = range(lax.axis_size(axis))
    route = [(i - distance, i) for i in devices if i - distance in devices]
    return lax.ppermute(block, axis, route)


def sigmoid(value):
    return 1.0 / (1.0 + jnp.exp(-value))


def silu_grad(value):
    sigmoid_val = sigmoid(value)
    return sigmoid_val * (1.0 + value * (1.0 - sigmoid_val))


def dot_left(left, right):
    return mm(left, right, 0, 0)


def dot_right(left, right):
    return mm(left, right, 1, 1)


def strict_lower(size):
    rows = lax.broadcasted_iota(jnp.int32, (size, size), 0)
    cols = lax.broadcasted_iota(jnp.int32, (size, size), 1)
    return rows > cols, rows >= cols, rows ^ cols


def unit_lower_inverse(low, apart):
    size = low.shape[0]
    inverse = jnp.where(apart == 0, 1.0, 0.0) - jnp.where(apart == 1, low, 0.0)
    step = 2
    while step < size:
        between = jnp.where((apart >= step) & (apart < 2 * step), low, 0.0)
        inner = inverse.astype(bf16)
        inverse = inverse - mm(inner, mm(between, inner))
        step *= 2
    return inverse


def conv_silu(ext_ref, col, conv_ref, part, lane, length, taps, pad):
    summed = None
    for tap in range(taps):
        term = conv_ref[part, tap : tap + 1, lane] * ext_ref[pl.ds(pad - taps + 1 + tap, length), col]
        summed = term if summed is None else summed + term
    return summed


def delta_local_kernel(heads, taps, proj_ref, halo_ref, conv_ref, beta_ref, tri_ref, keep_ref, move_ref, offset_ref, ext_ref):
    length = proj_ref.shape[1]
    width = heads * HEAD
    pad = halo_ref.shape[1]
    ext_ref[0:pad, :] = halo_ref[0].astype(f32)
    ext_ref[pad : pad + length, :] = proj_ref[0].astype(f32)
    below, upto, apart = strict_lower(length)
    for h in range(heads):
        lane = slice(h * HEAD, (h + 1) * HEAD)

        def act(part):
            col = slice(part * width + h * HEAD, part * width + (h + 1) * HEAD)
            summed = conv_silu(ext_ref, col, conv_ref, part, lane, length, taps, pad)
            return summed * sigmoid(summed)

        def unit(value):
            return value * lax.rsqrt(jnp.sum(value * value, axis=-1, keepdims=True) + norm_eps)

        query = unit(act(0)).astype(bf16)
        key = unit(act(1)).astype(bf16)
        value = act(2).astype(bf16)
        beta = beta_ref[0, :, h : h + 1]
        low = jnp.where(below, beta * mm(key, key, 1, 1), 0.0)
        inverse = unit_lower_inverse(low, apart).astype(bf16)
        targets = jnp.concatenate([beta * key.astype(f32), beta * value.astype(f32)], axis=1)
        solved = mm(inverse, targets)
        solved_low = solved.astype(bf16)
        scores = jnp.where(upto, mm(query, key, 1, 1), 0.0).astype(bf16)
        passed = mm(scores, solved_low)
        moved = mm(key, solved_low, 0, 0)
        tri_ref[0, h] = inverse
        keep_ref[0, h, :, 0:HEAD] = (query.astype(f32) - passed[:, :HEAD]).astype(bf16)
        keep_ref[0, h, :, HEAD : 2 * HEAD] = passed[:, HEAD:].astype(bf16)
        keep_ref[0, h, :, 2 * HEAD :] = solved_low
        move_ref[0, h] = (-moved[:, :HEAD]).astype(bf16)
        offset_ref[0, h] = moved[:, HEAD:].astype(bf16)


def delta_local(proj, halo, conv_weight, beta):
    seqs, length, width3 = proj.shape
    heads = beta.shape[2]
    taps = conv_weight.shape[1]
    pad = halo.shape[1]

    def whole(shape):
        return pl.BlockSpec((1,) + shape, lambda s: (s,) + (0,) * len(shape))

    return pl.pallas_call(
        functools.partial(delta_local_kernel, heads, taps),
        grid=(seqs,),
        in_specs=[
            whole((length, width3)),
            whole((pad, width3)),
            pl.BlockSpec(conv_weight.shape, lambda s: (0, 0, 0)),
            whole((length, heads)),
        ],
        out_specs=[
            whole((heads, length, length)),
            whole((heads, length, 4 * HEAD)),
            whole((heads, HEAD, HEAD)),
            whole((heads, HEAD, HEAD)),
        ],
        out_shape=[
            jax.ShapeDtypeStruct((seqs, heads, length, length), bf16),
            jax.ShapeDtypeStruct((seqs, heads, length, 4 * HEAD), bf16),
            jax.ShapeDtypeStruct((seqs, heads, HEAD, HEAD), bf16),
            jax.ShapeDtypeStruct((seqs, heads, HEAD, HEAD), bf16),
        ],
        scratch_shapes=[pltpu.VMEM((pad + length, width3), f32)],
        compiler_params=pltpu.CompilerParams(vmem_limit_bytes=40 << 20),
        name="delta_local",
    )(proj, halo, conv_weight, beta)


def exchange_kernel(devices, chains, backward, *refs):
    if backward:
        move_all, offset_in, state_out, offset_all, states, send_one, recv_one, send_two, recv_two = refs
    else:
        (move_in, offset_in, state_out, move_all, norm_out, offset_all, states,
         send_zero, recv_zero, send_one, recv_one, send_two, recv_two) = refs
    me = lax.axis_index("seq")
    barrier = pltpu.get_barrier_semaphore()
    for turn in range(1, devices):
        pl.semaphore_signal(
            barrier, inc=1, device_id={"seq": lax.rem(me + turn, devices)}, device_id_type=MESH
        )
    pl.semaphore_wait(barrier, devices - 1)

    def remote(src, dst, send, recv, device):
        return pltpu.make_async_remote_copy(
            src_ref=src, dst_ref=dst, send_sem=send, recv_sem=recv,
            device_id={"seq": device}, device_id_type=MESH,
        )

    def send_maps(chain):
        if not backward:
            remote(move_in.at[chain], move_all.at[me], send_zero.at[chain], recv_zero.at[me], chain).start()
        remote(offset_in.at[chain], offset_all.at[me], send_one.at[chain], recv_one.at[me], chain).start()

    for chain in range(chains):
        @pl.when(me != chain)
        def _():
            send_maps(chain)

        @pl.when(me == chain)
        def _():
            if not backward:
                move_all[chain] = move_in[chain]
            offset_all[chain] = offset_in[chain]

    order = range(devices - 1, -1, -1) if backward else range(devices)

    @pl.when(me < chains)
    def _():
        state = jnp.zeros((HEAD, HEAD), f32)
        for at in order:
            states[at] = state.astype(bf16)

            @pl.when(me != at)
            def _():
                remote(states.at[at], state_out.at[me], send_two.at[at], recv_two.at[me], at).start()

            @pl.when(me == at)
            def _():
                state_out[me] = states[at]

            @pl.when(me != at)
            def _():
                if not backward:
                    remote(move_in.at[0], move_all.at[at], send_zero.at[0], recv_zero.at[at], at).wait_recv()
                remote(offset_in.at[0], offset_all.at[at], send_one.at[0], recv_one.at[at], at).wait_recv()

            state = state + mm(move_all[at], state, 0 if backward else 1, 0) + offset_all[at].astype(f32)
        if not backward:
            norm_out[...] = jnp.zeros_like(norm_out) + jnp.sqrt(jnp.sum(state * state, keepdims=True))
        for at in range(devices):
            @pl.when(me != at)
            def _():
                remote(states.at[at], state_out.at[0], send_two.at[at], recv_two.at[0], at).wait_send()

    if not backward:
        @pl.when(me >= chains)
        def _():
            norm_out[...] = jnp.zeros_like(norm_out)

    for chain in range(chains):
        @pl.when(me != chain)
        def _():
            if not backward:
                remote(move_in.at[chain], move_all.at[0], send_zero.at[chain], recv_zero.at[0], chain).wait_send()
            remote(offset_in.at[chain], offset_all.at[0], send_one.at[chain], recv_one.at[0], chain).wait_send()
            remote(states.at[0], state_out.at[chain], send_two.at[0], recv_two.at[chain], chain).wait_recv()


def exchange(devices, moves, offsets, backward):
    chains = offsets.shape[0]
    square = (HEAD, HEAD)
    dma = pltpu.SemaphoreType.DMA
    vmem = pl.BlockSpec(memory_space=pltpu.VMEM)
    scratch = [
        pltpu.VMEM((devices,) + square, bf16),
        pltpu.VMEM((devices,) + square, bf16),
    ]
    if not backward:
        scratch += [dma((chains,)), dma((devices,))]
    scratch += [dma((chains,)), dma((devices,)), dma((devices,)), dma((chains,))]
    out_shape = [jax.ShapeDtypeStruct((chains,) + square, bf16)]
    if not backward:
        out_shape += [
            jax.ShapeDtypeStruct((devices,) + square, bf16),
            jax.ShapeDtypeStruct((8, HEAD), f32),
        ]
    return pl.pallas_call(
        functools.partial(exchange_kernel, devices, chains, backward),
        in_specs=[vmem, vmem],
        out_specs=[vmem] * len(out_shape),
        out_shape=out_shape,
        scratch_shapes=scratch,
        compiler_params=pltpu.CompilerParams(
            collective_id=2 if backward else 1, has_side_effects=True, vmem_limit_bytes=24 << 20
        ),
        name="states_back" if backward else "states_forward",
    )(moves, offsets)


def delta_out_kernel(heads, keep_ref, state_ref, gate_ref, gain_ref, out_ref, fresh_ref, heads_ref):
    for h in range(heads):
        lane = slice(h * HEAD, (h + 1) * HEAD)
        state = state_ref[0, h]
        mixed = keep_ref[0, h, :, HEAD : 2 * HEAD].astype(f32) + mm(keep_ref[0, h, :, 0:HEAD], state)
        fresh = keep_ref[0, h, :, 3 * HEAD :].astype(f32) - mm(keep_ref[0, h, :, 2 * HEAD : 3 * HEAD], state)
        rstd = lax.rsqrt(jnp.mean(mixed * mixed, axis=-1, keepdims=True) + norm_eps)
        gate = gate_ref[0, :, lane]
        out_ref[0, :, lane] = mixed
        fresh_ref[0, :, lane] = fresh.astype(bf16)
        heads_ref[0, :, lane] = (mixed * rstd * gain_ref[...] * (gate * sigmoid(gate))).astype(bf16)


def delta_out(keep, state, gate_pre, out_gain):
    seqs, heads, length, _ = keep.shape
    width = heads * HEAD

    def whole(shape):
        return pl.BlockSpec((1,) + shape, lambda s: (s,) + (0,) * len(shape))

    return pl.pallas_call(
        functools.partial(delta_out_kernel, heads),
        grid=(seqs,),
        in_specs=[
            whole((heads, length, 4 * HEAD)),
            whole((heads, HEAD, HEAD)),
            whole((length, width)),
            pl.BlockSpec((1, HEAD), lambda s: (0, 0)),
        ],
        out_specs=[whole((length, width))] * 3,
        out_shape=[
            jax.ShapeDtypeStruct((seqs, length, width), f32),
            jax.ShapeDtypeStruct((seqs, length, width), bf16),
            jax.ShapeDtypeStruct((seqs, length, width), bf16),
        ],
        compiler_params=pltpu.CompilerParams(vmem_limit_bytes=32 << 20),
        name="delta_out",
    )(keep, state, gate_pre, out_gain.reshape(1, HEAD))


def head_back_kernel(heads, dheads_ref, mixed_ref, gate_ref, gain_ref, keep_ref, dmixed_ref, dgate_ref, dstate_ref, dgain_ref):
    gain = gain_ref[...]
    total = jnp.zeros((8, HEAD), f32)
    for h in range(heads):
        lane = slice(h * HEAD, (h + 1) * HEAD)
        dheads = dheads_ref[0, :, lane]
        mixed = mixed_ref[0, :, lane]
        gate = gate_ref[0, :, lane]
        sig = sigmoid(gate)
        act = gate * sig
        rstd = lax.rsqrt(jnp.mean(mixed * mixed, axis=-1, keepdims=True) + norm_eps)
        unit_out = mixed * rstd
        pulled = dheads * unit_out
        total = total + jnp.sum((pulled * act).reshape(-1, 8, HEAD), axis=0)
        dgate_ref[0, :, lane] = (pulled * gain * (sig * (1.0 + gate * (1.0 - sig)))).astype(bf16)
        dunit = dheads * gain * act
        dmixed = rstd * (dunit - unit_out * jnp.mean(dunit * unit_out, axis=-1, keepdims=True))
        dmixed_low = dmixed.astype(bf16)
        dmixed_ref[0, :, lane] = dmixed_low
        dstate_ref[0, h] = mm(keep_ref[0, h, :, 0:HEAD], dmixed_low, 0, 0).astype(bf16)
    dgain_ref[0] = total


def head_back(dheads, mixed, gate_pre, out_gain, keep):
    seqs, heads, length, _ = keep.shape
    width = heads * HEAD

    def whole(shape):
        return pl.BlockSpec((1,) + shape, lambda s: (s,) + (0,) * len(shape))

    return pl.pallas_call(
        functools.partial(head_back_kernel, heads),
        grid=(seqs,),
        in_specs=[
            whole((length, width)),
            whole((length, width)),
            whole((length, width)),
            pl.BlockSpec((1, HEAD), lambda s: (0, 0)),
            whole((heads, length, 4 * HEAD)),
        ],
        out_specs=[
            whole((length, width)),
            whole((length, width)),
            whole((heads, HEAD, HEAD)),
            whole((8, HEAD)),
        ],
        out_shape=[
            jax.ShapeDtypeStruct((seqs, length, width), bf16),
            jax.ShapeDtypeStruct((seqs, length, width), bf16),
            jax.ShapeDtypeStruct((seqs, heads, HEAD, HEAD), bf16),
            jax.ShapeDtypeStruct((seqs, 8, HEAD), f32),
        ],
        compiler_params=pltpu.CompilerParams(vmem_limit_bytes=32 << 20),
        name="head_back",
    )(dheads, mixed, gate_pre, out_gain.reshape(1, HEAD), keep)


def delta_back_kernel(
    heads, taps, proj_ref, halo_ref, conv_ref, beta_ref, slope_ref, tri_ref, fresh_ref, state_ref, grad_ref, dmixed_ref,
    dproj_ref, edge_ref, dconv_ref, dbeta_ref, ext_ref, dext_ref,
):
    length = proj_ref.shape[1]
    width = heads * HEAD
    pad = halo_ref.shape[1]
    ext_ref[0:pad, :] = halo_ref[0].astype(f32)
    ext_ref[pad : pad + length, :] = proj_ref[0].astype(f32)
    dext_ref[0:pad, :] = jnp.zeros((pad, 3 * width), f32)
    dext_ref[pad + length :, :] = jnp.zeros((pad, 3 * width), f32)
    below, upto, apart = strict_lower(length)
    dbeta_cols = []
    for h in range(heads):
        lane = slice(h * HEAD, (h + 1) * HEAD)

        def conv(part):
            col = slice(part * width + h * HEAD, part * width + (h + 1) * HEAD)
            return conv_silu(ext_ref, col, conv_ref, part, lane, length, taps, pad)

        pre_q, pre_k, pre_v = conv(0), conv(1), conv(2)
        sig_q, sig_k, sig_v = sigmoid(pre_q), sigmoid(pre_k), sigmoid(pre_v)
        act_q, act_k, act_v = pre_q * sig_q, pre_k * sig_k, pre_v * sig_v
        inv_q = lax.rsqrt(jnp.sum(act_q * act_q, axis=-1, keepdims=True) + norm_eps)
        inv_k = lax.rsqrt(jnp.sum(act_k * act_k, axis=-1, keepdims=True) + norm_eps)
        query_float, key_float = act_q * inv_q, act_k * inv_k
        query, key = query_float.astype(bf16), key_float.astype(bf16)
        value = act_v.astype(bf16)
        beta = beta_ref[0, :, h : h + 1]
        state = state_ref[0, h]
        grad = grad_ref[0, h]
        dmixed = dmixed_ref[0, :, lane]
        fresh = fresh_ref[0, :, lane]
        inner = mm(key, key, 1, 1)
        scores = jnp.where(upto, mm(query, key, 1, 1), 0.0)
        dfresh = mm(scores, dmixed, 0, 0) + mm(key, grad)
        pulled = mm(tri_ref[0, h], dfresh, 0, 0)
        dscores = jnp.where(upto, mm(dmixed, fresh, 1, 1), 0.0).astype(bf16)
        dquery = mm(dmixed, state, 1, 1) + mm(dscores, key)
        dvalue = beta * pulled
        dtri = jnp.where(below, -mm(pulled, fresh, 1, 1), 0.0)
        dinner = (beta * dtri).astype(bf16)
        dkey = (
            mm(dscores, query, 0, 0)
            + mm(fresh, grad, 1, 1)
            - mm(dvalue, state, 1, 1)
            + mm(dinner, key)
            + mm(dinner, key, 0, 0)
        )
        missing = value.astype(f32) - mm(key, state)
        dbeta_cols.append(
            jnp.sum(pulled * missing, axis=-1, keepdims=True) + jnp.sum(dtri * inner, axis=-1, keepdims=True)
        )
        dact_q = inv_q * (dquery - query_float * jnp.sum(dquery * query_float, axis=-1, keepdims=True))
        dact_k = inv_k * (dkey - key_float * jnp.sum(dkey * key_float, axis=-1, keepdims=True))
        for part, dact, sig, pre in ((0, dact_q, sig_q, pre_q), (1, dact_k, sig_k, pre_k), (2, dvalue, sig_v, pre_v)):
            col = slice(part * width + h * HEAD, part * width + (h + 1) * HEAD)
            dconv = dact * (sig * (1.0 + pre * (1.0 - sig)))
            dext_ref[pad : pad + length, col] = dconv
            for tap in range(taps):
                shifted = ext_ref[pl.ds(pad - taps + 1 + tap, length), col]
                dconv_ref[0, part, tap : tap + 1, lane] = jnp.sum(dconv * shifted, axis=0, keepdims=True)
    for part in range(3):
        for h in range(heads):
            lane = slice(h * HEAD, (h + 1) * HEAD)
            col = slice(part * width + h * HEAD, part * width + (h + 1) * HEAD)
            summed, edge = None, None
            for tap in range(taps):
                weight = conv_ref[part, tap : tap + 1, lane]
                term = weight * dext_ref[pl.ds(pad + taps - 1 - tap, length), col]
                before = weight * dext_ref[pl.ds(taps - 1 - tap, pad), col]
                summed = term if summed is None else summed + term
                edge = before if edge is None else edge + before
            dproj_ref[0, :, col] = summed.astype(bf16)
            edge_ref[0, 0:pad, col] = edge
            edge_ref[0, pad:, col] = summed[length - pad :, :]
    dbeta = jnp.concatenate(dbeta_cols, axis=1)
    dbeta_ref[0] = (dbeta * slope_ref[0]).astype(bf16)


def delta_back(proj, halo, conv_weight, beta, slope, tri, fresh, state, grad, dmixed):
    seqs, length, width3 = proj.shape
    heads = beta.shape[2]
    taps = conv_weight.shape[1]
    pad = halo.shape[1]
    width = width3 // 3

    def whole(shape):
        return pl.BlockSpec((1,) + shape, lambda s: (s,) + (0,) * len(shape))

    return pl.pallas_call(
        functools.partial(delta_back_kernel, heads, taps),
        grid=(seqs,),
        in_specs=[
            whole((length, width3)),
            whole((pad, width3)),
            pl.BlockSpec(conv_weight.shape, lambda s: (0, 0, 0)),
            whole((length, heads)),
            whole((length, heads)),
            whole((heads, length, length)),
            whole((length, width)),
            whole((heads, HEAD, HEAD)),
            whole((heads, HEAD, HEAD)),
            whole((length, width)),
        ],
        out_specs=[
            whole((length, width3)),
            whole((2 * pad, width3)),
            whole((3, taps, width)),
            whole((length, heads)),
        ],
        out_shape=[
            jax.ShapeDtypeStruct((seqs, length, width3), bf16),
            jax.ShapeDtypeStruct((seqs, 2 * pad, width3), f32),
            jax.ShapeDtypeStruct((seqs, 3, taps, width), f32),
            jax.ShapeDtypeStruct((seqs, length, heads), bf16),
        ],
        scratch_shapes=[
            pltpu.VMEM((pad + length, width3), f32),
            pltpu.VMEM((2 * pad + length, width3), f32),
        ],
        compiler_params=pltpu.CompilerParams(vmem_limit_bytes=40 << 20),
        name="delta_back",
    )(proj, halo, conv_weight, beta, slope, tri, fresh, state, grad, dmixed)


def ceil_to(value, unit):
    return -(-value // unit) * unit


class Line:
    def __init__(self, devices, part, ups, downs, out, sems, chunk, lag, whole):
        self.n, self.part, self.ups, self.downs, self.out, self.sems = devices, part, ups, downs, out, sems
        self.chunk, self.lag, self.whole = chunk, lag, whole
        self.chunks = part.shape[0] // chunk
        self.me = lax.axis_index("tp")
        self.pieces = 1 if whole else devices
        self.width = part.shape[1] // self.pieces
        self.last = (devices - 2) * lag
        self.steps = self.chunks + self.last

    @staticmethod
    def scratch(rows, cols, devices, chunk, whole):
        count = (rows // chunk) * (1 if whole else devices)
        return [pltpu.VMEM((rows, cols), bf16)] * 2 + [pltpu.SemaphoreType.DMA((4, count))]

    def copy(self, source, way, k, piece):
        at = (pl.ds(pl.multiple_of(k * self.chunk, self.chunk), self.chunk), slice(piece * self.width, (piece + 1) * self.width))
        target = self.ups if way == 0 else self.downs
        sem = k * self.pieces + piece
        other = self.me + 1 if way == 0 else self.me - 1
        return pltpu.make_async_remote_copy(
            src_ref=source.at[at], dst_ref=target.at[at],
            send_sem=self.sems.at[way, sem], recv_sem=self.sems.at[2 + way, sem],
            device_id={"tp": other}, device_id_type=MESH,
        )

    def begin(self):
        for way, end in ((0, 0), (1, self.n - 1)):
            @pl.when(self.me == end)
            def _():
                def send(k, carry):
                    for piece in range(self.pieces):
                        if self.whole or piece != end:
                            self.copy(self.part, way, k, piece).start()
                    return carry
                lax.fori_loop(0, self.chunks, send, 0)

    def forward(self, way, k):
        me, n = self.me, self.n
        held = self.ups if way == 0 else self.downs
        rows = pl.ds(pl.multiple_of(k * self.chunk, self.chunk), self.chunk)
        for piece in range(self.pieces):
            if self.whole:
                gets, goes = None, me < n - 1 if way == 0 else me > 0
            else:
                gets, goes = (piece >= me, piece > me) if way == 0 else (piece <= me, piece < me)
            cols = slice(piece * self.width, (piece + 1) * self.width)

            def take():
                self.copy(self.part, way, k, piece).wait_recv()

                @pl.when(goes)
                def _():
                    held[rows, cols] = (held[rows, cols].astype(f32) + self.part[rows, cols].astype(f32)).astype(bf16)
                    self.copy(held, way, k, piece).start()

            if gets is None:
                take()
            else:
                pl.when(gets)(take)

    def finish(self, k):
        me, n = self.me, self.n
        rows = pl.ds(pl.multiple_of(k * self.chunk, self.chunk), self.chunk)
        if self.whole:
            @pl.when(me == 0)
            def _():
                self.out[rows, :] = self.part[rows, :].astype(f32) + self.downs[rows, :].astype(f32)

            @pl.when(me == n - 1)
            def _():
                self.out[rows, :] = self.part[rows, :].astype(f32) + self.ups[rows, :].astype(f32)

            @pl.when((me > 0) & (me < n - 1))
            def _():
                self.out[rows, :] = (
                    self.ups[rows, :].astype(f32) - self.part[rows, :].astype(f32) + self.downs[rows, :].astype(f32)
                )
        else:
            for piece in range(n):
                @pl.when(me == piece)
                def _():
                    cols = slice(piece * self.width, (piece + 1) * self.width)
                    total = self.part[rows, cols].astype(f32)
                    if piece > 0:
                        total = total + self.ups[rows, cols].astype(f32)
                    if piece < n - 1:
                        total = total + self.downs[rows, cols].astype(f32)
                    self.out[rows, :] = total

    def step(self, i):
        me, n = self.me, self.n
        up = i - (me - 1) * self.lag
        down = i - (n - 2 - me) * self.lag

        @pl.when((me > 0) & (up >= 0) & (up < self.chunks))
        def _():
            self.forward(0, up)

        @pl.when((me < n - 1) & (down >= 0) & (down < self.chunks))
        def _():
            self.forward(1, down)

        done = i - self.last

        @pl.when((done >= 0) & (done < self.chunks))
        def _():
            self.finish(done)

    def end(self):
        def drain(k, carry):
            for way in range(2):
                for piece in range(self.pieces):
                    if self.whole:
                        goes = self.me < self.n - 1 if way == 0 else self.me > 0
                    else:
                        goes = piece > self.me if way == 0 else piece < self.me

                    @pl.when(goes)
                    def _():
                        self.copy(self.part, way, k, piece).wait_send()
            return carry
        lax.fori_loop(0, self.chunks, drain, 0)


class Scatter:
    def __init__(self, devices, jobs, held, gots, outs, sends, recvs, unit, lag, ahead, wait):
        self.ahead, self.wait = ahead, wait
        self.n, self.jobs, self.held, self.gots, self.outs = devices, jobs, held, gots, outs
        self.sends, self.recvs, self.unit, self.lag = sends, recvs, unit, lag
        self.bits = devices.bit_length() - 1
        self.me = lax.axis_index("seq")
        tokens = jobs[0][1].shape[0]
        self.block = jobs[0][0].shape[0] * jobs[0][0].shape[1] // tokens // devices
        self.turned = self.block % 128 != 0
        self.chunks = sum(y.shape[1] for _, y in jobs) // unit
        self.steps = self.chunks + wait + (self.bits - 2) * lag

    @staticmethod
    def scratch(devices, rows, cols, unit):
        chunks, bits, block = cols // unit, devices.bit_length() - 1, rows // devices
        shapes = [pltpu.VMEM((chunks, devices // 2, block, unit), bf16)]
        shapes += [pltpu.VMEM((chunks, devices >> (s + 1), block, unit), bf16) for s in range(bits)]
        return shapes + [pltpu.SemaphoreType.DMA((bits, chunks))] * 2

    def power(self, stage, chunk):
        if stage == 0:
            return 1
        odd = lax.rem(chunk, 2)
        return odd * (1 << (self.bits - stage)) + (1 - odd) * (1 << stage)

    def bit(self, stage, chunk):
        return lax.rem(self.me // self.power(stage, chunk), 2)

    def partner(self, stage, chunk):
        return self.me + (1 - 2 * self.bit(stage, chunk)) * self.power(stage, chunk)

    def start_of_kept(self, stage, chunk):
        at = 0
        for s in range(1, stage):
            at = at + self.bit(s, chunk) * (self.n >> (s + 1))
        return at

    def copy(self, stage, chunk):
        count = self.n >> (stage + 1)
        if stage == 0:
            at = 0
        else:
            at = self.start_of_kept(stage, chunk) + (1 - self.bit(stage, chunk)) * count
        return pltpu.make_async_remote_copy(
            src_ref=self.held.at[chunk, pl.ds(at, count)], dst_ref=self.gots[stage].at[chunk],
            send_sem=self.sends.at[stage, chunk], recv_sem=self.recvs.at[stage, chunk],
            device_id={"seq": self.partner(stage, chunk)}, device_id_type=MESH,
        )

    def products(self, chunk, core, use):
        low = 0
        for x, y in self.jobs:
            count = y.shape[1] // self.unit

            @pl.when((chunk >= low) & (chunk < low + count))
            def _():
                right = y[:, pl.ds(pl.multiple_of((chunk - low) * self.unit, self.unit), self.unit)]

                def one(j, carry):
                    target = core
                    for s in range(1, self.bits):
                        target = target + lax.rem(j // (self.n >> (s + 1)), 2) * self.power(s, chunk)
                    mine = pl.ds(pl.multiple_of(target * self.block, self.block), self.block)
                    use(j, mm(x[mine, :], right) if self.turned else mm(x[:, mine], right, 0, 0))
                    return carry
                lax.fori_loop(0, self.n // 2, one, 0, unroll=True)
            low += count

    def produce(self, i):
        core = lax.rem(self.me, 2)

        @pl.when(i < self.chunks)
        def _():
            def put(j, value):
                self.held[i, j] = value.astype(bf16)
            self.products(i, 1 - core, put)
            self.copy(0, i).start()

        first = i - 1

        @pl.when((first >= 0) & (first < self.chunks))
        def _():
            self.copy(0, first).wait()

            def put(j, value):
                self.held[first, j] = (value + self.gots[0][first, j].astype(f32)).astype(bf16)
            self.products(first, core, put)
            self.copy(1, first).start()

    def consume(self, i):
        for stage in range(1, self.bits):
            chunk = i - (stage - 1) * self.lag

            @pl.when((chunk >= 0) & (chunk < self.chunks))
            def _():
                self.copy(stage, chunk).wait()
                count = self.n >> (stage + 1)
                base = self.start_of_kept(stage + 1, chunk)
                if stage < self.bits - 1:
                    for j in range(count):
                        self.held[chunk, base + j] = (
                            self.held[chunk, base + j].astype(f32) + self.gots[stage][chunk, j].astype(f32)
                        ).astype(bf16)
                    self.copy(stage + 1, chunk).start()
                else:
                    low = 0
                    for (x, y), out in zip(self.jobs, self.outs):
                        size = y.shape[1] // self.unit

                        @pl.when((chunk >= low) & (chunk < low + size))
                        def _():
                            cols = pl.ds(pl.multiple_of((chunk - low) * self.unit, self.unit), self.unit)
                            total = self.held[chunk, base].astype(f32) + self.gots[stage][chunk, 0].astype(f32)
                            out[:, cols] = total.astype(out.dtype)
                        low += size

    def step(self, i):
        for turn in range(self.ahead):
            self.produce(i * self.ahead + turn)
        self.consume(i - self.wait)


def greet(seq_devices, tp_devices, over_seq, over_tp):
    seq, tp = lax.axis_index("seq"), lax.axis_index("tp")
    barrier = pltpu.get_barrier_semaphore()
    peers = 0
    if over_seq:
        peers = seq_devices.bit_length() - 1
        for b in range(peers):
            other = seq + (1 - 2 * lax.rem(seq // (1 << b), 2)) * (1 << b)
            pl.semaphore_signal(barrier, inc=1, device_id={"seq": other}, device_id_type=MESH)
    if over_tp:
        @pl.when(tp > 0)
        def _():
            pl.semaphore_signal(barrier, inc=1, device_id={"tp": tp - 1}, device_id_type=MESH)

        @pl.when(tp < tp_devices - 1)
        def _():
            pl.semaphore_signal(barrier, inc=1, device_id={"tp": tp + 1}, device_id_type=MESH)
        peers = peers + jnp.minimum(tp, 1) + jnp.minimum(tp_devices - 1 - tp, 1)
    pl.semaphore_wait(barrier, peers)


def combined_kernel(seq_devices, tp_devices, jobs, lines, unit, chunk, scatter_lag, line_lag, ahead, wait, *refs):
    refs = list(refs)

    def take(count):
        out = refs[:count]
        del refs[:count]
        return out

    bits = seq_devices.bit_length() - 1
    lefts = take(max([x for x, _ in jobs], default=-1) + 1)
    rights = take(len(jobs))
    parts = take(len(lines))
    job_outs = take(len(jobs))
    line_outs = take(len(lines))
    flows = []
    if jobs:
        held, *rest = take(1 + bits + 2)
        gots, (sends, recvs) = rest[:bits], rest[bits:]
        pairs = [(lefts[x], y) for (x, _), y in zip(jobs, rights)]
        flows.append(Scatter(seq_devices, pairs, held, gots, job_outs, sends, recvs, unit, scatter_lag, ahead, wait))
    for part, out, whole in zip(parts, line_outs, lines):
        ups, downs, sems = take(3)
        flows.append(Line(tp_devices, part, ups, downs, out, sems, chunk, line_lag, whole))
    greet(seq_devices, tp_devices, len(jobs) > 0, len(lines) > 0)
    for flow in flows:
        if isinstance(flow, Line):
            flow.begin()

    def step(i, carry):
        for flow in flows:
            flow.step(i)
        return carry
    lax.fori_loop(0, max(flow.steps for flow in flows), step, 0)
    for flow in flows:
        if isinstance(flow, Line):
            flow.end()


def combined(seq_devices, tp_devices, lefts, jobs, parts, lines, ident, unit=256, chunk=64, scatter_lag=2, line_lag=2, ahead=2, wait=3):
    jobs = [(x, jnp.pad(y, ((0, 0), (0, ceil_to(y.shape[1], unit) - y.shape[1])))) for x, y in jobs]
    out_shape, scratch = [], []
    for x, y in jobs:
        out_shape.append(jax.ShapeDtypeStruct((lefts[x].shape[1] // seq_devices, y.shape[1]), bf16))
    if jobs:
        columns = lefts[0].shape[1]
        if columns // seq_devices % 128:
            lefts = [left.T for left in lefts]
    for part, whole in zip(parts, lines):
        rows, cols = part.shape
        out_shape.append(jax.ShapeDtypeStruct((rows, cols if whole else cols // tp_devices), f32))
    if jobs:
        scratch += Scatter.scratch(seq_devices, columns, sum(y.shape[1] for _, y in jobs), unit)
    for part, whole in zip(parts, lines):
        scratch += Line.scratch(*part.shape, tp_devices, chunk, whole)
    vmem = pl.BlockSpec(memory_space=pltpu.VMEM)
    return pl.pallas_call(
        functools.partial(
            combined_kernel, seq_devices, tp_devices, [(x, None) for x, _ in jobs], lines, unit, chunk, scatter_lag, line_lag, ahead, wait
        ),
        in_specs=[vmem] * (len(lefts) + len(jobs) + len(parts)),
        out_specs=[vmem] * len(out_shape),
        out_shape=out_shape,
        scratch_shapes=scratch,
        compiler_params=pltpu.CompilerParams(
            collective_id=ident, has_side_effects=True, vmem_limit_bytes=60 << 20
        ),
        name="sums_%d" % ident,
    )(*lefts, *[y for _, y in jobs], *parts)


def small_sums_kernel(seq_devices, tp_devices, both_rows, vec_ref, rows_ref, seq_out, both_out, rows_out, got_seq, got_rows, total, sems):
    seq, tp = lax.axis_index("seq"), lax.axis_index("tp")
    barrier = pltpu.get_barrier_semaphore()
    peers = [("seq", lax.rem(seq + turn, seq_devices)) for turn in range(1, seq_devices)]
    peers += [("tp", lax.rem(tp + turn, tp_devices)) for turn in range(1, tp_devices)]
    for axis, other in peers:
        pl.semaphore_signal(barrier, inc=1, device_id={axis: other}, device_id_type=MESH)
    pl.semaphore_wait(barrier, len(peers))

    def remote(src, dst, at, axis, other):
        return pltpu.make_async_remote_copy(
            src_ref=src, dst_ref=dst, send_sem=sems.at[0, at], recv_sem=sems.at[1, at],
            device_id={axis: other}, device_id_type=MESH,
        )

    copies = []
    for turn in range(1, tp_devices):
        copies.append(remote(rows_ref, got_rows.at[turn], turn, "tp", lax.rem(tp + turn, tp_devices)))
    for turn in range(1, seq_devices):
        copies.append(remote(vec_ref, got_seq.at[turn], tp_devices + turn, "seq", lax.rem(seq + turn, seq_devices)))
    for copy in copies:
        copy.start()
    for copy in copies:
        copy.wait()
    rows_total, seq_total = rows_ref[...], vec_ref[...]
    for turn in range(1, tp_devices):
        rows_total = rows_total + got_rows[turn]
    for turn in range(1, seq_devices):
        seq_total = seq_total + got_seq[turn]
    rows_out[...] = rows_total
    split = vec_ref.shape[0] - both_rows
    seq_out[...] = seq_total[:split]
    total[...] = seq_total[split:]
    both_out[tp] = seq_total[split:]
    copies = []
    for turn in range(1, tp_devices):
        at = tp_devices + seq_devices + turn
        copies.append(remote(total, both_out.at[tp], at, "tp", lax.rem(tp + turn, tp_devices)))
    for copy in copies:
        copy.start()
    for copy in copies:
        copy.wait()


def small_sums(seq_devices, tp_devices, seq_rows, both_rows, rows):
    vec = jnp.concatenate([seq_rows, both_rows], axis=0)
    split, both = seq_rows.shape[0], both_rows.shape[0]
    vmem = pl.BlockSpec(memory_space=pltpu.VMEM)
    return pl.pallas_call(
        functools.partial(small_sums_kernel, seq_devices, tp_devices, both),
        in_specs=[vmem] * 2,
        out_specs=[vmem] * 3,
        out_shape=[
            jax.ShapeDtypeStruct((split, HEAD), f32),
            jax.ShapeDtypeStruct((tp_devices, both, HEAD), f32),
            jax.ShapeDtypeStruct(rows.shape, f32),
        ],
        scratch_shapes=[
            pltpu.VMEM((seq_devices,) + vec.shape, f32),
            pltpu.VMEM((tp_devices,) + rows.shape, f32),
            pltpu.VMEM((both, HEAD), f32),
            pltpu.SemaphoreType.DMA((2, 2 * tp_devices + seq_devices)),
        ],
        compiler_params=pltpu.CompilerParams(
            collective_id=6, has_side_effects=True, vmem_limit_bytes=16 << 20
        ),
        name="small_sums",
    )(vec, rows)


def as_rows(value, rows):
    flat = value.reshape(-1)
    return jnp.pad(flat, (0, rows * HEAD - flat.shape[0])).reshape(rows, HEAD)


def on_device(
    tokens,
    seq_lengths,
    norm_gain,
    w_query,
    w_key,
    w_value,
    w_gate,
    w_beta,
    beta_bias,
    conv_weight,
    out_gain,
    w_out,
    ffn_gain,
    w_ffn_gate,
    w_ffn_up,
    w_ffn_down,
    cotangent,
):
    seqs_here, local_len, model_dim = tokens.shape
    row_count = seqs_here * local_len
    heads_here = w_beta.shape[1]
    local_width = w_query.shape[1]
    halo_pad = 8
    seq_index = lax.axis_index("seq")
    seq_devices = lax.axis_size("seq")
    tp_index = lax.axis_index("tp")
    slice_width = model_dim // lax.axis_size("tp")
    positions = seq_index * local_len + jnp.arange(local_len, dtype=jnp.int32)
    live_rows = (positions[None, :] < seq_lengths[:, None]).astype(f32).reshape(row_count, 1)
    inputs = tokens.reshape(row_count, model_dim).astype(f32)
    rstd_one = lax.rsqrt(jnp.mean(inputs * inputs, axis=-1, keepdims=True) + norm_eps)
    normed_one = (inputs * rstd_one * norm_gain).astype(bf16)
    w_proj = jnp.concatenate([w_query, w_key, w_value], axis=1)
    proj_low = jnp.dot(normed_one, w_proj, preferred_element_type=f32).astype(bf16)
    gate_pre = jnp.dot(normed_one, w_gate, preferred_element_type=f32)
    beta_pre = jnp.dot(normed_one, w_beta, preferred_element_type=f32) + beta_bias
    beta_sig = jax.nn.sigmoid(beta_pre)
    beta_val = live_rows * beta_sig
    proj_seq = proj_low.reshape(seqs_here, local_len, 3 * local_width)
    halo_rows = from_behind(proj_seq[:, local_len - halo_pad :, :], "seq", 1)
    beta_seq = beta_val.reshape(seqs_here, local_len, heads_here)
    gate_seq = gate_pre.reshape(seqs_here, local_len, local_width)

    tri, keep, move, offset = delta_local(proj_seq, halo_rows, conv_weight, beta_seq)
    chains = seqs_here * heads_here
    flat = (chains, HEAD, HEAD)
    deep = (seqs_here, heads_here, HEAD, HEAD)
    state_in, moves, norms = exchange(seq_devices, move.reshape(flat), offset.reshape(flat), False)
    state_in = state_in.reshape(deep)
    mixed, fresh, heads_seq = delta_out(keep, state_in, gate_seq, out_gain)
    heads_out = heads_seq.reshape(row_count, local_width)

    tp_devices = lax.axis_size("tp")
    sums = functools.partial(combined, seq_devices, tp_devices)
    attn_part = jnp.dot(heads_out, w_out, preferred_element_type=f32).astype(bf16)
    (attn_sum,) = sums([], [], [attn_part], [True], 3, chunk=32)
    hidden_one = inputs + live_rows * attn_sum
    rstd_two = lax.rsqrt(jnp.mean(hidden_one * hidden_one, axis=-1, keepdims=True) + norm_eps)
    normed_two = (hidden_one * rstd_two * ffn_gain).astype(bf16)
    ffn_gate_pre = jnp.dot(normed_two, w_ffn_gate, preferred_element_type=f32)
    ffn_up_pre = jnp.dot(normed_two, w_ffn_up, preferred_element_type=f32)
    ffn_silu = jax.nn.silu(ffn_gate_pre)
    ffn_hidden = (ffn_silu * ffn_up_pre).astype(bf16)
    ffn_part = jnp.dot(ffn_hidden, w_ffn_down, preferred_element_type=f32).astype(bf16)
    grad_low = cotangent.reshape(row_count, model_dim)
    grad_two = grad_low.astype(f32)
    dffn_hidden = dot_right(grad_low, w_ffn_down)
    dffn_gate = (dffn_hidden * ffn_up_pre * silu_grad(ffn_gate_pre)).astype(bf16)
    dffn_up = (dffn_hidden * ffn_silu).astype(bf16)
    dnormed_part_two = (dot_right(dffn_gate, w_ffn_gate) + dot_right(dffn_up, w_ffn_up)).astype(bf16)
    dffn_both = jnp.concatenate([dffn_gate, dffn_up], axis=1)
    ffn_width = w_ffn_gate.shape[1]
    early = min(ffn_width // 2 // 256 * 256 + 256, ffn_width)
    dw_both, dw_down_early, dnormed_two = sums(
        [normed_two, grad_low],
        [(0, dffn_both), (1, ffn_hidden[:, :early])],
        [dnormed_part_two],
        [True],
        4,
        chunk=32,
        ahead=1,
        wait=5,
        scatter_lag=4,
    )
    ffn_part, dnormed_two = lax.optimization_barrier((ffn_part, dnormed_two))
    ffn_slice = lax.psum_scatter(ffn_part, "tp", scatter_dimension=1, tiled=True)
    scaled_two = dnormed_two * ffn_gain
    grad_one = (
        grad_two
        + rstd_two * scaled_two
        - hidden_one * rstd_two**3 * jnp.mean(scaled_two * hidden_one, axis=-1, keepdims=True)
    )
    ffn_gain_term = lax.dynamic_slice_in_dim(
        jnp.sum(dnormed_two * hidden_one * rstd_two, axis=0), tp_index * slice_width, slice_width, 0
    )
    dattn = (live_rows * grad_one).astype(bf16)
    dheads = dot_right(dattn, w_out).reshape(seqs_here, local_len, local_width)

    dmixed, dgate_seq, dstate, dgain_parts = head_back(dheads, mixed, gate_seq, out_gain, keep)
    dout_gain = jnp.sum(dgain_parts, axis=(0, 1))
    dgate_pre = dgate_seq.reshape(row_count, local_width)
    (state_grad,) = exchange(seq_devices, moves, dstate.reshape(flat), True)
    slope = (live_rows * beta_sig * (1.0 - beta_sig)).reshape(seqs_here, local_len, heads_here)
    dproj_seq, edges, dconv_parts, dbeta_seq = delta_back(
        proj_seq, halo_rows, conv_weight, beta_seq, slope, tri, fresh, state_in, state_grad.reshape(deep), dmixed
    )
    dbeta_pre = dbeta_seq.reshape(row_count, heads_here)
    dbias = jnp.sum(dbeta_pre.astype(f32), axis=0)
    halo_grad = from_behind(edges[:, :halo_pad], "seq", -1)
    last_rows = (edges[:, halo_pad:] + halo_grad).astype(bf16)
    dproj_low = jnp.concatenate([dproj_seq[:, : local_len - halo_pad], last_rows], axis=1)
    dproj_low = dproj_low.reshape(row_count, 3 * local_width)
    dconv = jnp.sum(dconv_parts, axis=0)

    dnormed_part = (
        dot_right(dproj_low, w_proj) + dot_right(dgate_pre, w_gate) + dot_right(dbeta_pre, w_beta)
    )
    dense_right = jnp.concatenate([dproj_low, dgate_pre, dbeta_pre], axis=1)
    dnormed_part, ffn_slice = lax.optimization_barrier((dnormed_part.astype(bf16), ffn_slice))
    dw_down, dw_first, dw_out, dnormed_one = sums(
        [grad_low, normed_one, dattn],
        [(0, ffn_hidden[:, early:]), (1, dense_right), (2, heads_out)],
        [dnormed_part],
        [False],
        5,
        chunk=32,
        ahead=1,
        wait=5,
        scatter_lag=4,
    )

    def own_slice(value):
        return lax.dynamic_slice_in_dim(value, tp_index * slice_width, slice_width, value.ndim - 1)

    out_tokens = (own_slice(hidden_one) + ffn_slice.astype(f32)).astype(bf16).reshape(
        seqs_here, local_len, slice_width
    )
    inputs_slice = own_slice(inputs)
    scaled_one = dnormed_one * own_slice(norm_gain)
    gain_term = jnp.sum(dnormed_one * inputs_slice * rstd_one, axis=0)
    conv_rows = dconv.size // HEAD
    bias_rows = jnp.pad(dbias.reshape(1, heads_here), ((0, 7), (0, HEAD - heads_here)))
    slice_rows = slice_width // HEAD
    both_rows = ceil_to(2 * slice_rows + 2, 8)
    both = as_rows(
        jnp.concatenate([ffn_gain_term, gain_term, dout_gain, norms[0]]), both_rows
    )
    seq_total, both_total, row_total = small_sums(
        seq_devices,
        tp_devices,
        jnp.concatenate([dconv.reshape(conv_rows, HEAD), bias_rows], axis=0),
        both,
        as_rows(jnp.sum(scaled_one * inputs_slice, axis=-1), ceil_to(row_count // HEAD, 8)),
    )
    row_dot = (row_total.reshape(-1)[:row_count] / model_dim).reshape(row_count, 1)
    grad_in = own_slice(grad_one) + rstd_one * scaled_one - inputs_slice * rstd_one**3 * row_dot
    tokens_grad = grad_in.reshape(seqs_here, local_len, slice_width)
    ffn_gain_grad = both_total[:, :slice_rows].reshape(model_dim)
    gain_grad = both_total[:, slice_rows : 2 * slice_rows].reshape(model_dim)
    head_total = jnp.sum(both_total[:, 2 * slice_rows : 2 * slice_rows + 2], axis=0)
    lw = local_width

    def wide(value):
        return value.astype(f32)

    return (
        out_tokens,
        tokens_grad,
        gain_grad,
        wide(dw_first[:, :lw]),
        wide(dw_first[:, lw : 2 * lw]),
        wide(dw_first[:, 2 * lw : 3 * lw]),
        wide(dw_first[:, 3 * lw : 4 * lw]),
        wide(dw_first[:, 4 * lw : 4 * lw + heads_here]),
        seq_total[conv_rows, :heads_here],
        seq_total[:conv_rows].reshape(dconv.shape),
        head_total[0],
        wide(dw_out[:, :lw].T),
        ffn_gain_grad,
        wide(dw_both[:, :ffn_width]),
        wide(dw_both[:, ffn_width : 2 * ffn_width]),
        wide(jnp.concatenate([dw_down_early[:, :early].T, dw_down[:, : ffn_width - early].T], axis=0)),
        head_total[1, 0] / (seqs_here * HEADS),
    )


def solution(mesh):
    in_specs = (
        P(None, "seq", None),
        P(),
        P(),
        P(None, "tp"),
        P(None, "tp"),
        P(None, "tp"),
        P(None, "tp"),
        P(None, "tp"),
        P("tp"),
        P(None, None, "tp"),
        P(),
        P("tp", None),
        P(),
        P(None, "tp"),
        P(None, "tp"),
        P("tp", None),
        P(None, "seq", None),
    )
    out_specs = (
        P(None, "seq", "tp"),
        P(None, "seq", "tp"),
        P(),
        P("seq", "tp"),
        P("seq", "tp"),
        P("seq", "tp"),
        P("seq", "tp"),
        P("seq", "tp"),
        P("tp"),
        P(None, None, "tp"),
        P(),
        P("tp", "seq"),
        P(),
        P("seq", "tp"),
        P("seq", "tp"),
        P("tp", "seq"),
        P(),
    )
    return jax.shard_map(
        on_device, mesh=mesh, in_specs=in_specs, out_specs=out_specs, check_vma=False
    )
```

```python
import functools

import jax
import jax.numpy as jnp
from jax import lax
from jax.experimental import pallas as pl
from jax.experimental.pallas import tpu as pltpu
from jax.sharding import PartitionSpec as P

HEADS = 16
HEAD = 128

norm_eps = 1e-06
f32 = jnp.float32
bf16 = jnp.bfloat16
MESH = pl.DeviceIdType.MESH
VM = pltpu.VMEM


def mm(left, right, contract_left=1, contract_right=0):
    return lax.dot_general(
        left.astype(bf16),
        right.astype(bf16),
        (((contract_left,), (contract_right,)), ((), ())),
        preferred_element_type=f32,
    )


def from_behind(block, axis, distance):
    devices = range(lax.axis_size(axis))
    route = [(i - distance, i) for i in devices if i - distance in devices]
    return lax.ppermute(block, axis, route)


def sigmoid(value):
    return 1.0 / (1.0 + jnp.exp(-value))


def silu_grad(value):
    sigmoid_val = sigmoid(value)
    return sigmoid_val * (1.0 + value * (1.0 - sigmoid_val))


def dot_left(left, right):
    return mm(left, right, 0, 0)


def dot_right(left, right):
    return mm(left, right, 1, 1)


def strict_lower(size):
    rows = lax.broadcasted_iota(jnp.int32, (size, size), 0)
    cols = lax.broadcasted_iota(jnp.int32, (size, size), 1)
    return rows > cols, rows >= cols, rows ^ cols


def unit_lower_inverse(low, apart):
    size = low.shape[0]
    inverse = jnp.where(apart == 0, 1.0, 0.0) - jnp.where(apart == 1, low, 0.0)
    step = 2
    while step < size:
        between = jnp.where((apart >= step) & (apart < 2 * step), low, 0.0)
        inner = inverse.astype(bf16)
        inverse = inverse - mm(inner, mm(between, inner))
        step *= 2
    return inverse


def conv_silu(ext_ref, col, conv_ref, part, lane, length, taps, pad):
    summed = None
    for tap in range(taps):
        term = conv_ref[part, tap : tap + 1, lane] * ext_ref[pl.ds(pad - taps + 1 + tap, length), col]
        summed = term if summed is None else summed + term
    return summed


def delta_local_kernel(heads, taps, proj_ref, halo_ref, conv_ref, beta_ref, tri_ref, keep_ref, move_ref, offset_ref, ext_ref):
    length = proj_ref.shape[2]
    width = heads * HEAD
    pad = halo_ref.shape[2]
    for part in range(3):
        col = slice(part * width, (part + 1) * width)
        ext_ref[0:pad, col] = halo_ref[part, 0].astype(f32)
        ext_ref[pad : pad + length, col] = proj_ref[part, 0].astype(f32)
    below, upto, apart = strict_lower(length)
    for h in range(heads):
        lane = slice(h * HEAD, (h + 1) * HEAD)

        def act(part):
            col = slice(part * width + h * HEAD, part * width + (h + 1) * HEAD)
            summed = conv_silu(ext_ref, col, conv_ref, part, lane, length, taps, pad)
            return summed * sigmoid(summed)

        def unit(value):
            return value * lax.rsqrt(jnp.sum(value * value, axis=-1, keepdims=True) + norm_eps)

        query = unit(act(0)).astype(bf16)
        key = unit(act(1)).astype(bf16)
        value = act(2).astype(bf16)
        beta = beta_ref[0, :, h : h + 1]
        low = jnp.where(below, beta * mm(key, key, 1, 1), 0.0)
        inverse = unit_lower_inverse(low, apart).astype(bf16)
        targets = jnp.concatenate([beta * key.astype(f32), beta * value.astype(f32)], axis=1)
        solved = mm(inverse, targets)
        solved_low = solved.astype(bf16)
        scores = jnp.where(upto, mm(query, key, 1, 1), 0.0).astype(bf16)
        passed = mm(scores, solved_low)
        moved = mm(key, solved_low, 0, 0)
        tri_ref[0, h] = inverse
        keep_ref[0, h, :, 0:HEAD] = (query.astype(f32) - passed[:, :HEAD]).astype(bf16)
        keep_ref[0, h, :, HEAD : 2 * HEAD] = passed[:, HEAD:].astype(bf16)
        keep_ref[0, h, :, 2 * HEAD :] = solved_low
        move_ref[0, h] = (-moved[:, :HEAD]).astype(bf16)
        offset_ref[0, h] = moved[:, HEAD:].astype(bf16)


def delta_local(proj, halo, conv_weight, beta):
    _, seqs, length, width = proj.shape
    width3 = 3 * width
    heads = beta.shape[2]
    taps = conv_weight.shape[1]
    pad = halo.shape[2]

    def whole(shape):
        return pl.BlockSpec((1,) + shape, lambda s: (s,) + (0,) * len(shape))

    return pl.pallas_call(
        functools.partial(delta_local_kernel, heads, taps),
        grid=(seqs,),
        in_specs=[
            pl.BlockSpec((3, 1, length, width), lambda s: (0, s, 0, 0)),
            pl.BlockSpec((3, 1, pad, width), lambda s: (0, s, 0, 0)),
            pl.BlockSpec(conv_weight.shape, lambda s: (0, 0, 0)),
            whole((length, heads)),
        ],
        out_specs=[
            whole((heads, length, length)),
            whole((heads, length, 4 * HEAD)),
            whole((heads, HEAD, HEAD)),
            whole((heads, HEAD, HEAD)),
        ],
        out_shape=[
            jax.ShapeDtypeStruct((seqs, heads, length, length), bf16),
            jax.ShapeDtypeStruct((seqs, heads, length, 4 * HEAD), bf16),
            jax.ShapeDtypeStruct((seqs, heads, HEAD, HEAD), bf16),
            jax.ShapeDtypeStruct((seqs, heads, HEAD, HEAD), bf16),
        ],
        scratch_shapes=[pltpu.VMEM((pad + length, width3), f32)],
        compiler_params=pltpu.CompilerParams(vmem_limit_bytes=62 << 20),
        name="delta_local",
    )(proj, halo, conv_weight, beta)


def exchange_kernel(devices, chains, backward, *refs):
    if backward:
        move_all, offset_in, state_out, offset_all, states, send_one, recv_one, send_two, recv_two = refs
    else:
        (move_in, offset_in, cot_hbm, w_down_hbm, state_out, move_all, norm_out, dhid_ref, offset_all, states,
         send_zero, recv_zero, send_one, recv_one, send_two, recv_two, cot_ref, w_down_ref, load_sem) = refs
        loads = [
            pltpu.make_async_copy(cot_hbm, cot_ref, load_sem.at[0]),
            pltpu.make_async_copy(w_down_hbm, w_down_ref, load_sem.at[1]),
        ]
        for load in loads:
            load.start()
    me = lax.axis_index("seq")
    barrier = pltpu.get_barrier_semaphore()
    for turn in range(1, devices):
        pl.semaphore_signal(
            barrier, inc=1, device_id={"seq": lax.rem(me + turn, devices)}, device_id_type=MESH
        )
    pl.semaphore_wait(barrier, devices - 1)

    def remote(src, dst, send, recv, device):
        return pltpu.make_async_remote_copy(
            src_ref=src, dst_ref=dst, send_sem=send, recv_sem=recv,
            device_id={"seq": device}, device_id_type=MESH,
        )

    def send_maps(chain):
        if not backward:
            remote(move_in.at[chain], move_all.at[me], send_zero.at[chain], recv_zero.at[me], chain).start()
        remote(offset_in.at[chain], offset_all.at[me], send_one.at[chain], recv_one.at[me], chain).start()

    for chain in range(chains):
        @pl.when(me != chain)
        def _():
            send_maps(chain)

        @pl.when(me == chain)
        def _():
            if not backward:
                move_all[chain] = move_in[chain]
            offset_all[chain] = offset_in[chain]

    order = range(devices - 1, -1, -1) if backward else range(devices)

    def beside(first, last):
        def rows(q, carry):
            at = pl.ds(pl.multiple_of(q * 128, 128), 128)
            dhid_ref[at, :] = mm(cot_ref[at, :], w_down_ref[...], 1, 1).astype(bf16)
            return carry
        lax.fori_loop(first, last, rows, 0)

    if not backward:
        for load in loads:
            load.wait()
        blocks = dhid_ref.shape[0] // 128
        beside(0, blocks // 2)

    @pl.when(me < chains)
    def _():
        state = jnp.zeros((HEAD, HEAD), f32)
        for at in order:
            states[at] = state.astype(bf16)

            @pl.when(me != at)
            def _():
                remote(states.at[at], state_out.at[me], send_two.at[at], recv_two.at[me], at).start()

            @pl.when(me == at)
            def _():
                state_out[me] = states[at]

            @pl.when(me != at)
            def _():
                if not backward:
                    remote(move_in.at[0], move_all.at[at], send_zero.at[0], recv_zero.at[at], at).wait_recv()
                remote(offset_in.at[0], offset_all.at[at], send_one.at[0], recv_one.at[at], at).wait_recv()

            state = state + mm(move_all[at], state, 0 if backward else 1, 0) + offset_all[at].astype(f32)
        if not backward:
            norm_out[...] = jnp.zeros_like(norm_out) + jnp.sqrt(jnp.sum(state * state, keepdims=True))
        for at in range(devices):
            @pl.when(me != at)
            def _():
                remote(states.at[at], state_out.at[0], send_two.at[at], recv_two.at[0], at).wait_send()

    if not backward:
        @pl.when(me >= chains)
        def _():
            norm_out[...] = jnp.zeros_like(norm_out)

    if not backward:
        beside(blocks // 2, blocks)

    for chain in range(chains):
        @pl.when(me != chain)
        def _():
            if not backward:
                remote(move_in.at[chain], move_all.at[0], send_zero.at[chain], recv_zero.at[0], chain).wait_send()
            remote(offset_in.at[chain], offset_all.at[0], send_one.at[chain], recv_one.at[0], chain).wait_send()
            remote(states.at[0], state_out.at[chain], send_two.at[0], recv_two.at[chain], chain).wait_recv()


def exchange(devices, moves, offsets, backward, cot=None, w_down=None):
    chains = offsets.shape[0]
    square = (HEAD, HEAD)
    dma = pltpu.SemaphoreType.DMA
    vmem = pl.BlockSpec(memory_space=pltpu.VMEM)
    scratch = [
        pltpu.VMEM((devices,) + square, bf16),
        pltpu.VMEM((devices,) + square, bf16),
    ]
    if not backward:
        scratch += [dma((chains,)), dma((devices,))]
    scratch += [dma((chains,)), dma((devices,)), dma((devices,)), dma((chains,))]
    out_shape = [jax.ShapeDtypeStruct((chains,) + square, bf16)]
    extra = []
    if not backward:
        extra = [cot, w_down]
        scratch += [pltpu.VMEM(cot.shape, bf16), pltpu.VMEM(w_down.shape, bf16), dma((2,))]
        out_shape += [
            jax.ShapeDtypeStruct((devices,) + square, bf16),
            jax.ShapeDtypeStruct((8, HEAD), f32),
            jax.ShapeDtypeStruct((cot.shape[0], w_down.shape[0]), bf16),
        ]
    return pl.pallas_call(
        functools.partial(exchange_kernel, devices, chains, backward),
        in_specs=[vmem, vmem] + [pl.BlockSpec(memory_space=pltpu.HBM)] * len(extra),
        out_specs=[vmem] * len(out_shape),
        out_shape=out_shape,
        scratch_shapes=scratch,
        compiler_params=pltpu.CompilerParams(
            collective_id=2 if backward else 1, has_side_effects=True, vmem_limit_bytes=62 << 20
        ),
        name="states_back" if backward else "states_forward",
    )(moves, offsets, *extra)


def delta_out_kernel(heads, keep_ref, state_ref, gate_ref, gain_ref, out_ref, fresh_ref, heads_ref):
    for h in range(heads):
        lane = slice(h * HEAD, (h + 1) * HEAD)
        state = state_ref[0, h]
        mixed = keep_ref[0, h, :, HEAD : 2 * HEAD].astype(f32) + mm(keep_ref[0, h, :, 0:HEAD], state)
        fresh = keep_ref[0, h, :, 3 * HEAD :].astype(f32) - mm(keep_ref[0, h, :, 2 * HEAD : 3 * HEAD], state)
        rstd = lax.rsqrt(jnp.mean(mixed * mixed, axis=-1, keepdims=True) + norm_eps)
        gate = gate_ref[0, :, lane]
        out_ref[0, :, lane] = mixed
        fresh_ref[0, :, lane] = fresh.astype(bf16)
        heads_ref[0, :, lane] = (mixed * rstd * gain_ref[...] * (gate * sigmoid(gate))).astype(bf16)


def delta_out(keep, state, gate_pre, out_gain):
    seqs, heads, length, _ = keep.shape
    width = heads * HEAD

    def whole(shape):
        return pl.BlockSpec((1,) + shape, lambda s: (s,) + (0,) * len(shape))

    return pl.pallas_call(
        functools.partial(delta_out_kernel, heads),
        grid=(seqs,),
        in_specs=[
            whole((heads, length, 4 * HEAD)),
            whole((heads, HEAD, HEAD)),
            whole((length, width)),
            pl.BlockSpec((1, HEAD), lambda s: (0, 0)),
        ],
        out_specs=[whole((length, width))] * 3,
        out_shape=[
            jax.ShapeDtypeStruct((seqs, length, width), f32),
            jax.ShapeDtypeStruct((seqs, length, width), bf16),
            jax.ShapeDtypeStruct((seqs, length, width), bf16),
        ],
        compiler_params=pltpu.CompilerParams(vmem_limit_bytes=62 << 20),
        name="delta_out",
    )(keep, state, gate_pre, out_gain.reshape(1, HEAD))


def head_back_kernel(heads, dheads_ref, mixed_ref, gate_ref, gain_ref, keep_ref, dmixed_ref, dgate_ref, dstate_ref, dgain_ref):
    gain = gain_ref[...]
    total = jnp.zeros((8, HEAD), f32)
    for h in range(heads):
        lane = slice(h * HEAD, (h + 1) * HEAD)
        dheads = dheads_ref[0, :, lane]
        mixed = mixed_ref[0, :, lane]
        gate = gate_ref[0, :, lane]
        sig = sigmoid(gate)
        act = gate * sig
        rstd = lax.rsqrt(jnp.mean(mixed * mixed, axis=-1, keepdims=True) + norm_eps)
        unit_out = mixed * rstd
        pulled = dheads * unit_out
        total = total + jnp.sum((pulled * act).reshape(-1, 8, HEAD), axis=0)
        dgate_ref[0, :, lane] = (pulled * gain * (sig * (1.0 + gate * (1.0 - sig)))).astype(bf16)
        dunit = dheads * gain * act
        dmixed = rstd * (dunit - unit_out * jnp.mean(dunit * unit_out, axis=-1, keepdims=True))
        dmixed_low = dmixed.astype(bf16)
        dmixed_ref[0, :, lane] = dmixed_low
        dstate_ref[0, h] = mm(keep_ref[0, h, :, 0:HEAD], dmixed_low, 0, 0).astype(bf16)
    dgain_ref[0] = total


def head_back(dheads, mixed, gate_pre, out_gain, keep):
    seqs, heads, length, _ = keep.shape
    width = heads * HEAD

    def whole(shape):
        return pl.BlockSpec((1,) + shape, lambda s: (s,) + (0,) * len(shape))

    return pl.pallas_call(
        functools.partial(head_back_kernel, heads),
        grid=(seqs,),
        in_specs=[
            whole((length, width)),
            whole((length, width)),
            whole((length, width)),
            pl.BlockSpec((1, HEAD), lambda s: (0, 0)),
            whole((heads, length, 4 * HEAD)),
        ],
        out_specs=[
            whole((length, width)),
            whole((length, width)),
            whole((heads, HEAD, HEAD)),
            whole((8, HEAD)),
        ],
        out_shape=[
            jax.ShapeDtypeStruct((seqs, length, width), bf16),
            jax.ShapeDtypeStruct((seqs, length, width), bf16),
            jax.ShapeDtypeStruct((seqs, heads, HEAD, HEAD), bf16),
            jax.ShapeDtypeStruct((seqs, 8, HEAD), f32),
        ],
        compiler_params=pltpu.CompilerParams(vmem_limit_bytes=62 << 20),
        name="head_back",
    )(dheads, mixed, gate_pre, out_gain.reshape(1, HEAD), keep)


def delta_back_kernel(
    heads, taps, proj_ref, halo_ref, conv_ref, beta_ref, slope_ref, tri_ref, fresh_ref, state_ref, grad_ref, dmixed_ref,
    dproj_ref, edge_ref, dconv_ref, dbeta_ref, ext_ref, dext_ref,
):
    length = proj_ref.shape[2]
    width = heads * HEAD
    pad = halo_ref.shape[2]
    for part in range(3):
        col = slice(part * width, (part + 1) * width)
        ext_ref[0:pad, col] = halo_ref[part, 0].astype(f32)
        ext_ref[pad : pad + length, col] = proj_ref[part, 0].astype(f32)
    dext_ref[0:pad, :] = jnp.zeros((pad, 3 * width), f32)
    dext_ref[pad + length :, :] = jnp.zeros((pad, 3 * width), f32)
    below, upto, apart = strict_lower(length)
    dbeta_cols = []
    for h in range(heads):
        lane = slice(h * HEAD, (h + 1) * HEAD)

        def conv(part):
            col = slice(part * width + h * HEAD, part * width + (h + 1) * HEAD)
            return conv_silu(ext_ref, col, conv_ref, part, lane, length, taps, pad)

        pre_q, pre_k, pre_v = conv(0), conv(1), conv(2)
        sig_q, sig_k, sig_v = sigmoid(pre_q), sigmoid(pre_k), sigmoid(pre_v)
        act_q, act_k, act_v = pre_q * sig_q, pre_k * sig_k, pre_v * sig_v
        inv_q = lax.rsqrt(jnp.sum(act_q * act_q, axis=-1, keepdims=True) + norm_eps)
        inv_k = lax.rsqrt(jnp.sum(act_k * act_k, axis=-1, keepdims=True) + norm_eps)
        query_float, key_float = act_q * inv_q, act_k * inv_k
        query, key = query_float.astype(bf16), key_float.astype(bf16)
        value = act_v.astype(bf16)
        beta = beta_ref[0, :, h : h + 1]
        state = state_ref[0, h]
        grad = grad_ref[0, h]
        dmixed = dmixed_ref[0, :, lane]
        fresh = fresh_ref[0, :, lane]
        inner = mm(key, key, 1, 1)
        scores = jnp.where(upto, mm(query, key, 1, 1), 0.0)
        dfresh = mm(scores, dmixed, 0, 0) + mm(key, grad)
        pulled = mm(tri_ref[0, h], dfresh, 0, 0)
        dscores = jnp.where(upto, mm(dmixed, fresh, 1, 1), 0.0).astype(bf16)
        dquery = mm(dmixed, state, 1, 1) + mm(dscores, key)
        dvalue = beta * pulled
        dtri = jnp.where(below, -mm(pulled, fresh, 1, 1), 0.0)
        dinner = (beta * dtri).astype(bf16)
        dkey = (
            mm(dscores, query, 0, 0)
            + mm(fresh, grad, 1, 1)
            - mm(dvalue, state, 1, 1)
            + mm(dinner, key)
            + mm(dinner, key, 0, 0)
        )
        missing = value.astype(f32) - mm(key, state)
        dbeta_cols.append(
            jnp.sum(pulled * missing, axis=-1, keepdims=True) + jnp.sum(dtri * inner, axis=-1, keepdims=True)
        )
        dact_q = inv_q * (dquery - query_float * jnp.sum(dquery * query_float, axis=-1, keepdims=True))
        dact_k = inv_k * (dkey - key_float * jnp.sum(dkey * key_float, axis=-1, keepdims=True))
        for part, dact, sig, pre in ((0, dact_q, sig_q, pre_q), (1, dact_k, sig_k, pre_k), (2, dvalue, sig_v, pre_v)):
            col = slice(part * width + h * HEAD, part * width + (h + 1) * HEAD)
            dconv = dact * (sig * (1.0 + pre * (1.0 - sig)))
            dext_ref[pad : pad + length, col] = dconv
            for tap in range(taps):
                shifted = ext_ref[pl.ds(pad - taps + 1 + tap, length), col]
                dconv_ref[0, part, tap : tap + 1, lane] = jnp.sum(dconv * shifted, axis=0, keepdims=True)
    for part in range(3):
        for h in range(heads):
            lane = slice(h * HEAD, (h + 1) * HEAD)
            col = slice(part * width + h * HEAD, part * width + (h + 1) * HEAD)
            summed, edge = None, None
            for tap in range(taps):
                weight = conv_ref[part, tap : tap + 1, lane]
                term = weight * dext_ref[pl.ds(pad + taps - 1 - tap, length), col]
                before = weight * dext_ref[pl.ds(taps - 1 - tap, pad), col]
                summed = term if summed is None else summed + term
                edge = before if edge is None else edge + before
            dproj_ref[0, :, col] = summed.astype(bf16)
            edge_ref[0, 0:pad, col] = edge
            edge_ref[0, pad:, col] = summed[length - pad :, :]
    dbeta = jnp.concatenate(dbeta_cols, axis=1)
    dbeta_ref[0] = (dbeta * slope_ref[0]).astype(bf16)


def delta_back(proj, halo, conv_weight, beta, slope, tri, fresh, state, grad, dmixed):
    _, seqs, length, width = proj.shape
    width3 = 3 * width
    heads = beta.shape[2]
    taps = conv_weight.shape[1]
    pad = halo.shape[2]

    def whole(shape):
        return pl.BlockSpec((1,) + shape, lambda s: (s,) + (0,) * len(shape))

    return pl.pallas_call(
        functools.partial(delta_back_kernel, heads, taps),
        grid=(seqs,),
        in_specs=[
            pl.BlockSpec((3, 1, length, width), lambda s: (0, s, 0, 0)),
            pl.BlockSpec((3, 1, pad, width), lambda s: (0, s, 0, 0)),
            pl.BlockSpec(conv_weight.shape, lambda s: (0, 0, 0)),
            whole((length, heads)),
            whole((length, heads)),
            whole((heads, length, length)),
            whole((length, width)),
            whole((heads, HEAD, HEAD)),
            whole((heads, HEAD, HEAD)),
            whole((length, width)),
        ],
        out_specs=[
            whole((length, width3)),
            whole((2 * pad, width3)),
            whole((3, taps, width)),
            whole((length, heads)),
        ],
        out_shape=[
            jax.ShapeDtypeStruct((seqs, length, width3), bf16),
            jax.ShapeDtypeStruct((seqs, 2 * pad, width3), f32),
            jax.ShapeDtypeStruct((seqs, 3, taps, width), f32),
            jax.ShapeDtypeStruct((seqs, length, heads), bf16),
        ],
        scratch_shapes=[
            pltpu.VMEM((pad + length, width3), f32),
            pltpu.VMEM((2 * pad + length, width3), f32),
        ],
        compiler_params=pltpu.CompilerParams(vmem_limit_bytes=62 << 20),
        name="delta_back",
    )(proj, halo, conv_weight, beta, slope, tri, fresh, state, grad, dmixed)


def first_kernel(
    seq_devices, tokens_ref, gain_ref, w_beta_ref, bias_ref, live_ref, *refs
):
    (w_query, w_key, w_value, w_gate, normed_ref, rstd_ref, proj_ref, halo_ref, gate_ref, beta_ref, slope_ref,
     weights, halo_in, load_sem, send_sem, recv_sem) = refs
    rows, dim = tokens_ref.shape
    seqs, pad, _ = halo_in.shape
    length = rows // seqs
    me = lax.axis_index("seq")
    loads = [
        pltpu.make_async_copy(source, weights.at[at], load_sem.at[at])
        for at, source in enumerate((w_query, w_key, w_value, w_gate))
    ]
    for load in loads:
        load.start()
    barrier = pltpu.get_barrier_semaphore()

    @pl.when(me > 0)
    def _():
        pl.semaphore_signal(barrier, inc=1, device_id={"seq": me - 1}, device_id_type=MESH)

    @pl.when(me < seq_devices - 1)
    def _():
        pl.semaphore_signal(barrier, inc=1, device_id={"seq": me + 1}, device_id_type=MESH)

    gain = gain_ref[...]

    def norm(q, carry):
        at = pl.ds(pl.multiple_of(q * 128, 128), 128)
        value = tokens_ref[at, :].astype(f32)
        scale = lax.rsqrt(jnp.mean(value * value, axis=-1, keepdims=True) + norm_eps)
        rstd_ref[at, :] = scale
        normed_ref[at, :] = (value * scale * gain).astype(bf16)
        return carry
    lax.fori_loop(0, rows // 128, norm, 0)
    pl.semaphore_wait(barrier, jnp.minimum(me, 1) + jnp.minimum(seq_devices - 1 - me, 1))

    def halo_copy(s):
        return pltpu.make_async_remote_copy(
            src_ref=tokens_ref.at[pl.ds((s + 1) * length - pad, pad)], dst_ref=halo_in.at[s],
            send_sem=send_sem.at[s], recv_sem=recv_sem.at[s],
            device_id={"seq": me + 1}, device_id_type=MESH,
        )

    @pl.when(me < seq_devices - 1)
    def _():
        for s in range(seqs):
            halo_copy(s).start()

    sig = sigmoid(mm(normed_ref[...], w_beta_ref[...]) + bias_ref[...])
    beta = live_ref[...] * sig
    beta_ref[...] = beta
    slope_ref[...] = beta * (1.0 - sig)
    for part in range(4):
        loads[part].wait()

        def some(q, carry):
            at = pl.ds(pl.multiple_of(q * 256, 256), 256)
            product = mm(normed_ref[at, :], weights[part])
            if part < 3:
                proj_ref[part, at, :] = product.astype(bf16)
            else:
                gate_ref[at, :] = product
            return carry
        lax.fori_loop(0, rows // 256, some, 0)

    @pl.when(me > 0)
    def _():
        for s in range(seqs):
            halo_copy(s).wait_recv()
        value = halo_in[...].reshape(seqs * pad, dim).astype(f32)
        scale = lax.rsqrt(jnp.mean(value * value, axis=-1, keepdims=True) + norm_eps)
        normed = (value * scale * gain).astype(bf16)
        for part in range(3):
            halo_ref[part] = mm(normed, weights[part]).astype(bf16)

    @pl.when(me == 0)
    def _():
        halo_ref[...] = jnp.zeros_like(halo_ref)

    @pl.when(me < seq_devices - 1)
    def _():
        for s in range(seqs):
            halo_copy(s).wait_send()


def first(seq_devices, seqs, tokens, gain, w_query, w_key, w_value, w_gate, w_beta, bias, live):
    rows, dim = tokens.shape
    width, heads = w_query.shape[1], w_beta.shape[1]
    pad = 16
    vmem, hbm = pl.BlockSpec(memory_space=pltpu.VMEM), pl.BlockSpec(memory_space=pltpu.HBM)
    out_shape = [
        jax.ShapeDtypeStruct((rows, dim), bf16),
        jax.ShapeDtypeStruct((rows, 1), f32),
        jax.ShapeDtypeStruct((3, rows, width), bf16),
        jax.ShapeDtypeStruct((3, seqs * pad, width), bf16),
        jax.ShapeDtypeStruct((rows, width), f32),
        jax.ShapeDtypeStruct((rows, heads), f32),
        jax.ShapeDtypeStruct((rows, heads), f32),
    ]
    return pl.pallas_call(
        functools.partial(first_kernel, seq_devices),
        in_specs=[vmem] * 5 + [hbm] * 4,
        out_specs=[vmem] * len(out_shape),
        out_shape=out_shape,
        scratch_shapes=[
            pltpu.VMEM((4, dim, width), bf16),
            pltpu.VMEM((seqs, pad, dim), bf16),
            pltpu.SemaphoreType.DMA((4,)),
            pltpu.SemaphoreType.DMA((seqs,)),
            pltpu.SemaphoreType.DMA((seqs,)),
        ],
        compiler_params=pltpu.CompilerParams(
            collective_id=7, has_side_effects=True, vmem_limit_bytes=62 << 20
        ),
        name="first_norm_projections",
    )(tokens, gain.reshape(1, dim), w_beta, bias.reshape(1, heads), live, w_query, w_key, w_value, w_gate)


def ceil_to(value, unit):
    return -(-value // unit) * unit


class Line:
    def __init__(self, devices, part, ups, downs, out, sems, chunk, lag, whole, done=None):
        self.done = done
        self.n, self.part, self.ups, self.downs, self.out, self.sems = devices, part, ups, downs, out, sems
        self.chunk, self.lag, self.whole = chunk, lag, whole
        self.chunks = part.shape[0] // chunk
        self.me = lax.axis_index("tp")
        self.pieces = 1 if whole else devices
        self.width = part.shape[1] // self.pieces
        self.last = (devices - 2) * lag
        self.steps = self.chunks + self.last

    @staticmethod
    def scratch(rows, cols, devices, chunk, whole):
        count = (rows // chunk) * (1 if whole else devices)
        return [pltpu.VMEM((rows, cols), bf16)] * 2 + [pltpu.SemaphoreType.DMA((4, count))]

    def copy(self, source, way, k, piece):
        at = (pl.ds(pl.multiple_of(k * self.chunk, self.chunk), self.chunk), slice(piece * self.width, (piece + 1) * self.width))
        target = self.ups if way == 0 else self.downs
        sem = k * self.pieces + piece
        other = self.me + 1 if way == 0 else self.me - 1
        return pltpu.make_async_remote_copy(
            src_ref=source.at[at], dst_ref=target.at[at],
            send_sem=self.sems.at[way, sem], recv_sem=self.sems.at[2 + way, sem],
            device_id={"tp": other}, device_id_type=MESH,
        )

    def begin(self, first, count):
        for way, end in ((0, 0), (1, self.n - 1)):
            @pl.when(self.me == end)
            def _():
                def send(k, carry):
                    for piece in range(self.pieces) if way else reversed(range(self.pieces)):
                        if self.whole or piece != end:
                            self.copy(self.part, way, k, piece).start()
                    return carry
                lax.fori_loop(first, first + count, send, 0)

    def forward(self, way, k):
        me, n = self.me, self.n
        held = self.ups if way == 0 else self.downs
        rows = pl.ds(pl.multiple_of(k * self.chunk, self.chunk), self.chunk)
        for piece in range(self.pieces):
            if self.whole:
                gets, goes = None, me < n - 1 if way == 0 else me > 0
            else:
                gets, goes = (piece >= me, piece > me) if way == 0 else (piece <= me, piece < me)
            cols = slice(piece * self.width, (piece + 1) * self.width)

            def take():
                self.copy(self.part, way, k, piece).wait_recv()

                @pl.when(goes)
                def _():
                    held[rows, cols] = (held[rows, cols].astype(f32) + self.part[rows, cols].astype(f32)).astype(bf16)
                    self.copy(held, way, k, piece).start()

            if gets is None:
                take()
            else:
                pl.when(gets)(take)

    def give(self, k, total):
        if self.done is None:
            self.out[pl.ds(pl.multiple_of(k * self.chunk, self.chunk), self.chunk), :] = total
        else:
            self.done(k, total)

    def finish(self, k):
        me, n = self.me, self.n
        rows = pl.ds(pl.multiple_of(k * self.chunk, self.chunk), self.chunk)
        if self.whole:
            @pl.when(me == 0)
            def _():
                self.give(k, self.part[rows, :].astype(f32) + self.downs[rows, :].astype(f32))

            @pl.when(me == n - 1)
            def _():
                self.give(k, self.part[rows, :].astype(f32) + self.ups[rows, :].astype(f32))

            @pl.when((me > 0) & (me < n - 1))
            def _():
                both = self.ups[rows, :].astype(f32) - self.part[rows, :].astype(f32)
                self.give(k, both + self.downs[rows, :].astype(f32))
        else:
            for piece in range(n):
                @pl.when(me == piece)
                def _():
                    cols = slice(piece * self.width, (piece + 1) * self.width)
                    total = self.part[rows, cols].astype(f32)
                    if piece > 0:
                        total = total + self.ups[rows, cols].astype(f32)
                    if piece < n - 1:
                        total = total + self.downs[rows, cols].astype(f32)
                    self.give(k, total)

    def step(self, i):
        me, n = self.me, self.n
        up = i - (me - 1) * self.lag
        down = i - (n - 2 - me) * self.lag

        @pl.when((me > 0) & (up >= 0) & (up < self.chunks))
        def _():
            self.forward(0, up)

        @pl.when((me < n - 1) & (down >= 0) & (down < self.chunks))
        def _():
            self.forward(1, down)

        done = i - self.last

        @pl.when((done >= 0) & (done < self.chunks))
        def _():
            self.finish(done)

    def end(self):
        def drain(k, carry):
            for way in range(2):
                for piece in range(self.pieces):
                    if self.whole:
                        goes = self.me < self.n - 1 if way == 0 else self.me > 0
                    else:
                        goes = piece > self.me if way == 0 else piece < self.me

                    @pl.when(goes)
                    def _():
                        self.copy(self.part, way, k, piece).wait_send()
            return carry
        lax.fori_loop(0, self.chunks, drain, 0)


class Scatter:
    def __init__(self, devices, jobs, held, gots, outs, sends, recvs, unit, lag, ahead, wait):
        self.ahead, self.wait = ahead, wait
        self.n, self.jobs, self.held, self.gots, self.outs = devices, jobs, held, gots, outs
        self.sends, self.recvs, self.unit, self.lag = sends, recvs, unit, lag
        self.bits = devices.bit_length() - 1
        self.me = lax.axis_index("seq")
        tokens = jobs[0][1].shape[0]
        self.block = jobs[0][0].shape[0] * jobs[0][0].shape[1] // tokens // devices
        self.turned = self.block % 128 != 0
        self.chunks = sum(size for _, _, _, size in jobs) // unit
        self.steps = self.chunks + wait + (self.bits - 2) * lag

    @staticmethod
    def scratch(devices, rows, cols, unit):
        chunks, bits, block = cols // unit, devices.bit_length() - 1, rows // devices
        shapes = [pltpu.VMEM((chunks, devices // 2, block, unit), bf16)]
        shapes += [pltpu.VMEM((chunks, devices >> (s + 1), block, unit), bf16) for s in range(bits)]
        return shapes + [pltpu.SemaphoreType.DMA((bits, chunks))] * 2

    def power(self, stage, chunk):
        if stage == 0:
            return 1
        odd = lax.rem(chunk, 2)
        return odd * (1 << (self.bits - stage)) + (1 - odd) * (1 << stage)

    def bit(self, stage, chunk):
        return lax.rem(self.me // self.power(stage, chunk), 2)

    def partner(self, stage, chunk):
        return self.me + (1 - 2 * self.bit(stage, chunk)) * self.power(stage, chunk)

    def start_of_kept(self, stage, chunk):
        at = 0
        for s in range(1, stage):
            at = at + self.bit(s, chunk) * (self.n >> (s + 1))
        return at

    def copy(self, stage, chunk):
        count = self.n >> (stage + 1)
        if stage == 0:
            at = 0
        else:
            at = self.start_of_kept(stage, chunk) + (1 - self.bit(stage, chunk)) * count
        return pltpu.make_async_remote_copy(
            src_ref=self.held.at[chunk, pl.ds(at, count)], dst_ref=self.gots[stage].at[chunk],
            send_sem=self.sends.at[stage, chunk], recv_sem=self.recvs.at[stage, chunk],
            device_id={"seq": self.partner(stage, chunk)}, device_id_type=MESH,
        )

    def products(self, chunk, core, use):
        low = 0
        for x, y, start, size in self.jobs:
            count = size // self.unit

            @pl.when((chunk >= low) & (chunk < low + count))
            def _():
                right = y[:, pl.ds(pl.multiple_of(start + (chunk - low) * self.unit, 128), self.unit)]

                def one(j, carry):
                    target = core
                    for s in range(1, self.bits):
                        target = target + lax.rem(j // (self.n >> (s + 1)), 2) * self.power(s, chunk)
                    mine = pl.ds(pl.multiple_of(target * self.block, self.block), self.block)
                    use(j, mm(x[mine, :], right) if self.turned else mm(x[:, mine], right, 0, 0))
                    return carry
                lax.fori_loop(0, self.n // 2, one, 0, unroll=True)
            low += count

    def produce(self, i):
        core = lax.rem(self.me, 2)

        @pl.when(i < self.chunks)
        def _():
            def put(j, value):
                self.held[i, j] = value.astype(bf16)
            self.products(i, 1 - core, put)
            self.copy(0, i).start()

        first = i - 1

        @pl.when((first >= 0) & (first < self.chunks))
        def _():
            self.copy(0, first).wait()

            def put(j, value):
                self.held[first, j] = (value + self.gots[0][first, j].astype(f32)).astype(bf16)
            self.products(first, core, put)
            self.copy(1, first).start()

    def consume(self, i):
        for stage in range(1, self.bits):
            chunk = i - (stage - 1) * self.lag

            @pl.when((chunk >= 0) & (chunk < self.chunks))
            def _():
                self.copy(stage, chunk).wait()
                count = self.n >> (stage + 1)
                base = self.start_of_kept(stage + 1, chunk)
                if stage < self.bits - 1:
                    for j in range(count):
                        self.held[chunk, base + j] = (
                            self.held[chunk, base + j].astype(f32) + self.gots[stage][chunk, j].astype(f32)
                        ).astype(bf16)
                    self.copy(stage + 1, chunk).start()
                else:
                    low = 0
                    for (_, _, _, size), out in zip(self.jobs, self.outs):
                        size = size // self.unit

                        @pl.when((chunk >= low) & (chunk < low + size))
                        def _():
                            cols = pl.ds(pl.multiple_of((chunk - low) * self.unit, self.unit), self.unit)
                            total = self.held[chunk, base].astype(f32) + self.gots[stage][chunk, 0].astype(f32)
                            out[:, cols] = total.astype(out.dtype)
                        low += size

    def step(self, i):
        for turn in range(self.ahead):
            self.produce(i * self.ahead + turn)
        self.consume(i - self.wait)


def greet(seq_devices, tp_devices, over_seq, over_tp):
    seq, tp = lax.axis_index("seq"), lax.axis_index("tp")
    barrier = pltpu.get_barrier_semaphore()
    peers = 0
    if over_seq:
        peers = seq_devices.bit_length() - 1
        for b in range(peers):
            other = seq + (1 - 2 * lax.rem(seq // (1 << b), 2)) * (1 << b)
            pl.semaphore_signal(barrier, inc=1, device_id={"seq": other}, device_id_type=MESH)
    if over_tp:
        @pl.when(tp > 0)
        def _():
            pl.semaphore_signal(barrier, inc=1, device_id={"tp": tp - 1}, device_id_type=MESH)

        @pl.when(tp < tp_devices - 1)
        def _():
            pl.semaphore_signal(barrier, inc=1, device_id={"tp": tp + 1}, device_id_type=MESH)
        peers = peers + jnp.minimum(tp, 1) + jnp.minimum(tp_devices - 1 - tp, 1)
    pl.semaphore_wait(barrier, peers)


def combined_kernel(seq_devices, tp_devices, jobs, lines, unit, chunk, scatter_lag, line_lag, ahead, wait, *refs):
    refs = list(refs)

    def take(count):
        out = refs[:count]
        del refs[:count]
        return out

    bits = seq_devices.bit_length() - 1
    lefts = take(max([x for x, _ in jobs], default=-1) + 1)
    rights = take(len(jobs))
    parts = take(len(lines))
    job_outs = take(len(jobs))
    line_outs = take(len(lines))
    flows = []
    if jobs:
        held, *rest = take(1 + bits + 2)
        gots, (sends, recvs) = rest[:bits], rest[bits:]
        pairs = [(lefts[x], y, 0, y.shape[1]) for (x, _), y in zip(jobs, rights)]
        flows.append(Scatter(seq_devices, pairs, held, gots, job_outs, sends, recvs, unit, scatter_lag, ahead, wait))
    for part, out, whole in zip(parts, line_outs, lines):
        ups, downs, sems = take(3)
        flows.append(Line(tp_devices, part, ups, downs, out, sems, chunk, line_lag, whole))
    greet(seq_devices, tp_devices, len(jobs) > 0, len(lines) > 0)
    for flow in flows:
        if isinstance(flow, Line):
            flow.begin(0, flow.chunks)

    def step(i, carry):
        for flow in flows:
            flow.step(i)
        return carry
    lax.fori_loop(0, max(flow.steps for flow in flows), step, 0)
    for flow in flows:
        if isinstance(flow, Line):
            flow.end()


def combined(seq_devices, tp_devices, lefts, jobs, parts, lines, ident, unit=256, chunk=64, scatter_lag=2, line_lag=2, ahead=2, wait=3):
    jobs = [(x, jnp.pad(y, ((0, 0), (0, ceil_to(y.shape[1], unit) - y.shape[1])))) for x, y in jobs]
    out_shape, scratch = [], []
    for x, y in jobs:
        out_shape.append(jax.ShapeDtypeStruct((lefts[x].shape[1] // seq_devices, y.shape[1]), bf16))
    if jobs:
        columns = lefts[0].shape[1]
        if columns // seq_devices % 128:
            lefts = [left.T for left in lefts]
    for part, whole in zip(parts, lines):
        rows, cols = part.shape
        out_shape.append(jax.ShapeDtypeStruct((rows, cols if whole else cols // tp_devices), f32))
    if jobs:
        scratch += Scatter.scratch(seq_devices, columns, sum(y.shape[1] for _, y in jobs), unit)
    for part, whole in zip(parts, lines):
        scratch += Line.scratch(*part.shape, tp_devices, chunk, whole)
    vmem = pl.BlockSpec(memory_space=pltpu.VMEM)
    return pl.pallas_call(
        functools.partial(
            combined_kernel, seq_devices, tp_devices, [(x, None) for x, _ in jobs], lines, unit, chunk, scatter_lag, line_lag, ahead, wait
        ),
        in_specs=[vmem] * (len(lefts) + len(jobs) + len(parts)),
        out_specs=[vmem] * len(out_shape),
        out_shape=out_shape,
        scratch_shapes=scratch,
        compiler_params=pltpu.CompilerParams(
            collective_id=ident, has_side_effects=True, vmem_limit_bytes=62 << 20
        ),
        name="sums_%d" % ident,
    )(*lefts, *[y for _, y in jobs], *parts)


def small_sums_kernel(seq_devices, tp_devices, both_rows, vec_ref, rows_ref, seq_out, both_out, rows_out, got_seq, got_rows, total, sems):
    seq, tp = lax.axis_index("seq"), lax.axis_index("tp")
    barrier = pltpu.get_barrier_semaphore()
    peers = [("seq", lax.rem(seq + turn, seq_devices)) for turn in range(1, seq_devices)]
    peers += [("tp", lax.rem(tp + turn, tp_devices)) for turn in range(1, tp_devices)]
    for axis, other in peers:
        pl.semaphore_signal(barrier, inc=1, device_id={axis: other}, device_id_type=MESH)
    pl.semaphore_wait(barrier, len(peers))

    def remote(src, dst, at, axis, other):
        return pltpu.make_async_remote_copy(
            src_ref=src, dst_ref=dst, send_sem=sems.at[0, at], recv_sem=sems.at[1, at],
            device_id={axis: other}, device_id_type=MESH,
        )

    copies = []
    for turn in range(1, tp_devices):
        copies.append(remote(rows_ref, got_rows.at[turn], turn, "tp", lax.rem(tp + turn, tp_devices)))
    for turn in range(1, seq_devices):
        copies.append(remote(vec_ref, got_seq.at[turn], tp_devices + turn, "seq", lax.rem(seq + turn, seq_devices)))
    for copy in copies:
        copy.start()
    for copy in copies:
        copy.wait()
    rows_total, seq_total = rows_ref[...], vec_ref[...]
    for turn in range(1, tp_devices):
        rows_total = rows_total + got_rows[turn]
    for turn in range(1, seq_devices):
        seq_total = seq_total + got_seq[turn]
    rows_out[...] = rows_total
    split = vec_ref.shape[0] - both_rows
    seq_out[...] = seq_total[:split]
    total[...] = seq_total[split:]
    both_out[tp] = seq_total[split:]
    copies = []
    for turn in range(1, tp_devices):
        at = tp_devices + seq_devices + turn
        copies.append(remote(total, both_out.at[tp], at, "tp", lax.rem(tp + turn, tp_devices)))
    for copy in copies:
        copy.start()
    for copy in copies:
        copy.wait()


def small_sums(seq_devices, tp_devices, seq_rows, both_rows, rows):
    vec = jnp.concatenate([seq_rows, both_rows], axis=0)
    split, both = seq_rows.shape[0], both_rows.shape[0]
    vmem = pl.BlockSpec(memory_space=pltpu.VMEM)
    return pl.pallas_call(
        functools.partial(small_sums_kernel, seq_devices, tp_devices, both),
        in_specs=[vmem] * 2,
        out_specs=[vmem] * 3,
        out_shape=[
            jax.ShapeDtypeStruct((split, HEAD), f32),
            jax.ShapeDtypeStruct((tp_devices, both, HEAD), f32),
            jax.ShapeDtypeStruct(rows.shape, f32),
        ],
        scratch_shapes=[
            pltpu.VMEM((seq_devices,) + vec.shape, f32),
            pltpu.VMEM((tp_devices,) + rows.shape, f32),
            pltpu.VMEM((both, HEAD), f32),
            pltpu.SemaphoreType.DMA((2, 2 * tp_devices + seq_devices)),
        ],
        compiler_params=pltpu.CompilerParams(
            collective_id=6, has_side_effects=True, vmem_limit_bytes=62 << 20
        ),
        name="small_sums",
    )(vec, rows)


def as_rows(value, rows):
    flat = value.reshape(-1)
    return jnp.pad(flat, (0, rows * HEAD - flat.shape[0])).reshape(rows, HEAD)


def rows_of(k, size):
    return pl.ds(pl.multiple_of(k * size, size), size)


def put_own(out, at, value, axis_size):
    width = value.shape[1] // axis_size
    me = lax.axis_index("tp")
    for piece in range(axis_size):
        @pl.when(me == piece)
        def _():
            out[at, :] = value[:, piece * width : (piece + 1) * width]


def attention_ffn_kernel(
    tp_devices, chunk, lag, group,
    heads_ref, w_out_ref, tokens_ref, live_ref, gain_ref, w_gate_ref, w_up_ref, dhid_ref,
    normed_ref, dboth_ref, hid_ref, own_ref, hidden_ref, pulled_ref,
    part, ups, downs, sems,
):
    rows, dim = tokens_ref.shape
    ffn = w_gate_ref.shape[1]
    gap = dboth_ref.shape[1] // 2
    per = group // chunk
    if gap > ffn:
        dboth_ref[...] = jnp.zeros_like(dboth_ref)
    if hid_ref.shape[1] > ffn:
        hid_ref[:, ffn // 128 * 128 :] = jnp.zeros((rows, hid_ref.shape[1] - ffn // 128 * 128), bf16)

    def attn_done(k, total):
        at = rows_of(k, chunk)
        now = tokens_ref[at, :].astype(f32) + live_ref[at, :] * total
        hidden_ref[at, :] = now.astype(bf16)
        scale = lax.rsqrt(jnp.mean(now * now, axis=-1, keepdims=True) + norm_eps)
        normed_ref[at, :] = (now * scale * gain_ref[...]).astype(bf16)
        put_own(own_ref, at, now, tp_devices)

    line = Line(tp_devices, part, ups, downs, None, sems, chunk, lag, True, attn_done)

    def begin(q, carry):
        at = rows_of(q, 128)
        part[at, :] = mm(heads_ref[at, :], w_out_ref[...]).astype(bf16)
        return carry
    begin(0, 0)
    greet(1, tp_devices, False, True)
    line.begin(0, 128 // chunk)

    def rest(q, carry):
        begin(q, carry)
        line.begin(q * (128 // chunk), 128 // chunk)
        return carry
    lax.fori_loop(1, rows // 128, rest, 0)

    tile = 256
    full = ffn // tile
    feeds = -(-ffn // tile)
    items = feeds + dim // tile

    def feed(at, cols, up_cols):
        normed = normed_ref[at, :]
        gate = mm(normed, w_gate_ref[:, cols])
        up = mm(normed, w_up_ref[:, cols])
        sig = sigmoid(gate)
        act = gate * sig
        dhid = dhid_ref[at, cols].astype(f32)
        hid_ref[at, cols] = (act * up).astype(bf16)
        dboth_ref[at, cols] = (dhid * up * (sig * (1.0 + gate * (1.0 - sig)))).astype(bf16)
        dboth_ref[at, up_cols] = (dhid * act).astype(bf16)

    def item(q, w):
        at = rows_of(q, group)

        @pl.when(w < full)
        def _():
            start = pl.multiple_of(w * tile, tile)
            feed(at, pl.ds(start, tile), pl.ds(pl.multiple_of(gap + w * tile, 128), tile))

        if feeds > full:
            @pl.when(w == full)
            def _():
                feed(at, slice(full * tile, ffn), slice(gap + full * tile, gap + ffn))

        @pl.when((w >= feeds) & (w < items))
        def _():
            mine = rows_of(w - feeds, tile)
            total = mm(dboth_ref[at, 0:ffn], w_gate_ref[mine, :], 1, 1)
            total = total + mm(dboth_ref[at, gap : gap + ffn], w_up_ref[mine, :], 1, 1)
            pulled_ref[at, mine] = total.astype(bf16)

    first = line.last + per
    each = -(-items // per)
    groups = rows // group

    def lead(i, carry):
        line.step(i)
        return carry
    lax.fori_loop(0, first, lead, 0)

    def beside(i, carry):
        line.step(i)
        q, p = (i - first) // per, lax.rem(i - first, per)

        def work(w, carry):
            item(q, p * each + w)
            return carry
        lax.fori_loop(0, each, work, 0)
        return carry
    lax.fori_loop(first, first + per * (groups - 1), beside, 0)

    def tail(w, carry):
        item(groups - 1, w)
        return carry
    lax.fori_loop(0, items, tail, 0)
    line.end()


def attention_ffn(tp_devices, heads_out, w_out, tokens, live, gain, w_gate, w_up, dhid, chunk=32, lag=2, group=256):
    rows, dim = tokens.shape
    ffn = w_gate.shape[1]
    width = dim // tp_devices
    vmem = pl.BlockSpec(memory_space=pltpu.VMEM)
    out_shape = [
        jax.ShapeDtypeStruct((rows, dim), bf16),
        jax.ShapeDtypeStruct((rows, 2 * ceil_to(ffn, 128)), bf16),
        jax.ShapeDtypeStruct((rows, ceil_to(ffn, 256)), bf16),
        jax.ShapeDtypeStruct((rows, width), f32),
        jax.ShapeDtypeStruct((rows, dim), bf16),
        jax.ShapeDtypeStruct((rows, dim), bf16),
    ]
    return pl.pallas_call(
        functools.partial(attention_ffn_kernel, tp_devices, chunk, lag, group),
        in_specs=[vmem] * 8,
        out_specs=[vmem] * len(out_shape),
        out_shape=out_shape,
        scratch_shapes=[pltpu.VMEM((rows, dim), bf16)] + Line.scratch(rows, dim, tp_devices, chunk, True),
        compiler_params=pltpu.CompilerParams(
            collective_id=3, has_side_effects=True, vmem_limit_bytes=62 << 20
        ),
        name="attention_ffn",
    )(heads_out, w_out, tokens, live, gain.reshape(1, dim), w_gate, w_up, dhid)


def ffn_back_kernel(seq_devices, tp_devices, jobs, hid_at, unit, chunk, scatter_lag, line_lag, wait, lefts, *refs):
    refs = list(refs)

    def take(count):
        out = refs[:count]
        del refs[:count]
        return out

    bits = seq_devices.bit_length() - 1
    arrays = take(lefts)
    part, hidden_ref, cot_ref, live_ref, gain_ref, w_out_ref, w_down_hbm = take(7)
    outs = take(len(jobs))
    dattn_ref, done_ref, dheads_ref, dgain_ref, ffn_ref = take(5)
    held, *rest = take(1 + bits + 2)
    ups, downs, sems, w_down_ref, load_sem = take(5)
    load = pltpu.make_async_copy(w_down_hbm, w_down_ref, load_sem)
    load.start()
    rows, dim = part.shape

    def dnormed_done(k, total):
        at = rows_of(k, chunk)
        now = hidden_ref[at, :].astype(f32)
        scale = lax.rsqrt(jnp.mean(now * now, axis=-1, keepdims=True) + norm_eps)
        unit_rows = now * scale
        dgain_ref[...] += jnp.sum((total * unit_rows).reshape(-1, 8, dim), axis=0)
        scaled = total * gain_ref[...]
        grad = cot_ref[at, :].astype(f32) + scale * (
            scaled - unit_rows * jnp.mean(scaled * unit_rows, axis=-1, keepdims=True)
        )
        dattn_ref[at, :] = (live_ref[at, :] * grad).astype(bf16)
        put_own(done_ref, at, grad, tp_devices)

    pairs = [(arrays[x], arrays[y], start, size) for x, y, start, size in jobs]
    scatter = Scatter(seq_devices, pairs, held, rest[:bits], outs, rest[bits], rest[bits + 1], unit, scatter_lag, 1, wait)
    line = Line(tp_devices, part, ups, downs, None, sems, chunk, line_lag, True, dnormed_done)
    dgain_ref[...] = jnp.zeros_like(dgain_ref)
    greet(seq_devices, tp_devices, True, True)
    line.begin(0, line.chunks)
    per = 128 // chunk

    def step(i, carry):
        scatter.step(i)
        line.step(i)
        done = i - line.last

        @pl.when((done >= 0) & (done < line.chunks) & (lax.rem(done + line.chunks, per) == per - 1))
        def _():
            at = rows_of(done // per, 128)
            dheads_ref[at, :] = mm(dattn_ref[at, :], w_out_ref[...], 1, 1)

        @pl.when((i < line.chunks) & (lax.rem(i, per) == 1))
        def _():
            at = rows_of(i // per, 128)
            ffn_ref[at, :] = mm(arrays[hid_at][at, 0 : w_down_ref.shape[0]], w_down_ref[...]).astype(bf16)
        return carry
    load.wait()
    lax.fori_loop(0, max(scatter.steps, line.steps), step, 0)
    line.end()


def ffn_back(
    seq_devices, tp_devices, arrays, jobs, hid_at, part, hidden, cot, live, gain, w_out, w_down,
    unit=256, chunk=32, scatter_lag=4, line_lag=2, wait=5,
):
    rows, dim = part.shape
    if dim // seq_devices % 128:
        turned = [arrays[x].T for x, _, _, _ in jobs]
        jobs = [(len(arrays) + at, y, start, size) for at, (_, y, start, size) in enumerate(jobs)]
        arrays = arrays + turned
    vmem = pl.BlockSpec(memory_space=pltpu.VMEM)
    out_shape = [jax.ShapeDtypeStruct((dim // seq_devices, size), bf16) for _, _, _, size in jobs]
    out_shape += [
        jax.ShapeDtypeStruct((rows, dim), bf16),
        jax.ShapeDtypeStruct((rows, dim // tp_devices), f32),
        jax.ShapeDtypeStruct((rows, w_out.shape[0]), f32),
        jax.ShapeDtypeStruct((8, dim), f32),
        jax.ShapeDtypeStruct((rows, dim), bf16),
    ]
    scratch = Scatter.scratch(seq_devices, dim, sum(size for _, _, _, size in jobs), unit)
    scratch += Line.scratch(rows, dim, tp_devices, chunk, True)
    scratch += [pltpu.VMEM(w_down.shape, bf16), pltpu.SemaphoreType.DMA(())]
    return pl.pallas_call(
        functools.partial(
            ffn_back_kernel, seq_devices, tp_devices, jobs, hid_at, unit, chunk, scatter_lag, line_lag, wait, len(arrays)
        ),
        in_specs=[vmem] * (len(arrays) + 6) + [pl.BlockSpec(memory_space=pltpu.HBM)],
        out_specs=[vmem] * len(out_shape),
        out_shape=out_shape,
        scratch_shapes=scratch,
        compiler_params=pltpu.CompilerParams(
            collective_id=4, has_side_effects=True, vmem_limit_bytes=62 << 20
        ),
        name="ffn_back",
    )(*arrays, part, hidden, cot, live, gain.reshape(1, dim), w_out, w_down)


def on_device(
    tokens,
    seq_lengths,
    norm_gain,
    w_query,
    w_key,
    w_value,
    w_gate,
    w_beta,
    beta_bias,
    conv_weight,
    out_gain,
    w_out,
    ffn_gain,
    w_ffn_gate,
    w_ffn_up,
    w_ffn_down,
    cotangent,
):
    seqs_here, local_len, model_dim = tokens.shape
    row_count = seqs_here * local_len
    heads_here = w_beta.shape[1]
    local_width = w_query.shape[1]
    halo_pad = 16
    seq_index = lax.axis_index("seq")
    seq_devices = lax.axis_size("seq")
    tp_index = lax.axis_index("tp")
    slice_width = model_dim // lax.axis_size("tp")
    positions = seq_index * local_len + jnp.arange(local_len, dtype=jnp.int32)
    live_rows = (positions[None, :] < seq_lengths[:, None]).astype(f32).reshape(row_count, 1)
    tokens_flat = tokens.reshape(row_count, model_dim)
    grad_low = cotangent.reshape(row_count, model_dim)
    normed_one, rstd_one, proj, halo, gate_pre, beta_val, slope = first(
        seq_devices, seqs_here, tokens_flat, norm_gain, w_query, w_key, w_value, w_gate, w_beta, beta_bias, live_rows
    )
    w_proj = jnp.concatenate([w_query, w_key, w_value], axis=1)
    proj_seq = proj.reshape(3, seqs_here, local_len, local_width)
    halo_rows = halo.reshape(3, seqs_here, halo_pad, local_width)
    beta_seq = beta_val.reshape(seqs_here, local_len, heads_here)
    slope = slope.reshape(seqs_here, local_len, heads_here)
    gate_seq = gate_pre.reshape(seqs_here, local_len, local_width)

    tri, keep, move, offset = delta_local(proj_seq, halo_rows, conv_weight, beta_seq)
    chains = seqs_here * heads_here
    flat = (chains, HEAD, HEAD)
    deep = (seqs_here, heads_here, HEAD, HEAD)
    state_in, moves, norms, dffn_hidden = exchange(
        seq_devices, move.reshape(flat), offset.reshape(flat), False, grad_low, w_ffn_down
    )
    state_in = state_in.reshape(deep)
    mixed, fresh, heads_seq = delta_out(keep, state_in, gate_seq, out_gain)
    heads_out = heads_seq.reshape(row_count, local_width)

    tp_devices = lax.axis_size("tp")
    sums = functools.partial(combined, seq_devices, tp_devices)
    normed_two, dffn_both, ffn_hidden, hidden_own, hidden_low, dnormed_part_two = attention_ffn(
        tp_devices, heads_out, w_out, tokens_flat, live_rows, ffn_gain, w_ffn_gate, w_ffn_up, dffn_hidden
    )
    ffn_width = w_ffn_gate.shape[1]
    ffn_pad = ffn_hidden.shape[1]
    early = 256
    dw_both, dw_down_early, dattn, grad_own, dheads, dffn_gain, ffn_part = ffn_back(
        seq_devices,
        tp_devices,
        [normed_two, grad_low, dffn_both, ffn_hidden],
        [(0, 2, 0, dffn_both.shape[1]), (1, 3, 0, early)],
        3,
        dnormed_part_two,
        hidden_low,
        grad_low,
        live_rows,
        ffn_gain,
        w_out,
        w_ffn_down,
    )
    ffn_gain_term = lax.dynamic_slice_in_dim(jnp.sum(dffn_gain, axis=0), tp_index * slice_width, slice_width, 0)
    ffn_slice = lax.psum_scatter(ffn_part, "tp", scatter_dimension=1, tiled=True)
    dheads = dheads.reshape(seqs_here, local_len, local_width)

    dmixed, dgate_seq, dstate, dgain_parts = head_back(dheads, mixed, gate_seq, out_gain, keep)
    dout_gain = jnp.sum(dgain_parts, axis=(0, 1))
    dgate_pre = dgate_seq.reshape(row_count, local_width)
    (state_grad,) = exchange(seq_devices, moves, dstate.reshape(flat), True)
    dproj_seq, edges, dconv_parts, dbeta_seq = delta_back(
        proj_seq, halo_rows, conv_weight, beta_seq, slope, tri, fresh, state_in, state_grad.reshape(deep), dmixed
    )
    dbeta_pre = dbeta_seq.reshape(row_count, heads_here)
    dbias = jnp.sum(dbeta_pre.astype(f32), axis=0)
    halo_grad = from_behind(edges[:, :halo_pad], "seq", -1)
    last_rows = (edges[:, halo_pad:] + halo_grad).astype(bf16)
    dproj_low = jnp.concatenate([dproj_seq[:, : local_len - halo_pad], last_rows], axis=1)
    dproj_low = dproj_low.reshape(row_count, 3 * local_width)
    dconv = jnp.sum(dconv_parts, axis=0)

    dnormed_part = (
        dot_right(dproj_low, w_proj) + dot_right(dgate_pre, w_gate) + dot_right(dbeta_pre, w_beta)
    )
    dense_right = jnp.concatenate([dproj_low, dgate_pre, dbeta_pre], axis=1)
    dnormed_part, ffn_slice = lax.optimization_barrier((dnormed_part.astype(bf16), ffn_slice))
    dw_down, dw_first, dw_out, dnormed_one = sums(
        [grad_low, normed_one, dattn],
        [(0, ffn_hidden[:, early:]), (1, dense_right), (2, heads_out)],
        [dnormed_part],
        [False],
        5,
        chunk=32,
        ahead=1,
        wait=5,
        scatter_lag=4,
    )

    def own_slice(value):
        return lax.dynamic_slice_in_dim(value, tp_index * slice_width, slice_width, value.ndim - 1)

    out_tokens = (hidden_own + ffn_slice.astype(f32)).astype(bf16).reshape(
        seqs_here, local_len, slice_width
    )
    inputs_slice = own_slice(tokens_flat).astype(f32)
    scaled_one = dnormed_one * own_slice(norm_gain)
    gain_term = jnp.sum(dnormed_one * inputs_slice * rstd_one, axis=0)
    conv_rows = dconv.size // HEAD
    bias_rows = jnp.pad(dbias.reshape(1, heads_here), ((0, 7), (0, HEAD - heads_here)))
    slice_rows = slice_width // HEAD
    both_rows = ceil_to(2 * slice_rows + 2, 8)
    both = as_rows(
        jnp.concatenate([ffn_gain_term, gain_term, dout_gain, norms[0]]), both_rows
    )
    seq_total, both_total, row_total = small_sums(
        seq_devices,
        tp_devices,
        jnp.concatenate([dconv.reshape(conv_rows, HEAD), bias_rows], axis=0),
        both,
        as_rows(jnp.sum(scaled_one * inputs_slice, axis=-1), ceil_to(row_count // HEAD, 8)),
    )
    row_dot = (row_total.reshape(-1)[:row_count] / model_dim).reshape(row_count, 1)
    grad_in = grad_own + rstd_one * scaled_one - inputs_slice * rstd_one**3 * row_dot
    tokens_grad = grad_in.reshape(seqs_here, local_len, slice_width)
    ffn_gain_grad = both_total[:, :slice_rows].reshape(model_dim)
    gain_grad = both_total[:, slice_rows : 2 * slice_rows].reshape(model_dim)
    head_total = jnp.sum(both_total[:, 2 * slice_rows : 2 * slice_rows + 2], axis=0)
    lw = local_width

    def wide(value):
        return value.astype(f32)

    return (
        out_tokens,
        tokens_grad,
        gain_grad,
        wide(dw_first[:, :lw]),
        wide(dw_first[:, lw : 2 * lw]),
        wide(dw_first[:, 2 * lw : 3 * lw]),
        wide(dw_first[:, 3 * lw : 4 * lw]),
        wide(dw_first[:, 4 * lw : 4 * lw + heads_here]),
        seq_total[conv_rows, :heads_here],
        seq_total[:conv_rows].reshape(dconv.shape),
        head_total[0],
        wide(dw_out[:, :lw].T),
        ffn_gain_grad,
        wide(dw_both[:, :ffn_width]),
        wide(dw_both[:, dffn_both.shape[1] // 2 :][:, :ffn_width]),
        wide(jnp.concatenate([dw_down_early[:, :early], dw_down[:, : ffn_width - early]], axis=1).T),
        head_total[1, 0] / (seqs_here * HEADS),
    )


def solution(mesh):
    in_specs = (
        P(None, "seq", None),
        P(),
        P(),
        P(None, "tp"),
        P(None, "tp"),
        P(None, "tp"),
        P(None, "tp"),
        P(None, "tp"),
        P("tp"),
        P(None, None, "tp"),
        P(),
        P("tp", None),
        P(),
        P(None, "tp"),
        P(None, "tp"),
        P("tp", None),
        P(None, "seq", None),
    )
    out_specs = (
        P(None, "seq", "tp"),
        P(None, "seq", "tp"),
        P(),
        P("seq", "tp"),
        P("seq", "tp"),
        P("seq", "tp"),
        P("seq", "tp"),
        P("seq", "tp"),
        P("tp"),
        P(None, None, "tp"),
        P(),
        P("tp", "seq"),
        P(),
        P("seq", "tp"),
        P("seq", "tp"),
        P("tp", "seq"),
        P(),
    )
    return jax.shard_map(
        on_device, mesh=mesh, in_specs=in_specs, out_specs=out_specs, check_vma=False
    )
```

```python
import functools

import jax
import jax.numpy as jnp
from jax import lax
from jax.experimental import pallas as pl
from jax.experimental.pallas import tpu as pltpu
from jax.sharding import PartitionSpec as P

HEADS = 16
HEAD = 128

norm_eps = 1e-06
f32 = jnp.float32
bf16 = jnp.bfloat16
MESH = pl.DeviceIdType.MESH
VM = pltpu.VMEM


def mm(left, right, contract_left=1, contract_right=0):
    return lax.dot_general(
        left.astype(bf16),
        right.astype(bf16),
        (((contract_left,), (contract_right,)), ((), ())),
        preferred_element_type=f32,
    )


def from_behind(block, axis, distance):
    devices = range(lax.axis_size(axis))
    route = [(i - distance, i) for i in devices if i - distance in devices]
    return lax.ppermute(block, axis, route)


def sigmoid(value):
    return 1.0 / (1.0 + jnp.exp(-value))


def silu_grad(value):
    sigmoid_val = sigmoid(value)
    return sigmoid_val * (1.0 + value * (1.0 - sigmoid_val))


def dot_left(left, right):
    return mm(left, right, 0, 0)


def dot_right(left, right):
    return mm(left, right, 1, 1)


def strict_lower(size):
    rows = lax.broadcasted_iota(jnp.int32, (size, size), 0)
    cols = lax.broadcasted_iota(jnp.int32, (size, size), 1)
    return rows > cols, rows >= cols, rows ^ cols


def unit_lower_inverses(lows, apart):
    size = lows[0].shape[0]
    inverses = [jnp.where(apart == 0, 1.0, 0.0) - jnp.where(apart == 1, low, 0.0) for low in lows]
    step = 2
    while step < size:
        pair = (apart >= step) & (apart < 2 * step)
        between = [jnp.where(pair, low, 0.0).astype(bf16) for low in lows]
        inner = [inverse.astype(bf16) for inverse in inverses]
        right = [mm(left, at) for left, at in zip(between, inner)]
        inverses = [inverse - mm(at, value) for inverse, at, value in zip(inverses, inner, right)]
        step *= 2
    return inverses


def conv_silu(ext_ref, col, conv_ref, part, lane, length, taps, pad):
    summed = None
    for tap in range(taps):
        term = conv_ref[part, tap : tap + 1, lane] * ext_ref[pl.ds(pad - taps + 1 + tap, length), col]
        summed = term if summed is None else summed + term
    return summed


def delta_local_kernel(heads, taps, together, proj_ref, halo_ref, conv_ref, beta_ref, tri_ref, keep_ref, move_ref, offset_ref, ext_ref):
    length = proj_ref.shape[2]
    width = heads * HEAD
    pad = halo_ref.shape[2]
    for part in range(3):
        col = slice(part * width, (part + 1) * width)
        ext_ref[0:pad, col] = halo_ref[part, 0].astype(f32)
        ext_ref[pad : pad + length, col] = proj_ref[part, 0].astype(f32)
    below, upto, apart = strict_lower(length)

    def act(part, h):
        lane = slice(h * HEAD, (h + 1) * HEAD)
        col = slice(part * width + h * HEAD, part * width + (h + 1) * HEAD)
        summed = conv_silu(ext_ref, col, conv_ref, part, lane, length, taps, pad)
        return summed * sigmoid(summed)

    def unit(value):
        return value * lax.rsqrt(jnp.sum(value * value, axis=-1, keepdims=True) + norm_eps)

    for first_head in range(0, heads, together):
        some = range(first_head, min(first_head + together, heads))
        queries = [unit(act(0, h)).astype(bf16) for h in some]
        keys = [unit(act(1, h)).astype(bf16) for h in some]
        values = [act(2, h).astype(bf16) for h in some]
        betas = [beta_ref[0, :, h : h + 1] for h in some]
        lows = [jnp.where(below, beta * mm(key, key, 1, 1), 0.0) for beta, key in zip(betas, keys)]
        inverses = unit_lower_inverses(lows, apart)
        for h, query, key, value, beta, inverse in zip(some, queries, keys, values, betas, inverses):
            inverse = inverse.astype(bf16)
            targets = jnp.concatenate([beta * key.astype(f32), beta * value.astype(f32)], axis=1)
            solved_low = mm(inverse, targets).astype(bf16)
            scores = jnp.where(upto, mm(query, key, 1, 1), 0.0).astype(bf16)
            passed = mm(scores, solved_low)
            moved = mm(key, solved_low, 0, 0)
            tri_ref[0, h] = inverse
            keep_ref[0, h, :, 0:HEAD] = (query.astype(f32) - passed[:, :HEAD]).astype(bf16)
            keep_ref[0, h, :, HEAD : 2 * HEAD] = passed[:, HEAD:].astype(bf16)
            keep_ref[0, h, :, 2 * HEAD :] = solved_low
            move_ref[0, h] = (-moved[:, :HEAD]).astype(bf16)
            offset_ref[0, h] = moved[:, HEAD:].astype(bf16)


def delta_local(proj, halo, conv_weight, beta, together=4):
    _, seqs, length, width = proj.shape
    width3 = 3 * width
    heads = beta.shape[2]
    taps = conv_weight.shape[1]
    pad = halo.shape[2]

    def whole(shape):
        return pl.BlockSpec((1,) + shape, lambda s: (s,) + (0,) * len(shape))

    return pl.pallas_call(
        functools.partial(delta_local_kernel, heads, taps, together),
        grid=(seqs,),
        in_specs=[
            pl.BlockSpec((3, 1, length, width), lambda s: (0, s, 0, 0)),
            pl.BlockSpec((3, 1, pad, width), lambda s: (0, s, 0, 0)),
            pl.BlockSpec(conv_weight.shape, lambda s: (0, 0, 0)),
            whole((length, heads)),
        ],
        out_specs=[
            whole((heads, length, length)),
            whole((heads, length, 4 * HEAD)),
            whole((heads, HEAD, HEAD)),
            whole((heads, HEAD, HEAD)),
        ],
        out_shape=[
            jax.ShapeDtypeStruct((seqs, heads, length, length), bf16),
            jax.ShapeDtypeStruct((seqs, heads, length, 4 * HEAD), bf16),
            jax.ShapeDtypeStruct((seqs, heads, HEAD, HEAD), bf16),
            jax.ShapeDtypeStruct((seqs, heads, HEAD, HEAD), bf16),
        ],
        scratch_shapes=[pltpu.VMEM((pad + length, width3), f32)],
        compiler_params=pltpu.CompilerParams(vmem_limit_bytes=62 << 20),
        name="delta_local",
    )(proj, halo, conv_weight, beta)


def exchange_kernel(devices, chains, backward, *refs):
    if backward:
        move_all, offset_in, state_out, offset_all, states, send_one, recv_one, send_two, recv_two = refs
    else:
        (move_in, offset_in, cot_hbm, w_down_hbm, state_out, move_all, norm_out, dhid_ref, offset_all, states,
         send_zero, recv_zero, send_one, recv_one, send_two, recv_two, cot_ref, w_down_ref, load_sem) = refs
        loads = [
            pltpu.make_async_copy(cot_hbm, cot_ref, load_sem.at[0]),
            pltpu.make_async_copy(w_down_hbm, w_down_ref, load_sem.at[1]),
        ]
        for load in loads:
            load.start()
    me = lax.axis_index("seq")
    barrier = pltpu.get_barrier_semaphore()
    for turn in range(1, devices):
        pl.semaphore_signal(
            barrier, inc=1, device_id={"seq": lax.rem(me + turn, devices)}, device_id_type=MESH
        )
    pl.semaphore_wait(barrier, devices - 1)

    def remote(src, dst, send, recv, device):
        return pltpu.make_async_remote_copy(
            src_ref=src, dst_ref=dst, send_sem=send, recv_sem=recv,
            device_id={"seq": device}, device_id_type=MESH,
        )

    def send_maps(chain):
        if not backward:
            remote(move_in.at[chain], move_all.at[me], send_zero.at[chain], recv_zero.at[me], chain).start()
        remote(offset_in.at[chain], offset_all.at[me], send_one.at[chain], recv_one.at[me], chain).start()

    for chain in range(chains):
        @pl.when(me != chain)
        def _():
            send_maps(chain)

        @pl.when(me == chain)
        def _():
            if not backward:
                move_all[chain] = move_in[chain]
            offset_all[chain] = offset_in[chain]

    order = range(devices - 1, -1, -1) if backward else range(devices)

    def beside(first, last):
        def rows(q, carry):
            at = pl.ds(pl.multiple_of(q * 128, 128), 128)
            dhid_ref[at, :] = mm(cot_ref[at, :], w_down_ref[...], 1, 1).astype(bf16)
            return carry
        lax.fori_loop(first, last, rows, 0)

    if not backward:
        for load in loads:
            load.wait()
        blocks = dhid_ref.shape[0] // 128
        beside(0, blocks // 2)

    @pl.when(me < chains)
    def _():
        state = jnp.zeros((HEAD, HEAD), f32)
        for at in order:
            states[at] = state.astype(bf16)

            @pl.when(me != at)
            def _():
                remote(states.at[at], state_out.at[me], send_two.at[at], recv_two.at[me], at).start()

            @pl.when(me == at)
            def _():
                state_out[me] = states[at]

            @pl.when(me != at)
            def _():
                if not backward:
                    remote(move_in.at[0], move_all.at[at], send_zero.at[0], recv_zero.at[at], at).wait_recv()
                remote(offset_in.at[0], offset_all.at[at], send_one.at[0], recv_one.at[at], at).wait_recv()

            state = state + mm(move_all[at], state, 0 if backward else 1, 0) + offset_all[at].astype(f32)
        if not backward:
            norm_out[...] = jnp.zeros_like(norm_out) + jnp.sqrt(jnp.sum(state * state, keepdims=True))
        for at in range(devices):
            @pl.when(me != at)
            def _():
                remote(states.at[at], state_out.at[0], send_two.at[at], recv_two.at[0], at).wait_send()

    if not backward:
        @pl.when(me >= chains)
        def _():
            norm_out[...] = jnp.zeros_like(norm_out)

    if not backward:
        beside(blocks // 2, blocks)

    for chain in range(chains):
        @pl.when(me != chain)
        def _():
            if not backward:
                remote(move_in.at[chain], move_all.at[0], send_zero.at[chain], recv_zero.at[0], chain).wait_send()
            remote(offset_in.at[chain], offset_all.at[0], send_one.at[chain], recv_one.at[0], chain).wait_send()
            remote(states.at[0], state_out.at[chain], send_two.at[0], recv_two.at[chain], chain).wait_recv()


def exchange(devices, moves, offsets, backward, cot=None, w_down=None):
    chains = offsets.shape[0]
    square = (HEAD, HEAD)
    dma = pltpu.SemaphoreType.DMA
    vmem = pl.BlockSpec(memory_space=pltpu.VMEM)
    scratch = [
        pltpu.VMEM((devices,) + square, bf16),
        pltpu.VMEM((devices,) + square, bf16),
    ]
    if not backward:
        scratch += [dma((chains,)), dma((devices,))]
    scratch += [dma((chains,)), dma((devices,)), dma((devices,)), dma((chains,))]
    out_shape = [jax.ShapeDtypeStruct((chains,) + square, bf16)]
    extra = []
    if not backward:
        extra = [cot, w_down]
        scratch += [pltpu.VMEM(cot.shape, bf16), pltpu.VMEM(w_down.shape, bf16), dma((2,))]
        out_shape += [
            jax.ShapeDtypeStruct((devices,) + square, bf16),
            jax.ShapeDtypeStruct((8, HEAD), f32),
            jax.ShapeDtypeStruct((cot.shape[0], w_down.shape[0]), bf16),
        ]
    return pl.pallas_call(
        functools.partial(exchange_kernel, devices, chains, backward),
        in_specs=[vmem, vmem] + [pl.BlockSpec(memory_space=pltpu.HBM)] * len(extra),
        out_specs=[vmem] * len(out_shape),
        out_shape=out_shape,
        scratch_shapes=scratch,
        compiler_params=pltpu.CompilerParams(
            collective_id=2 if backward else 1, has_side_effects=True, vmem_limit_bytes=62 << 20
        ),
        name="states_back" if backward else "states_forward",
    )(moves, offsets, *extra)


def delta_out_kernel(heads, keep_ref, state_ref, gate_ref, gain_ref, out_ref, fresh_ref, heads_ref):
    for h in range(heads):
        lane = slice(h * HEAD, (h + 1) * HEAD)
        state = state_ref[0, h]
        mixed = keep_ref[0, h, :, HEAD : 2 * HEAD].astype(f32) + mm(keep_ref[0, h, :, 0:HEAD], state)
        fresh = keep_ref[0, h, :, 3 * HEAD :].astype(f32) - mm(keep_ref[0, h, :, 2 * HEAD : 3 * HEAD], state)
        rstd = lax.rsqrt(jnp.mean(mixed * mixed, axis=-1, keepdims=True) + norm_eps)
        gate = gate_ref[0, :, lane]
        out_ref[0, :, lane] = mixed
        fresh_ref[0, :, lane] = fresh.astype(bf16)
        heads_ref[0, :, lane] = (mixed * rstd * gain_ref[...] * (gate * sigmoid(gate))).astype(bf16)


def delta_out(keep, state, gate_pre, out_gain):
    seqs, heads, length, _ = keep.shape
    width = heads * HEAD

    def whole(shape):
        return pl.BlockSpec((1,) + shape, lambda s: (s,) + (0,) * len(shape))

    return pl.pallas_call(
        functools.partial(delta_out_kernel, heads),
        grid=(seqs,),
        in_specs=[
            whole((heads, length, 4 * HEAD)),
            whole((heads, HEAD, HEAD)),
            whole((length, width)),
            pl.BlockSpec((1, HEAD), lambda s: (0, 0)),
        ],
        out_specs=[whole((length, width))] * 3,
        out_shape=[
            jax.ShapeDtypeStruct((seqs, length, width), f32),
            jax.ShapeDtypeStruct((seqs, length, width), bf16),
            jax.ShapeDtypeStruct((seqs, length, width), bf16),
        ],
        compiler_params=pltpu.CompilerParams(vmem_limit_bytes=62 << 20),
        name="delta_out",
    )(keep, state, gate_pre, out_gain.reshape(1, HEAD))


def first_kernel(
    seq_devices, tokens_ref, gain_ref, w_beta_ref, bias_ref, live_ref, *refs
):
    (w_query, w_key, w_value, w_gate, normed_ref, rstd_ref, proj_ref, halo_ref, gate_ref, beta_ref, slope_ref,
     weights, halo_in, load_sem, send_sem, recv_sem) = refs
    rows, dim = tokens_ref.shape
    seqs, pad, _ = halo_in.shape
    length = rows // seqs
    me = lax.axis_index("seq")
    loads = [
        pltpu.make_async_copy(source, weights.at[at], load_sem.at[at])
        for at, source in enumerate((w_query, w_key, w_value, w_gate))
    ]
    for load in loads:
        load.start()
    barrier = pltpu.get_barrier_semaphore()

    @pl.when(me > 0)
    def _():
        pl.semaphore_signal(barrier, inc=1, device_id={"seq": me - 1}, device_id_type=MESH)

    @pl.when(me < seq_devices - 1)
    def _():
        pl.semaphore_signal(barrier, inc=1, device_id={"seq": me + 1}, device_id_type=MESH)

    gain = gain_ref[...]

    def norm(q, carry):
        at = pl.ds(pl.multiple_of(q * 128, 128), 128)
        value = tokens_ref[at, :].astype(f32)
        scale = lax.rsqrt(jnp.mean(value * value, axis=-1, keepdims=True) + norm_eps)
        rstd_ref[at, :] = scale
        normed_ref[at, :] = (value * scale * gain).astype(bf16)
        return carry
    lax.fori_loop(0, rows // 128, norm, 0)
    pl.semaphore_wait(barrier, jnp.minimum(me, 1) + jnp.minimum(seq_devices - 1 - me, 1))

    def halo_copy(s):
        return pltpu.make_async_remote_copy(
            src_ref=tokens_ref.at[pl.ds((s + 1) * length - pad, pad)], dst_ref=halo_in.at[s],
            send_sem=send_sem.at[s], recv_sem=recv_sem.at[s],
            device_id={"seq": me + 1}, device_id_type=MESH,
        )

    @pl.when(me < seq_devices - 1)
    def _():
        for s in range(seqs):
            halo_copy(s).start()

    sig = sigmoid(mm(normed_ref[...], w_beta_ref[...]) + bias_ref[...])
    beta = live_ref[...] * sig
    beta_ref[...] = beta
    slope_ref[...] = beta * (1.0 - sig)
    for part in range(4):
        loads[part].wait()

        def some(q, carry):
            at = pl.ds(pl.multiple_of(q * 256, 256), 256)
            product = mm(normed_ref[at, :], weights[part])
            if part < 3:
                proj_ref[part, at, :] = product.astype(bf16)
            else:
                gate_ref[at, :] = product
            return carry
        lax.fori_loop(0, rows // 256, some, 0)

    @pl.when(me > 0)
    def _():
        for s in range(seqs):
            halo_copy(s).wait_recv()
        value = halo_in[...].reshape(seqs * pad, dim).astype(f32)
        scale = lax.rsqrt(jnp.mean(value * value, axis=-1, keepdims=True) + norm_eps)
        normed = (value * scale * gain).astype(bf16)
        for part in range(3):
            halo_ref[part] = mm(normed, weights[part]).astype(bf16)

    @pl.when(me == 0)
    def _():
        halo_ref[...] = jnp.zeros_like(halo_ref)

    @pl.when(me < seq_devices - 1)
    def _():
        for s in range(seqs):
            halo_copy(s).wait_send()


def first(seq_devices, seqs, tokens, gain, w_query, w_key, w_value, w_gate, w_beta, bias, live):
    rows, dim = tokens.shape
    width, heads = w_query.shape[1], w_beta.shape[1]
    pad = 16
    vmem, hbm = pl.BlockSpec(memory_space=pltpu.VMEM), pl.BlockSpec(memory_space=pltpu.HBM)
    out_shape = [
        jax.ShapeDtypeStruct((rows, dim), bf16),
        jax.ShapeDtypeStruct((rows, 1), f32),
        jax.ShapeDtypeStruct((3, rows, width), bf16),
        jax.ShapeDtypeStruct((3, seqs * pad, width), bf16),
        jax.ShapeDtypeStruct((rows, width), f32),
        jax.ShapeDtypeStruct((rows, heads), f32),
        jax.ShapeDtypeStruct((rows, heads), f32),
    ]
    return pl.pallas_call(
        functools.partial(first_kernel, seq_devices),
        in_specs=[vmem] * 5 + [hbm] * 4,
        out_specs=[vmem] * len(out_shape),
        out_shape=out_shape,
        scratch_shapes=[
            pltpu.VMEM((4, dim, width), bf16),
            pltpu.VMEM((seqs, pad, dim), bf16),
            pltpu.SemaphoreType.DMA((4,)),
            pltpu.SemaphoreType.DMA((seqs,)),
            pltpu.SemaphoreType.DMA((seqs,)),
        ],
        compiler_params=pltpu.CompilerParams(
            collective_id=7, has_side_effects=True, vmem_limit_bytes=62 << 20
        ),
        name="first_norm_projections",
    )(tokens, gain.reshape(1, dim), w_beta, bias.reshape(1, heads), live, w_query, w_key, w_value, w_gate)


def ceil_to(value, unit):
    return -(-value // unit) * unit


class Line:
    def __init__(self, devices, part, ups, downs, out, sems, chunk, lag, whole, done=None):
        self.done = done
        self.n, self.part, self.ups, self.downs, self.out, self.sems = devices, part, ups, downs, out, sems
        self.chunk, self.lag, self.whole = chunk, lag, whole
        self.chunks = part.shape[0] // chunk
        self.me = lax.axis_index("tp")
        self.pieces = 1 if whole else devices
        self.width = part.shape[1] // self.pieces
        self.last = (devices - 2) * lag
        self.steps = self.chunks + self.last

    @staticmethod
    def scratch(rows, cols, devices, chunk, whole):
        count = (rows // chunk) * (1 if whole else devices)
        return [pltpu.VMEM((rows, cols), bf16)] * 2 + [pltpu.SemaphoreType.DMA((4, count))]

    def copy(self, source, way, k, piece):
        at = (pl.ds(pl.multiple_of(k * self.chunk, self.chunk), self.chunk), slice(piece * self.width, (piece + 1) * self.width))
        target = self.ups if way == 0 else self.downs
        sem = k * self.pieces + piece
        other = self.me + 1 if way == 0 else self.me - 1
        return pltpu.make_async_remote_copy(
            src_ref=source.at[at], dst_ref=target.at[at],
            send_sem=self.sems.at[way, sem], recv_sem=self.sems.at[2 + way, sem],
            device_id={"tp": other}, device_id_type=MESH,
        )

    def begin(self, first, count):
        for way, end in ((0, 0), (1, self.n - 1)):
            @pl.when(self.me == end)
            def _():
                def send(k, carry):
                    for piece in range(self.pieces) if way else reversed(range(self.pieces)):
                        if self.whole or piece != end:
                            self.copy(self.part, way, k, piece).start()
                    return carry
                lax.fori_loop(first, first + count, send, 0)

    def forward(self, way, k):
        me, n = self.me, self.n
        held = self.ups if way == 0 else self.downs
        rows = pl.ds(pl.multiple_of(k * self.chunk, self.chunk), self.chunk)
        for piece in range(self.pieces):
            if self.whole:
                gets, goes = None, me < n - 1 if way == 0 else me > 0
            else:
                gets, goes = (piece >= me, piece > me) if way == 0 else (piece <= me, piece < me)
            cols = slice(piece * self.width, (piece + 1) * self.width)

            def take():
                self.copy(self.part, way, k, piece).wait_recv()

                @pl.when(goes)
                def _():
                    held[rows, cols] = (held[rows, cols].astype(f32) + self.part[rows, cols].astype(f32)).astype(bf16)
                    self.copy(held, way, k, piece).start()

            if gets is None:
                take()
            else:
                pl.when(gets)(take)

    def give(self, k, total):
        if self.done is None:
            self.out[pl.ds(pl.multiple_of(k * self.chunk, self.chunk), self.chunk), :] = total
        else:
            self.done(k, total)

    def finish(self, k):
        me, n = self.me, self.n
        rows = pl.ds(pl.multiple_of(k * self.chunk, self.chunk), self.chunk)
        if self.whole:
            @pl.when(me == 0)
            def _():
                self.give(k, self.part[rows, :].astype(f32) + self.downs[rows, :].astype(f32))

            @pl.when(me == n - 1)
            def _():
                self.give(k, self.part[rows, :].astype(f32) + self.ups[rows, :].astype(f32))

            @pl.when((me > 0) & (me < n - 1))
            def _():
                both = self.ups[rows, :].astype(f32) - self.part[rows, :].astype(f32)
                self.give(k, both + self.downs[rows, :].astype(f32))
        else:
            for piece in range(n):
                @pl.when(me == piece)
                def _():
                    cols = slice(piece * self.width, (piece + 1) * self.width)
                    total = self.part[rows, cols].astype(f32)
                    if piece > 0:
                        total = total + self.ups[rows, cols].astype(f32)
                    if piece < n - 1:
                        total = total + self.downs[rows, cols].astype(f32)
                    self.give(k, total)

    def step(self, i):
        me, n = self.me, self.n
        up = i - (me - 1) * self.lag
        down = i - (n - 2 - me) * self.lag

        @pl.when((me > 0) & (up >= 0) & (up < self.chunks))
        def _():
            self.forward(0, up)

        @pl.when((me < n - 1) & (down >= 0) & (down < self.chunks))
        def _():
            self.forward(1, down)

        done = i - self.last

        @pl.when((done >= 0) & (done < self.chunks))
        def _():
            self.finish(done)

    def end(self):
        def drain(k, carry):
            for way in range(2):
                for piece in range(self.pieces):
                    if self.whole:
                        goes = self.me < self.n - 1 if way == 0 else self.me > 0
                    else:
                        goes = piece > self.me if way == 0 else piece < self.me

                    @pl.when(goes)
                    def _():
                        self.copy(self.part, way, k, piece).wait_send()
            return carry
        lax.fori_loop(0, self.chunks, drain, 0)


class Scatter:
    def __init__(self, devices, jobs, held, gots, outs, sends, recvs, unit, lag, ahead, wait):
        self.ahead, self.wait = ahead, wait
        self.n, self.jobs, self.held, self.gots, self.outs = devices, jobs, held, gots, outs
        self.sends, self.recvs, self.unit, self.lag = sends, recvs, unit, lag
        self.bits = devices.bit_length() - 1
        self.me = lax.axis_index("seq")
        self.block = jobs[0][0].shape[0] // devices
        self.chunks = sum(size for _, _, _, size in jobs) // unit
        self.steps = self.chunks + wait + (self.bits - 2) * lag

    @staticmethod
    def scratch(devices, rows, cols, unit):
        chunks, bits, block = cols // unit, devices.bit_length() - 1, rows // devices
        shapes = [pltpu.VMEM((chunks, devices // 2, block, unit), bf16)]
        shapes += [pltpu.VMEM((chunks, devices >> (s + 1), block, unit), bf16) for s in range(bits)]
        return shapes + [pltpu.SemaphoreType.DMA((bits, chunks))] * 2

    @staticmethod
    def turned(arrays, jobs, spaces):
        lefts = sorted({x for x, _, _, _ in jobs})
        for space, x in zip(spaces, lefts):
            def turn(j, carry):
                at = pl.ds(pl.multiple_of(j * 256, 256), 256)
                space[at, :] = arrays[x][:, at].T
                return carry
            lax.fori_loop(0, space.shape[0] // 256, turn, 0)
        return [(spaces[lefts.index(x)], arrays[y], start, size) for x, y, start, size in jobs]

    @staticmethod
    def spaces(arrays, jobs):
        return [pltpu.VMEM(arrays[x].shape[::-1], bf16) for x in sorted({x for x, _, _, _ in jobs})]

    def power(self, stage, chunk):
        if stage == 0:
            return 1
        odd = lax.rem(chunk, 2)
        return odd * (1 << (self.bits - stage)) + (1 - odd) * (1 << stage)

    def bit(self, stage, chunk):
        return lax.rem(self.me // self.power(stage, chunk), 2)

    def partner(self, stage, chunk):
        return self.me + (1 - 2 * self.bit(stage, chunk)) * self.power(stage, chunk)

    def start_of_kept(self, stage, chunk):
        at = 0
        for s in range(1, stage):
            at = at + self.bit(s, chunk) * (self.n >> (s + 1))
        return at

    def copy(self, stage, chunk):
        count = self.n >> (stage + 1)
        if stage == 0:
            at = 0
        else:
            at = self.start_of_kept(stage, chunk) + (1 - self.bit(stage, chunk)) * count
        return pltpu.make_async_remote_copy(
            src_ref=self.held.at[chunk, pl.ds(at, count)], dst_ref=self.gots[stage].at[chunk],
            send_sem=self.sends.at[stage, chunk], recv_sem=self.recvs.at[stage, chunk],
            device_id={"seq": self.partner(stage, chunk)}, device_id_type=MESH,
        )

    def products(self, chunk, core, use):
        low = 0
        for x, y, start, size in self.jobs:
            count = size // self.unit

            @pl.when((chunk >= low) & (chunk < low + count))
            def _():
                right = y[:, pl.ds(pl.multiple_of(start + (chunk - low) * self.unit, 128), self.unit)]

                values = []
                for j in range(self.n // 2):
                    target = core
                    for s in range(1, self.bits):
                        target = target + j // (self.n >> (s + 1)) % 2 * self.power(s, chunk)
                    mine = pl.ds(pl.multiple_of(target * self.block, self.block), self.block)
                    values.append(mm(x[mine, :], right))
                for j, value in enumerate(values):
                    use(j, value)
            low += count

    def produce(self, i):
        core = lax.rem(self.me, 2)

        @pl.when(i < self.chunks)
        def _():
            def put(j, value):
                self.held[i, j] = value.astype(bf16)
            self.products(i, 1 - core, put)
            self.copy(0, i).start()

        first = i - 1

        @pl.when((first >= 0) & (first < self.chunks))
        def _():
            self.copy(0, first).wait()

            def put(j, value):
                self.held[first, j] = (value + self.gots[0][first, j].astype(f32)).astype(bf16)
            self.products(first, core, put)
            self.copy(1, first).start()

    def consume(self, i):
        for stage in range(1, self.bits):
            chunk = i - (stage - 1) * self.lag

            @pl.when((chunk >= 0) & (chunk < self.chunks))
            def _():
                self.copy(stage, chunk).wait()
                count = self.n >> (stage + 1)
                base = self.start_of_kept(stage + 1, chunk)
                if stage < self.bits - 1:
                    for j in range(count):
                        self.held[chunk, base + j] = (
                            self.held[chunk, base + j].astype(f32) + self.gots[stage][chunk, j].astype(f32)
                        ).astype(bf16)
                    self.copy(stage + 1, chunk).start()
                else:
                    low = 0
                    for (_, _, _, size), out in zip(self.jobs, self.outs):
                        size = size // self.unit

                        @pl.when((chunk >= low) & (chunk < low + size))
                        def _():
                            cols = pl.ds(pl.multiple_of((chunk - low) * self.unit, self.unit), self.unit)
                            total = self.held[chunk, base].astype(f32) + self.gots[stage][chunk, 0].astype(f32)
                            out[:, cols] = total.astype(out.dtype)
                        low += size

    def step(self, i):
        for turn in range(self.ahead):
            self.produce(i * self.ahead + turn)
        self.consume(i - self.wait)


def greet(seq_devices, tp_devices, over_seq, over_tp):
    seq, tp = lax.axis_index("seq"), lax.axis_index("tp")
    barrier = pltpu.get_barrier_semaphore()
    peers = 0
    if over_seq:
        peers = seq_devices.bit_length() - 1
        for b in range(peers):
            other = seq + (1 - 2 * lax.rem(seq // (1 << b), 2)) * (1 << b)
            pl.semaphore_signal(barrier, inc=1, device_id={"seq": other}, device_id_type=MESH)
    if over_tp:
        @pl.when(tp > 0)
        def _():
            pl.semaphore_signal(barrier, inc=1, device_id={"tp": tp - 1}, device_id_type=MESH)

        @pl.when(tp < tp_devices - 1)
        def _():
            pl.semaphore_signal(barrier, inc=1, device_id={"tp": tp + 1}, device_id_type=MESH)
        peers = peers + jnp.minimum(tp, 1) + jnp.minimum(tp_devices - 1 - tp, 1)
    pl.semaphore_wait(barrier, peers)


def rows_of(k, size):
    return pl.ds(pl.multiple_of(k * size, size), size)


def put_own(out, at, value, axis_size):
    width = value.shape[1] // axis_size
    me = lax.axis_index("tp")
    for piece in range(axis_size):
        @pl.when(me == piece)
        def _():
            out[at, :] = value[:, piece * width : (piece + 1) * width]


def attention_ffn_kernel(
    tp_devices, chunk, lag, group,
    heads_ref, w_out_ref, tokens_ref, live_ref, gain_ref, w_gate_hbm, w_up_hbm, dhid_hbm,
    normed_ref, dboth_ref, hid_ref, own_ref, hidden_ref, pulled_ref,
    part, ups, downs, sems, w_gate_ref, w_up_ref, dhid_ref, load_sems,
):
    rows, dim = tokens_ref.shape
    ffn = w_gate_ref.shape[1]
    loads = [
        pltpu.make_async_copy(w_gate_hbm, w_gate_ref, load_sems.at[0]),
        pltpu.make_async_copy(w_up_hbm, w_up_ref, load_sems.at[1]),
        pltpu.make_async_copy(dhid_hbm, dhid_ref, load_sems.at[2]),
    ]
    for load in loads:
        load.start()
    gap = dboth_ref.shape[1] // 2
    per = group // chunk
    if gap > ffn:
        dboth_ref[...] = jnp.zeros_like(dboth_ref)
    if hid_ref.shape[1] > ffn:
        hid_ref[:, ffn // 128 * 128 :] = jnp.zeros((rows, hid_ref.shape[1] - ffn // 128 * 128), bf16)

    def attn_done(k, total):
        at = rows_of(k, chunk)
        now = tokens_ref[at, :].astype(f32) + live_ref[at, :] * total
        hidden_ref[at, :] = now.astype(bf16)
        scale = lax.rsqrt(jnp.mean(now * now, axis=-1, keepdims=True) + norm_eps)
        normed_ref[at, :] = (now * scale * gain_ref[...]).astype(bf16)
        put_own(own_ref, at, now, tp_devices)

    line = Line(tp_devices, part, ups, downs, None, sems, chunk, lag, True, attn_done)

    def begin(q, carry):
        at = rows_of(q, 128)
        part[at, :] = mm(heads_ref[at, :], w_out_ref[...]).astype(bf16)
        return carry
    begin(0, 0)
    greet(1, tp_devices, False, True)
    line.begin(0, 128 // chunk)

    def rest(q, carry):
        begin(q, carry)
        line.begin(q * (128 // chunk), 128 // chunk)
        return carry
    lax.fori_loop(1, rows // 128, rest, 0)

    tile = 256
    full = ffn // tile
    feeds = -(-ffn // tile)
    items = feeds + dim // tile

    def feed(at, cols, up_cols):
        normed = normed_ref[at, :]
        gate = mm(normed, w_gate_ref[:, cols])
        up = mm(normed, w_up_ref[:, cols])
        sig = sigmoid(gate)
        act = gate * sig
        dhid = dhid_ref[at, cols].astype(f32)
        hid_ref[at, cols] = (act * up).astype(bf16)
        dboth_ref[at, cols] = (dhid * up * (sig * (1.0 + gate * (1.0 - sig)))).astype(bf16)
        dboth_ref[at, up_cols] = (dhid * act).astype(bf16)

    def item(q, w):
        at = rows_of(q, group)

        @pl.when(w < full)
        def _():
            start = pl.multiple_of(w * tile, tile)
            feed(at, pl.ds(start, tile), pl.ds(pl.multiple_of(gap + w * tile, 128), tile))

        if feeds > full:
            @pl.when(w == full)
            def _():
                feed(at, slice(full * tile, ffn), slice(gap + full * tile, gap + ffn))

        @pl.when((w >= feeds) & (w < items))
        def _():
            mine = rows_of(w - feeds, tile)
            total = mm(dboth_ref[at, 0:ffn], w_gate_ref[mine, :], 1, 1)
            total = total + mm(dboth_ref[at, gap : gap + ffn], w_up_ref[mine, :], 1, 1)
            pulled_ref[at, mine] = total.astype(bf16)

    first = line.last + per
    each = -(-items // per)
    groups = rows // group

    def lead(i, carry):
        line.step(i)
        return carry
    lax.fori_loop(0, first, lead, 0)
    for load in loads:
        load.wait()

    def beside(i, carry):
        line.step(i)
        q, p = (i - first) // per, lax.rem(i - first, per)

        def work(w, carry):
            item(q, p * each + w)
            return carry
        lax.fori_loop(0, each, work, 0)
        return carry
    lax.fori_loop(first, first + per * (groups - 1), beside, 0)

    def tail(w, carry):
        item(groups - 1, w)
        return carry
    lax.fori_loop(0, items, tail, 0)
    line.end()


def attention_ffn(tp_devices, heads_out, w_out, tokens, live, gain, w_gate, w_up, dhid, chunk=32, lag=2, group=256):
    rows, dim = tokens.shape
    ffn = w_gate.shape[1]
    width = dim // tp_devices
    vmem = pl.BlockSpec(memory_space=pltpu.VMEM)
    out_shape = [
        jax.ShapeDtypeStruct((rows, dim), bf16),
        jax.ShapeDtypeStruct((rows, 2 * ceil_to(ffn, 128)), bf16),
        jax.ShapeDtypeStruct((rows, ceil_to(ffn, 256)), bf16),
        jax.ShapeDtypeStruct((rows, width), f32),
        jax.ShapeDtypeStruct((rows, dim), bf16),
        jax.ShapeDtypeStruct((rows, dim), bf16),
    ]
    return pl.pallas_call(
        functools.partial(attention_ffn_kernel, tp_devices, chunk, lag, group),
        in_specs=[vmem] * 5 + [pl.BlockSpec(memory_space=pltpu.HBM)] * 3,
        out_specs=[vmem] * len(out_shape),
        out_shape=out_shape,
        scratch_shapes=[pltpu.VMEM((rows, dim), bf16)]
        + Line.scratch(rows, dim, tp_devices, chunk, True)
        + [pltpu.VMEM(item.shape, bf16) for item in (w_gate, w_up, dhid)]
        + [pltpu.SemaphoreType.DMA((3,))],
        compiler_params=pltpu.CompilerParams(
            collective_id=3, has_side_effects=True, vmem_limit_bytes=62 << 20
        ),
        name="attention_ffn",
    )(heads_out, w_out, tokens, live, gain.reshape(1, dim), w_gate, w_up, dhid)


def paced(flow, pace, tick):
    @pl.when(lax.rem(tick * pace[0], pace[1]) < pace[0])
    def _():
        flow.step(tick * pace[0] // pace[1])


def paced_steps(flow, pace):
    return -(-flow.steps * pace[1] // pace[0])


def ffn_back_kernel(seq_devices, tp_devices, jobs, hid_at, unit, chunk, scatter_lag, line_lag, wait, pace, lefts, *refs):
    refs = list(refs)

    def take(count):
        out = refs[:count]
        del refs[:count]
        return out

    bits = seq_devices.bit_length() - 1
    arrays = take(lefts)
    part, hidden_ref, cot_ref, live_ref, gain_ref, w_out_ref, w_down_hbm = take(7)
    outs = take(len(jobs))
    dattn_ref, done_ref, dheads_ref, dgain_ref, ffn_ref = take(5)
    held, *rest = take(1 + bits + 2)
    ups, downs, sems, w_down_ref, load_sem = take(5)
    load = pltpu.make_async_copy(w_down_hbm, w_down_ref, load_sem)
    load.start()
    rows, dim = part.shape

    def dnormed_done(k, total):
        at = rows_of(k, chunk)
        now = hidden_ref[at, :].astype(f32)
        scale = lax.rsqrt(jnp.mean(now * now, axis=-1, keepdims=True) + norm_eps)
        unit_rows = now * scale
        dgain_ref[...] += jnp.sum((total * unit_rows).reshape(-1, 8, dim), axis=0)
        scaled = total * gain_ref[...]
        grad = cot_ref[at, :].astype(f32) + scale * (
            scaled - unit_rows * jnp.mean(scaled * unit_rows, axis=-1, keepdims=True)
        )
        dattn_ref[at, :] = (live_ref[at, :] * grad).astype(bf16)
        put_own(done_ref, at, grad, tp_devices)

    pairs = Scatter.turned(arrays, jobs, refs)
    scatter = Scatter(seq_devices, pairs, held, rest[:bits], outs, rest[bits], rest[bits + 1], unit, scatter_lag, 1, wait)
    line = Line(tp_devices, part, ups, downs, None, sems, chunk, line_lag, True, dnormed_done)
    dgain_ref[...] = jnp.zeros_like(dgain_ref)
    greet(seq_devices, tp_devices, True, True)
    line.begin(0, line.chunks)
    per = 128 // chunk

    def step(i, carry):
        paced(scatter, pace, i)
        line.step(i)
        done = i - line.last

        @pl.when((done >= 0) & (done < line.chunks) & (lax.rem(done + line.chunks, per) == per - 1))
        def _():
            at = rows_of(done // per, 128)
            dheads_ref[at, :] = mm(dattn_ref[at, :], w_out_ref[...], 1, 1)

        @pl.when((i < line.chunks) & (lax.rem(i, per) == 1))
        def _():
            at = rows_of(i // per, 128)
            ffn_ref[at, :] = mm(arrays[hid_at][at, 0 : w_down_ref.shape[0]], w_down_ref[...]).astype(bf16)
        return carry
    load.wait()
    lax.fori_loop(0, max(paced_steps(scatter, pace), line.steps), step, 0)
    line.end()


def ffn_back(
    seq_devices, tp_devices, arrays, jobs, hid_at, part, hidden, cot, live, gain, w_out, w_down,
    unit=256, chunk=32, scatter_lag=4, line_lag=2, wait=5, pace=(1, 1),
):
    rows, dim = part.shape
    vmem = pl.BlockSpec(memory_space=pltpu.VMEM)
    out_shape = [jax.ShapeDtypeStruct((dim // seq_devices, size), bf16) for _, _, _, size in jobs]
    out_shape += [
        jax.ShapeDtypeStruct((rows, dim), bf16),
        jax.ShapeDtypeStruct((rows, dim // tp_devices), f32),
        jax.ShapeDtypeStruct((rows, w_out.shape[0]), f32),
        jax.ShapeDtypeStruct((8, dim), f32),
        jax.ShapeDtypeStruct((rows, dim), bf16),
    ]
    scratch = Scatter.scratch(seq_devices, dim, sum(size for _, _, _, size in jobs), unit)
    scratch += Line.scratch(rows, dim, tp_devices, chunk, True)
    scratch += [pltpu.VMEM(w_down.shape, bf16), pltpu.SemaphoreType.DMA(())]
    scratch += Scatter.spaces(arrays, jobs)
    return pl.pallas_call(
        functools.partial(
            ffn_back_kernel, seq_devices, tp_devices, jobs, hid_at, unit, chunk, scatter_lag, line_lag, wait, pace, len(arrays)
        ),
        in_specs=[vmem] * (len(arrays) + 6) + [pl.BlockSpec(memory_space=pltpu.HBM)],
        out_specs=[vmem] * len(out_shape),
        out_shape=out_shape,
        scratch_shapes=scratch,
        compiler_params=pltpu.CompilerParams(
            collective_id=4, has_side_effects=True, vmem_limit_bytes=62 << 20
        ),
        name="ffn_back",
    )(*arrays, part, hidden, cot, live, gain.reshape(1, dim), w_out, w_down)


def greet_all(sizes):
    barrier = pltpu.get_barrier_semaphore()
    peers = 0
    for axis, size in sizes:
        me = lax.axis_index(axis)
        for turn in range(1, size):
            pl.semaphore_signal(barrier, inc=1, device_id={axis: lax.rem(me + turn, size)}, device_id_type=MESH)
        peers += size - 1
    pl.semaphore_wait(barrier, peers)


def remote(src, dst, send, recv, axis, device):
    return pltpu.make_async_remote_copy(
        src_ref=src, dst_ref=dst, send_sem=send, recv_sem=recv, device_id={axis: device}, device_id_type=MESH
    )


def delta_back_kernel(devices, taps, jobs, unit, scatter_lag, wait, count, *refs):
    refs = list(refs)

    def take(number):
        out = refs[:number]
        del refs[:number]
        return out

    bits = devices.bit_length() - 1
    arrays = take(count)
    (proj_ref, halo_ref, conv_ref, beta_ref, slope_ref, tri_ref, keep_ref, fresh_ref, state_ref, moves_ref,
     dheads_ref, mixed_ref, gate_ref, gain_ref) = take(14)
    outs = take(len(jobs))
    dense_ref, dconv_ref, dbias_ref, dgain_ref = take(4)
    held, *rest = take(1 + bits + 2)
    (ext_ref, dext_ref, dmixed_ref, offset_in, offset_all, states, grads, edge_out, edge_in, last_rows, dbeta_ref,
     send_one, recv_one, send_two, recv_two, edge_sems) = take(16)
    _, seqs, length, width = proj_ref.shape
    pad = halo_ref.shape[2]
    heads = width // HEAD
    chains = seqs * heads
    me = lax.axis_index("seq")
    pairs = Scatter.turned(arrays, jobs, refs)
    scatter = Scatter(devices, pairs, held, rest[:bits], outs, rest[bits], rest[bits + 1], unit, scatter_lag, 1, wait)

    def flow(first, last):
        def step(i, carry):
            scatter.step(i)
            return carry
        lax.fori_loop(first, last, step, 0)

    dconv_ref[...] = jnp.zeros_like(dconv_ref)
    dgain_ref[...] = jnp.zeros_like(dgain_ref)
    dbeta_ref[...] = jnp.zeros_like(dbeta_ref)
    dext_ref[...] = jnp.zeros_like(dext_ref)
    together = ext_ref.shape[0]
    groups = heads // together

    def lanes(h):
        return pl.ds(pl.multiple_of(h * HEAD, HEAD), HEAD)

    def head_back(it, carry):
        s = it // groups
        rows = rows_of(s, length)
        gain = gain_ref[...]
        for j in range(together):
            h = lax.rem(it, groups) * together + j
            lane = lanes(h)
            dheads = dheads_ref[rows, lane]
            mixed = mixed_ref[s, :, lane]
            gate = gate_ref[s, :, lane]
            sig = sigmoid(gate)
            act = gate * sig
            rstd = lax.rsqrt(jnp.mean(mixed * mixed, axis=-1, keepdims=True) + norm_eps)
            unit_out = mixed * rstd
            pulled = dheads * unit_out
            dgain_ref[...] += jnp.sum((pulled * act).reshape(-1, 8, HEAD), axis=0)
            dense_ref[rows, lanes(3 * heads + h)] = (pulled * gain * (sig * (1.0 + gate * (1.0 - sig)))).astype(bf16)
            dunit = dheads * gain * act
            dmixed = (rstd * (dunit - unit_out * jnp.mean(dunit * unit_out, axis=-1, keepdims=True))).astype(bf16)
            dmixed_ref[s, :, lane] = dmixed
            offset_in[s * heads + h] = mm(keep_ref[s, h, :, 0:HEAD], dmixed, 0, 0).astype(bf16)
        return carry

    def chain_maps(chain):
        return remote(offset_in.at[chain], offset_all.at[me], send_one.at[chain], recv_one.at[me], "seq", chain)

    lax.fori_loop(0, seqs * groups, head_back, 0)
    greet_all([("seq", devices)])
    for chain in range(chains):
        @pl.when(me != chain)
        def _():
            chain_maps(chain).start()

        @pl.when(me == chain)
        def _():
            offset_all[chain] = offset_in[chain]
    flow(0, 2)

    @pl.when(me < chains)
    def _():
        state = jnp.zeros((HEAD, HEAD), f32)
        for at in range(devices - 1, -1, -1):
            states[at] = state.astype(bf16)

            @pl.when(me != at)
            def _():
                remote(states.at[at], grads.at[me], send_two.at[at], recv_two.at[me], "seq", at).start()
                remote(offset_in.at[0], offset_all.at[at], send_one.at[0], recv_one.at[at], "seq", at).wait_recv()

            @pl.when(me == at)
            def _():
                grads[me] = states[at]
            state = state + mm(moves_ref[at], state, 0, 0) + offset_all[at].astype(f32)
        for at in range(devices):
            @pl.when(me != at)
            def _():
                remote(states.at[at], grads.at[0], send_two.at[at], recv_two.at[0], "seq", at).wait_send()
    flow(2, 4)
    for chain in range(chains):
        @pl.when(me != chain)
        def _():
            chain_maps(chain).wait_send()
            remote(states.at[0], grads.at[chain], send_two.at[0], recv_two.at[chain], "seq", chain).wait_recv()

    below, upto, _ = strict_lower(length)

    def column(ref, s, h):
        value = ref[s]
        at = lax.broadcasted_iota(jnp.int32, value.shape, 1)
        return jnp.sum(jnp.where(at == h, value, 0.0), axis=1, keepdims=True)

    def heads_at_once(s, hs):
        rows = rows_of(s, length)
        slots = range(len(hs))
        for slot, h in enumerate(hs):
            for part in range(3):
                ext_ref[slot, part, 0:pad, :] = halo_ref[part, s, :, lanes(h)].astype(f32)
                ext_ref[slot, part, pad : pad + length, :] = proj_ref[part, s, :, lanes(h)].astype(f32)

        def conv(slot, h, part):
            summed = None
            for tap in range(taps):
                term = (
                    conv_ref[part, tap : tap + 1, lanes(h)]
                    * ext_ref[slot, part, pl.ds(pad - taps + 1 + tap, length), :]
                )
                summed = term if summed is None else summed + term
            return summed

        def both(function, *lists):
            return [function(*items) for items in zip(*lists)]

        def normed(pre):
            act = pre * sigmoid(pre)
            scale = lax.rsqrt(jnp.sum(act * act, axis=-1, keepdims=True) + norm_eps)
            return act * scale

        queries = both(lambda slot, h: normed(conv(slot, h, 0)).astype(bf16), slots, hs)
        keys = both(lambda slot, h: normed(conv(slot, h, 1)).astype(bf16), slots, hs)
        states = [state_ref[s, h] for h in hs]
        exits = [grads[s * heads + h] for h in hs]
        dmixeds = [dmixed_ref[s, :, lanes(h)] for h in hs]
        freshes = [fresh_ref[s, :, lanes(h)] for h in hs]
        betas = [column(beta_ref, s, h) for h in hs]
        scores = both(lambda q, k: jnp.where(upto, mm(q, k, 1, 1), 0.0).astype(bf16), queries, keys)
        dfresh = both(lambda p, d, k, g: (mm(p, d, 0, 0) + mm(k, g)).astype(bf16), scores, dmixeds, keys, exits)
        pulls = both(lambda h, d: mm(tri_ref[s, h], d, 0, 0), hs, dfresh)
        dscores = both(lambda d, f: jnp.where(upto, mm(d, f, 1, 1), 0.0).astype(bf16), dmixeds, freshes)
        dvalues = both(lambda beta, pulled: beta * pulled, betas, pulls)
        dtris = both(lambda pulled, f: jnp.where(below, -mm(pulled, f, 1, 1), 0.0), pulls, freshes)
        inners = both(lambda dtri, k: jnp.sum(dtri * mm(k, k, 1, 1), axis=-1, keepdims=True), dtris, keys)
        dinners = both(lambda beta, dtri: (beta * dtri).astype(bf16), betas, dtris)
        dqueries = both(lambda d, st, p, k: mm(d, st, 1, 1) + mm(p, k), dmixeds, states, dscores, keys)
        dkeys = both(
            lambda p, q, f, g, v, st: mm(p, q, 0, 0) + mm(f, g, 1, 1) - mm(v, st, 1, 1),
            dscores, queries, freshes, exits, dvalues, states,
        )
        dkeys = both(lambda d, g, k: d + mm(g, k) + mm(g, k, 0, 0), dkeys, dinners, keys)
        reads = both(mm, keys, states)
        at = lax.broadcasted_iota(jnp.int32, (length, HEAD), 1)
        for slot, h, pulled, read, inner, dquery, dkey, dvalue in zip(
            slots, hs, pulls, reads, inners, dqueries, dkeys, dvalues
        ):
            for part, dout in ((0, dquery), (1, dkey), (2, dvalue)):
                pre = conv(slot, h, part)
                sig = sigmoid(pre)
                act = pre * sig
                if part == 2:
                    dact = dout
                    missing = act.astype(bf16).astype(f32) - read
                    dbeta = jnp.sum(pulled * missing, axis=-1, keepdims=True) + inner
                    dbeta_ref[s] += jnp.where(at == h, dbeta * column(slope_ref, s, h), 0.0)
                else:
                    scale = lax.rsqrt(jnp.sum(act * act, axis=-1, keepdims=True) + norm_eps)
                    unit_act = act * scale
                    dact = scale * (dout - unit_act * jnp.sum(dout * unit_act, axis=-1, keepdims=True))
                dconv = dact * (sig * (1.0 + pre * (1.0 - sig)))
                dext_ref[slot, part, pad : pad + length, :] = dconv
                for tap in range(taps):
                    shifted = ext_ref[slot, part, pl.ds(pad - taps + 1 + tap, length), :]
                    dconv_ref[part, tap : tap + 1, lanes(h)] += jnp.sum(dconv * shifted, axis=0, keepdims=True)
                summed, edge = None, None
                for tap in range(taps):
                    weight = conv_ref[part, tap : tap + 1, lanes(h)]
                    term = weight * dext_ref[slot, part, pl.ds(pad + taps - 1 - tap, length), :]
                    before = weight * dext_ref[slot, part, pl.ds(taps - 1 - tap, pad), :]
                    summed = term if summed is None else summed + term
                    edge = before if edge is None else edge + before
                col = lanes(part * heads + h)
                dense_ref[rows, col] = summed.astype(bf16)
                edge_out[s, :, col] = edge
                last_rows[s, :, col] = summed[length - pad :, :]

    start = 4
    each = -(-(scatter.steps - start) // (seqs * groups + 1))

    def some_heads(it, carry):
        heads_at_once(it // groups, [lax.rem(it, groups) * together + j for j in range(together)])
        flow(start + it * each, start + (it + 1) * each)
        return carry
    lax.fori_loop(0, seqs * groups, some_heads, 0)

    def edge_copy(other):
        return remote(edge_out, edge_in, edge_sems.at[0], edge_sems.at[1], "seq", other)

    @pl.when(me > 0)
    def _():
        edge_copy(me - 1).start()
    dbias = jnp.zeros((1, HEAD), f32)
    for s in range(seqs):
        low = dbeta_ref[s].astype(bf16)
        dense_ref[s * length : (s + 1) * length, 4 * width : 4 * width + HEAD] = low
        dbias = dbias + jnp.sum(low.astype(f32), axis=0, keepdims=True)
    dbias_ref[...] = dbias
    spare = dense_ref.shape[1] - 4 * width - HEAD
    if spare:
        dense_ref[:, 4 * width + HEAD :] = jnp.zeros((seqs * length, spare), bf16)
    flow(start + seqs * groups * each, scatter.steps)

    @pl.when(me < devices - 1)
    def _():
        edge_copy(0).wait_recv()
        for s in range(seqs):
            dense_ref[(s + 1) * length - pad : (s + 1) * length, 0 : 3 * width] = (last_rows[s] + edge_in[s]).astype(bf16)

    @pl.when(me > 0)
    def _():
        edge_copy(0).wait_send()


def delta_back(devices, arrays, jobs, inputs, unit=256, scatter_lag=4, wait=5, at_once=4):
    dim = arrays[jobs[0][0]].shape[1]
    proj, halo, conv_weight = inputs[:3]
    _, seqs, length, width = proj.shape
    pad = halo.shape[2]
    heads = width // HEAD
    chains = seqs * heads
    taps = conv_weight.shape[1]
    square = (HEAD, HEAD)
    dma = pltpu.SemaphoreType.DMA
    vmem = pl.BlockSpec(memory_space=pltpu.VMEM)
    out_shape = [jax.ShapeDtypeStruct((dim // devices, size), bf16) for _, _, _, size in jobs]
    out_shape += [
        jax.ShapeDtypeStruct((seqs * length, ceil_to(4 * width + HEAD, unit)), bf16),
        jax.ShapeDtypeStruct(conv_weight.shape, f32),
        jax.ShapeDtypeStruct((1, HEAD), f32),
        jax.ShapeDtypeStruct((8, HEAD), f32),
    ]
    together = min(at_once, heads)
    scratch = Scatter.scratch(devices, dim, sum(size for _, _, _, size in jobs), unit)
    scratch += [
        pltpu.VMEM((together, 3, pad + length, HEAD), f32),
        pltpu.VMEM((together, 3, 2 * pad + length, HEAD), f32),
        pltpu.VMEM((seqs, length, width), bf16),
        pltpu.VMEM((chains,) + square, bf16),
        pltpu.VMEM((devices,) + square, bf16),
        pltpu.VMEM((devices,) + square, bf16),
        pltpu.VMEM((chains,) + square, bf16),
        pltpu.VMEM((seqs, pad, 3 * width), f32),
        pltpu.VMEM((seqs, pad, 3 * width), f32),
        pltpu.VMEM((seqs, pad, 3 * width), f32),
        pltpu.VMEM((seqs, length, HEAD), f32),
        dma((chains,)), dma((devices,)), dma((devices,)), dma((chains,)), dma((2,)),
    ]
    scratch += Scatter.spaces(arrays, jobs)
    return pl.pallas_call(
        functools.partial(delta_back_kernel, devices, taps, jobs, unit, scatter_lag, wait, len(arrays)),
        in_specs=[vmem] * (len(arrays) + len(inputs)),
        out_specs=[vmem] * len(out_shape),
        out_shape=out_shape,
        scratch_shapes=scratch,
        compiler_params=pltpu.CompilerParams(
            collective_id=2, has_side_effects=True, vmem_limit_bytes=62 << 20
        ),
        name="delta_back",
    )(*arrays, *inputs)


def last_kernel(seq_devices, tp_devices, jobs, unit, chunk, scatter_lag, line_lag, wait, pace, count, both, late_rows, *refs):
    refs = list(refs)

    def take(number):
        out = refs[:number]
        del refs[:number]
        return out

    bits = seq_devices.bit_length() - 1
    arrays = take(count)
    dense_ref, w_beta_ref, tokens_ref, rstd_ref, gain_ref, grad_ref, early_ref = take(7)
    sources = take(4)
    outs = take(len(jobs))
    tokens_grad_ref, seq_out, both_out = take(3)
    held, *rest = take(1 + bits + 2)
    part, ups, downs, line_sems = take(4)
    (weights, load_sems, scaled_ref, dgain_ref, dots, dots_in, early_in, late, late_in, total,
     early_sems, late_sems, dot_sems, both_sems) = take(14)
    seq, tp = lax.axis_index("seq"), lax.axis_index("tp")
    rows, dim = part.shape
    width = weights.shape[2]
    own = dim // tp_devices
    heads = w_beta_ref.shape[1]
    loads = [pltpu.make_async_copy(source, weights.at[at], load_sems.at[at]) for at, source in enumerate(sources)]
    for load in loads:
        load.start()
    dgain_ref[...] = jnp.zeros_like(dgain_ref)
    dots[...] = jnp.zeros_like(dots)
    late[...] = jnp.zeros_like(late)
    greet_all([("seq", seq_devices), ("tp", tp_devices)])

    def to_peers(src, slots, sems, axis, size):
        me = lax.axis_index(axis)
        return [
            remote(src, slots.at[turn], sems.at[0, turn], sems.at[1, turn], axis, lax.rem(me + turn, size))
            for turn in range(1, size)
        ]

    early_copies = to_peers(early_ref, early_in, early_sems, "seq", seq_devices)
    for copy in early_copies:
        copy.start()

    def done(k, value):
        at = rows_of(k, chunk)
        x = tokens_ref[at, :].astype(f32)
        unit_rows = x * rstd_ref[at, :]
        dgain_ref[...] += jnp.sum((value * unit_rows).reshape(-1, 8, own), axis=0)
        scaled = value * gain_ref[...]
        scaled_ref[at, :] = scaled
        dot = jnp.sum(scaled * x, axis=-1, keepdims=True)
        per = HEAD // chunk
        place = lax.broadcasted_iota(jnp.int32, (chunk, HEAD), 0) + lax.rem(k, per) * chunk
        lane = lax.broadcasted_iota(jnp.int32, (chunk, HEAD), 1)
        dots[pl.ds(k // per, 1), :] += jnp.sum(jnp.where(place == lane, dot, 0.0), axis=0, keepdims=True)

    pairs = Scatter.turned(arrays, jobs, refs)
    scatter = Scatter(seq_devices, pairs, held, rest[:bits], outs, rest[bits], rest[bits + 1], unit, scatter_lag, 1, wait)
    line = Line(tp_devices, part, ups, downs, None, line_sems, chunk, line_lag, False, done)
    per = HEAD // chunk
    groups = rows // HEAD
    for load in loads:
        load.wait()

    def step(i, carry):
        @pl.when(i < groups)
        def _():
            at = rows_of(i, HEAD)
            value = mm(dense_ref[at, 4 * width : 4 * width + heads], w_beta_ref[...], 1, 1)
            for w in range(4):
                value = value + mm(dense_ref[at, w * width : (w + 1) * width], weights[w], 1, 1)
            part[at, :] = value.astype(bf16)
            line.begin(i * per, per)
        paced(scatter, pace, i)
        line.step(i)
        for at, act in ((0, send_late), (gap, send_total), (2 * gap, finish_tokens)):
            pl.when(i == line.steps + at)(act)
        return carry

    late_copies = to_peers(late, late_in, late_sems, "seq", seq_devices)
    dot_copies = to_peers(dots, dots_in, dot_sems, "tp", tp_devices)
    both_copies = [
        remote(total, both_out.at[tp], both_sems.at[0, turn], both_sems.at[1, turn], "tp", lax.rem(tp + turn, tp_devices))
        for turn in range(1, tp_devices)
    ]
    gap = 4

    def send_late():
        dgain = jnp.sum(dgain_ref[...], axis=0, keepdims=True)
        for at in range(own // HEAD):
            late[at : at + 1, :] = dgain[:, at * HEAD : (at + 1) * HEAD]
        for copy in late_copies + dot_copies:
            copy.start()

    def send_total():
        for copy in early_copies + late_copies:
            copy.wait()
        early_total = early_ref[...]
        late_total = late[...]
        for turn in range(1, seq_devices):
            early_total = early_total + early_in[turn]
            late_total = late_total + late_in[turn]
        split = early_ref.shape[0] - both
        seq_out[...] = early_total[:split]
        total[0:both, :] = early_total[split:]
        total[both:, :] = late_total
        both_out[tp] = total[...]
        for copy in both_copies:
            copy.start()

    def finish_tokens():
        for copy in dot_copies:
            copy.wait()
        dot_total = dots[...]
        for turn in range(1, tp_devices):
            dot_total = dot_total + dots_in[turn]
        dots[...] = dot_total / dim
        eye = lax.broadcasted_iota(jnp.int32, (HEAD, HEAD), 0) == lax.broadcasted_iota(jnp.int32, (HEAD, HEAD), 1)

        def finish(q, carry):
            at = rows_of(q, HEAD)
            dot = jnp.sum(jnp.where(eye, dots[pl.ds(q, 1), :], 0.0), axis=1, keepdims=True)
            scale = rstd_ref[at, :]
            x = tokens_ref[at, :].astype(f32)
            tokens_grad_ref[at, :] = grad_ref[at, :] + scale * scaled_ref[at, :] - x * (scale * scale * scale) * dot
            return carry
        lax.fori_loop(0, groups, finish, 0)

    lax.fori_loop(0, max(paced_steps(scatter, pace), line.steps + 2 * gap + 1), step, 0)
    line.end()
    for copy in both_copies:
        copy.wait()


def last(
    seq_devices, tp_devices, arrays, jobs, dense, w_beta, tokens_own, rstd, gain_own, grad_own, early, both, sources,
    unit=256, chunk=32, scatter_lag=4, line_lag=2, wait=5, pace=(2, 3),
):
    dim = arrays[jobs[0][0]].shape[1]
    rows, own = tokens_own.shape
    width = sources[0].shape[1]
    late_rows = ceil_to(own // HEAD, 8)
    dot_rows = ceil_to(rows // HEAD, 8)
    dma = pltpu.SemaphoreType.DMA
    vmem, hbm = pl.BlockSpec(memory_space=pltpu.VMEM), pl.BlockSpec(memory_space=pltpu.HBM)
    out_shape = [jax.ShapeDtypeStruct((dim // seq_devices, size), bf16) for _, _, _, size in jobs]
    out_shape += [
        jax.ShapeDtypeStruct((rows, own), f32),
        jax.ShapeDtypeStruct((early.shape[0] - both, HEAD), f32),
        jax.ShapeDtypeStruct((tp_devices, both + late_rows, HEAD), f32),
    ]
    scratch = Scatter.scratch(seq_devices, dim, sum(size for _, _, _, size in jobs), unit)
    scratch += [pltpu.VMEM((rows, dim), bf16)] + Line.scratch(rows, dim, tp_devices, chunk, False)
    scratch += [
        pltpu.VMEM((4, dim, width), bf16),
        dma((4,)),
        pltpu.VMEM((rows, own), f32),
        pltpu.VMEM((8, own), f32),
        pltpu.VMEM((dot_rows, HEAD), f32),
        pltpu.VMEM((tp_devices, dot_rows, HEAD), f32),
        pltpu.VMEM((seq_devices,) + early.shape, f32),
        pltpu.VMEM((late_rows, HEAD), f32),
        pltpu.VMEM((seq_devices, late_rows, HEAD), f32),
        pltpu.VMEM((both + late_rows, HEAD), f32),
        dma((2, seq_devices)), dma((2, seq_devices)), dma((2, tp_devices)), dma((2, tp_devices)),
    ]
    scratch += Scatter.spaces(arrays, jobs)
    return pl.pallas_call(
        functools.partial(
            last_kernel, seq_devices, tp_devices, jobs, unit, chunk, scatter_lag, line_lag, wait, pace, len(arrays), both, late_rows
        ),
        in_specs=[vmem] * (len(arrays) + 7) + [hbm] * 4,
        out_specs=[vmem] * len(out_shape),
        out_shape=out_shape,
        scratch_shapes=scratch,
        compiler_params=pltpu.CompilerParams(
            collective_id=5, has_side_effects=True, vmem_limit_bytes=62 << 20
        ),
        name="last_sums",
    )(*arrays, dense, w_beta, tokens_own, rstd, gain_own, grad_own, early, *sources)


def as_rows(value, rows):
    flat = value.reshape(-1)
    return jnp.pad(flat, (0, rows * HEAD - flat.shape[0])).reshape(rows, HEAD)


def on_device(
    tokens,
    seq_lengths,
    norm_gain,
    w_query,
    w_key,
    w_value,
    w_gate,
    w_beta,
    beta_bias,
    conv_weight,
    out_gain,
    w_out,
    ffn_gain,
    w_ffn_gate,
    w_ffn_up,
    w_ffn_down,
    cotangent,
):
    seqs_here, local_len, model_dim = tokens.shape
    row_count = seqs_here * local_len
    heads_here = w_beta.shape[1]
    local_width = w_query.shape[1]
    halo_pad = 16
    seq_index = lax.axis_index("seq")
    seq_devices = lax.axis_size("seq")
    tp_index = lax.axis_index("tp")
    slice_width = model_dim // lax.axis_size("tp")
    positions = seq_index * local_len + jnp.arange(local_len, dtype=jnp.int32)
    live_rows = (positions[None, :] < seq_lengths[:, None]).astype(f32).reshape(row_count, 1)
    tokens_flat = tokens.reshape(row_count, model_dim)
    grad_low = cotangent.reshape(row_count, model_dim)
    normed_one, rstd_one, proj, halo, gate_pre, beta_val, slope = first(
        seq_devices, seqs_here, tokens_flat, norm_gain, w_query, w_key, w_value, w_gate, w_beta, beta_bias, live_rows
    )
    proj_seq = proj.reshape(3, seqs_here, local_len, local_width)
    halo_rows = halo.reshape(3, seqs_here, halo_pad, local_width)
    beta_seq = beta_val.reshape(seqs_here, local_len, heads_here)
    slope = slope.reshape(seqs_here, local_len, heads_here)
    gate_seq = gate_pre.reshape(seqs_here, local_len, local_width)

    tri, keep, move, offset = delta_local(proj_seq, halo_rows, conv_weight, beta_seq)
    chains = seqs_here * heads_here
    flat = (chains, HEAD, HEAD)
    deep = (seqs_here, heads_here, HEAD, HEAD)
    state_in, moves, norms, dffn_hidden = exchange(
        seq_devices, move.reshape(flat), offset.reshape(flat), False, grad_low, w_ffn_down
    )
    state_in = state_in.reshape(deep)
    mixed, fresh, heads_seq = delta_out(keep, state_in, gate_seq, out_gain)
    heads_out = heads_seq.reshape(row_count, local_width)

    tp_devices = lax.axis_size("tp")
    normed_two, dffn_both, ffn_hidden, hidden_own, hidden_low, dnormed_part_two = attention_ffn(
        tp_devices, heads_out, w_out, tokens_flat, live_rows, ffn_gain, w_ffn_gate, w_ffn_up, dffn_hidden
    )
    ffn_width = w_ffn_gate.shape[1]
    ffn_pad = ffn_hidden.shape[1]
    early = 256
    dw_both, dw_down_early, dattn, grad_own, dheads, dffn_gain, ffn_part = ffn_back(
        seq_devices,
        tp_devices,
        [normed_two, grad_low, dffn_both, ffn_hidden],
        [(0, 2, 0, dffn_both.shape[1]), (1, 3, 0, early)],
        3,
        dnormed_part_two,
        hidden_low,
        grad_low,
        live_rows,
        ffn_gain,
        w_out,
        w_ffn_down,
    )
    ffn_slice = lax.psum_scatter(ffn_part, "tp", scatter_dimension=1, tiled=True)

    def own_slice(value):
        return lax.dynamic_slice_in_dim(value, tp_index * slice_width, slice_width, value.ndim - 1)

    dw_down, dw_out, dense, dconv, dbias, dgain = delta_back(
        seq_devices,
        [grad_low, ffn_hidden, dattn, heads_out],
        [(0, 1, early, ffn_pad - early), (2, 3, 0, local_width)],
        [
            proj_seq, halo_rows, conv_weight, beta_seq, slope, tri, keep, fresh, state_in, moves,
            dheads, mixed, gate_seq, out_gain.reshape(1, HEAD),
        ],
    )
    slice_rows = slice_width // HEAD
    both_rows = ceil_to(slice_rows + 2, 8)
    conv_rows = dconv.size // HEAD
    both = as_rows(
        jnp.concatenate([own_slice(jnp.sum(dffn_gain, axis=0)), jnp.sum(dgain, axis=0), norms[0]]), both_rows
    )
    early_rows = jnp.concatenate(
        [dconv.reshape(conv_rows, HEAD), jnp.pad(dbias, ((0, 7), (0, 0))), both], axis=0
    )
    dense, ffn_slice = lax.optimization_barrier((dense, ffn_slice))
    dw_first, tokens_grad, seq_total, both_total = last(
        seq_devices,
        tp_devices,
        [normed_one, dense],
        [(0, 1, 0, dense.shape[1])],
        dense,
        w_beta,
        own_slice(tokens_flat),
        rstd_one,
        own_slice(norm_gain).reshape(1, slice_width),
        grad_own,
        early_rows,
        both_rows,
        [w_query, w_key, w_value, w_gate],
    )
    out_tokens = (hidden_own + ffn_slice.astype(f32)).astype(bf16).reshape(seqs_here, local_len, slice_width)
    lw = local_width

    def wide(value):
        return value.astype(f32)

    return (
        out_tokens,
        tokens_grad.reshape(seqs_here, local_len, slice_width),
        both_total[:, both_rows : both_rows + slice_rows].reshape(model_dim),
        wide(dw_first[:, :lw]),
        wide(dw_first[:, lw : 2 * lw]),
        wide(dw_first[:, 2 * lw : 3 * lw]),
        wide(dw_first[:, 3 * lw : 4 * lw]),
        wide(dw_first[:, 4 * lw : 4 * lw + heads_here]),
        seq_total[conv_rows, :heads_here],
        seq_total[:conv_rows].reshape(dconv.shape),
        jnp.sum(both_total[:, slice_rows], axis=0),
        wide(dw_out.T),
        both_total[:, :slice_rows].reshape(model_dim),
        wide(dw_both[:, :ffn_width]),
        wide(dw_both[:, dffn_both.shape[1] // 2 :][:, :ffn_width]),
        wide(jnp.concatenate([dw_down_early, dw_down], axis=1).T[:ffn_width]),
        jnp.sum(both_total[:, slice_rows + 1, 0]) / (seqs_here * HEADS),
    )


def solution(mesh):
    in_specs = (
        P(None, "seq", None),
        P(),
        P(),
        P(None, "tp"),
        P(None, "tp"),
        P(None, "tp"),
        P(None, "tp"),
        P(None, "tp"),
        P("tp"),
        P(None, None, "tp"),
        P(),
        P("tp", None),
        P(),
        P(None, "tp"),
        P(None, "tp"),
        P("tp", None),
        P(None, "seq", None),
    )
    out_specs = (
        P(None, "seq", "tp"),
        P(None, "seq", "tp"),
        P(),
        P("seq", "tp"),
        P("seq", "tp"),
        P("seq", "tp"),
        P("seq", "tp"),
        P("seq", "tp"),
        P("tp"),
        P(None, None, "tp"),
        P(),
        P("tp", "seq"),
        P(),
        P("seq", "tp"),
        P("seq", "tp"),
        P("tp", "seq"),
        P(),
    )
    return jax.shard_map(
        on_device, mesh=mesh, in_specs=in_specs, out_specs=out_specs, check_vma=False
    )
```

```python
import functools

import jax
import jax.numpy as jnp
from jax import lax
from jax.experimental import pallas as pl
from jax.experimental.pallas import tpu as pltpu
from jax.sharding import PartitionSpec as P

HEADS = 16
HEAD = 128

norm_eps = 1e-06
f32 = jnp.float32
bf16 = jnp.bfloat16
MESH = pl.DeviceIdType.MESH
VM = pltpu.VMEM


def mm(left, right, contract_left=1, contract_right=0):
    return lax.dot_general(
        left.astype(bf16),
        right.astype(bf16),
        (((contract_left,), (contract_right,)), ((), ())),
        preferred_element_type=f32,
    )


def from_behind(block, axis, distance):
    devices = range(lax.axis_size(axis))
    route = [(i - distance, i) for i in devices if i - distance in devices]
    return lax.ppermute(block, axis, route)


def sigmoid(value):
    return 1.0 / (1.0 + jnp.exp(-value))


def silu_grad(value):
    sigmoid_val = sigmoid(value)
    return sigmoid_val * (1.0 + value * (1.0 - sigmoid_val))


def dot_left(left, right):
    return mm(left, right, 0, 0)


def dot_right(left, right):
    return mm(left, right, 1, 1)


def strict_lower(size):
    rows = lax.broadcasted_iota(jnp.int32, (size, size), 0)
    cols = lax.broadcasted_iota(jnp.int32, (size, size), 1)
    return rows > cols, rows >= cols, rows ^ cols


def unit_lower_inverses(lows, apart):
    size = lows[0].shape[0]
    inverses = [jnp.where(apart == 0, 1.0, 0.0) - jnp.where(apart == 1, low, 0.0) for low in lows]
    step = 2
    while step < size:
        pair = (apart >= step) & (apart < 2 * step)
        between = [jnp.where(pair, low, 0.0).astype(bf16) for low in lows]
        inner = [inverse.astype(bf16) for inverse in inverses]
        right = [mm(left, at) for left, at in zip(between, inner)]
        inverses = [inverse - mm(at, value) for inverse, at, value in zip(inverses, inner, right)]
        step *= 2
    return inverses


def conv_silu(ext_ref, col, conv_ref, part, lane, length, taps, pad):
    summed = None
    for tap in range(taps):
        term = conv_ref[part, tap : tap + 1, lane] * ext_ref[pl.ds(pad - taps + 1 + tap, length), col]
        summed = term if summed is None else summed + term
    return summed


def delta_forward_kernel(
    devices, taps, proj_ref, halo_ref, conv_ref, beta_ref, gate_ref, gain_ref,
    tri_ref, query_ref, state_ref, moves_ref, norm_ref, mixed_ref, fresh_ref, heads_ref,
    ext_ref, keep_ref, move_in, offset_in, offset_all, states, send_zero, recv_zero, send_one, recv_one, send_two, recv_two,
):
    _, seqs, length, width = proj_ref.shape
    pad = halo_ref.shape[2]
    heads = width // HEAD
    chains = seqs * heads
    me = lax.axis_index("seq")
    peers = greet_axis("seq", devices)
    below, upto, apart = strict_lower(length)
    some = range(heads)

    def act(part, h):
        lane = slice(h * HEAD, (h + 1) * HEAD)
        col = slice(part * width + h * HEAD, part * width + (h + 1) * HEAD)
        summed = conv_silu(ext_ref, col, conv_ref, part, lane, length, taps, pad)
        return summed * sigmoid(summed)

    def unit(value):
        return value * lax.rsqrt(jnp.sum(value * value, axis=-1, keepdims=True) + norm_eps)

    def send_maps(chain):
        remote(move_in.at[chain], moves_ref.at[me], send_zero.at[chain], recv_zero.at[me], "seq", chain).start()
        remote(offset_in.at[chain], offset_all.at[me], send_one.at[chain], recv_one.at[me], "seq", chain).start()

    def local(s, carry):
        for part in range(3):
            col = slice(part * width, (part + 1) * width)
            ext_ref[0:pad, col] = halo_ref[part, s].astype(f32)
            ext_ref[pad : pad + length, col] = proj_ref[part, s].astype(f32)
        queries = [unit(act(0, h)).astype(bf16) for h in some]
        keys = [unit(act(1, h)).astype(bf16) for h in some]
        values = [act(2, h).astype(bf16) for h in some]
        betas = [beta_ref[s, :, h : h + 1] for h in some]
        lows = [jnp.where(below, beta * mm(key, key, 1, 1), 0.0) for beta, key in zip(betas, keys)]
        inverses = unit_lower_inverses(lows, apart)
        for h, query, key, value, beta, inverse in zip(some, queries, keys, values, betas, inverses):
            inverse = inverse.astype(bf16)
            targets = jnp.concatenate([beta * key.astype(f32), beta * value.astype(f32)], axis=1)
            solved_low = mm(inverse, targets).astype(bf16)
            scores = jnp.where(upto, mm(query, key, 1, 1), 0.0).astype(bf16)
            passed = mm(scores, solved_low)
            moved = mm(key, solved_low, 0, 0)
            tri_ref[s, h] = inverse
            query_ref[s, h] = (query.astype(f32) - passed[:, :HEAD]).astype(bf16)
            keep_ref[s, h, :, 0:HEAD] = passed[:, HEAD:].astype(bf16)
            keep_ref[s, h, :, HEAD:] = solved_low
            move_in[s * heads + h] = (-moved[:, :HEAD]).astype(bf16)
            offset_in[s * heads + h] = moved[:, HEAD:].astype(bf16)

        @pl.when(s == 0)
        def _():
            meet(peers)
        for h in some:
            chain = s * heads + h

            @pl.when(me != chain)
            def _():
                send_maps(chain)

            @pl.when(me == chain)
            def _():
                moves_ref[me] = move_in[chain]
                offset_all[me] = offset_in[chain]
        return carry
    lax.fori_loop(0, seqs, local, 0)

    @pl.when(me < chains)
    def _():
        state = jnp.zeros((HEAD, HEAD), f32)
        for at in range(devices):
            states[at] = state.astype(bf16)

            @pl.when(me != at)
            def _():
                remote(states.at[at], state_ref.at[me], send_two.at[at], recv_two.at[me], "seq", at).start()
                remote(move_in.at[0], moves_ref.at[at], send_zero.at[0], recv_zero.at[at], "seq", at).wait_recv()
                remote(offset_in.at[0], offset_all.at[at], send_one.at[0], recv_one.at[at], "seq", at).wait_recv()

            @pl.when(me == at)
            def _():
                state_ref[me] = states[at]
            state = state + mm(moves_ref[at], state) + offset_all[at].astype(f32)
        norm_ref[...] = jnp.zeros_like(norm_ref) + jnp.sqrt(jnp.sum(state * state, keepdims=True))
        for at in range(devices):
            @pl.when(me != at)
            def _():
                remote(states.at[at], state_ref.at[0], send_two.at[at], recv_two.at[0], "seq", at).wait_send()

    @pl.when(me >= chains)
    def _():
        norm_ref[...] = jnp.zeros_like(norm_ref)
    for chain in range(chains):
        @pl.when(me != chain)
        def _():
            remote(move_in.at[chain], moves_ref.at[0], send_zero.at[chain], recv_zero.at[0], "seq", chain).wait_send()
            remote(offset_in.at[chain], offset_all.at[0], send_one.at[chain], recv_one.at[0], "seq", chain).wait_send()
            remote(states.at[0], state_ref.at[chain], send_two.at[0], recv_two.at[chain], "seq", chain).wait_recv()

    def out(s, carry):
        for h in some:
            lane = slice(h * HEAD, (h + 1) * HEAD)
            state = state_ref[s * heads + h]
            mixed = keep_ref[s, h, :, 0:HEAD].astype(f32) + mm(query_ref[s, h], state)
            fresh = keep_ref[s, h, :, 2 * HEAD :].astype(f32) - mm(keep_ref[s, h, :, HEAD : 2 * HEAD], state)
            rstd = lax.rsqrt(jnp.mean(mixed * mixed, axis=-1, keepdims=True) + norm_eps)
            gate = gate_ref[s, :, lane]
            mixed_ref[s, :, lane] = mixed
            fresh_ref[s, :, lane] = fresh.astype(bf16)
            heads_ref[s, :, lane] = (mixed * rstd * gain_ref[...] * (gate * sigmoid(gate))).astype(bf16)
        return carry
    lax.fori_loop(0, seqs, out, 0)


def delta_forward(devices, proj, halo, conv_weight, beta, gate, gain):
    _, seqs, length, width = proj.shape
    pad = halo.shape[2]
    heads = width // HEAD
    chains = seqs * heads
    square = (HEAD, HEAD)
    dma = pltpu.SemaphoreType.DMA
    vmem = pl.BlockSpec(memory_space=pltpu.VMEM)
    out_shape = [
        jax.ShapeDtypeStruct((seqs, heads, length, length), bf16),
        jax.ShapeDtypeStruct((seqs, heads, length, HEAD), bf16),
        jax.ShapeDtypeStruct((chains,) + square, bf16),
        jax.ShapeDtypeStruct((devices,) + square, bf16),
        jax.ShapeDtypeStruct((8, HEAD), f32),
        jax.ShapeDtypeStruct((seqs, length, width), f32),
        jax.ShapeDtypeStruct((seqs, length, width), bf16),
        jax.ShapeDtypeStruct((seqs, length, width), bf16),
    ]
    return pl.pallas_call(
        functools.partial(delta_forward_kernel, devices, conv_weight.shape[1]),
        in_specs=[vmem] * 6,
        out_specs=[vmem] * len(out_shape),
        out_shape=out_shape,
        scratch_shapes=[
            pltpu.VMEM((pad + length, 3 * width), f32),
            pltpu.VMEM((seqs, heads, length, 3 * HEAD), bf16),
            pltpu.VMEM((chains,) + square, bf16),
            pltpu.VMEM((chains,) + square, bf16),
            pltpu.VMEM((devices,) + square, bf16),
            pltpu.VMEM((devices,) + square, bf16),
            dma((chains,)), dma((devices,)), dma((chains,)), dma((devices,)), dma((devices,)), dma((chains,)),
        ],
        compiler_params=pltpu.CompilerParams(
            collective_id=1, has_side_effects=True, vmem_limit_bytes=62 << 20
        ),
        name="delta_forward",
    )(proj, halo, conv_weight, beta, gate, gain.reshape(1, HEAD))


def first_kernel(
    seq_devices, tp_devices, tokens_ref, gain_ref, w_beta_ref, bias_ref, lengths_ref, *refs
):
    (w_query, w_key, w_value, w_gate, normed_ref, rstd_ref, proj_ref, halo_ref, gate_ref, beta_ref, slope_ref,
     live_ref, own_ref, weights, halo_in, load_sem, send_sem, recv_sem) = refs
    rows, dim = tokens_ref.shape
    seqs, pad, _ = halo_in.shape
    length = rows // seqs
    me = lax.axis_index("seq")
    loads = [
        pltpu.make_async_copy(source, weights.at[at], load_sem.at[at])
        for at, source in enumerate((w_query, w_key, w_value, w_gate))
    ]
    for load in loads:
        load.start()
    barrier = pltpu.get_barrier_semaphore()

    @pl.when(me > 0)
    def _():
        pl.semaphore_signal(barrier, inc=1, device_id={"seq": me - 1}, device_id_type=MESH)

    @pl.when(me < seq_devices - 1)
    def _():
        pl.semaphore_signal(barrier, inc=1, device_id={"seq": me + 1}, device_id_type=MESH)

    gain = gain_ref[...]

    def norm(q, carry):
        at = pl.ds(pl.multiple_of(q * 128, 128), 128)
        value = tokens_ref[at, :].astype(f32)
        scale = lax.rsqrt(jnp.mean(value * value, axis=-1, keepdims=True) + norm_eps)
        rstd_ref[at, :] = scale
        normed_ref[at, :] = (value * scale * gain).astype(bf16)
        return carry
    lax.fori_loop(0, rows // 128, norm, 0)
    pl.semaphore_wait(barrier, jnp.minimum(me, 1) + jnp.minimum(seq_devices - 1 - me, 1))

    def halo_copy(s):
        return pltpu.make_async_remote_copy(
            src_ref=tokens_ref.at[pl.ds((s + 1) * length - pad, pad)], dst_ref=halo_in.at[s],
            send_sem=send_sem.at[s], recv_sem=recv_sem.at[s],
            device_id={"seq": me + 1}, device_id_type=MESH,
        )

    @pl.when(me < seq_devices - 1)
    def _():
        for s in range(seqs):
            halo_copy(s).start()

    for s in range(seqs):
        position = me * length + lax.broadcasted_iota(jnp.int32, (length, 1), 0)
        live_ref[s * length : (s + 1) * length, :] = jnp.where(position < lengths_ref[0:1, s : s + 1], 1.0, 0.0)
    width = own_ref.shape[1]
    for piece in range(tp_devices):
        @pl.when(lax.axis_index("tp") == piece)
        def _():
            own_ref[...] = tokens_ref[:, piece * width : (piece + 1) * width]
    sig = sigmoid(mm(normed_ref[...], w_beta_ref[...], 1, 1) + bias_ref[...])
    beta = live_ref[...] * sig
    beta_ref[...] = beta
    slope_ref[...] = beta * (1.0 - sig)
    for part in range(4):
        loads[part].wait()

        def some(q, carry):
            at = pl.ds(pl.multiple_of(q * 256, 256), 256)
            product = mm(normed_ref[at, :], weights[part])
            if part < 3:
                proj_ref[part, at, :] = product.astype(bf16)
            else:
                gate_ref[at, :] = product
            return carry
        lax.fori_loop(0, rows // 256, some, 0)

    @pl.when(me > 0)
    def _():
        for s in range(seqs):
            halo_copy(s).wait_recv()
        value = halo_in[...].reshape(seqs * pad, dim).astype(f32)
        scale = lax.rsqrt(jnp.mean(value * value, axis=-1, keepdims=True) + norm_eps)
        normed = (value * scale * gain).astype(bf16)
        for part in range(3):
            halo_ref[part] = mm(normed, weights[part]).astype(bf16)

    @pl.when(me == 0)
    def _():
        halo_ref[...] = jnp.zeros_like(halo_ref)

    @pl.when(me < seq_devices - 1)
    def _():
        for s in range(seqs):
            halo_copy(s).wait_send()


def first(seq_devices, tp_devices, tokens, gain, w_query, w_key, w_value, w_gate, w_beta, bias, lengths):
    rows, dim = tokens.shape
    width, heads = w_query.shape[1], w_beta.shape[0]
    seqs = lengths.shape[0]
    pad = 16
    vmem, hbm = pl.BlockSpec(memory_space=pltpu.VMEM), pl.BlockSpec(memory_space=pltpu.HBM)
    out_shape = [
        jax.ShapeDtypeStruct((rows, dim), bf16),
        jax.ShapeDtypeStruct((rows, 1), f32),
        jax.ShapeDtypeStruct((3, rows, width), bf16),
        jax.ShapeDtypeStruct((3, seqs * pad, width), bf16),
        jax.ShapeDtypeStruct((rows, width), f32),
        jax.ShapeDtypeStruct((rows, heads), f32),
        jax.ShapeDtypeStruct((rows, heads), f32),
        jax.ShapeDtypeStruct((rows, 1), f32),
        jax.ShapeDtypeStruct((rows, dim // tp_devices), bf16),
    ]
    return pl.pallas_call(
        functools.partial(first_kernel, seq_devices, tp_devices),
        in_specs=[vmem] * 5 + [hbm] * 4,
        out_specs=[vmem] * len(out_shape),
        out_shape=out_shape,
        scratch_shapes=[
            pltpu.VMEM((4, dim, width), bf16),
            pltpu.VMEM((seqs, pad, dim), bf16),
            pltpu.SemaphoreType.DMA((4,)),
            pltpu.SemaphoreType.DMA((seqs,)),
            pltpu.SemaphoreType.DMA((seqs,)),
        ],
        compiler_params=pltpu.CompilerParams(
            collective_id=7, has_side_effects=True, vmem_limit_bytes=62 << 20
        ),
        name="first_norm_projections",
    )(tokens, gain.reshape(1, dim), w_beta, bias.reshape(1, heads), lengths.reshape(1, seqs), w_query, w_key, w_value, w_gate)


def ceil_to(value, unit):
    return -(-value // unit) * unit


class Line:
    def __init__(self, devices, part, ups, downs, out, sems, chunk, lag, whole, done=None):
        self.done = done
        self.n, self.part, self.ups, self.downs, self.out, self.sems = devices, part, ups, downs, out, sems
        self.chunk, self.lag, self.whole = chunk, lag, whole
        self.chunks = part.shape[0] // chunk
        self.me = lax.axis_index("tp")
        self.pieces = 1 if whole else devices
        self.width = part.shape[1] // self.pieces
        self.last = (devices - 2) * lag
        self.steps = self.chunks + self.last

    @staticmethod
    def scratch(rows, cols, devices, chunk, whole):
        count = (rows // chunk) * (1 if whole else devices)
        return [pltpu.VMEM((rows, cols), bf16)] * 2 + [pltpu.SemaphoreType.DMA((4, count))]

    def copy(self, source, way, k, piece):
        at = (pl.ds(pl.multiple_of(k * self.chunk, self.chunk), self.chunk), slice(piece * self.width, (piece + 1) * self.width))
        target = self.ups if way == 0 else self.downs
        sem = k * self.pieces + piece
        other = self.me + 1 if way == 0 else self.me - 1
        return pltpu.make_async_remote_copy(
            src_ref=source.at[at], dst_ref=target.at[at],
            send_sem=self.sems.at[way, sem], recv_sem=self.sems.at[2 + way, sem],
            device_id={"tp": other}, device_id_type=MESH,
        )

    def begin(self, first, count):
        for way, end in ((0, 0), (1, self.n - 1)):
            @pl.when(self.me == end)
            def _():
                def send(k, carry):
                    for piece in range(self.pieces) if way else reversed(range(self.pieces)):
                        if self.whole or piece != end:
                            self.copy(self.part, way, k, piece).start()
                    return carry
                lax.fori_loop(first, first + count, send, 0)

    def forward(self, way, k):
        me, n = self.me, self.n
        held = self.ups if way == 0 else self.downs
        rows = pl.ds(pl.multiple_of(k * self.chunk, self.chunk), self.chunk)
        for piece in range(self.pieces):
            if self.whole:
                gets, goes = None, me < n - 1 if way == 0 else me > 0
            else:
                gets, goes = (piece >= me, piece > me) if way == 0 else (piece <= me, piece < me)
            cols = slice(piece * self.width, (piece + 1) * self.width)

            def take():
                self.copy(self.part, way, k, piece).wait_recv()

                @pl.when(goes)
                def _():
                    held[rows, cols] = (held[rows, cols].astype(f32) + self.part[rows, cols].astype(f32)).astype(bf16)
                    self.copy(held, way, k, piece).start()

            if gets is None:
                take()
            else:
                pl.when(gets)(take)

    def give(self, k, total):
        if self.done is None:
            self.out[pl.ds(pl.multiple_of(k * self.chunk, self.chunk), self.chunk), :] = total
        else:
            self.done(k, total)

    def finish(self, k):
        me, n = self.me, self.n
        rows = pl.ds(pl.multiple_of(k * self.chunk, self.chunk), self.chunk)
        if self.whole:
            @pl.when(me == 0)
            def _():
                self.give(k, self.part[rows, :].astype(f32) + self.downs[rows, :].astype(f32))

            @pl.when(me == n - 1)
            def _():
                self.give(k, self.part[rows, :].astype(f32) + self.ups[rows, :].astype(f32))

            @pl.when((me > 0) & (me < n - 1))
            def _():
                both = self.ups[rows, :].astype(f32) - self.part[rows, :].astype(f32)
                self.give(k, both + self.downs[rows, :].astype(f32))
        else:
            for piece in range(n):
                @pl.when(me == piece)
                def _():
                    cols = slice(piece * self.width, (piece + 1) * self.width)
                    total = self.part[rows, cols].astype(f32)
                    if piece > 0:
                        total = total + self.ups[rows, cols].astype(f32)
                    if piece < n - 1:
                        total = total + self.downs[rows, cols].astype(f32)
                    self.give(k, total)

    def step(self, i):
        me, n = self.me, self.n
        up = i - (me - 1) * self.lag
        down = i - (n - 2 - me) * self.lag

        @pl.when((me > 0) & (up >= 0) & (up < self.chunks))
        def _():
            self.forward(0, up)

        @pl.when((me < n - 1) & (down >= 0) & (down < self.chunks))
        def _():
            self.forward(1, down)

        done = i - self.last

        @pl.when((done >= 0) & (done < self.chunks))
        def _():
            self.finish(done)

    def end(self):
        def drain(k, carry):
            for way in range(2):
                for piece in range(self.pieces):
                    if self.whole:
                        goes = self.me < self.n - 1 if way == 0 else self.me > 0
                    else:
                        goes = piece > self.me if way == 0 else piece < self.me

                    @pl.when(goes)
                    def _():
                        self.copy(self.part, way, k, piece).wait_send()
            return carry
        lax.fori_loop(0, self.chunks, drain, 0)


class Scatter:
    def __init__(self, devices, jobs, held, gots, outs, sends, recvs, unit, lag, ahead, wait):
        self.ahead, self.wait = ahead, wait
        self.n, self.jobs, self.held, self.gots, self.outs = devices, jobs, held, gots, outs
        self.sends, self.recvs, self.unit, self.lag = sends, recvs, unit, lag
        self.bits = devices.bit_length() - 1
        self.me = lax.axis_index("seq")
        self.block = jobs[0][0].shape[0] // devices
        self.chunks = sum(size for _, _, _, size in jobs) // unit
        self.steps = self.chunks + wait + (self.bits - 2) * lag

    @staticmethod
    def scratch(devices, rows, cols, unit):
        chunks, bits, block = cols // unit, devices.bit_length() - 1, rows // devices
        shapes = [pltpu.VMEM((chunks, devices // 2, block, unit), bf16)]
        shapes += [pltpu.VMEM((chunks, devices >> (s + 1), block, unit), bf16) for s in range(bits)]
        return shapes + [pltpu.SemaphoreType.DMA((bits, chunks))] * 2

    @staticmethod
    def turn(arrays, jobs, spaces):
        for space, x in zip(spaces, sorted({x for x, _, _, _ in jobs})):
            def one(j, carry):
                at = pl.ds(pl.multiple_of(j * 256, 256), 256)
                space[at, :] = arrays[x][:, at].T
                return carry
            lax.fori_loop(0, space.shape[0] // 256, one, 0)

    @staticmethod
    def turns(arrays, jobs, spaces):
        lefts = sorted({x for x, _, _, _ in jobs})
        return [(spaces[lefts.index(x)], arrays[y], start, size) for x, y, start, size in jobs]

    @staticmethod
    def turned(arrays, jobs, spaces):
        Scatter.turn(arrays, jobs, spaces)
        return Scatter.turns(arrays, jobs, spaces)

    @staticmethod
    def spaces(arrays, jobs):
        return [pltpu.VMEM(arrays[x].shape[::-1], bf16) for x in sorted({x for x, _, _, _ in jobs})]

    def power(self, stage, chunk):
        if stage == 0:
            return 1
        odd = lax.rem(chunk, 2)
        return odd * (1 << (self.bits - stage)) + (1 - odd) * (1 << stage)

    def bit(self, stage, chunk):
        return lax.rem(self.me // self.power(stage, chunk), 2)

    def partner(self, stage, chunk):
        return self.me + (1 - 2 * self.bit(stage, chunk)) * self.power(stage, chunk)

    def start_of_kept(self, stage, chunk):
        at = 0
        for s in range(1, stage):
            at = at + self.bit(s, chunk) * (self.n >> (s + 1))
        return at

    def copy(self, stage, chunk):
        count = self.n >> (stage + 1)
        if stage == 0:
            at = 0
        else:
            at = self.start_of_kept(stage, chunk) + (1 - self.bit(stage, chunk)) * count
        return pltpu.make_async_remote_copy(
            src_ref=self.held.at[chunk, pl.ds(at, count)], dst_ref=self.gots[stage].at[chunk],
            send_sem=self.sends.at[stage, chunk], recv_sem=self.recvs.at[stage, chunk],
            device_id={"seq": self.partner(stage, chunk)}, device_id_type=MESH,
        )

    def products(self, chunk, core, use):
        low = 0
        for x, y, start, size in self.jobs:
            count = size // self.unit

            @pl.when((chunk >= low) & (chunk < low + count))
            def _():
                right = y[:, pl.ds(pl.multiple_of(start + (chunk - low) * self.unit, 128), self.unit)]

                values = []
                for j in range(self.n // 2):
                    target = core
                    for s in range(1, self.bits):
                        target = target + j // (self.n >> (s + 1)) % 2 * self.power(s, chunk)
                    mine = pl.ds(pl.multiple_of(target * self.block, self.block), self.block)
                    values.append(mm(x[mine, :], right))
                for j, value in enumerate(values):
                    use(j, value)
            low += count

    def produce(self, i):
        core = lax.rem(self.me, 2)

        @pl.when(i < self.chunks)
        def _():
            def put(j, value):
                self.held[i, j] = value.astype(bf16)
            self.products(i, 1 - core, put)
            self.copy(0, i).start()

        first = i - 1

        @pl.when((first >= 0) & (first < self.chunks))
        def _():
            self.copy(0, first).wait()

            def put(j, value):
                self.held[first, j] = (value + self.gots[0][first, j].astype(f32)).astype(bf16)
            self.products(first, core, put)
            self.copy(1, first).start()

    def consume(self, i):
        for stage in range(1, self.bits):
            chunk = i - (stage - 1) * self.lag

            @pl.when((chunk >= 0) & (chunk < self.chunks))
            def _():
                self.copy(stage, chunk).wait()
                count = self.n >> (stage + 1)
                base = self.start_of_kept(stage + 1, chunk)
                if stage < self.bits - 1:
                    for j in range(count):
                        self.held[chunk, base + j] = (
                            self.held[chunk, base + j].astype(f32) + self.gots[stage][chunk, j].astype(f32)
                        ).astype(bf16)
                    self.copy(stage + 1, chunk).start()
                else:
                    low = 0
                    for (_, _, _, size), out in zip(self.jobs, self.outs):
                        size = size // self.unit

                        @pl.when((chunk >= low) & (chunk < low + size))
                        def _():
                            cols = pl.ds(pl.multiple_of((chunk - low) * self.unit, self.unit), self.unit)
                            total = self.held[chunk, base].astype(f32) + self.gots[stage][chunk, 0].astype(f32)
                            out[:, cols] = total.astype(out.dtype)
                        low += size

    def step(self, i):
        for turn in range(self.ahead):
            self.produce(i * self.ahead + turn)
        self.consume(i - self.wait)


def greet_line(tp_devices):
    tp = lax.axis_index("tp")
    barrier = pltpu.get_barrier_semaphore()

    @pl.when(tp > 0)
    def _():
        pl.semaphore_signal(barrier, inc=1, device_id={"tp": tp - 1}, device_id_type=MESH)

    @pl.when(tp < tp_devices - 1)
    def _():
        pl.semaphore_signal(barrier, inc=1, device_id={"tp": tp + 1}, device_id_type=MESH)
    return jnp.minimum(tp, 1) + jnp.minimum(tp_devices - 1 - tp, 1)


def greet_halving(seq_devices):
    seq = lax.axis_index("seq")
    barrier = pltpu.get_barrier_semaphore()
    bits = seq_devices.bit_length() - 1
    for b in range(bits):
        other = seq + (1 - 2 * lax.rem(seq // (1 << b), 2)) * (1 << b)
        pl.semaphore_signal(barrier, inc=1, device_id={"seq": other}, device_id_type=MESH)
    return bits


def greet_axis(axis, size):
    me = lax.axis_index(axis)
    barrier = pltpu.get_barrier_semaphore()
    for turn in range(1, size):
        pl.semaphore_signal(barrier, inc=1, device_id={axis: lax.rem(me + turn, size)}, device_id_type=MESH)
    return size - 1


def meet(peers):
    pl.semaphore_wait(pltpu.get_barrier_semaphore(), peers)


def unstaged(refs, count, order=None):
    spaces, sems = refs[-count - 1 : -1], refs[-1]
    loads = [pltpu.make_async_copy(refs[at], spaces[at], sems.at[at]) for at in range(count)]
    for at in order or range(count):
        loads[at].start()
    return loads, list(spaces) + list(refs[count : -count - 1])


def staging(arrays):
    return [pltpu.VMEM(item.shape, item.dtype) for item in arrays] + [pltpu.SemaphoreType.DMA((len(arrays),))]


def rows_of(k, size):
    return pl.ds(pl.multiple_of(k * size, size), size)


def put_own(out, at, value, axis_size):
    width = value.shape[1] // axis_size
    me = lax.axis_index("tp")
    for piece in range(axis_size):
        @pl.when(me == piece)
        def _():
            out[at, :] = value[:, piece * width : (piece + 1) * width]


def attention_ffn_kernel(
    tp_devices, chunk, lag, group,
    *refs
):
    peers = greet_line(tp_devices)
    loads, refs = unstaged(refs, 9, [0, 1, 2, 3, 4, 8, 7, 5, 6])
    (heads_ref, w_out_ref, tokens_ref, live_ref, gain_ref, w_gate_ref, w_up_ref, w_down_ref, cot_ref,
     normed_ref, dboth_ref, hid_ref, own_ref, hidden_ref, pulled_ref, part, ups, downs, sems, dhid_ref) = refs
    rows, dim = tokens_ref.shape
    ffn = w_gate_ref.shape[1]
    gap = dboth_ref.shape[1] // 2
    per = group // chunk
    if gap > ffn:
        dboth_ref[...] = jnp.zeros_like(dboth_ref)
    if hid_ref.shape[1] > ffn:
        hid_ref[:, ffn // 128 * 128 :] = jnp.zeros((rows, hid_ref.shape[1] - ffn // 128 * 128), bf16)

    def attn_done(k, total):
        at = rows_of(k, chunk)
        now = tokens_ref[at, :].astype(f32) + live_ref[at, :] * total
        hidden_ref[at, :] = now.astype(bf16)
        scale = lax.rsqrt(jnp.mean(now * now, axis=-1, keepdims=True) + norm_eps)
        normed_ref[at, :] = (now * scale * gain_ref[...]).astype(bf16)
        put_own(own_ref, at, now, tp_devices)

    line = Line(tp_devices, part, ups, downs, None, sems, chunk, lag, True, attn_done)

    def begin(q, carry):
        at = rows_of(q, 128)
        part[at, :] = mm(heads_ref[at, :], w_out_ref[...]).astype(bf16)
        return carry
    loads[0].wait()
    loads[1].wait()
    begin(0, 0)
    meet(peers)
    line.begin(0, 128 // chunk)

    def rest(q, carry):
        begin(q, carry)
        line.begin(q * (128 // chunk), 128 // chunk)
        return carry
    lax.fori_loop(1, rows // 128, rest, 0)

    tile = 256
    full = ffn // tile
    feeds = -(-ffn // tile)
    items = feeds + dim // tile

    def feed(at, cols, up_cols):
        normed = normed_ref[at, :]
        gate = mm(normed, w_gate_ref[:, cols])
        up = mm(normed, w_up_ref[:, cols])
        sig = sigmoid(gate)
        act = gate * sig
        dhid = dhid_ref[at, cols].astype(f32)
        hid_ref[at, cols] = (act * up).astype(bf16)
        dboth_ref[at, cols] = (dhid * up * (sig * (1.0 + gate * (1.0 - sig)))).astype(bf16)
        dboth_ref[at, up_cols] = (dhid * act).astype(bf16)

    def item(q, w):
        at = rows_of(q, group)

        @pl.when(w < full)
        def _():
            start = pl.multiple_of(w * tile, tile)
            feed(at, pl.ds(start, tile), pl.ds(pl.multiple_of(gap + w * tile, 128), tile))

        if feeds > full:
            @pl.when(w == full)
            def _():
                feed(at, slice(full * tile, ffn), slice(gap + full * tile, gap + ffn))

        @pl.when((w >= feeds) & (w < items))
        def _():
            mine = rows_of(w - feeds, tile)
            total = mm(dboth_ref[at, 0:ffn], w_gate_ref[mine, :], 1, 1)
            total = total + mm(dboth_ref[at, gap : gap + ffn], w_up_ref[mine, :], 1, 1)
            pulled_ref[at, mine] = total.astype(bf16)

    first = max(line.last + per, rows // 64 + 1)
    each = -(-items // per)
    groups = rows // group

    for load in loads[2:]:
        load.wait()

    def lead(i, carry):
        line.step(i)
        at = rows_of(i - 1, 64)

        @pl.when((i >= 1) & (i <= rows // 64))
        def _():
            dhid_ref[at, :] = mm(cot_ref[at, :], w_down_ref[...], 1, 1).astype(bf16)
        return carry
    lax.fori_loop(0, first, lead, 0)

    def beside(i, carry):
        line.step(i)
        q, p = (i - first) // per, lax.rem(i - first, per)

        def work(w, carry):
            item(q, p * each + w)
            return carry
        lax.fori_loop(0, each, work, 0)
        return carry
    lax.fori_loop(first, first + per * (groups - 1), beside, 0)

    def tail(w, carry):
        item(groups - 1, w)
        return carry
    lax.fori_loop(0, items, tail, 0)
    line.end()


def attention_ffn(tp_devices, heads_out, w_out, tokens, live, gain, w_gate, w_up, w_down, cot, chunk=32, lag=2, group=256):
    rows, dim = tokens.shape
    ffn = w_gate.shape[1]
    width = dim // tp_devices
    inputs = (heads_out, w_out, tokens, live, gain.reshape(1, dim), w_gate, w_up, w_down, cot)
    vmem = pl.BlockSpec(memory_space=pltpu.VMEM)
    out_shape = [
        jax.ShapeDtypeStruct((rows, dim), bf16),
        jax.ShapeDtypeStruct((rows, 2 * ceil_to(ffn, 128)), bf16),
        jax.ShapeDtypeStruct((rows, ceil_to(ffn, 256)), bf16),
        jax.ShapeDtypeStruct((rows, width), f32),
        jax.ShapeDtypeStruct((rows, dim), bf16),
        jax.ShapeDtypeStruct((rows, dim), bf16),
    ]
    return pl.pallas_call(
        functools.partial(attention_ffn_kernel, tp_devices, chunk, lag, group),
        in_specs=[pl.BlockSpec(memory_space=pltpu.HBM)] * len(inputs),
        out_specs=[vmem] * len(out_shape),
        out_shape=out_shape,
        scratch_shapes=[pltpu.VMEM((rows, dim), bf16)]
        + Line.scratch(rows, dim, tp_devices, chunk, True)
        + [pltpu.VMEM((rows, ffn), bf16)]
        + staging(inputs),
        compiler_params=pltpu.CompilerParams(
            collective_id=3, has_side_effects=True, vmem_limit_bytes=62 << 20
        ),
        name="attention_ffn",
    )(*inputs)


def paced(flow, pace, tick):
    @pl.when(lax.rem(tick * pace[0], pace[1]) < pace[0])
    def _():
        flow.step(tick * pace[0] // pace[1])


def paced_steps(flow, pace):
    return -(-flow.steps * pace[1] // pace[0])


def ffn_back_kernel(seq_devices, tp_devices, jobs, hid_at, cot_at, unit, chunk, scatter_lag, line_lag, wait, pace, lefts, *refs):
    peers = greet_halving(seq_devices) + greet_line(tp_devices)
    loads, refs = unstaged(refs, lefts + 6, [lefts] + list(range(lefts)) + list(range(lefts + 1, lefts + 6)))

    def take(count):
        out = refs[:count]
        del refs[:count]
        return out

    bits = seq_devices.bit_length() - 1
    arrays = take(lefts)
    part, hidden_ref, live_ref, gain_ref, w_out_ref, w_down_ref = take(6)
    cot_ref = arrays[cot_at]
    outs = take(len(jobs))
    dattn_ref, done_ref, dheads_ref, dgain_ref, ffn_ref = take(5)
    held, *rest = take(1 + bits + 2)
    ups, downs, sems = take(3)
    rows, dim = part.shape

    def dnormed_done(k, total):
        at = rows_of(k, chunk)
        now = hidden_ref[at, :].astype(f32)
        scale = lax.rsqrt(jnp.mean(now * now, axis=-1, keepdims=True) + norm_eps)
        unit_rows = now * scale
        dgain_ref[...] += jnp.sum((total * unit_rows).reshape(-1, 8, dim), axis=0)
        scaled = total * gain_ref[...]
        grad = cot_ref[at, :].astype(f32) + scale * (
            scaled - unit_rows * jnp.mean(scaled * unit_rows, axis=-1, keepdims=True)
        )
        dattn_ref[at, :] = (live_ref[at, :] * grad).astype(bf16)
        put_own(done_ref, at, grad, tp_devices)

    line = Line(tp_devices, part, ups, downs, None, sems, chunk, line_lag, True, dnormed_done)
    dgain_ref[...] = jnp.zeros_like(dgain_ref)
    loads[lefts].wait()
    meet(peers)
    line.begin(0, line.chunks)
    for load in loads[:lefts]:
        load.wait()
    pairs = Scatter.turned(arrays, jobs, refs)
    scatter = Scatter(seq_devices, pairs, held, rest[:bits], outs, rest[bits], rest[bits + 1], unit, scatter_lag, 1, wait)
    for load in loads[lefts + 1 :]:
        load.wait()
    per = 128 // chunk

    def step(i, carry):
        paced(scatter, pace, i)
        line.step(i)
        done = i - line.last

        @pl.when((done >= 0) & (done < line.chunks) & (lax.rem(done + line.chunks, per) == per - 1))
        def _():
            at = rows_of(done // per, 128)
            dheads_ref[at, :] = mm(dattn_ref[at, :], w_out_ref[...], 1, 1)

        @pl.when((i < line.chunks) & (lax.rem(i, per) == 1))
        def _():
            at = rows_of(i // per, 128)
            ffn_ref[at, :] = mm(arrays[hid_at][at, 0 : w_down_ref.shape[0]], w_down_ref[...]).astype(bf16)
        return carry
    lax.fori_loop(0, max(paced_steps(scatter, pace), line.steps), step, 0)
    line.end()


def ffn_back(
    seq_devices, tp_devices, arrays, jobs, hid_at, cot_at, part, hidden, live, gain, w_out, w_down,
    unit=256, chunk=32, scatter_lag=4, line_lag=2, wait=5, pace=(1, 1),
):
    rows, dim = part.shape
    vmem = pl.BlockSpec(memory_space=pltpu.VMEM)
    out_shape = [jax.ShapeDtypeStruct((dim // seq_devices, size), bf16) for _, _, _, size in jobs]
    out_shape += [
        jax.ShapeDtypeStruct((rows, dim), bf16),
        jax.ShapeDtypeStruct((rows, dim // tp_devices), f32),
        jax.ShapeDtypeStruct((rows, w_out.shape[0]), f32),
        jax.ShapeDtypeStruct((8, dim), f32),
        jax.ShapeDtypeStruct((rows, dim), bf16),
    ]
    scratch = Scatter.scratch(seq_devices, dim, sum(size for _, _, _, size in jobs), unit)
    scratch += Line.scratch(rows, dim, tp_devices, chunk, True)
    scratch += Scatter.spaces(arrays, jobs)
    inputs = [*arrays, part, hidden, live, gain.reshape(1, dim), w_out, w_down]
    scratch += staging(inputs)
    return pl.pallas_call(
        functools.partial(
            ffn_back_kernel, seq_devices, tp_devices, jobs, hid_at, cot_at, unit, chunk, scatter_lag, line_lag, wait, pace, len(arrays)
        ),
        in_specs=[pl.BlockSpec(memory_space=pltpu.HBM)] * len(inputs),
        out_specs=[vmem] * len(out_shape),
        out_shape=out_shape,
        scratch_shapes=scratch,
        compiler_params=pltpu.CompilerParams(
            collective_id=4, has_side_effects=True, vmem_limit_bytes=62 << 20
        ),
        name="ffn_back",
    )(*inputs)


def remote(src, dst, send, recv, axis, device):
    return pltpu.make_async_remote_copy(
        src_ref=src, dst_ref=dst, send_sem=send, recv_sem=recv, device_id={axis: device}, device_id_type=MESH
    )


def delta_back_kernel(devices, taps, jobs, unit, scatter_lag, wait, count, *refs):
    peers = greet_axis("seq", devices)
    soon = [count + 10, count + 11, count + 12, count + 13, count + 6]
    later = list(range(count)) + [count + 9]
    rest_of_loads = [at for at in range(count + 14) if at not in soon + later]
    loads, refs = unstaged(refs, count + 14, soon + later + rest_of_loads)

    def take(number):
        out = refs[:number]
        del refs[:number]
        return out

    def arrived(which):
        for at in which:
            loads[at].wait()

    bits = devices.bit_length() - 1
    arrays = take(count)
    (proj_ref, halo_ref, conv_ref, beta_ref, slope_ref, tri_ref, keep_ref, fresh_ref, state_ref, moves_ref,
     dheads_ref, mixed_ref, gate_ref, gain_ref) = take(14)
    outs = take(len(jobs))
    dense_ref, dconv_ref, dbias_ref, dgain_ref = take(4)
    held, *rest = take(1 + bits + 2)
    (ext_ref, dext_ref, dmixed_ref, offset_in, offset_all, states, grads, edge_out, edge_in, last_rows, dbeta_ref,
     send_one, recv_one, send_two, recv_two, edge_sems) = take(16)
    _, seqs, length, width = proj_ref.shape
    pad = halo_ref.shape[2]
    heads = width // HEAD
    chains = seqs * heads
    me = lax.axis_index("seq")
    arrived(soon)
    scatter = Scatter(devices, Scatter.turns(arrays, jobs, refs), held, rest[:bits], outs, rest[bits], rest[bits + 1], unit, scatter_lag, 1, wait)

    def flow(first, last):
        def step(i, carry):
            scatter.step(i)
            return carry
        lax.fori_loop(first, last, step, 0)

    dconv_ref[...] = jnp.zeros_like(dconv_ref)
    dgain_ref[...] = jnp.zeros_like(dgain_ref)
    dbeta_ref[...] = jnp.zeros_like(dbeta_ref)
    dext_ref[...] = jnp.zeros_like(dext_ref)
    together = ext_ref.shape[0]
    groups = heads // together

    def lanes(h):
        return pl.ds(pl.multiple_of(h * HEAD, HEAD), HEAD)

    def head_back(it, carry):
        s = it // groups
        rows = rows_of(s, length)
        gain = gain_ref[...]
        for j in range(together):
            h = lax.rem(it, groups) * together + j
            lane = lanes(h)
            dheads = dheads_ref[rows, lane]
            mixed = mixed_ref[s, :, lane]
            gate = gate_ref[s, :, lane]
            sig = sigmoid(gate)
            act = gate * sig
            rstd = lax.rsqrt(jnp.mean(mixed * mixed, axis=-1, keepdims=True) + norm_eps)
            unit_out = mixed * rstd
            pulled = dheads * unit_out
            dgain_ref[...] += jnp.sum((pulled * act).reshape(-1, 8, HEAD), axis=0)
            dense_ref[rows, lanes(3 * heads + h)] = (pulled * gain * (sig * (1.0 + gate * (1.0 - sig)))).astype(bf16)
            dunit = dheads * gain * act
            dmixed = (rstd * (dunit - unit_out * jnp.mean(dunit * unit_out, axis=-1, keepdims=True))).astype(bf16)
            dmixed_ref[s, :, lane] = dmixed
            offset_in[s * heads + h] = mm(keep_ref[s, h, :, 0:HEAD], dmixed, 0, 0).astype(bf16)
        return carry

    def chain_maps(chain):
        return remote(offset_in.at[chain], offset_all.at[me], send_one.at[chain], recv_one.at[me], "seq", chain)

    lax.fori_loop(0, seqs * groups, head_back, 0)
    meet(peers)
    for chain in range(chains):
        @pl.when(me != chain)
        def _():
            chain_maps(chain).start()

        @pl.when(me == chain)
        def _():
            offset_all[chain] = offset_in[chain]
    arrived(later)
    Scatter.turn(arrays, jobs, refs)
    flow(0, 2)

    @pl.when(me < chains)
    def _():
        state = jnp.zeros((HEAD, HEAD), f32)
        for at in range(devices - 1, -1, -1):
            states[at] = state.astype(bf16)

            @pl.when(me != at)
            def _():
                remote(states.at[at], grads.at[me], send_two.at[at], recv_two.at[me], "seq", at).start()
                remote(offset_in.at[0], offset_all.at[at], send_one.at[0], recv_one.at[at], "seq", at).wait_recv()

            @pl.when(me == at)
            def _():
                grads[me] = states[at]
            state = state + mm(moves_ref[at], state, 0, 0) + offset_all[at].astype(f32)
        for at in range(devices):
            @pl.when(me != at)
            def _():
                remote(states.at[at], grads.at[0], send_two.at[at], recv_two.at[0], "seq", at).wait_send()
    flow(2, 4)
    for chain in range(chains):
        @pl.when(me != chain)
        def _():
            chain_maps(chain).wait_send()
            remote(states.at[0], grads.at[chain], send_two.at[0], recv_two.at[chain], "seq", chain).wait_recv()

    arrived(rest_of_loads)
    below, upto, _ = strict_lower(length)

    def column(ref, s, h):
        value = ref[s]
        at = lax.broadcasted_iota(jnp.int32, value.shape, 1)
        return jnp.sum(jnp.where(at == h, value, 0.0), axis=1, keepdims=True)

    def heads_at_once(s, hs):
        rows = rows_of(s, length)
        slots = range(len(hs))
        for slot, h in enumerate(hs):
            for part in range(3):
                ext_ref[slot, part, 0:pad, :] = halo_ref[part, s, :, lanes(h)].astype(f32)
                ext_ref[slot, part, pad : pad + length, :] = proj_ref[part, s, :, lanes(h)].astype(f32)

        def conv(slot, h, part):
            summed = None
            for tap in range(taps):
                term = (
                    conv_ref[part, tap : tap + 1, lanes(h)]
                    * ext_ref[slot, part, pl.ds(pad - taps + 1 + tap, length), :]
                )
                summed = term if summed is None else summed + term
            return summed

        def both(function, *lists):
            return [function(*items) for items in zip(*lists)]

        def normed(pre):
            act = pre * sigmoid(pre)
            scale = lax.rsqrt(jnp.sum(act * act, axis=-1, keepdims=True) + norm_eps)
            return act * scale

        queries = both(lambda slot, h: normed(conv(slot, h, 0)).astype(bf16), slots, hs)
        keys = both(lambda slot, h: normed(conv(slot, h, 1)).astype(bf16), slots, hs)
        states = [state_ref[s * heads + h] for h in hs]
        exits = [grads[s * heads + h] for h in hs]
        dmixeds = [dmixed_ref[s, :, lanes(h)] for h in hs]
        freshes = [fresh_ref[s, :, lanes(h)] for h in hs]
        betas = [column(beta_ref, s, h) for h in hs]
        scores = both(lambda q, k: jnp.where(upto, mm(q, k, 1, 1), 0.0).astype(bf16), queries, keys)
        dfresh = both(lambda p, d, k, g: (mm(p, d, 0, 0) + mm(k, g)).astype(bf16), scores, dmixeds, keys, exits)
        pulls = both(lambda h, d: mm(tri_ref[s, h], d, 0, 0), hs, dfresh)
        dscores = both(lambda d, f: jnp.where(upto, mm(d, f, 1, 1), 0.0).astype(bf16), dmixeds, freshes)
        dvalues = both(lambda beta, pulled: beta * pulled, betas, pulls)
        dtris = both(lambda pulled, f: jnp.where(below, -mm(pulled, f, 1, 1), 0.0), pulls, freshes)
        inners = both(lambda dtri, k: jnp.sum(dtri * mm(k, k, 1, 1), axis=-1, keepdims=True), dtris, keys)
        dinners = both(lambda beta, dtri: (beta * dtri).astype(bf16), betas, dtris)
        dqueries = both(lambda d, st, p, k: mm(d, st, 1, 1) + mm(p, k), dmixeds, states, dscores, keys)
        dkeys = both(
            lambda p, q, f, g, v, st: mm(p, q, 0, 0) + mm(f, g, 1, 1) - mm(v, st, 1, 1),
            dscores, queries, freshes, exits, dvalues, states,
        )
        dkeys = both(lambda d, g, k: d + mm(g, k) + mm(g, k, 0, 0), dkeys, dinners, keys)
        reads = both(mm, keys, states)
        at = lax.broadcasted_iota(jnp.int32, (length, HEAD), 1)
        for slot, h, pulled, read, inner, dquery, dkey, dvalue in zip(
            slots, hs, pulls, reads, inners, dqueries, dkeys, dvalues
        ):
            for part, dout in ((0, dquery), (1, dkey), (2, dvalue)):
                pre = conv(slot, h, part)
                sig = sigmoid(pre)
                act = pre * sig
                if part == 2:
                    dact = dout
                    missing = act.astype(bf16).astype(f32) - read
                    dbeta = jnp.sum(pulled * missing, axis=-1, keepdims=True) + inner
                    dbeta_ref[s] += jnp.where(at == h, dbeta * column(slope_ref, s, h), 0.0)
                else:
                    scale = lax.rsqrt(jnp.sum(act * act, axis=-1, keepdims=True) + norm_eps)
                    unit_act = act * scale
                    dact = scale * (dout - unit_act * jnp.sum(dout * unit_act, axis=-1, keepdims=True))
                dconv = dact * (sig * (1.0 + pre * (1.0 - sig)))
                dext_ref[slot, part, pad : pad + length, :] = dconv
                for tap in range(taps):
                    shifted = ext_ref[slot, part, pl.ds(pad - taps + 1 + tap, length), :]
                    dconv_ref[part, tap : tap + 1, lanes(h)] += jnp.sum(dconv * shifted, axis=0, keepdims=True)
                summed, edge = None, None
                for tap in range(taps):
                    weight = conv_ref[part, tap : tap + 1, lanes(h)]
                    term = weight * dext_ref[slot, part, pl.ds(pad + taps - 1 - tap, length), :]
                    before = weight * dext_ref[slot, part, pl.ds(taps - 1 - tap, pad), :]
                    summed = term if summed is None else summed + term
                    edge = before if edge is None else edge + before
                col = lanes(part * heads + h)
                dense_ref[rows, col] = summed.astype(bf16)
                edge_out[s, :, col] = edge
                last_rows[s, :, col] = summed[length - pad :, :]

    start = 4
    each = -(-(scatter.steps - start) // (seqs * groups + 1))

    def some_heads(it, carry):
        heads_at_once(it // groups, [lax.rem(it, groups) * together + j for j in range(together)])
        flow(start + it * each, start + (it + 1) * each)
        return carry
    lax.fori_loop(0, seqs * groups, some_heads, 0)

    def edge_copy(other):
        return remote(edge_out, edge_in, edge_sems.at[0], edge_sems.at[1], "seq", other)

    @pl.when(me > 0)
    def _():
        edge_copy(me - 1).start()
    dbias = jnp.zeros((1, HEAD), f32)
    for s in range(seqs):
        low = dbeta_ref[s].astype(bf16)
        dense_ref[s * length : (s + 1) * length, 4 * width : 4 * width + HEAD] = low
        dbias = dbias + jnp.sum(low.astype(f32), axis=0, keepdims=True)
    dbias_ref[...] = dbias
    spare = dense_ref.shape[1] - 4 * width - HEAD
    if spare:
        dense_ref[:, 4 * width + HEAD :] = jnp.zeros((seqs * length, spare), bf16)
    flow(start + seqs * groups * each, scatter.steps)

    @pl.when(me < devices - 1)
    def _():
        edge_copy(0).wait_recv()
        for s in range(seqs):
            dense_ref[(s + 1) * length - pad : (s + 1) * length, 0 : 3 * width] = (last_rows[s] + edge_in[s]).astype(bf16)

    @pl.when(me > 0)
    def _():
        edge_copy(0).wait_send()


def delta_back(devices, arrays, jobs, inputs, unit=256, scatter_lag=2, wait=3, at_once=4):
    dim = arrays[jobs[0][0]].shape[1]
    proj, halo, conv_weight = inputs[:3]
    _, seqs, length, width = proj.shape
    pad = halo.shape[2]
    heads = width // HEAD
    chains = seqs * heads
    taps = conv_weight.shape[1]
    square = (HEAD, HEAD)
    dma = pltpu.SemaphoreType.DMA
    vmem = pl.BlockSpec(memory_space=pltpu.VMEM)
    out_shape = [jax.ShapeDtypeStruct((dim // devices, size), bf16) for _, _, _, size in jobs]
    out_shape += [
        jax.ShapeDtypeStruct((seqs * length, ceil_to(4 * width + HEAD, unit)), bf16),
        jax.ShapeDtypeStruct(conv_weight.shape, f32),
        jax.ShapeDtypeStruct((1, HEAD), f32),
        jax.ShapeDtypeStruct((8, HEAD), f32),
    ]
    together = min(at_once, heads)
    scratch = Scatter.scratch(devices, dim, sum(size for _, _, _, size in jobs), unit)
    scratch += [
        pltpu.VMEM((together, 3, pad + length, HEAD), f32),
        pltpu.VMEM((together, 3, 2 * pad + length, HEAD), f32),
        pltpu.VMEM((seqs, length, width), bf16),
        pltpu.VMEM((chains,) + square, bf16),
        pltpu.VMEM((devices,) + square, bf16),
        pltpu.VMEM((devices,) + square, bf16),
        pltpu.VMEM((chains,) + square, bf16),
        pltpu.VMEM((seqs, pad, 3 * width), f32),
        pltpu.VMEM((seqs, pad, 3 * width), f32),
        pltpu.VMEM((seqs, pad, 3 * width), f32),
        pltpu.VMEM((seqs, length, HEAD), f32),
        dma((chains,)), dma((devices,)), dma((devices,)), dma((chains,)), dma((2,)),
    ]
    scratch += Scatter.spaces(arrays, jobs) + staging([*arrays, *inputs])
    return pl.pallas_call(
        functools.partial(delta_back_kernel, devices, taps, jobs, unit, scatter_lag, wait, len(arrays)),
        in_specs=[pl.BlockSpec(memory_space=pltpu.HBM)] * (len(arrays) + len(inputs)),
        out_specs=[vmem] * len(out_shape),
        out_shape=out_shape,
        scratch_shapes=scratch,
        compiler_params=pltpu.CompilerParams(
            collective_id=2, has_side_effects=True, vmem_limit_bytes=62 << 20
        ),
        name="delta_back",
    )(*arrays, *inputs)


def last_kernel(seq_devices, tp_devices, jobs, unit, chunk, scatter_lag, line_lag, wait, pace, count, late_rows, *refs):
    peers = greet_axis("seq", seq_devices) + greet_axis("tp", tp_devices)
    soon = [count, count + 1] + list(range(count + 11, count + 15))
    later = [at for at in range(count + 15) if at not in soon]
    loads, refs = unstaged(refs, count + 15, soon + later)

    def take(number):
        out = refs[:number]
        del refs[:number]
        return out

    bits = seq_devices.bit_length() - 1
    arrays = take(count)
    dense_ref, w_beta_ref, tokens_ref, rstd_ref, gain_ref, grad_ref = take(6)
    dconv_ref, dbias_ref, dffn_gain_ref, head_gain_ref, norms_ref = take(5)
    weights = take(4)
    outs = take(len(jobs))
    tokens_grad_ref, conv_out, bias_out, gain_out, ffn_gain_out, head_out = take(6)
    held, *rest = take(1 + bits + 2)
    part, ups, downs, line_sems = take(4)
    (scaled_ref, dgain_ref, dots, dots_in, early_in, late, late_in, total,
     early_sems, late_sems, dot_sems, both_sems, early_ref, both_out) = take(14)
    seq, tp = lax.axis_index("seq"), lax.axis_index("tp")
    rows, dim = part.shape
    width = weights[0].shape[1]
    own = dim // tp_devices
    heads = w_beta_ref.shape[0]
    dgain_ref[...] = jnp.zeros_like(dgain_ref)
    dots[...] = jnp.zeros_like(dots)
    late[...] = jnp.zeros_like(late)
    for at in soon:
        loads[at].wait()
    meet(peers)
    for at in later:
        loads[at].wait()

    parts, taps, _ = dconv_ref.shape
    conv_rows = parts * taps * (width // HEAD)
    slices = own // HEAD
    split = conv_rows + 8
    both = early_ref.shape[0] - split

    def conv_places():
        for p in range(parts):
            for tap in range(taps):
                for c in range(width // HEAD):
                    row = (p * taps + tap) * (width // HEAD) + c
                    yield row, (p, slice(tap, tap + 1), slice(c * HEAD, (c + 1) * HEAD))

    early_ref[...] = jnp.zeros_like(early_ref)
    for row, place in conv_places():
        early_ref[row : row + 1, :] = dconv_ref[place]
    early_ref[conv_rows : conv_rows + 1, :] = dbias_ref[...]
    ffn_gain_sum = jnp.sum(dffn_gain_ref[...], axis=0, keepdims=True)
    for piece in range(tp_devices):
        @pl.when(tp == piece)
        def _():
            for c in range(slices):
                low = piece * own + c * HEAD
                early_ref[split + c : split + c + 1, :] = ffn_gain_sum[:, low : low + HEAD]
    early_ref[split + slices : split + slices + 1, :] = jnp.sum(head_gain_ref[...], axis=0, keepdims=True)
    early_ref[split + slices + 1 : split + slices + 2, :] = norms_ref[0:1, :]

    def to_peers(src, slots, sems, axis, size):
        me = lax.axis_index(axis)
        return [
            remote(src, slots.at[turn], sems.at[0, turn], sems.at[1, turn], axis, lax.rem(me + turn, size))
            for turn in range(1, size)
        ]

    early_copies = to_peers(early_ref, early_in, early_sems, "seq", seq_devices)
    for copy in early_copies:
        copy.start()

    def done(k, value):
        at = rows_of(k, chunk)
        x = tokens_ref[at, :].astype(f32)
        unit_rows = x * rstd_ref[at, :]
        dgain_ref[...] += jnp.sum((value * unit_rows).reshape(-1, 8, own), axis=0)
        scaled = value * gain_ref[...]
        scaled_ref[at, :] = scaled
        dot = jnp.sum(scaled * x, axis=-1, keepdims=True)
        per = HEAD // chunk
        place = lax.broadcasted_iota(jnp.int32, (chunk, HEAD), 0) + lax.rem(k, per) * chunk
        lane = lax.broadcasted_iota(jnp.int32, (chunk, HEAD), 1)
        dots[pl.ds(k // per, 1), :] += jnp.sum(jnp.where(place == lane, dot, 0.0), axis=0, keepdims=True)

    pairs = Scatter.turned(arrays, jobs, refs)
    scatter = Scatter(seq_devices, pairs, held, rest[:bits], outs, rest[bits], rest[bits + 1], unit, scatter_lag, 1, wait)
    line = Line(tp_devices, part, ups, downs, None, line_sems, chunk, line_lag, False, done)
    per = HEAD // chunk
    groups = rows // HEAD

    def step(i, carry):
        @pl.when(i < groups)
        def _():
            at = rows_of(i, HEAD)
            value = mm(dense_ref[at, 4 * width : 4 * width + heads], w_beta_ref[...])
            for w in range(4):
                value = value + mm(dense_ref[at, w * width : (w + 1) * width], weights[w][...], 1, 1)
            part[at, :] = value.astype(bf16)
            line.begin(i * per, per)
        paced(scatter, pace, i)
        line.step(i)
        for at, act in ((0, send_late), (gap, send_total), (2 * gap, finish_tokens)):
            pl.when(i == line.steps + at)(act)
        return carry

    late_copies = to_peers(late, late_in, late_sems, "seq", seq_devices)
    dot_copies = to_peers(dots, dots_in, dot_sems, "tp", tp_devices)
    both_copies = [
        remote(total, both_out.at[tp], both_sems.at[0, turn], both_sems.at[1, turn], "tp", lax.rem(tp + turn, tp_devices))
        for turn in range(1, tp_devices)
    ]
    gap = 4

    def send_late():
        dgain = jnp.sum(dgain_ref[...], axis=0, keepdims=True)
        for at in range(own // HEAD):
            late[at : at + 1, :] = dgain[:, at * HEAD : (at + 1) * HEAD]
        for copy in late_copies + dot_copies:
            copy.start()

    def send_total():
        for copy in early_copies + late_copies:
            copy.wait()
        early_total = early_ref[...]
        late_total = late[...]
        for turn in range(1, seq_devices):
            early_total = early_total + early_in[turn]
            late_total = late_total + late_in[turn]
        for row, place in conv_places():
            conv_out[place] = early_total[row : row + 1]
        bias_out[...] = early_total[conv_rows : conv_rows + 1]
        total[0:both, :] = early_total[split:]
        total[both:, :] = late_total
        both_out[tp] = total[...]
        for copy in both_copies:
            copy.start()

    def finish_tokens():
        for copy in dot_copies:
            copy.wait()
        dot_total = dots[...]
        for turn in range(1, tp_devices):
            dot_total = dot_total + dots_in[turn]
        dots[...] = dot_total / dim
        eye = lax.broadcasted_iota(jnp.int32, (HEAD, HEAD), 0) == lax.broadcasted_iota(jnp.int32, (HEAD, HEAD), 1)

        def finish(q, carry):
            at = rows_of(q, HEAD)
            dot = jnp.sum(jnp.where(eye, dots[pl.ds(q, 1), :], 0.0), axis=1, keepdims=True)
            scale = rstd_ref[at, :]
            x = tokens_ref[at, :].astype(f32)
            tokens_grad_ref[at, :] = grad_ref[at, :] + scale * scaled_ref[at, :] - x * (scale * scale * scale) * dot
            return carry
        lax.fori_loop(0, groups, finish, 0)

    lax.fori_loop(0, max(paced_steps(scatter, pace), line.steps + 2 * gap + 1), step, 0)
    line.end()
    for copy in both_copies:
        copy.wait()
    heads_total = jnp.zeros((2, HEAD), f32)
    for at in range(tp_devices):
        ffn_gain_out[at * slices : (at + 1) * slices, :] = both_out[at, 0:slices]
        gain_out[at * slices : (at + 1) * slices, :] = both_out[at, both : both + slices]
        heads_total = heads_total + both_out[at, slices : slices + 2]
    head_out[...] = heads_total


def last(
    seq_devices, tp_devices, arrays, jobs, dense, w_beta, tokens_own, rstd, gain_own, grad_own, small, sources,
    unit=256, chunk=32, scatter_lag=4, line_lag=2, wait=5, pace=(2, 3),
):
    dim = arrays[jobs[0][0]].shape[1]
    rows, own = tokens_own.shape
    width = sources[0].shape[1]
    late_rows = ceil_to(own // HEAD, 8)
    dot_rows = ceil_to(rows // HEAD, 8)
    dma = pltpu.SemaphoreType.DMA
    vmem, hbm = pl.BlockSpec(memory_space=pltpu.VMEM), pl.BlockSpec(memory_space=pltpu.HBM)
    out_shape = [jax.ShapeDtypeStruct((dim // seq_devices, size), bf16) for _, _, _, size in jobs]
    out_shape += [
        jax.ShapeDtypeStruct((rows, own), f32),
        jax.ShapeDtypeStruct(small[0].shape, f32),
        jax.ShapeDtypeStruct((1, HEAD), f32),
        jax.ShapeDtypeStruct((dim // HEAD, HEAD), f32),
        jax.ShapeDtypeStruct((dim // HEAD, HEAD), f32),
        jax.ShapeDtypeStruct((2, HEAD), f32),
    ]
    both = ceil_to(own // HEAD + 2, 8)
    early = small[0].size // HEAD + 8 + both
    scratch = Scatter.scratch(seq_devices, dim, sum(size for _, _, _, size in jobs), unit)
    scratch += [pltpu.VMEM((rows, dim), bf16)] + Line.scratch(rows, dim, tp_devices, chunk, False)
    scratch += [
        pltpu.VMEM((rows, own), f32),
        pltpu.VMEM((8, own), f32),
        pltpu.VMEM((dot_rows, HEAD), f32),
        pltpu.VMEM((tp_devices, dot_rows, HEAD), f32),
        pltpu.VMEM((seq_devices, early, HEAD), f32),
        pltpu.VMEM((late_rows, HEAD), f32),
        pltpu.VMEM((seq_devices, late_rows, HEAD), f32),
        pltpu.VMEM((both + late_rows, HEAD), f32),
        dma((2, seq_devices)), dma((2, seq_devices)), dma((2, tp_devices)), dma((2, tp_devices)),
        pltpu.VMEM((early, HEAD), f32),
        pltpu.VMEM((tp_devices, both + late_rows, HEAD), f32),
    ]
    inputs = [*arrays, dense, w_beta, tokens_own, rstd, gain_own, grad_own, *small, *sources]
    scratch += Scatter.spaces(arrays, jobs) + staging(inputs)
    return pl.pallas_call(
        functools.partial(
            last_kernel, seq_devices, tp_devices, jobs, unit, chunk, scatter_lag, line_lag, wait, pace, len(arrays), late_rows
        ),
        in_specs=[hbm] * len(inputs),
        out_specs=[vmem] * len(out_shape),
        out_shape=out_shape,
        scratch_shapes=scratch,
        compiler_params=pltpu.CompilerParams(
            collective_id=5, has_side_effects=True, vmem_limit_bytes=62 << 20
        ),
        name="last_sums",
    )(*inputs)


def on_device(
    tokens,
    seq_lengths,
    norm_gain,
    w_query,
    w_key,
    w_value,
    w_gate,
    w_beta,
    beta_bias,
    conv_weight,
    out_gain,
    w_out,
    ffn_gain,
    w_ffn_gate,
    w_ffn_up,
    w_ffn_down,
    cotangent,
):
    seqs_here, local_len, model_dim = tokens.shape
    row_count = seqs_here * local_len
    heads_here = w_beta.shape[1]
    local_width = w_query.shape[1]
    halo_pad = 16
    seq_devices = lax.axis_size("seq")
    tp_index = lax.axis_index("tp")
    tp_devices = lax.axis_size("tp")
    slice_width = model_dim // lax.axis_size("tp")
    tokens_flat = tokens.reshape(row_count, model_dim)
    grad_low = cotangent.reshape(row_count, model_dim)
    normed_one, rstd_one, proj, halo, gate_pre, beta_val, slope, live_rows, tokens_own = first(
        seq_devices, tp_devices, tokens_flat, norm_gain, w_query, w_key, w_value, w_gate, w_beta.T, beta_bias, seq_lengths
    )
    proj_seq = proj.reshape(3, seqs_here, local_len, local_width)
    halo_rows = halo.reshape(3, seqs_here, halo_pad, local_width)
    beta_seq = beta_val.reshape(seqs_here, local_len, heads_here)
    slope = slope.reshape(seqs_here, local_len, heads_here)
    gate_seq = gate_pre.reshape(seqs_here, local_len, local_width)

    tri, keep, state_in, moves, norms, mixed, fresh, heads_seq = delta_forward(
        seq_devices, proj_seq, halo_rows, conv_weight, beta_seq, gate_seq, out_gain
    )
    heads_out = heads_seq.reshape(row_count, local_width)

    normed_two, dffn_both, ffn_hidden, hidden_own, hidden_low, dnormed_part_two = attention_ffn(
        tp_devices, heads_out, w_out, tokens_flat, live_rows, ffn_gain, w_ffn_gate, w_ffn_up, w_ffn_down, grad_low
    )
    ffn_width = w_ffn_gate.shape[1]
    ffn_pad = ffn_hidden.shape[1]
    early = min(768, ffn_pad - 256)
    dw_both, dw_down_early, dattn, grad_own, dheads, dffn_gain, ffn_part = ffn_back(
        seq_devices,
        tp_devices,
        [normed_two, grad_low, dffn_both, ffn_hidden],
        [(0, 2, 0, dffn_both.shape[1]), (1, 3, 0, early)],
        3,
        1,
        dnormed_part_two,
        hidden_low,
        live_rows,
        ffn_gain,
        w_out,
        w_ffn_down,
    )
    ffn_slice = lax.psum_scatter(ffn_part, "tp", scatter_dimension=1, tiled=True)

    def own_slice(value):
        return lax.dynamic_slice_in_dim(value, tp_index * slice_width, slice_width, value.ndim - 1)

    dw_down, dw_out, dense, dconv, dbias, dgain = delta_back(
        seq_devices,
        [grad_low, ffn_hidden, dattn, heads_out],
        [(0, 1, early, ffn_pad - early), (2, 3, 0, local_width)],
        [
            proj_seq, halo_rows, conv_weight, beta_seq, slope, tri, keep, fresh, state_in, moves,
            dheads, mixed, gate_seq, out_gain.reshape(1, HEAD),
        ],
    )
    dense, ffn_slice = lax.optimization_barrier((dense, ffn_slice))
    dw_first, tokens_grad, conv_grad, bias_grad, gain_grad, ffn_gain_grad, head_total = last(
        seq_devices,
        tp_devices,
        [normed_one, dense],
        [(0, 1, 0, dense.shape[1])],
        dense,
        w_beta.T,
        tokens_own,
        rstd_one,
        own_slice(norm_gain).reshape(1, slice_width),
        grad_own,
        [dconv, dbias, dffn_gain, dgain, norms],
        [w_query, w_key, w_value, w_gate],
    )
    out_tokens = (hidden_own + ffn_slice.astype(f32)).astype(bf16).reshape(seqs_here, local_len, slice_width)
    lw = local_width

    def wide(value):
        return value.astype(f32)

    return (
        out_tokens,
        tokens_grad.reshape(seqs_here, local_len, slice_width),
        gain_grad.reshape(model_dim),
        wide(dw_first[:, :lw]),
        wide(dw_first[:, lw : 2 * lw]),
        wide(dw_first[:, 2 * lw : 3 * lw]),
        wide(dw_first[:, 3 * lw : 4 * lw]),
        wide(dw_first[:, 4 * lw : 4 * lw + heads_here]),
        bias_grad[0, :heads_here],
        conv_grad,
        head_total[0],
        wide(dw_out.T),
        ffn_gain_grad.reshape(model_dim),
        wide(dw_both[:, :ffn_width]),
        wide(dw_both[:, dffn_both.shape[1] // 2 :][:, :ffn_width]),
        wide(jnp.concatenate([dw_down_early, dw_down], axis=1).T[:ffn_width]),
        head_total[1, 0] / (seqs_here * HEADS),
    )


def solution(mesh):
    in_specs = (
        P(None, "seq", None),
        P(),
        P(),
        P(None, "tp"),
        P(None, "tp"),
        P(None, "tp"),
        P(None, "tp"),
        P(None, "tp"),
        P("tp"),
        P(None, None, "tp"),
        P(),
        P("tp", None),
        P(),
        P(None, "tp"),
        P(None, "tp"),
        P("tp", None),
        P(None, "seq", None),
    )
    out_specs = (
        P(None, "seq", "tp"),
        P(None, "seq", "tp"),
        P(),
        P("seq", "tp"),
        P("seq", "tp"),
        P("seq", "tp"),
        P("seq", "tp"),
        P("seq", "tp"),
        P("tp"),
        P(None, None, "tp"),
        P(),
        P("tp", "seq"),
        P(),
        P("seq", "tp"),
        P("seq", "tp"),
        P("tp", "seq"),
        P(),
    )
    return jax.shard_map(
        on_device, mesh=mesh, in_specs=in_specs, out_specs=out_specs, check_vma=False
    )
```

```python
import functools

import jax
import jax.numpy as jnp
from jax import lax
from jax.experimental import pallas as pl
from jax.experimental.pallas import tpu as pltpu
from jax.sharding import PartitionSpec as P

HEADS = 16
HEAD = 128

norm_eps = 1e-06
f32 = jnp.float32
bf16 = jnp.bfloat16
MESH = pl.DeviceIdType.MESH
VM = pltpu.VMEM


def mm(left, right, contract_left=1, contract_right=0):
    return lax.dot_general(
        left.astype(bf16),
        right.astype(bf16),
        (((contract_left,), (contract_right,)), ((), ())),
        preferred_element_type=f32,
    )


def from_behind(block, axis, distance):
    devices = range(lax.axis_size(axis))
    route = [(i - distance, i) for i in devices if i - distance in devices]
    return lax.ppermute(block, axis, route)


def sigmoid(value):
    return 1.0 / (1.0 + jnp.exp(-value))


def silu_grad(value):
    sigmoid_val = sigmoid(value)
    return sigmoid_val * (1.0 + value * (1.0 - sigmoid_val))


def dot_left(left, right):
    return mm(left, right, 0, 0)


def dot_right(left, right):
    return mm(left, right, 1, 1)


def strict_lower(size):
    rows = lax.broadcasted_iota(jnp.int32, (size, size), 0)
    cols = lax.broadcasted_iota(jnp.int32, (size, size), 1)
    return rows > cols, rows >= cols, rows ^ cols


def unit_lower_inverses(lows, apart):
    size = lows[0].shape[0]
    inverses = [jnp.where(apart == 0, 1.0, 0.0) - jnp.where(apart == 1, low, 0.0) for low in lows]
    step = 2
    while step < size:
        pair = (apart >= step) & (apart < 2 * step)
        between = [jnp.where(pair, low, 0.0).astype(bf16) for low in lows]
        inner = [inverse.astype(bf16) for inverse in inverses]
        right = [mm(left, at) for left, at in zip(between, inner)]
        inverses = [inverse - mm(at, value) for inverse, at, value in zip(inverses, inner, right)]
        step *= 2
    return inverses


def conv_silu(ext_ref, col, conv_ref, part, lane, length, taps, pad):
    summed = None
    for tap in range(taps):
        term = conv_ref[part, tap : tap + 1, lane] * ext_ref[pl.ds(pad - taps + 1 + tap, length), col]
        summed = term if summed is None else summed + term
    return summed


def delta_forward_kernel(
    devices, taps, proj_ref, halo_ref, conv_ref, beta_ref, gate_ref, gain_ref,
    tri_ref, query_ref, state_ref, moves_ref, norm_ref, mixed_ref, fresh_ref, heads_ref,
    ext_ref, keep_ref, move_in, offset_in, offset_all, states, send_zero, recv_zero, send_one, recv_one, send_two, recv_two,
):
    _, seqs, length, width = proj_ref.shape
    pad = halo_ref.shape[2]
    heads = width // HEAD
    chains = seqs * heads
    me = lax.axis_index("seq")
    peers = greet_axis("seq", devices)
    below, upto, apart = strict_lower(length)
    some = range(heads)

    def act(part, h):
        lane = slice(h * HEAD, (h + 1) * HEAD)
        col = slice(part * width + h * HEAD, part * width + (h + 1) * HEAD)
        summed = conv_silu(ext_ref, col, conv_ref, part, lane, length, taps, pad)
        return summed * sigmoid(summed)

    def unit(value):
        return value * lax.rsqrt(jnp.sum(value * value, axis=-1, keepdims=True) + norm_eps)

    def send_maps(chain):
        remote(move_in.at[chain], moves_ref.at[me], send_zero.at[chain], recv_zero.at[me], "seq", chain).start()
        remote(offset_in.at[chain], offset_all.at[me], send_one.at[chain], recv_one.at[me], "seq", chain).start()

    def local(s, carry):
        for part in range(3):
            col = slice(part * width, (part + 1) * width)
            ext_ref[0:pad, col] = halo_ref[part, s].astype(f32)
            ext_ref[pad : pad + length, col] = proj_ref[part, s].astype(f32)
        queries = [unit(act(0, h)).astype(bf16) for h in some]
        keys = [unit(act(1, h)).astype(bf16) for h in some]
        values = [act(2, h).astype(bf16) for h in some]
        betas = [beta_ref[s, :, h : h + 1] for h in some]
        lows = [jnp.where(below, beta * mm(key, key, 1, 1), 0.0) for beta, key in zip(betas, keys)]
        inverses = unit_lower_inverses(lows, apart)
        for h, query, key, value, beta, inverse in zip(some, queries, keys, values, betas, inverses):
            inverse = inverse.astype(bf16)
            targets = jnp.concatenate([beta * key.astype(f32), beta * value.astype(f32)], axis=1)
            solved_low = mm(inverse, targets).astype(bf16)
            scores = jnp.where(upto, mm(query, key, 1, 1), 0.0).astype(bf16)
            passed = mm(scores, solved_low)
            moved = mm(key, solved_low, 0, 0)
            tri_ref[s, h] = inverse
            query_ref[s, h] = (query.astype(f32) - passed[:, :HEAD]).astype(bf16)
            keep_ref[s, h, :, 0:HEAD] = passed[:, HEAD:].astype(bf16)
            keep_ref[s, h, :, HEAD:] = solved_low
            move_in[s * heads + h] = (-moved[:, :HEAD]).astype(bf16)
            offset_in[s * heads + h] = moved[:, HEAD:].astype(bf16)

        @pl.when(s == 0)
        def _():
            meet(peers)
        for h in some:
            chain = s * heads + h

            @pl.when(me != chain)
            def _():
                send_maps(chain)

            @pl.when(me == chain)
            def _():
                moves_ref[me] = move_in[chain]
                offset_all[me] = offset_in[chain]
        return carry
    lax.fori_loop(0, seqs, local, 0)

    @pl.when(me < chains)
    def _():
        state = jnp.zeros((HEAD, HEAD), f32)
        for at in range(devices):
            states[at] = state.astype(bf16)

            @pl.when(me != at)
            def _():
                remote(states.at[at], state_ref.at[me], send_two.at[at], recv_two.at[me], "seq", at).start()
                remote(move_in.at[0], moves_ref.at[at], send_zero.at[0], recv_zero.at[at], "seq", at).wait_recv()
                remote(offset_in.at[0], offset_all.at[at], send_one.at[0], recv_one.at[at], "seq", at).wait_recv()

            @pl.when(me == at)
            def _():
                state_ref[me] = states[at]
            state = state + mm(moves_ref[at], state) + offset_all[at].astype(f32)
        norm_ref[...] = jnp.zeros_like(norm_ref) + jnp.sqrt(jnp.sum(state * state, keepdims=True))
        for at in range(devices):
            @pl.when(me != at)
            def _():
                remote(states.at[at], state_ref.at[0], send_two.at[at], recv_two.at[0], "seq", at).wait_send()

    @pl.when(me >= chains)
    def _():
        norm_ref[...] = jnp.zeros_like(norm_ref)
    for chain in range(chains):
        @pl.when(me != chain)
        def _():
            remote(move_in.at[chain], moves_ref.at[0], send_zero.at[chain], recv_zero.at[0], "seq", chain).wait_send()
            remote(offset_in.at[chain], offset_all.at[0], send_one.at[chain], recv_one.at[0], "seq", chain).wait_send()
            remote(states.at[0], state_ref.at[chain], send_two.at[0], recv_two.at[chain], "seq", chain).wait_recv()

    def out(s, carry):
        for h in some:
            lane = slice(h * HEAD, (h + 1) * HEAD)
            state = state_ref[s * heads + h]
            mixed = keep_ref[s, h, :, 0:HEAD].astype(f32) + mm(query_ref[s, h], state)
            fresh = keep_ref[s, h, :, 2 * HEAD :].astype(f32) - mm(keep_ref[s, h, :, HEAD : 2 * HEAD], state)
            rstd = lax.rsqrt(jnp.mean(mixed * mixed, axis=-1, keepdims=True) + norm_eps)
            gate = gate_ref[s, :, lane]
            mixed_ref[s, :, lane] = mixed
            fresh_ref[s, :, lane] = fresh.astype(bf16)
            heads_ref[s, :, lane] = (mixed * rstd * gain_ref[...] * (gate * sigmoid(gate))).astype(bf16)
        return carry
    lax.fori_loop(0, seqs, out, 0)


def delta_forward(devices, proj, halo, conv_weight, beta, gate, gain):
    _, seqs, length, width = proj.shape
    pad = halo.shape[2]
    heads = width // HEAD
    chains = seqs * heads
    square = (HEAD, HEAD)
    dma = pltpu.SemaphoreType.DMA
    vmem = pl.BlockSpec(memory_space=pltpu.VMEM)
    out_shape = [
        jax.ShapeDtypeStruct((seqs, heads, length, length), bf16),
        jax.ShapeDtypeStruct((seqs, heads, length, HEAD), bf16),
        jax.ShapeDtypeStruct((chains,) + square, bf16),
        jax.ShapeDtypeStruct((devices,) + square, bf16),
        jax.ShapeDtypeStruct((8, HEAD), f32),
        jax.ShapeDtypeStruct((seqs, length, width), f32),
        jax.ShapeDtypeStruct((seqs, length, width), bf16),
        jax.ShapeDtypeStruct((seqs, length, width), bf16),
    ]
    return pl.pallas_call(
        functools.partial(delta_forward_kernel, devices, conv_weight.shape[1]),
        in_specs=[vmem] * 6,
        out_specs=[vmem] * len(out_shape),
        out_shape=out_shape,
        scratch_shapes=[
            pltpu.VMEM((pad + length, 3 * width), f32),
            pltpu.VMEM((seqs, heads, length, 3 * HEAD), bf16),
            pltpu.VMEM((chains,) + square, bf16),
            pltpu.VMEM((chains,) + square, bf16),
            pltpu.VMEM((devices,) + square, bf16),
            pltpu.VMEM((devices,) + square, bf16),
            dma((chains,)), dma((devices,)), dma((chains,)), dma((devices,)), dma((devices,)), dma((chains,)),
        ],
        compiler_params=pltpu.CompilerParams(
            collective_id=1, has_side_effects=True, vmem_limit_bytes=62 << 20
        ),
        name="delta_forward",
    )(proj, halo, conv_weight, beta, gate, gain.reshape(1, HEAD))


def first_kernel(
    seq_devices, tp_devices, tokens_ref, gain_ref, w_beta_ref, bias_ref, lengths_ref, *refs
):
    (w_query, w_key, w_value, w_gate, normed_ref, rstd_ref, proj_ref, halo_ref, gate_ref, beta_ref, slope_ref,
     live_ref, own_ref, weights, halo_in, load_sem, send_sem, recv_sem) = refs
    rows, dim = tokens_ref.shape
    seqs, pad, _ = halo_in.shape
    length = rows // seqs
    me = lax.axis_index("seq")
    loads = [
        pltpu.make_async_copy(source, weights.at[at], load_sem.at[at])
        for at, source in enumerate((w_query, w_key, w_value, w_gate))
    ]
    for load in loads:
        load.start()
    barrier = pltpu.get_barrier_semaphore()

    @pl.when(me > 0)
    def _():
        pl.semaphore_signal(barrier, inc=1, device_id={"seq": me - 1}, device_id_type=MESH)

    @pl.when(me < seq_devices - 1)
    def _():
        pl.semaphore_signal(barrier, inc=1, device_id={"seq": me + 1}, device_id_type=MESH)

    gain = gain_ref[...]

    def norm(q, carry):
        at = pl.ds(pl.multiple_of(q * 128, 128), 128)
        value = tokens_ref[at, :].astype(f32)
        scale = lax.rsqrt(jnp.mean(value * value, axis=-1, keepdims=True) + norm_eps)
        rstd_ref[at, :] = scale
        normed_ref[at, :] = (value * scale * gain).astype(bf16)
        return carry
    lax.fori_loop(0, rows // 128, norm, 0)
    pl.semaphore_wait(barrier, jnp.minimum(me, 1) + jnp.minimum(seq_devices - 1 - me, 1))

    def halo_copy(s):
        return pltpu.make_async_remote_copy(
            src_ref=tokens_ref.at[pl.ds((s + 1) * length - pad, pad)], dst_ref=halo_in.at[s],
            send_sem=send_sem.at[s], recv_sem=recv_sem.at[s],
            device_id={"seq": me + 1}, device_id_type=MESH,
        )

    @pl.when(me < seq_devices - 1)
    def _():
        for s in range(seqs):
            halo_copy(s).start()

    for s in range(seqs):
        position = me * length + lax.broadcasted_iota(jnp.int32, (length, 1), 0)
        live_ref[s * length : (s + 1) * length, :] = jnp.where(position < lengths_ref[0:1, s : s + 1], 1.0, 0.0)
    width = own_ref.shape[1]
    for piece in range(tp_devices):
        @pl.when(lax.axis_index("tp") == piece)
        def _():
            own_ref[...] = tokens_ref[:, piece * width : (piece + 1) * width]
    sig = sigmoid(mm(normed_ref[...], w_beta_ref[...], 1, 1) + bias_ref[...])
    beta = live_ref[...] * sig
    beta_ref[...] = beta
    slope_ref[...] = beta * (1.0 - sig)
    for part in range(4):
        loads[part].wait()

        def some(q, carry):
            at = pl.ds(pl.multiple_of(q * 256, 256), 256)
            product = mm(normed_ref[at, :], weights[part])
            if part < 3:
                proj_ref[part, at, :] = product.astype(bf16)
            else:
                gate_ref[at, :] = product
            return carry
        lax.fori_loop(0, rows // 256, some, 0)

    @pl.when(me > 0)
    def _():
        for s in range(seqs):
            halo_copy(s).wait_recv()
        value = halo_in[...].reshape(seqs * pad, dim).astype(f32)
        scale = lax.rsqrt(jnp.mean(value * value, axis=-1, keepdims=True) + norm_eps)
        normed = (value * scale * gain).astype(bf16)
        for part in range(3):
            halo_ref[part] = mm(normed, weights[part]).astype(bf16)

    @pl.when(me == 0)
    def _():
        halo_ref[...] = jnp.zeros_like(halo_ref)

    @pl.when(me < seq_devices - 1)
    def _():
        for s in range(seqs):
            halo_copy(s).wait_send()


def first(seq_devices, tp_devices, tokens, gain, w_query, w_key, w_value, w_gate, w_beta, bias, lengths):
    rows, dim = tokens.shape
    width, heads = w_query.shape[1], w_beta.shape[0]
    seqs = lengths.shape[0]
    pad = 16
    vmem, hbm = pl.BlockSpec(memory_space=pltpu.VMEM), pl.BlockSpec(memory_space=pltpu.HBM)
    out_shape = [
        jax.ShapeDtypeStruct((rows, dim), bf16),
        jax.ShapeDtypeStruct((rows, 1), f32),
        jax.ShapeDtypeStruct((3, rows, width), bf16),
        jax.ShapeDtypeStruct((3, seqs * pad, width), bf16),
        jax.ShapeDtypeStruct((rows, width), f32),
        jax.ShapeDtypeStruct((rows, heads), f32),
        jax.ShapeDtypeStruct((rows, heads), f32),
        jax.ShapeDtypeStruct((rows, 1), f32),
        jax.ShapeDtypeStruct((rows, dim // tp_devices), bf16),
    ]
    return pl.pallas_call(
        functools.partial(first_kernel, seq_devices, tp_devices),
        in_specs=[vmem] * 5 + [hbm] * 4,
        out_specs=[vmem] * len(out_shape),
        out_shape=out_shape,
        scratch_shapes=[
            pltpu.VMEM((4, dim, width), bf16),
            pltpu.VMEM((seqs, pad, dim), bf16),
            pltpu.SemaphoreType.DMA((4,)),
            pltpu.SemaphoreType.DMA((seqs,)),
            pltpu.SemaphoreType.DMA((seqs,)),
        ],
        compiler_params=pltpu.CompilerParams(
            collective_id=7, has_side_effects=True, vmem_limit_bytes=62 << 20
        ),
        name="first_norm_projections",
    )(tokens, gain.reshape(1, dim), w_beta, bias.reshape(1, heads), lengths.reshape(1, seqs), w_query, w_key, w_value, w_gate)


def ceil_to(value, unit):
    return -(-value // unit) * unit


class Line:
    def __init__(self, devices, part, ups, downs, out, sems, chunk, lag, whole, done=None):
        self.done = done
        self.n, self.part, self.ups, self.downs, self.out, self.sems = devices, part, ups, downs, out, sems
        self.chunk, self.lag, self.whole = chunk, lag, whole
        self.chunks = part.shape[0] // chunk
        self.me = lax.axis_index("tp")
        self.pieces = 1 if whole else devices
        self.width = part.shape[1] // self.pieces
        self.last = (devices - 2) * lag
        self.steps = self.chunks + self.last

    @staticmethod
    def scratch(rows, cols, devices, chunk, whole):
        count = (rows // chunk) * (1 if whole else devices)
        return [pltpu.VMEM((rows, cols), bf16)] * 2 + [pltpu.SemaphoreType.DMA((4, count))]

    def copy(self, source, way, k, piece):
        at = (pl.ds(pl.multiple_of(k * self.chunk, self.chunk), self.chunk), slice(piece * self.width, (piece + 1) * self.width))
        target = self.ups if way == 0 else self.downs
        sem = k * self.pieces + piece
        other = self.me + 1 if way == 0 else self.me - 1
        return pltpu.make_async_remote_copy(
            src_ref=source.at[at], dst_ref=target.at[at],
            send_sem=self.sems.at[way, sem], recv_sem=self.sems.at[2 + way, sem],
            device_id={"tp": other}, device_id_type=MESH,
        )

    def begin(self, first, count):
        for way, end in ((0, 0), (1, self.n - 1)):
            @pl.when(self.me == end)
            def _():
                def send(k, carry):
                    for piece in range(self.pieces) if way else reversed(range(self.pieces)):
                        if self.whole or piece != end:
                            self.copy(self.part, way, k, piece).start()
                    return carry
                lax.fori_loop(first, first + count, send, 0)

    def forward(self, way, k):
        me, n = self.me, self.n
        held = self.ups if way == 0 else self.downs
        rows = pl.ds(pl.multiple_of(k * self.chunk, self.chunk), self.chunk)
        for piece in range(self.pieces):
            if self.whole:
                gets, goes = None, me < n - 1 if way == 0 else me > 0
            else:
                gets, goes = (piece >= me, piece > me) if way == 0 else (piece <= me, piece < me)
            cols = slice(piece * self.width, (piece + 1) * self.width)

            def take():
                self.copy(self.part, way, k, piece).wait_recv()

                @pl.when(goes)
                def _():
                    held[rows, cols] = (held[rows, cols].astype(f32) + self.part[rows, cols].astype(f32)).astype(bf16)
                    self.copy(held, way, k, piece).start()

            if gets is None:
                take()
            else:
                pl.when(gets)(take)

    def give(self, k, total):
        if self.done is None:
            self.out[pl.ds(pl.multiple_of(k * self.chunk, self.chunk), self.chunk), :] = total
        else:
            self.done(k, total)

    def finish(self, k):
        me, n = self.me, self.n
        rows = pl.ds(pl.multiple_of(k * self.chunk, self.chunk), self.chunk)
        if self.whole:
            @pl.when(me == 0)
            def _():
                self.give(k, self.part[rows, :].astype(f32) + self.downs[rows, :].astype(f32))

            @pl.when(me == n - 1)
            def _():
                self.give(k, self.part[rows, :].astype(f32) + self.ups[rows, :].astype(f32))

            @pl.when((me > 0) & (me < n - 1))
            def _():
                both = self.ups[rows, :].astype(f32) - self.part[rows, :].astype(f32)
                self.give(k, both + self.downs[rows, :].astype(f32))
        else:
            for piece in range(n):
                @pl.when(me == piece)
                def _():
                    cols = slice(piece * self.width, (piece + 1) * self.width)
                    total = self.part[rows, cols].astype(f32)
                    if piece > 0:
                        total = total + self.ups[rows, cols].astype(f32)
                    if piece < n - 1:
                        total = total + self.downs[rows, cols].astype(f32)
                    self.give(k, total)

    def step(self, i):
        me, n = self.me, self.n
        up = i - (me - 1) * self.lag
        down = i - (n - 2 - me) * self.lag

        @pl.when((me > 0) & (up >= 0) & (up < self.chunks))
        def _():
            self.forward(0, up)

        @pl.when((me < n - 1) & (down >= 0) & (down < self.chunks))
        def _():
            self.forward(1, down)

        done = i - self.last

        @pl.when((done >= 0) & (done < self.chunks))
        def _():
            self.finish(done)

    def end(self):
        def drain(k, carry):
            for way in range(2):
                for piece in range(self.pieces):
                    if self.whole:
                        goes = self.me < self.n - 1 if way == 0 else self.me > 0
                    else:
                        goes = piece > self.me if way == 0 else piece < self.me

                    @pl.when(goes)
                    def _():
                        self.copy(self.part, way, k, piece).wait_send()
            return carry
        lax.fori_loop(0, self.chunks, drain, 0)


class Scatter:
    def __init__(self, devices, jobs, held, gots, outs, sends, recvs, unit, lag, ahead, wait):
        self.ahead, self.wait = ahead, wait
        self.n, self.jobs, self.held, self.gots, self.outs = devices, jobs, held, gots, outs
        self.sends, self.recvs, self.unit, self.lag = sends, recvs, unit, lag
        self.bits = devices.bit_length() - 1
        self.me = lax.axis_index("seq")
        self.block = jobs[0][0].shape[0] // devices
        self.chunks = sum(size for _, _, _, size in jobs) // unit
        self.steps = self.chunks + wait + (self.bits - 2) * lag

    @staticmethod
    def scratch(devices, rows, cols, unit):
        chunks, bits, block = cols // unit, devices.bit_length() - 1, rows // devices
        shapes = [pltpu.VMEM((chunks, devices // 2, block, unit), bf16)]
        shapes += [pltpu.VMEM((chunks, devices >> (s + 1), block, unit), bf16) for s in range(bits)]
        return shapes + [pltpu.SemaphoreType.DMA((bits, chunks))] * 2

    @staticmethod
    def turn(arrays, jobs, spaces):
        for space, x in zip(spaces, sorted({x for x, _, _, _ in jobs})):
            def one(j, carry):
                at = pl.ds(pl.multiple_of(j * 256, 256), 256)
                space[at, :] = arrays[x][:, at].T
                return carry
            lax.fori_loop(0, space.shape[0] // 256, one, 0)

    @staticmethod
    def turns(arrays, jobs, spaces):
        lefts = sorted({x for x, _, _, _ in jobs})
        return [(spaces[lefts.index(x)], arrays[y], start, size) for x, y, start, size in jobs]

    @staticmethod
    def turned(arrays, jobs, spaces):
        Scatter.turn(arrays, jobs, spaces)
        return Scatter.turns(arrays, jobs, spaces)

    @staticmethod
    def spaces(arrays, jobs):
        return [pltpu.VMEM(arrays[x].shape[::-1], bf16) for x in sorted({x for x, _, _, _ in jobs})]

    def power(self, stage, chunk):
        if stage == 0:
            return 1
        odd = lax.rem(chunk, 2)
        return odd * (1 << (self.bits - stage)) + (1 - odd) * (1 << stage)

    def bit(self, stage, chunk):
        return lax.rem(self.me // self.power(stage, chunk), 2)

    def partner(self, stage, chunk):
        return self.me + (1 - 2 * self.bit(stage, chunk)) * self.power(stage, chunk)

    def start_of_kept(self, stage, chunk):
        at = 0
        for s in range(1, stage):
            at = at + self.bit(s, chunk) * (self.n >> (s + 1))
        return at

    def copy(self, stage, chunk):
        count = self.n >> (stage + 1)
        if stage == 0:
            at = 0
        else:
            at = self.start_of_kept(stage, chunk) + (1 - self.bit(stage, chunk)) * count
        return pltpu.make_async_remote_copy(
            src_ref=self.held.at[chunk, pl.ds(at, count)], dst_ref=self.gots[stage].at[chunk],
            send_sem=self.sends.at[stage, chunk], recv_sem=self.recvs.at[stage, chunk],
            device_id={"seq": self.partner(stage, chunk)}, device_id_type=MESH,
        )

    def products(self, chunk, core, use):
        low = 0
        for x, y, start, size in self.jobs:
            count = size // self.unit

            @pl.when((chunk >= low) & (chunk < low + count))
            def _():
                right = y[:, pl.ds(pl.multiple_of(start + (chunk - low) * self.unit, 128), self.unit)]

                values = []
                for j in range(self.n // 2):
                    target = core
                    for s in range(1, self.bits):
                        target = target + j // (self.n >> (s + 1)) % 2 * self.power(s, chunk)
                    mine = pl.ds(pl.multiple_of(target * self.block, self.block), self.block)
                    values.append(mm(x[mine, :], right))
                for j, value in enumerate(values):
                    use(j, value)
            low += count

    def produce(self, i):
        core = lax.rem(self.me, 2)

        @pl.when(i < self.chunks)
        def _():
            def put(j, value):
                self.held[i, j] = value.astype(bf16)
            self.products(i, 1 - core, put)
            self.copy(0, i).start()

        first = i - 1

        @pl.when((first >= 0) & (first < self.chunks))
        def _():
            self.copy(0, first).wait()

            def put(j, value):
                self.held[first, j] = (value + self.gots[0][first, j].astype(f32)).astype(bf16)
            self.products(first, core, put)
            self.copy(1, first).start()

    def consume(self, i):
        for stage in range(1, self.bits):
            chunk = i - (stage - 1) * self.lag

            @pl.when((chunk >= 0) & (chunk < self.chunks))
            def _():
                self.copy(stage, chunk).wait()
                count = self.n >> (stage + 1)
                base = self.start_of_kept(stage + 1, chunk)
                if stage < self.bits - 1:
                    for j in range(count):
                        self.held[chunk, base + j] = (
                            self.held[chunk, base + j].astype(f32) + self.gots[stage][chunk, j].astype(f32)
                        ).astype(bf16)
                    self.copy(stage + 1, chunk).start()
                else:
                    low = 0
                    for (_, _, _, size), out in zip(self.jobs, self.outs):
                        size = size // self.unit

                        @pl.when((chunk >= low) & (chunk < low + size))
                        def _():
                            cols = pl.ds(pl.multiple_of((chunk - low) * self.unit, self.unit), self.unit)
                            total = self.held[chunk, base].astype(f32) + self.gots[stage][chunk, 0].astype(f32)
                            out[:, cols] = total.astype(out.dtype)
                        low += size

    def step(self, i):
        for turn in range(self.ahead):
            self.produce(i * self.ahead + turn)
        self.consume(i - self.wait)


def greet_line(tp_devices):
    tp = lax.axis_index("tp")
    barrier = pltpu.get_barrier_semaphore()

    @pl.when(tp > 0)
    def _():
        pl.semaphore_signal(barrier, inc=1, device_id={"tp": tp - 1}, device_id_type=MESH)

    @pl.when(tp < tp_devices - 1)
    def _():
        pl.semaphore_signal(barrier, inc=1, device_id={"tp": tp + 1}, device_id_type=MESH)
    return jnp.minimum(tp, 1) + jnp.minimum(tp_devices - 1 - tp, 1)


def greet_halving(seq_devices):
    seq = lax.axis_index("seq")
    barrier = pltpu.get_barrier_semaphore()
    bits = seq_devices.bit_length() - 1
    for b in range(bits):
        other = seq + (1 - 2 * lax.rem(seq // (1 << b), 2)) * (1 << b)
        pl.semaphore_signal(barrier, inc=1, device_id={"seq": other}, device_id_type=MESH)
    return bits


def greet_axis(axis, size):
    me = lax.axis_index(axis)
    barrier = pltpu.get_barrier_semaphore()
    for turn in range(1, size):
        pl.semaphore_signal(barrier, inc=1, device_id={axis: lax.rem(me + turn, size)}, device_id_type=MESH)
    return size - 1


def meet(peers):
    pl.semaphore_wait(pltpu.get_barrier_semaphore(), peers)


def unstaged(refs, count, order=None):
    spaces, sems = refs[-count - 1 : -1], refs[-1]
    loads = [pltpu.make_async_copy(refs[at], spaces[at], sems.at[at]) for at in range(count)]
    for at in order or range(count):
        loads[at].start()
    return loads, list(spaces) + list(refs[count : -count - 1])


def staging(arrays):
    return [pltpu.VMEM(item.shape, item.dtype) for item in arrays] + [pltpu.SemaphoreType.DMA((len(arrays),))]


def rows_of(k, size):
    return pl.ds(pl.multiple_of(k * size, size), size)


def put_own(out, at, value, axis_size):
    width = value.shape[1] // axis_size
    me = lax.axis_index("tp")
    for piece in range(axis_size):
        @pl.when(me == piece)
        def _():
            out[at, :] = value[:, piece * width : (piece + 1) * width]


def attention_ffn_kernel(
    tp_devices, chunk, lag, group,
    *refs
):
    peers = greet_line(tp_devices)
    loads, refs = unstaged(refs, 9, [0, 1, 2, 3, 4, 8, 7, 5, 6])
    (heads_ref, w_out_ref, tokens_ref, live_ref, gain_ref, w_gate_ref, w_up_ref, w_down_ref, cot_ref,
     normed_ref, dboth_ref, hid_ref, own_ref, hidden_ref, pulled_ref, part, ups, downs, sems, dhid_ref) = refs
    rows, dim = tokens_ref.shape
    ffn = w_gate_ref.shape[1]
    gap = dboth_ref.shape[1] // 2
    per = group // chunk
    if gap > ffn:
        dboth_ref[...] = jnp.zeros_like(dboth_ref)
    if hid_ref.shape[1] > ffn:
        hid_ref[:, ffn // 128 * 128 :] = jnp.zeros((rows, hid_ref.shape[1] - ffn // 128 * 128), bf16)

    def attn_done(k, total):
        at = rows_of(k, chunk)
        now = tokens_ref[at, :].astype(f32) + live_ref[at, :] * total
        hidden_ref[at, :] = now.astype(bf16)
        scale = lax.rsqrt(jnp.mean(now * now, axis=-1, keepdims=True) + norm_eps)
        normed_ref[at, :] = (now * scale * gain_ref[...]).astype(bf16)
        put_own(own_ref, at, now, tp_devices)

    line = Line(tp_devices, part, ups, downs, None, sems, chunk, lag, True, attn_done)

    def begin(q, carry):
        at = rows_of(q, 128)
        part[at, :] = mm(heads_ref[at, :], w_out_ref[...]).astype(bf16)
        return carry
    loads[0].wait()
    loads[1].wait()
    begin(0, 0)
    meet(peers)
    line.begin(0, 128 // chunk)

    def rest(q, carry):
        begin(q, carry)
        line.begin(q * (128 // chunk), 128 // chunk)
        return carry
    lax.fori_loop(1, rows // 128, rest, 0)

    tile = 256
    full = ffn // tile
    feeds = -(-ffn // tile)
    items = feeds + dim // tile

    def feed(at, cols, up_cols):
        normed = normed_ref[at, :]
        gate = mm(normed, w_gate_ref[:, cols])
        up = mm(normed, w_up_ref[:, cols])
        sig = sigmoid(gate)
        act = gate * sig
        dhid = dhid_ref[at, cols].astype(f32)
        hid_ref[at, cols] = (act * up).astype(bf16)
        dboth_ref[at, cols] = (dhid * up * (sig * (1.0 + gate * (1.0 - sig)))).astype(bf16)
        dboth_ref[at, up_cols] = (dhid * act).astype(bf16)

    def item(q, w):
        at = rows_of(q, group)

        @pl.when(w < full)
        def _():
            start = pl.multiple_of(w * tile, tile)
            feed(at, pl.ds(start, tile), pl.ds(pl.multiple_of(gap + w * tile, 128), tile))

        if feeds > full:
            @pl.when(w == full)
            def _():
                feed(at, slice(full * tile, ffn), slice(gap + full * tile, gap + ffn))

        @pl.when((w >= feeds) & (w < items))
        def _():
            mine = rows_of(w - feeds, tile)
            total = mm(dboth_ref[at, 0:ffn], w_gate_ref[mine, :], 1, 1)
            total = total + mm(dboth_ref[at, gap : gap + ffn], w_up_ref[mine, :], 1, 1)
            pulled_ref[at, mine] = total.astype(bf16)

    first = max(line.last + per, rows // 64 + 1)
    each = -(-items // per)
    groups = rows // group

    for load in loads[2:]:
        load.wait()

    def lead(i, carry):
        line.step(i)
        at = rows_of(i - 1, 64)

        @pl.when((i >= 1) & (i <= rows // 64))
        def _():
            dhid_ref[at, :] = mm(cot_ref[at, :], w_down_ref[...], 1, 1).astype(bf16)
        return carry
    lax.fori_loop(0, first, lead, 0)

    def beside(i, carry):
        line.step(i)
        q, p = (i - first) // per, lax.rem(i - first, per)

        def work(w, carry):
            item(q, p * each + w)
            return carry
        lax.fori_loop(0, each, work, 0)
        return carry
    lax.fori_loop(first, first + per * (groups - 1), beside, 0)

    def tail(w, carry):
        item(groups - 1, w)
        return carry
    lax.fori_loop(0, items, tail, 0)
    line.end()


def attention_ffn(tp_devices, heads_out, w_out, tokens, live, gain, w_gate, w_up, w_down, cot, chunk=32, lag=2, group=256):
    rows, dim = tokens.shape
    ffn = w_gate.shape[1]
    width = dim // tp_devices
    inputs = (heads_out, w_out, tokens, live, gain.reshape(1, dim), w_gate, w_up, w_down, cot)
    vmem = pl.BlockSpec(memory_space=pltpu.VMEM)
    out_shape = [
        jax.ShapeDtypeStruct((rows, dim), bf16),
        jax.ShapeDtypeStruct((rows, 2 * ceil_to(ffn, 128)), bf16),
        jax.ShapeDtypeStruct((rows, ceil_to(ffn, 256)), bf16),
        jax.ShapeDtypeStruct((rows, width), f32),
        jax.ShapeDtypeStruct((rows, dim), bf16),
        jax.ShapeDtypeStruct((rows, dim), bf16),
    ]
    return pl.pallas_call(
        functools.partial(attention_ffn_kernel, tp_devices, chunk, lag, group),
        in_specs=[pl.BlockSpec(memory_space=pltpu.HBM)] * len(inputs),
        out_specs=[vmem] * len(out_shape),
        out_shape=out_shape,
        scratch_shapes=[pltpu.VMEM((rows, dim), bf16)]
        + Line.scratch(rows, dim, tp_devices, chunk, True)
        + [pltpu.VMEM((rows, ffn), bf16)]
        + staging(inputs),
        compiler_params=pltpu.CompilerParams(
            collective_id=3, has_side_effects=True, vmem_limit_bytes=62 << 20
        ),
        name="attention_ffn",
    )(*inputs)


def paced(flow, pace, tick):
    @pl.when(lax.rem(tick * pace[0], pace[1]) < pace[0])
    def _():
        flow.step(tick * pace[0] // pace[1])


def paced_steps(flow, pace):
    return -(-flow.steps * pace[1] // pace[0])


def ffn_back_kernel(seq_devices, tp_devices, jobs, hid_at, cot_at, unit, chunk, scatter_lag, line_lag, wait, pace, lefts, *refs):
    peers = greet_halving(seq_devices) + greet_line(tp_devices)
    loads, refs = unstaged(refs, lefts + 6, [lefts] + list(range(lefts)) + list(range(lefts + 1, lefts + 6)))

    def take(count):
        out = refs[:count]
        del refs[:count]
        return out

    bits = seq_devices.bit_length() - 1
    arrays = take(lefts)
    part, hidden_ref, live_ref, gain_ref, w_out_ref, w_down_ref = take(6)
    cot_ref = arrays[cot_at]
    outs = take(len(jobs))
    dattn_ref, done_ref, dheads_ref, dgain_ref, ffn_ref = take(5)
    held, *rest = take(1 + bits + 2)
    ups, downs, sems = take(3)
    rows, dim = part.shape

    def dnormed_done(k, total):
        at = rows_of(k, chunk)
        now = hidden_ref[at, :].astype(f32)
        scale = lax.rsqrt(jnp.mean(now * now, axis=-1, keepdims=True) + norm_eps)
        unit_rows = now * scale
        dgain_ref[...] += jnp.sum((total * unit_rows).reshape(-1, 8, dim), axis=0)
        scaled = total * gain_ref[...]
        grad = cot_ref[at, :].astype(f32) + scale * (
            scaled - unit_rows * jnp.mean(scaled * unit_rows, axis=-1, keepdims=True)
        )
        dattn_ref[at, :] = (live_ref[at, :] * grad).astype(bf16)
        put_own(done_ref, at, grad, tp_devices)

    line = Line(tp_devices, part, ups, downs, None, sems, chunk, line_lag, True, dnormed_done)
    dgain_ref[...] = jnp.zeros_like(dgain_ref)
    loads[lefts].wait()
    meet(peers)
    line.begin(0, line.chunks)
    for load in loads[:lefts]:
        load.wait()
    pairs = Scatter.turned(arrays, jobs, refs)
    scatter = Scatter(seq_devices, pairs, held, rest[:bits], outs, rest[bits], rest[bits + 1], unit, scatter_lag, 1, wait)
    for load in loads[lefts + 1 :]:
        load.wait()
    per = 128 // chunk

    def step(i, carry):
        paced(scatter, pace, i)
        line.step(i)
        done = i - line.last

        @pl.when((done >= 0) & (done < line.chunks) & (lax.rem(done + line.chunks, per) == per - 1))
        def _():
            at = rows_of(done // per, 128)
            dheads_ref[at, :] = mm(dattn_ref[at, :], w_out_ref[...], 1, 1)

        @pl.when((i < line.chunks) & (lax.rem(i, per) == 1))
        def _():
            at = rows_of(i // per, 128)
            ffn_ref[at, :] = mm(arrays[hid_at][at, 0 : w_down_ref.shape[0]], w_down_ref[...]).astype(bf16)
        return carry
    lax.fori_loop(0, max(paced_steps(scatter, pace), line.steps), step, 0)
    line.end()


def ffn_back(
    seq_devices, tp_devices, arrays, jobs, hid_at, cot_at, part, hidden, live, gain, w_out, w_down,
    unit=256, chunk=32, scatter_lag=4, line_lag=2, wait=5, pace=(1, 1),
):
    rows, dim = part.shape
    vmem = pl.BlockSpec(memory_space=pltpu.VMEM)
    out_shape = [jax.ShapeDtypeStruct((dim // seq_devices, size), bf16) for _, _, _, size in jobs]
    out_shape += [
        jax.ShapeDtypeStruct((rows, dim), bf16),
        jax.ShapeDtypeStruct((rows, dim // tp_devices), f32),
        jax.ShapeDtypeStruct((rows, w_out.shape[0]), f32),
        jax.ShapeDtypeStruct((8, dim), f32),
        jax.ShapeDtypeStruct((rows, dim), bf16),
    ]
    scratch = Scatter.scratch(seq_devices, dim, sum(size for _, _, _, size in jobs), unit)
    scratch += Line.scratch(rows, dim, tp_devices, chunk, True)
    scratch += Scatter.spaces(arrays, jobs)
    inputs = [*arrays, part, hidden, live, gain.reshape(1, dim), w_out, w_down]
    scratch += staging(inputs)
    return pl.pallas_call(
        functools.partial(
            ffn_back_kernel, seq_devices, tp_devices, jobs, hid_at, cot_at, unit, chunk, scatter_lag, line_lag, wait, pace, len(arrays)
        ),
        in_specs=[pl.BlockSpec(memory_space=pltpu.HBM)] * len(inputs),
        out_specs=[vmem] * len(out_shape),
        out_shape=out_shape,
        scratch_shapes=scratch,
        compiler_params=pltpu.CompilerParams(
            collective_id=4, has_side_effects=True, vmem_limit_bytes=62 << 20
        ),
        name="ffn_back",
    )(*inputs)


def remote(src, dst, send, recv, axis, device):
    return pltpu.make_async_remote_copy(
        src_ref=src, dst_ref=dst, send_sem=send, recv_sem=recv, device_id={axis: device}, device_id_type=MESH
    )


def delta_back_kernel(devices, taps, jobs, unit, scatter_lag, wait, count, *refs):
    peers = greet_axis("seq", devices)
    soon = [count + 10, count + 11, count + 12, count + 13, count + 6]
    later = list(range(count)) + [count + 9]
    rest_of_loads = [at for at in range(count + 14) if at not in soon + later]
    loads, refs = unstaged(refs, count + 14, soon + later + rest_of_loads)

    def take(number):
        out = refs[:number]
        del refs[:number]
        return out

    def arrived(which):
        for at in which:
            loads[at].wait()

    bits = devices.bit_length() - 1
    arrays = take(count)
    (proj_ref, halo_ref, conv_ref, beta_ref, slope_ref, tri_ref, keep_ref, fresh_ref, state_ref, moves_ref,
     dheads_ref, mixed_ref, gate_ref, gain_ref) = take(14)
    outs = take(len(jobs))
    dense_ref, dconv_ref, dbias_ref, dgain_ref = take(4)
    held, *rest = take(1 + bits + 2)
    (ext_ref, dext_ref, dmixed_ref, offset_in, offset_all, states, grads, edge_out, edge_in, last_rows, dbeta_ref,
     send_one, recv_one, send_two, recv_two, edge_sems) = take(16)
    _, seqs, length, width = proj_ref.shape
    pad = halo_ref.shape[2]
    heads = width // HEAD
    chains = seqs * heads
    me = lax.axis_index("seq")
    arrived(soon)
    scatter = Scatter(devices, Scatter.turns(arrays, jobs, refs), held, rest[:bits], outs, rest[bits], rest[bits + 1], unit, scatter_lag, 1, wait)

    def flow(first, last):
        def step(i, carry):
            scatter.step(i)
            return carry
        lax.fori_loop(first, last, step, 0)

    dconv_ref[...] = jnp.zeros_like(dconv_ref)
    dgain_ref[...] = jnp.zeros_like(dgain_ref)
    dbeta_ref[...] = jnp.zeros_like(dbeta_ref)
    dext_ref[...] = jnp.zeros_like(dext_ref)
    together = ext_ref.shape[0]
    groups = heads // together

    def lanes(h):
        return pl.ds(pl.multiple_of(h * HEAD, HEAD), HEAD)

    def head_back(it, carry):
        s = it // groups
        rows = rows_of(s, length)
        gain = gain_ref[...]
        for j in range(together):
            h = lax.rem(it, groups) * together + j
            lane = lanes(h)
            dheads = dheads_ref[rows, lane]
            mixed = mixed_ref[s, :, lane]
            gate = gate_ref[s, :, lane]
            sig = sigmoid(gate)
            act = gate * sig
            rstd = lax.rsqrt(jnp.mean(mixed * mixed, axis=-1, keepdims=True) + norm_eps)
            unit_out = mixed * rstd
            pulled = dheads * unit_out
            dgain_ref[...] += jnp.sum((pulled * act).reshape(-1, 8, HEAD), axis=0)
            dense_ref[rows, lanes(3 * heads + h)] = (pulled * gain * (sig * (1.0 + gate * (1.0 - sig)))).astype(bf16)
            dunit = dheads * gain * act
            dmixed = (rstd * (dunit - unit_out * jnp.mean(dunit * unit_out, axis=-1, keepdims=True))).astype(bf16)
            dmixed_ref[s, :, lane] = dmixed
            offset_in[s * heads + h] = mm(keep_ref[s, h, :, 0:HEAD], dmixed, 0, 0).astype(bf16)
        return carry

    def chain_maps(chain):
        return remote(offset_in.at[chain], offset_all.at[me], send_one.at[chain], recv_one.at[me], "seq", chain)

    lax.fori_loop(0, seqs * groups, head_back, 0)
    meet(peers)
    for chain in range(chains):
        @pl.when(me != chain)
        def _():
            chain_maps(chain).start()

        @pl.when(me == chain)
        def _():
            offset_all[chain] = offset_in[chain]
    arrived(later)
    Scatter.turn(arrays, jobs, refs)
    flow(0, 2)

    @pl.when(me < chains)
    def _():
        state = jnp.zeros((HEAD, HEAD), f32)
        for at in range(devices - 1, -1, -1):
            states[at] = state.astype(bf16)

            @pl.when(me != at)
            def _():
                remote(states.at[at], grads.at[me], send_two.at[at], recv_two.at[me], "seq", at).start()
                remote(offset_in.at[0], offset_all.at[at], send_one.at[0], recv_one.at[at], "seq", at).wait_recv()

            @pl.when(me == at)
            def _():
                grads[me] = states[at]
            state = state + mm(moves_ref[at], state, 0, 0) + offset_all[at].astype(f32)
        for at in range(devices):
            @pl.when(me != at)
            def _():
                remote(states.at[at], grads.at[0], send_two.at[at], recv_two.at[0], "seq", at).wait_send()
    flow(2, 4)
    for chain in range(chains):
        @pl.when(me != chain)
        def _():
            chain_maps(chain).wait_send()
            remote(states.at[0], grads.at[chain], send_two.at[0], recv_two.at[chain], "seq", chain).wait_recv()

    arrived(rest_of_loads)
    below, upto, _ = strict_lower(length)

    def column(ref, s, h):
        value = ref[s]
        at = lax.broadcasted_iota(jnp.int32, value.shape, 1)
        return jnp.sum(jnp.where(at == h, value, 0.0), axis=1, keepdims=True)

    def heads_at_once(s, hs):
        rows = rows_of(s, length)
        slots = range(len(hs))
        for slot, h in enumerate(hs):
            for part in range(3):
                ext_ref[slot, part, 0:pad, :] = halo_ref[part, s, :, lanes(h)].astype(f32)
                ext_ref[slot, part, pad : pad + length, :] = proj_ref[part, s, :, lanes(h)].astype(f32)

        def conv(slot, h, part):
            summed = None
            for tap in range(taps):
                term = (
                    conv_ref[part, tap : tap + 1, lanes(h)]
                    * ext_ref[slot, part, pl.ds(pad - taps + 1 + tap, length), :]
                )
                summed = term if summed is None else summed + term
            return summed

        def both(function, *lists):
            return [function(*items) for items in zip(*lists)]

        def normed(pre):
            act = pre * sigmoid(pre)
            scale = lax.rsqrt(jnp.sum(act * act, axis=-1, keepdims=True) + norm_eps)
            return act * scale

        queries = both(lambda slot, h: normed(conv(slot, h, 0)).astype(bf16), slots, hs)
        keys = both(lambda slot, h: normed(conv(slot, h, 1)).astype(bf16), slots, hs)
        states = [state_ref[s * heads + h] for h in hs]
        exits = [grads[s * heads + h] for h in hs]
        dmixeds = [dmixed_ref[s, :, lanes(h)] for h in hs]
        freshes = [fresh_ref[s, :, lanes(h)] for h in hs]
        betas = [column(beta_ref, s, h) for h in hs]
        scores = both(lambda q, k: jnp.where(upto, mm(q, k, 1, 1), 0.0).astype(bf16), queries, keys)
        dfresh = both(lambda p, d, k, g: (mm(p, d, 0, 0) + mm(k, g)).astype(bf16), scores, dmixeds, keys, exits)
        pulls = both(lambda h, d: mm(tri_ref[s, h], d, 0, 0), hs, dfresh)
        dscores = both(lambda d, f: jnp.where(upto, mm(d, f, 1, 1), 0.0).astype(bf16), dmixeds, freshes)
        dvalues = both(lambda beta, pulled: beta * pulled, betas, pulls)
        dtris = both(lambda pulled, f: jnp.where(below, -mm(pulled, f, 1, 1), 0.0), pulls, freshes)
        inners = both(lambda dtri, k: jnp.sum(dtri * mm(k, k, 1, 1), axis=-1, keepdims=True), dtris, keys)
        dinners = both(lambda beta, dtri: (beta * dtri).astype(bf16), betas, dtris)
        dqueries = both(lambda d, st, p, k: mm(d, st, 1, 1) + mm(p, k), dmixeds, states, dscores, keys)
        dkeys = both(
            lambda p, q, f, g, v, st: mm(p, q, 0, 0) + mm(f, g, 1, 1) - mm(v, st, 1, 1),
            dscores, queries, freshes, exits, dvalues, states,
        )
        dkeys = both(lambda d, g, k: d + mm(g, k) + mm(g, k, 0, 0), dkeys, dinners, keys)
        reads = both(mm, keys, states)
        at = lax.broadcasted_iota(jnp.int32, (length, HEAD), 1)
        for slot, h, pulled, read, inner, dquery, dkey, dvalue in zip(
            slots, hs, pulls, reads, inners, dqueries, dkeys, dvalues
        ):
            for part, dout in ((0, dquery), (1, dkey), (2, dvalue)):
                pre = conv(slot, h, part)
                sig = sigmoid(pre)
                act = pre * sig
                if part == 2:
                    dact = dout
                    missing = act.astype(bf16).astype(f32) - read
                    dbeta = jnp.sum(pulled * missing, axis=-1, keepdims=True) + inner
                    dbeta_ref[s] += jnp.where(at == h, dbeta * column(slope_ref, s, h), 0.0)
                else:
                    scale = lax.rsqrt(jnp.sum(act * act, axis=-1, keepdims=True) + norm_eps)
                    unit_act = act * scale
                    dact = scale * (dout - unit_act * jnp.sum(dout * unit_act, axis=-1, keepdims=True))
                dconv = dact * (sig * (1.0 + pre * (1.0 - sig)))
                dext_ref[slot, part, pad : pad + length, :] = dconv
                for tap in range(taps):
                    shifted = ext_ref[slot, part, pl.ds(pad - taps + 1 + tap, length), :]
                    dconv_ref[part, tap : tap + 1, lanes(h)] += jnp.sum(dconv * shifted, axis=0, keepdims=True)
                summed, edge = None, None
                for tap in range(taps):
                    weight = conv_ref[part, tap : tap + 1, lanes(h)]
                    term = weight * dext_ref[slot, part, pl.ds(pad + taps - 1 - tap, length), :]
                    before = weight * dext_ref[slot, part, pl.ds(taps - 1 - tap, pad), :]
                    summed = term if summed is None else summed + term
                    edge = before if edge is None else edge + before
                col = lanes(part * heads + h)
                dense_ref[rows, col] = summed.astype(bf16)
                edge_out[s, :, col] = edge
                last_rows[s, :, col] = summed[length - pad :, :]

    start = 4
    each = -(-(scatter.steps - start) // (seqs * groups + 1))

    def some_heads(it, carry):
        heads_at_once(it // groups, [lax.rem(it, groups) * together + j for j in range(together)])
        flow(start + it * each, start + (it + 1) * each)
        return carry
    lax.fori_loop(0, seqs * groups, some_heads, 0)

    def edge_copy(other):
        return remote(edge_out, edge_in, edge_sems.at[0], edge_sems.at[1], "seq", other)

    @pl.when(me > 0)
    def _():
        edge_copy(me - 1).start()
    dbias = jnp.zeros((1, HEAD), f32)
    for s in range(seqs):
        low = dbeta_ref[s].astype(bf16)
        dense_ref[s * length : (s + 1) * length, 4 * width : 4 * width + HEAD] = low
        dbias = dbias + jnp.sum(low.astype(f32), axis=0, keepdims=True)
    dbias_ref[...] = dbias
    spare = dense_ref.shape[1] - 4 * width - HEAD
    if spare:
        dense_ref[:, 4 * width + HEAD :] = jnp.zeros((seqs * length, spare), bf16)
    flow(start + seqs * groups * each, scatter.steps)

    @pl.when(me < devices - 1)
    def _():
        edge_copy(0).wait_recv()
        for s in range(seqs):
            dense_ref[(s + 1) * length - pad : (s + 1) * length, 0 : 3 * width] = (last_rows[s] + edge_in[s]).astype(bf16)

    @pl.when(me > 0)
    def _():
        edge_copy(0).wait_send()


def delta_back(devices, arrays, jobs, inputs, unit=256, scatter_lag=2, wait=3, at_once=4):
    dim = arrays[jobs[0][0]].shape[1]
    proj, halo, conv_weight = inputs[:3]
    _, seqs, length, width = proj.shape
    pad = halo.shape[2]
    heads = width // HEAD
    chains = seqs * heads
    taps = conv_weight.shape[1]
    square = (HEAD, HEAD)
    dma = pltpu.SemaphoreType.DMA
    vmem = pl.BlockSpec(memory_space=pltpu.VMEM)
    out_shape = [jax.ShapeDtypeStruct((dim // devices, size), bf16) for _, _, _, size in jobs]
    out_shape += [
        jax.ShapeDtypeStruct((seqs * length, ceil_to(4 * width + HEAD, unit)), bf16),
        jax.ShapeDtypeStruct(conv_weight.shape, f32),
        jax.ShapeDtypeStruct((1, HEAD), f32),
        jax.ShapeDtypeStruct((8, HEAD), f32),
    ]
    together = min(at_once, heads)
    scratch = Scatter.scratch(devices, dim, sum(size for _, _, _, size in jobs), unit)
    scratch += [
        pltpu.VMEM((together, 3, pad + length, HEAD), f32),
        pltpu.VMEM((together, 3, 2 * pad + length, HEAD), f32),
        pltpu.VMEM((seqs, length, width), bf16),
        pltpu.VMEM((chains,) + square, bf16),
        pltpu.VMEM((devices,) + square, bf16),
        pltpu.VMEM((devices,) + square, bf16),
        pltpu.VMEM((chains,) + square, bf16),
        pltpu.VMEM((seqs, pad, 3 * width), f32),
        pltpu.VMEM((seqs, pad, 3 * width), f32),
        pltpu.VMEM((seqs, pad, 3 * width), f32),
        pltpu.VMEM((seqs, length, HEAD), f32),
        dma((chains,)), dma((devices,)), dma((devices,)), dma((chains,)), dma((2,)),
    ]
    scratch += Scatter.spaces(arrays, jobs) + staging([*arrays, *inputs])
    return pl.pallas_call(
        functools.partial(delta_back_kernel, devices, taps, jobs, unit, scatter_lag, wait, len(arrays)),
        in_specs=[pl.BlockSpec(memory_space=pltpu.HBM)] * (len(arrays) + len(inputs)),
        out_specs=[vmem] * len(out_shape),
        out_shape=out_shape,
        scratch_shapes=scratch,
        compiler_params=pltpu.CompilerParams(
            collective_id=2, has_side_effects=True, vmem_limit_bytes=62 << 20
        ),
        name="delta_back",
    )(*arrays, *inputs)


def last_kernel(seq_devices, tp_devices, jobs, unit, chunk, scatter_lag, line_lag, wait, pace, count, late_rows, *refs):
    peers = greet_axis("seq", seq_devices) + greet_axis("tp", tp_devices)
    soon = [count, count + 1] + list(range(count + 11, count + 15))
    later = [at for at in range(count + 15) if at not in soon]
    loads, refs = unstaged(refs, count + 15, soon + later)

    def take(number):
        out = refs[:number]
        del refs[:number]
        return out

    bits = seq_devices.bit_length() - 1
    arrays = take(count)
    dense_ref, w_beta_ref, tokens_ref, rstd_ref, gain_all_ref, grad_ref = take(6)
    dconv_ref, dbias_ref, dffn_gain_ref, head_gain_ref, norms_ref = take(5)
    weights = take(4)
    outs = take(len(jobs))
    tokens_grad_ref, conv_out, bias_out, gain_out, ffn_gain_out, head_out = take(6)
    held, *rest = take(1 + bits + 2)
    part, ups, downs, line_sems = take(4)
    (scaled_ref, dgain_ref, dots, dots_in, early_in, late, late_in, total,
     early_sems, late_sems, dot_sems, both_sems, early_ref, both_out, gain_ref) = take(15)
    seq, tp = lax.axis_index("seq"), lax.axis_index("tp")
    rows, dim = part.shape
    width = weights[0].shape[1]
    own = dim // tp_devices
    heads = w_beta_ref.shape[0]
    dgain_ref[...] = jnp.zeros_like(dgain_ref)
    dots[...] = jnp.zeros_like(dots)
    late[...] = jnp.zeros_like(late)
    for at in soon:
        loads[at].wait()
    meet(peers)
    for at in later:
        loads[at].wait()

    parts, taps, _ = dconv_ref.shape
    conv_rows = parts * taps * (width // HEAD)
    slices = own // HEAD
    split = conv_rows + 8
    both = early_ref.shape[0] - split

    def conv_places():
        for p in range(parts):
            for tap in range(taps):
                for c in range(width // HEAD):
                    row = (p * taps + tap) * (width // HEAD) + c
                    yield row, (p, slice(tap, tap + 1), slice(c * HEAD, (c + 1) * HEAD))

    put_own(gain_ref, slice(0, 1), gain_all_ref[...], tp_devices)
    early_ref[...] = jnp.zeros_like(early_ref)
    for row, place in conv_places():
        early_ref[row : row + 1, :] = dconv_ref[place]
    early_ref[conv_rows : conv_rows + 1, :] = dbias_ref[...]
    ffn_gain_sum = jnp.sum(dffn_gain_ref[...], axis=0, keepdims=True)
    for piece in range(tp_devices):
        @pl.when(tp == piece)
        def _():
            for c in range(slices):
                low = piece * own + c * HEAD
                early_ref[split + c : split + c + 1, :] = ffn_gain_sum[:, low : low + HEAD]
    early_ref[split + slices : split + slices + 1, :] = jnp.sum(head_gain_ref[...], axis=0, keepdims=True)
    early_ref[split + slices + 1 : split + slices + 2, :] = norms_ref[0:1, :]

    def to_peers(src, slots, sems, axis, size):
        me = lax.axis_index(axis)
        return [
            remote(src, slots.at[turn], sems.at[0, turn], sems.at[1, turn], axis, lax.rem(me + turn, size))
            for turn in range(1, size)
        ]

    early_copies = to_peers(early_ref, early_in, early_sems, "seq", seq_devices)
    for copy in early_copies:
        copy.start()

    def done(k, value):
        at = rows_of(k, chunk)
        x = tokens_ref[at, :].astype(f32)
        unit_rows = x * rstd_ref[at, :]
        dgain_ref[...] += jnp.sum((value * unit_rows).reshape(-1, 8, own), axis=0)
        scaled = value * gain_ref[...]
        scaled_ref[at, :] = scaled
        dot = jnp.sum(scaled * x, axis=-1, keepdims=True)
        per = HEAD // chunk
        place = lax.broadcasted_iota(jnp.int32, (chunk, HEAD), 0) + lax.rem(k, per) * chunk
        lane = lax.broadcasted_iota(jnp.int32, (chunk, HEAD), 1)
        dots[pl.ds(k // per, 1), :] += jnp.sum(jnp.where(place == lane, dot, 0.0), axis=0, keepdims=True)

    pairs = Scatter.turned(arrays, jobs, refs)
    scatter = Scatter(seq_devices, pairs, held, rest[:bits], outs, rest[bits], rest[bits + 1], unit, scatter_lag, 1, wait)
    line = Line(tp_devices, part, ups, downs, None, line_sems, chunk, line_lag, False, done)
    per = HEAD // chunk
    groups = rows // HEAD
    part_rows = 256

    def step(i, carry):
        @pl.when(i < rows // part_rows)
        def _():
            at = rows_of(i, part_rows)
            value = mm(dense_ref[at, 4 * width : 4 * width + heads], w_beta_ref[...])
            for w in range(4):
                value = value + mm(dense_ref[at, w * width : (w + 1) * width], weights[w][...], 1, 1)
            part[at, :] = value.astype(bf16)
            line.begin(i * (part_rows // chunk), part_rows // chunk)
        paced(scatter, pace, i)
        line.step(i)
        for at, act in ((0, send_late), (gap, send_total), (2 * gap, finish_tokens)):
            pl.when(i == line.steps + at)(act)
        return carry

    late_copies = to_peers(late, late_in, late_sems, "seq", seq_devices)
    dot_copies = to_peers(dots, dots_in, dot_sems, "tp", tp_devices)
    both_copies = [
        remote(total, both_out.at[tp], both_sems.at[0, turn], both_sems.at[1, turn], "tp", lax.rem(tp + turn, tp_devices))
        for turn in range(1, tp_devices)
    ]
    gap = 4

    def send_late():
        dgain = jnp.sum(dgain_ref[...], axis=0, keepdims=True)
        for at in range(own // HEAD):
            late[at : at + 1, :] = dgain[:, at * HEAD : (at + 1) * HEAD]
        for copy in late_copies + dot_copies:
            copy.start()

    def send_total():
        for copy in early_copies + late_copies:
            copy.wait()
        early_total = early_ref[...]
        late_total = late[...]
        for turn in range(1, seq_devices):
            early_total = early_total + early_in[turn]
            late_total = late_total + late_in[turn]
        for row, place in conv_places():
            conv_out[place] = early_total[row : row + 1]
        bias_out[...] = early_total[conv_rows : conv_rows + 1]
        total[0:both, :] = early_total[split:]
        total[both:, :] = late_total
        both_out[tp] = total[...]
        for copy in both_copies:
            copy.start()

    def finish_tokens():
        for copy in dot_copies:
            copy.wait()
        dot_total = dots[...]
        for turn in range(1, tp_devices):
            dot_total = dot_total + dots_in[turn]
        dots[...] = dot_total / dim
        eye = lax.broadcasted_iota(jnp.int32, (HEAD, HEAD), 0) == lax.broadcasted_iota(jnp.int32, (HEAD, HEAD), 1)

        def finish(q, carry):
            at = rows_of(q, HEAD)
            dot = jnp.sum(jnp.where(eye, dots[pl.ds(q, 1), :], 0.0), axis=1, keepdims=True)
            scale = rstd_ref[at, :]
            x = tokens_ref[at, :].astype(f32)
            tokens_grad_ref[at, :] = grad_ref[at, :] + scale * scaled_ref[at, :] - x * (scale * scale * scale) * dot
            return carry
        lax.fori_loop(0, groups, finish, 0)

    lax.fori_loop(0, max(paced_steps(scatter, pace), line.steps + 2 * gap + 1), step, 0)
    line.end()
    for copy in both_copies:
        copy.wait()
    heads_total = jnp.zeros((2, HEAD), f32)
    for at in range(tp_devices):
        ffn_gain_out[at * slices : (at + 1) * slices, :] = both_out[at, 0:slices]
        gain_out[at * slices : (at + 1) * slices, :] = both_out[at, both : both + slices]
        heads_total = heads_total + both_out[at, slices : slices + 2]
    head_out[...] = heads_total


def last(
    seq_devices, tp_devices, arrays, jobs, dense, w_beta, tokens_own, rstd, gain, grad_own, small, sources,
    unit=256, chunk=32, scatter_lag=4, line_lag=2, wait=5, pace=(2, 3),
):
    dim = arrays[jobs[0][0]].shape[1]
    rows, own = tokens_own.shape
    width = sources[0].shape[1]
    late_rows = ceil_to(own // HEAD, 8)
    dot_rows = ceil_to(rows // HEAD, 8)
    dma = pltpu.SemaphoreType.DMA
    vmem, hbm = pl.BlockSpec(memory_space=pltpu.VMEM), pl.BlockSpec(memory_space=pltpu.HBM)
    out_shape = [jax.ShapeDtypeStruct((dim // seq_devices, size), bf16) for _, _, _, size in jobs]
    out_shape += [
        jax.ShapeDtypeStruct((rows, own), f32),
        jax.ShapeDtypeStruct(small[0].shape, f32),
        jax.ShapeDtypeStruct((1, HEAD), f32),
        jax.ShapeDtypeStruct((dim // HEAD, HEAD), f32),
        jax.ShapeDtypeStruct((dim // HEAD, HEAD), f32),
        jax.ShapeDtypeStruct((2, HEAD), f32),
    ]
    both = ceil_to(own // HEAD + 2, 8)
    early = small[0].size // HEAD + 8 + both
    scratch = Scatter.scratch(seq_devices, dim, sum(size for _, _, _, size in jobs), unit)
    scratch += [pltpu.VMEM((rows, dim), bf16)] + Line.scratch(rows, dim, tp_devices, chunk, False)
    scratch += [
        pltpu.VMEM((rows, own), f32),
        pltpu.VMEM((8, own), f32),
        pltpu.VMEM((dot_rows, HEAD), f32),
        pltpu.VMEM((tp_devices, dot_rows, HEAD), f32),
        pltpu.VMEM((seq_devices, early, HEAD), f32),
        pltpu.VMEM((late_rows, HEAD), f32),
        pltpu.VMEM((seq_devices, late_rows, HEAD), f32),
        pltpu.VMEM((both + late_rows, HEAD), f32),
        dma((2, seq_devices)), dma((2, seq_devices)), dma((2, tp_devices)), dma((2, tp_devices)),
        pltpu.VMEM((early, HEAD), f32),
        pltpu.VMEM((tp_devices, both + late_rows, HEAD), f32),
        pltpu.VMEM((1, own), f32),
    ]
    inputs = [*arrays, dense, w_beta, tokens_own, rstd, gain, grad_own, *small, *sources]
    scratch += Scatter.spaces(arrays, jobs) + staging(inputs)
    return pl.pallas_call(
        functools.partial(
            last_kernel, seq_devices, tp_devices, jobs, unit, chunk, scatter_lag, line_lag, wait, pace, len(arrays), late_rows
        ),
        in_specs=[hbm] * len(inputs),
        out_specs=[vmem] * len(out_shape),
        out_shape=out_shape,
        scratch_shapes=scratch,
        compiler_params=pltpu.CompilerParams(
            collective_id=5, has_side_effects=True, vmem_limit_bytes=62 << 20
        ),
        name="last_sums",
    )(*inputs)


def on_device(
    tokens,
    seq_lengths,
    norm_gain,
    w_query,
    w_key,
    w_value,
    w_gate,
    w_beta,
    beta_bias,
    conv_weight,
    out_gain,
    w_out,
    ffn_gain,
    w_ffn_gate,
    w_ffn_up,
    w_ffn_down,
    cotangent,
):
    seqs_here, local_len, model_dim = tokens.shape
    row_count = seqs_here * local_len
    heads_here = w_beta.shape[1]
    local_width = w_query.shape[1]
    halo_pad = 16
    seq_devices = lax.axis_size("seq")
    tp_devices = lax.axis_size("tp")
    slice_width = model_dim // lax.axis_size("tp")
    tokens_flat = tokens.reshape(row_count, model_dim)
    grad_low = cotangent.reshape(row_count, model_dim)
    normed_one, rstd_one, proj, halo, gate_pre, beta_val, slope, live_rows, tokens_own = first(
        seq_devices, tp_devices, tokens_flat, norm_gain, w_query, w_key, w_value, w_gate, w_beta.T, beta_bias, seq_lengths
    )
    proj_seq = proj.reshape(3, seqs_here, local_len, local_width)
    halo_rows = halo.reshape(3, seqs_here, halo_pad, local_width)
    beta_seq = beta_val.reshape(seqs_here, local_len, heads_here)
    slope = slope.reshape(seqs_here, local_len, heads_here)
    gate_seq = gate_pre.reshape(seqs_here, local_len, local_width)

    tri, keep, state_in, moves, norms, mixed, fresh, heads_seq = delta_forward(
        seq_devices, proj_seq, halo_rows, conv_weight, beta_seq, gate_seq, out_gain
    )
    heads_out = heads_seq.reshape(row_count, local_width)

    normed_two, dffn_both, ffn_hidden, hidden_own, hidden_low, dnormed_part_two = attention_ffn(
        tp_devices, heads_out, w_out, tokens_flat, live_rows, ffn_gain, w_ffn_gate, w_ffn_up, w_ffn_down, grad_low
    )
    ffn_width = w_ffn_gate.shape[1]
    ffn_pad = ffn_hidden.shape[1]
    early = min(768, ffn_pad - 256)
    dw_both, dw_down_early, dattn, grad_own, dheads, dffn_gain, ffn_part = ffn_back(
        seq_devices,
        tp_devices,
        [normed_two, grad_low, dffn_both, ffn_hidden],
        [(0, 2, 0, dffn_both.shape[1]), (1, 3, 0, early)],
        3,
        1,
        dnormed_part_two,
        hidden_low,
        live_rows,
        ffn_gain,
        w_out,
        w_ffn_down,
    )
    ffn_slice = lax.psum_scatter(ffn_part, "tp", scatter_dimension=1, tiled=True)

    dw_down, dw_out, dense, dconv, dbias, dgain = delta_back(
        seq_devices,
        [grad_low, ffn_hidden, dattn, heads_out],
        [(0, 1, early, ffn_pad - early), (2, 3, 0, local_width)],
        [
            proj_seq, halo_rows, conv_weight, beta_seq, slope, tri, keep, fresh, state_in, moves,
            dheads, mixed, gate_seq, out_gain.reshape(1, HEAD),
        ],
    )
    dense, ffn_slice = lax.optimization_barrier((dense, ffn_slice))
    dw_first, tokens_grad, conv_grad, bias_grad, gain_grad, ffn_gain_grad, head_total = last(
        seq_devices,
        tp_devices,
        [normed_one, dense],
        [(0, 1, 0, dense.shape[1])],
        dense,
        w_beta.T,
        tokens_own,
        rstd_one,
        norm_gain.reshape(1, model_dim),
        grad_own,
        [dconv, dbias, dffn_gain, dgain, norms],
        [w_query, w_key, w_value, w_gate],
    )
    out_tokens = (hidden_own + ffn_slice.astype(f32)).astype(bf16).reshape(seqs_here, local_len, slice_width)
    lw = local_width

    def wide(value):
        return value.astype(f32)

    return (
        out_tokens,
        tokens_grad.reshape(seqs_here, local_len, slice_width),
        gain_grad.reshape(model_dim),
        wide(dw_first[:, :lw]),
        wide(dw_first[:, lw : 2 * lw]),
        wide(dw_first[:, 2 * lw : 3 * lw]),
        wide(dw_first[:, 3 * lw : 4 * lw]),
        wide(dw_first[:, 4 * lw : 4 * lw + heads_here]),
        bias_grad[0, :heads_here],
        conv_grad,
        head_total[0],
        wide(dw_out.T),
        ffn_gain_grad.reshape(model_dim),
        wide(dw_both[:, :ffn_width]),
        wide(dw_both[:, dffn_both.shape[1] // 2 :][:, :ffn_width]),
        wide(jnp.concatenate([dw_down_early, dw_down], axis=1).T[:ffn_width]),
        head_total[1, 0] / (seqs_here * HEADS),
    )


def solution(mesh):
    in_specs = (
        P(None, "seq", None),
        P(),
        P(),
        P(None, "tp"),
        P(None, "tp"),
        P(None, "tp"),
        P(None, "tp"),
        P(None, "tp"),
        P("tp"),
        P(None, None, "tp"),
        P(),
        P("tp", None),
        P(),
        P(None, "tp"),
        P(None, "tp"),
        P("tp", None),
        P(None, "seq", None),
    )
    out_specs = (
        P(None, "seq", "tp"),
        P(None, "seq", "tp"),
        P(),
        P("seq", "tp"),
        P("seq", "tp"),
        P("seq", "tp"),
        P("seq", "tp"),
        P("seq", "tp"),
        P("tp"),
        P(None, None, "tp"),
        P(),
        P("tp", "seq"),
        P(),
        P("seq", "tp"),
        P("seq", "tp"),
        P("tp", "seq"),
        P(),
    )
    return jax.shard_map(
        on_device, mesh=mesh, in_specs=in_specs, out_specs=out_specs, check_vma=False
    )
```

```python
import functools

import jax
import jax.numpy as jnp
from jax import lax
from jax.experimental import pallas as pl
from jax.experimental.pallas import tpu as pltpu
from jax.sharding import PartitionSpec as P

HEADS = 16
HEAD = 128

norm_eps = 1e-06
f32 = jnp.float32
bf16 = jnp.bfloat16
MESH = pl.DeviceIdType.MESH
VM = pltpu.VMEM


def mm(left, right, contract_left=1, contract_right=0):
    return lax.dot_general(
        left.astype(bf16),
        right.astype(bf16),
        (((contract_left,), (contract_right,)), ((), ())),
        preferred_element_type=f32,
    )


def from_behind(block, axis, distance):
    devices = range(lax.axis_size(axis))
    route = [(i - distance, i) for i in devices if i - distance in devices]
    return lax.ppermute(block, axis, route)


def sigmoid(value):
    return 1.0 / (1.0 + jnp.exp(-value))


def silu_grad(value):
    sigmoid_val = sigmoid(value)
    return sigmoid_val * (1.0 + value * (1.0 - sigmoid_val))


def dot_left(left, right):
    return mm(left, right, 0, 0)


def dot_right(left, right):
    return mm(left, right, 1, 1)


def strict_lower(size):
    rows = lax.broadcasted_iota(jnp.int32, (size, size), 0)
    cols = lax.broadcasted_iota(jnp.int32, (size, size), 1)
    return rows > cols, rows >= cols, rows ^ cols


def unit_lower_inverses(lows, apart):
    size = lows[0].shape[0]
    inverses = [jnp.where(apart == 0, 1.0, 0.0) - jnp.where(apart == 1, low, 0.0) for low in lows]
    step = 2
    while step < size:
        pair = (apart >= step) & (apart < 2 * step)
        between = [jnp.where(pair, low, 0.0).astype(bf16) for low in lows]
        inner = [inverse.astype(bf16) for inverse in inverses]
        right = [mm(left, at) for left, at in zip(between, inner)]
        inverses = [inverse - mm(at, value) for inverse, at, value in zip(inverses, inner, right)]
        step *= 2
    return inverses


def conv_silu(ext_ref, col, conv_ref, part, lane, length, taps, pad):
    summed = None
    for tap in range(taps):
        term = conv_ref[part, tap : tap + 1, lane] * ext_ref[pl.ds(pad - taps + 1 + tap, length), col]
        summed = term if summed is None else summed + term
    return summed


def delta_forward_kernel(
    devices, taps, proj_ref, halo_ref, conv_ref, beta_ref, gate_ref, gain_ref,
    tri_ref, query_ref, state_ref, moves_ref, norm_ref, mixed_ref, fresh_ref, heads_ref,
    ext_ref, keep_ref, move_in, offset_in, offset_all, states, send_zero, recv_zero, send_one, recv_one, send_two, recv_two,
):
    _, seqs, length, width = proj_ref.shape
    pad = halo_ref.shape[2]
    heads = width // HEAD
    chains = seqs * heads
    me = lax.axis_index("seq")
    peers = greet_axis("seq", devices)
    below, upto, apart = strict_lower(length)
    some = range(heads)

    def act(part, h):
        lane = slice(h * HEAD, (h + 1) * HEAD)
        col = slice(part * width + h * HEAD, part * width + (h + 1) * HEAD)
        summed = conv_silu(ext_ref, col, conv_ref, part, lane, length, taps, pad)
        return summed * sigmoid(summed)

    def unit(value):
        return value * lax.rsqrt(jnp.sum(value * value, axis=-1, keepdims=True) + norm_eps)

    def send_maps(chain):
        remote(move_in.at[chain], moves_ref.at[me], send_zero.at[chain], recv_zero.at[me], "seq", chain).start()
        remote(offset_in.at[chain], offset_all.at[me], send_one.at[chain], recv_one.at[me], "seq", chain).start()

    def local(s, carry):
        for part in range(3):
            col = slice(part * width, (part + 1) * width)
            ext_ref[0:pad, col] = halo_ref[part, s].astype(f32)
            ext_ref[pad : pad + length, col] = proj_ref[part, s].astype(f32)
        queries = [unit(act(0, h)).astype(bf16) for h in some]
        keys = [unit(act(1, h)).astype(bf16) for h in some]
        values = [act(2, h).astype(bf16) for h in some]
        betas = [beta_ref[s, :, h : h + 1] for h in some]
        lows = [jnp.where(below, beta * mm(key, key, 1, 1), 0.0) for beta, key in zip(betas, keys)]
        inverses = unit_lower_inverses(lows, apart)
        for h, query, key, value, beta, inverse in zip(some, queries, keys, values, betas, inverses):
            inverse = inverse.astype(bf16)
            targets = jnp.concatenate([beta * key.astype(f32), beta * value.astype(f32)], axis=1)
            solved_low = mm(inverse, targets).astype(bf16)
            scores = jnp.where(upto, mm(query, key, 1, 1), 0.0).astype(bf16)
            passed = mm(scores, solved_low)
            moved = mm(key, solved_low, 0, 0)
            tri_ref[s, h] = inverse
            query_ref[s, h] = (query.astype(f32) - passed[:, :HEAD]).astype(bf16)
            keep_ref[s, h, :, 0:HEAD] = passed[:, HEAD:].astype(bf16)
            keep_ref[s, h, :, HEAD:] = solved_low
            move_in[s * heads + h] = (-moved[:, :HEAD]).astype(bf16)
            offset_in[s * heads + h] = moved[:, HEAD:].astype(bf16)

        @pl.when(s == 0)
        def _():
            meet(peers)
        for h in some:
            chain = s * heads + h

            @pl.when(me != chain)
            def _():
                send_maps(chain)

            @pl.when(me == chain)
            def _():
                moves_ref[me] = move_in[chain]
                offset_all[me] = offset_in[chain]
        return carry
    lax.fori_loop(0, seqs, local, 0)

    @pl.when(me < chains)
    def _():
        state = jnp.zeros((HEAD, HEAD), f32)
        for at in range(devices):
            states[at] = state.astype(bf16)

            @pl.when(me != at)
            def _():
                remote(states.at[at], state_ref.at[me], send_two.at[at], recv_two.at[me], "seq", at).start()
                remote(move_in.at[0], moves_ref.at[at], send_zero.at[0], recv_zero.at[at], "seq", at).wait_recv()
                remote(offset_in.at[0], offset_all.at[at], send_one.at[0], recv_one.at[at], "seq", at).wait_recv()

            @pl.when(me == at)
            def _():
                state_ref[me] = states[at]
            state = state + mm(moves_ref[at], state) + offset_all[at].astype(f32)
        norm_ref[...] = jnp.zeros_like(norm_ref) + jnp.sqrt(jnp.sum(state * state, keepdims=True))
        for at in range(devices):
            @pl.when(me != at)
            def _():
                remote(states.at[at], state_ref.at[0], send_two.at[at], recv_two.at[0], "seq", at).wait_send()

    @pl.when(me >= chains)
    def _():
        norm_ref[...] = jnp.zeros_like(norm_ref)
    for chain in range(chains):
        @pl.when(me != chain)
        def _():
            remote(move_in.at[chain], moves_ref.at[0], send_zero.at[chain], recv_zero.at[0], "seq", chain).wait_send()
            remote(offset_in.at[chain], offset_all.at[0], send_one.at[chain], recv_one.at[0], "seq", chain).wait_send()
            remote(states.at[0], state_ref.at[chain], send_two.at[0], recv_two.at[chain], "seq", chain).wait_recv()

    def out(s, carry):
        for h in some:
            lane = slice(h * HEAD, (h + 1) * HEAD)
            state = state_ref[s * heads + h]
            mixed = keep_ref[s, h, :, 0:HEAD].astype(f32) + mm(query_ref[s, h], state)
            fresh = keep_ref[s, h, :, 2 * HEAD :].astype(f32) - mm(keep_ref[s, h, :, HEAD : 2 * HEAD], state)
            rstd = lax.rsqrt(jnp.mean(mixed * mixed, axis=-1, keepdims=True) + norm_eps)
            gate = gate_ref[s, :, lane]
            mixed_ref[s, :, lane] = mixed
            fresh_ref[s, :, lane] = fresh.astype(bf16)
            heads_ref[s, :, lane] = (mixed * rstd * gain_ref[...] * (gate * sigmoid(gate))).astype(bf16)
        return carry
    lax.fori_loop(0, seqs, out, 0)


def delta_forward(devices, proj, halo, conv_weight, beta, gate, gain):
    _, seqs, length, width = proj.shape
    pad = halo.shape[2]
    heads = width // HEAD
    chains = seqs * heads
    square = (HEAD, HEAD)
    dma = pltpu.SemaphoreType.DMA
    vmem = pl.BlockSpec(memory_space=pltpu.VMEM)
    out_shape = [
        jax.ShapeDtypeStruct((seqs, heads, length, length), bf16),
        jax.ShapeDtypeStruct((seqs, heads, length, HEAD), bf16),
        jax.ShapeDtypeStruct((chains,) + square, bf16),
        jax.ShapeDtypeStruct((devices,) + square, bf16),
        jax.ShapeDtypeStruct((8, HEAD), f32),
        jax.ShapeDtypeStruct((seqs, length, width), f32),
        jax.ShapeDtypeStruct((seqs, length, width), bf16),
        jax.ShapeDtypeStruct((seqs, length, width), bf16),
    ]
    return pl.pallas_call(
        functools.partial(delta_forward_kernel, devices, conv_weight.shape[1]),
        in_specs=[vmem] * 6,
        out_specs=[vmem] * len(out_shape),
        out_shape=out_shape,
        scratch_shapes=[
            pltpu.VMEM((pad + length, 3 * width), f32),
            pltpu.VMEM((seqs, heads, length, 3 * HEAD), bf16),
            pltpu.VMEM((chains,) + square, bf16),
            pltpu.VMEM((chains,) + square, bf16),
            pltpu.VMEM((devices,) + square, bf16),
            pltpu.VMEM((devices,) + square, bf16),
            dma((chains,)), dma((devices,)), dma((chains,)), dma((devices,)), dma((devices,)), dma((chains,)),
        ],
        compiler_params=pltpu.CompilerParams(
            collective_id=1, has_side_effects=True, vmem_limit_bytes=62 << 20
        ),
        name="delta_forward",
    )(proj, halo, conv_weight, beta, gate, gain.reshape(1, HEAD))


def first_kernel(
    seq_devices, tp_devices, tokens_ref, gain_ref, w_beta_ref, bias_ref, lengths_ref, *refs
):
    (w_query, w_key, w_value, w_gate, normed_ref, rstd_ref, proj_ref, halo_ref, gate_ref, beta_ref, slope_ref,
     live_ref, own_ref, weights, halo_in, load_sem, send_sem, recv_sem) = refs
    rows, dim = tokens_ref.shape
    seqs, pad, _ = halo_in.shape
    length = rows // seqs
    me = lax.axis_index("seq")
    loads = [
        pltpu.make_async_copy(source, weights.at[at], load_sem.at[at])
        for at, source in enumerate((w_query, w_key, w_value, w_gate))
    ]
    for load in loads:
        load.start()
    barrier = pltpu.get_barrier_semaphore()

    @pl.when(me > 0)
    def _():
        pl.semaphore_signal(barrier, inc=1, device_id={"seq": me - 1}, device_id_type=MESH)

    @pl.when(me < seq_devices - 1)
    def _():
        pl.semaphore_signal(barrier, inc=1, device_id={"seq": me + 1}, device_id_type=MESH)

    gain = gain_ref[...]

    def norm(q, carry):
        at = pl.ds(pl.multiple_of(q * 128, 128), 128)
        value = tokens_ref[at, :].astype(f32)
        scale = lax.rsqrt(jnp.mean(value * value, axis=-1, keepdims=True) + norm_eps)
        rstd_ref[at, :] = scale
        normed_ref[at, :] = (value * scale * gain).astype(bf16)
        return carry
    lax.fori_loop(0, rows // 128, norm, 0)
    pl.semaphore_wait(barrier, jnp.minimum(me, 1) + jnp.minimum(seq_devices - 1 - me, 1))

    def halo_copy(s):
        return pltpu.make_async_remote_copy(
            src_ref=tokens_ref.at[pl.ds((s + 1) * length - pad, pad)], dst_ref=halo_in.at[s],
            send_sem=send_sem.at[s], recv_sem=recv_sem.at[s],
            device_id={"seq": me + 1}, device_id_type=MESH,
        )

    @pl.when(me < seq_devices - 1)
    def _():
        for s in range(seqs):
            halo_copy(s).start()

    for s in range(seqs):
        position = me * length + lax.broadcasted_iota(jnp.int32, (length, 1), 0)
        live_ref[s * length : (s + 1) * length, :] = jnp.where(position < lengths_ref[0:1, s : s + 1], 1.0, 0.0)
    width = own_ref.shape[1]
    for piece in range(tp_devices):
        @pl.when(lax.axis_index("tp") == piece)
        def _():
            own_ref[...] = tokens_ref[:, piece * width : (piece + 1) * width]
    sig = sigmoid(mm(normed_ref[...], w_beta_ref[...], 1, 1) + bias_ref[...])
    beta = live_ref[...] * sig
    beta_ref[...] = beta
    slope_ref[...] = beta * (1.0 - sig)
    for part in range(4):
        loads[part].wait()

        def some(q, carry):
            at = pl.ds(pl.multiple_of(q * 512, 512), 512)
            product = mm(normed_ref[at, :], weights[part])
            if part < 3:
                proj_ref[part, at, :] = product.astype(bf16)
            else:
                gate_ref[at, :] = product
            return carry
        lax.fori_loop(0, rows // 512, some, 0)

    @pl.when(me > 0)
    def _():
        for s in range(seqs):
            halo_copy(s).wait_recv()
        value = halo_in[...].reshape(seqs * pad, dim).astype(f32)
        scale = lax.rsqrt(jnp.mean(value * value, axis=-1, keepdims=True) + norm_eps)
        normed = (value * scale * gain).astype(bf16)
        for part in range(3):
            halo_ref[part] = mm(normed, weights[part]).astype(bf16)

    @pl.when(me == 0)
    def _():
        halo_ref[...] = jnp.zeros_like(halo_ref)

    @pl.when(me < seq_devices - 1)
    def _():
        for s in range(seqs):
            halo_copy(s).wait_send()


def first(seq_devices, tp_devices, tokens, gain, w_query, w_key, w_value, w_gate, w_beta, bias, lengths):
    rows, dim = tokens.shape
    width, heads = w_query.shape[1], w_beta.shape[0]
    seqs = lengths.shape[0]
    pad = 16
    vmem, hbm = pl.BlockSpec(memory_space=pltpu.VMEM), pl.BlockSpec(memory_space=pltpu.HBM)
    out_shape = [
        jax.ShapeDtypeStruct((rows, dim), bf16),
        jax.ShapeDtypeStruct((rows, 1), f32),
        jax.ShapeDtypeStruct((3, rows, width), bf16),
        jax.ShapeDtypeStruct((3, seqs * pad, width), bf16),
        jax.ShapeDtypeStruct((rows, width), f32),
        jax.ShapeDtypeStruct((rows, heads), f32),
        jax.ShapeDtypeStruct((rows, heads), f32),
        jax.ShapeDtypeStruct((rows, 1), f32),
        jax.ShapeDtypeStruct((rows, dim // tp_devices), bf16),
    ]
    return pl.pallas_call(
        functools.partial(first_kernel, seq_devices, tp_devices),
        in_specs=[vmem] * 5 + [hbm] * 4,
        out_specs=[vmem] * len(out_shape),
        out_shape=out_shape,
        scratch_shapes=[
            pltpu.VMEM((4, dim, width), bf16),
            pltpu.VMEM((seqs, pad, dim), bf16),
            pltpu.SemaphoreType.DMA((4,)),
            pltpu.SemaphoreType.DMA((seqs,)),
            pltpu.SemaphoreType.DMA((seqs,)),
        ],
        compiler_params=pltpu.CompilerParams(
            collective_id=7, has_side_effects=True, vmem_limit_bytes=62 << 20
        ),
        name="first_norm_projections",
    )(tokens, gain.reshape(1, dim), w_beta, bias.reshape(1, heads), lengths.reshape(1, seqs), w_query, w_key, w_value, w_gate)


def ceil_to(value, unit):
    return -(-value // unit) * unit


class Line:
    def __init__(self, devices, part, ups, downs, out, sems, chunk, lag, whole, done=None):
        self.done = done
        self.n, self.part, self.ups, self.downs, self.out, self.sems = devices, part, ups, downs, out, sems
        self.chunk, self.lag, self.whole = chunk, lag, whole
        self.chunks = part.shape[0] // chunk
        self.me = lax.axis_index("tp")
        self.pieces = 1 if whole else devices
        self.width = part.shape[1] // self.pieces
        self.last = (devices - 2) * lag
        self.steps = self.chunks + self.last

    @staticmethod
    def scratch(rows, cols, devices, chunk, whole):
        count = (rows // chunk) * (1 if whole else devices)
        return [pltpu.VMEM((rows, cols), bf16)] * 2 + [pltpu.SemaphoreType.DMA((4, count))]

    def copy(self, source, way, k, piece):
        at = (pl.ds(pl.multiple_of(k * self.chunk, self.chunk), self.chunk), slice(piece * self.width, (piece + 1) * self.width))
        target = self.ups if way == 0 else self.downs
        sem = k * self.pieces + piece
        other = self.me + 1 if way == 0 else self.me - 1
        return pltpu.make_async_remote_copy(
            src_ref=source.at[at], dst_ref=target.at[at],
            send_sem=self.sems.at[way, sem], recv_sem=self.sems.at[2 + way, sem],
            device_id={"tp": other}, device_id_type=MESH,
        )

    def begin(self, first, count):
        for way, end in ((0, 0), (1, self.n - 1)):
            @pl.when(self.me == end)
            def _():
                def send(k, carry):
                    for piece in range(self.pieces) if way else reversed(range(self.pieces)):
                        if self.whole or piece != end:
                            self.copy(self.part, way, k, piece).start()
                    return carry
                lax.fori_loop(first, first + count, send, 0)

    def forward(self, way, k):
        me, n = self.me, self.n
        held = self.ups if way == 0 else self.downs
        rows = pl.ds(pl.multiple_of(k * self.chunk, self.chunk), self.chunk)
        for piece in range(self.pieces):
            if self.whole:
                gets, goes = None, me < n - 1 if way == 0 else me > 0
            else:
                gets, goes = (piece >= me, piece > me) if way == 0 else (piece <= me, piece < me)
            cols = slice(piece * self.width, (piece + 1) * self.width)

            def take():
                self.copy(self.part, way, k, piece).wait_recv()

                @pl.when(goes)
                def _():
                    held[rows, cols] = (held[rows, cols].astype(f32) + self.part[rows, cols].astype(f32)).astype(bf16)
                    self.copy(held, way, k, piece).start()

            if gets is None:
                take()
            else:
                pl.when(gets)(take)

    def give(self, k, total):
        if self.done is None:
            self.out[pl.ds(pl.multiple_of(k * self.chunk, self.chunk), self.chunk), :] = total
        else:
            self.done(k, total)

    def finish(self, k):
        me, n = self.me, self.n
        rows = pl.ds(pl.multiple_of(k * self.chunk, self.chunk), self.chunk)
        if self.whole:
            @pl.when(me == 0)
            def _():
                self.give(k, self.part[rows, :].astype(f32) + self.downs[rows, :].astype(f32))

            @pl.when(me == n - 1)
            def _():
                self.give(k, self.part[rows, :].astype(f32) + self.ups[rows, :].astype(f32))

            @pl.when((me > 0) & (me < n - 1))
            def _():
                both = self.ups[rows, :].astype(f32) - self.part[rows, :].astype(f32)
                self.give(k, both + self.downs[rows, :].astype(f32))
        else:
            for piece in range(n):
                @pl.when(me == piece)
                def _():
                    cols = slice(piece * self.width, (piece + 1) * self.width)
                    total = self.part[rows, cols].astype(f32)
                    if piece > 0:
                        total = total + self.ups[rows, cols].astype(f32)
                    if piece < n - 1:
                        total = total + self.downs[rows, cols].astype(f32)
                    self.give(k, total)

    def step(self, i):
        me, n = self.me, self.n
        up = i - (me - 1) * self.lag
        down = i - (n - 2 - me) * self.lag

        @pl.when((me > 0) & (up >= 0) & (up < self.chunks))
        def _():
            self.forward(0, up)

        @pl.when((me < n - 1) & (down >= 0) & (down < self.chunks))
        def _():
            self.forward(1, down)

        done = i - self.last

        @pl.when((done >= 0) & (done < self.chunks))
        def _():
            self.finish(done)

    def end(self):
        def drain(k, carry):
            for way in range(2):
                for piece in range(self.pieces):
                    if self.whole:
                        goes = self.me < self.n - 1 if way == 0 else self.me > 0
                    else:
                        goes = piece > self.me if way == 0 else piece < self.me

                    @pl.when(goes)
                    def _():
                        self.copy(self.part, way, k, piece).wait_send()
            return carry
        lax.fori_loop(0, self.chunks, drain, 0)


class Scatter:
    def __init__(self, devices, jobs, held, gots, outs, sends, recvs, unit, lag, ahead, wait):
        self.ahead, self.wait = ahead, wait
        self.n, self.jobs, self.held, self.gots, self.outs = devices, jobs, held, gots, outs
        self.sends, self.recvs, self.unit, self.lag = sends, recvs, unit, lag
        self.bits = devices.bit_length() - 1
        self.me = lax.axis_index("seq")
        self.block = jobs[0][0].shape[0] // devices
        self.chunks = sum(size for _, _, _, size in jobs) // unit
        self.steps = self.chunks + wait + (self.bits - 2) * lag

    @staticmethod
    def scratch(devices, rows, cols, unit):
        chunks, bits, block = cols // unit, devices.bit_length() - 1, rows // devices
        shapes = [pltpu.VMEM((chunks, devices // 2, block, unit), bf16)]
        shapes += [pltpu.VMEM((chunks, devices >> (s + 1), block, unit), bf16) for s in range(bits)]
        return shapes + [pltpu.SemaphoreType.DMA((bits, chunks))] * 2

    @staticmethod
    def turn(arrays, jobs, spaces):
        for space, x in zip(spaces, sorted({x for x, _, _, _ in jobs})):
            def one(j, carry):
                at = pl.ds(pl.multiple_of(j * 256, 256), 256)
                space[at, :] = arrays[x][:, at].T
                return carry
            lax.fori_loop(0, space.shape[0] // 256, one, 0)

    @staticmethod
    def turns(arrays, jobs, spaces):
        lefts = sorted({x for x, _, _, _ in jobs})
        return [(spaces[lefts.index(x)], arrays[y], start, size) for x, y, start, size in jobs]

    @staticmethod
    def turned(arrays, jobs, spaces):
        Scatter.turn(arrays, jobs, spaces)
        return Scatter.turns(arrays, jobs, spaces)

    @staticmethod
    def spaces(arrays, jobs):
        return [pltpu.VMEM(arrays[x].shape[::-1], bf16) for x in sorted({x for x, _, _, _ in jobs})]

    def power(self, stage, chunk):
        if stage == 0:
            return 1
        odd = lax.rem(chunk, 2)
        return odd * (1 << (self.bits - stage)) + (1 - odd) * (1 << stage)

    def bit(self, stage, chunk):
        return lax.rem(self.me // self.power(stage, chunk), 2)

    def partner(self, stage, chunk):
        return self.me + (1 - 2 * self.bit(stage, chunk)) * self.power(stage, chunk)

    def start_of_kept(self, stage, chunk):
        at = 0
        for s in range(1, stage):
            at = at + self.bit(s, chunk) * (self.n >> (s + 1))
        return at

    def copy(self, stage, chunk):
        count = self.n >> (stage + 1)
        if stage == 0:
            at = 0
        else:
            at = self.start_of_kept(stage, chunk) + (1 - self.bit(stage, chunk)) * count
        return pltpu.make_async_remote_copy(
            src_ref=self.held.at[chunk, pl.ds(at, count)], dst_ref=self.gots[stage].at[chunk],
            send_sem=self.sends.at[stage, chunk], recv_sem=self.recvs.at[stage, chunk],
            device_id={"seq": self.partner(stage, chunk)}, device_id_type=MESH,
        )

    def products(self, chunk, core, use):
        low = 0
        for x, y, start, size in self.jobs:
            count = size // self.unit

            @pl.when((chunk >= low) & (chunk < low + count))
            def _():
                right = y[:, pl.ds(pl.multiple_of(start + (chunk - low) * self.unit, 128), self.unit)]

                values = []
                for j in range(self.n // 2):
                    target = core
                    for s in range(1, self.bits):
                        target = target + j // (self.n >> (s + 1)) % 2 * self.power(s, chunk)
                    mine = pl.ds(pl.multiple_of(target * self.block, self.block), self.block)
                    values.append(mm(x[mine, :], right))
                for j, value in enumerate(values):
                    use(j, value)
            low += count

    def produce(self, i):
        core = lax.rem(self.me, 2)

        @pl.when(i < self.chunks)
        def _():
            def put(j, value):
                self.held[i, j] = value.astype(bf16)
            self.products(i, 1 - core, put)
            self.copy(0, i).start()

        first = i - 1

        @pl.when((first >= 0) & (first < self.chunks))
        def _():
            self.copy(0, first).wait()

            def put(j, value):
                self.held[first, j] = (value + self.gots[0][first, j].astype(f32)).astype(bf16)
            self.products(first, core, put)
            self.copy(1, first).start()

    def consume(self, i):
        for stage in range(1, self.bits):
            chunk = i - (stage - 1) * self.lag

            @pl.when((chunk >= 0) & (chunk < self.chunks))
            def _():
                self.copy(stage, chunk).wait()
                count = self.n >> (stage + 1)
                base = self.start_of_kept(stage + 1, chunk)
                if stage < self.bits - 1:
                    for j in range(count):
                        self.held[chunk, base + j] = (
                            self.held[chunk, base + j].astype(f32) + self.gots[stage][chunk, j].astype(f32)
                        ).astype(bf16)
                    self.copy(stage + 1, chunk).start()
                else:
                    low = 0
                    for (_, _, _, size), out in zip(self.jobs, self.outs):
                        size = size // self.unit

                        @pl.when((chunk >= low) & (chunk < low + size))
                        def _():
                            cols = pl.ds(pl.multiple_of((chunk - low) * self.unit, self.unit), self.unit)
                            total = self.held[chunk, base].astype(f32) + self.gots[stage][chunk, 0].astype(f32)
                            out[:, cols] = total.astype(out.dtype)
                        low += size

    def step(self, i):
        for turn in range(self.ahead):
            self.produce(i * self.ahead + turn)
        self.consume(i - self.wait)


def greet_line(tp_devices):
    tp = lax.axis_index("tp")
    barrier = pltpu.get_barrier_semaphore()

    @pl.when(tp > 0)
    def _():
        pl.semaphore_signal(barrier, inc=1, device_id={"tp": tp - 1}, device_id_type=MESH)

    @pl.when(tp < tp_devices - 1)
    def _():
        pl.semaphore_signal(barrier, inc=1, device_id={"tp": tp + 1}, device_id_type=MESH)
    return jnp.minimum(tp, 1) + jnp.minimum(tp_devices - 1 - tp, 1)


def greet_halving(seq_devices):
    seq = lax.axis_index("seq")
    barrier = pltpu.get_barrier_semaphore()
    bits = seq_devices.bit_length() - 1
    for b in range(bits):
        other = seq + (1 - 2 * lax.rem(seq // (1 << b), 2)) * (1 << b)
        pl.semaphore_signal(barrier, inc=1, device_id={"seq": other}, device_id_type=MESH)
    return bits


def greet_axis(axis, size):
    me = lax.axis_index(axis)
    barrier = pltpu.get_barrier_semaphore()
    for turn in range(1, size):
        pl.semaphore_signal(barrier, inc=1, device_id={axis: lax.rem(me + turn, size)}, device_id_type=MESH)
    return size - 1


def meet(peers):
    pl.semaphore_wait(pltpu.get_barrier_semaphore(), peers)


def unstaged(refs, count, order=None):
    spaces, sems = refs[-count - 1 : -1], refs[-1]
    loads = [pltpu.make_async_copy(refs[at], spaces[at], sems.at[at]) for at in range(count)]
    for at in order or range(count):
        loads[at].start()
    return loads, list(spaces) + list(refs[count : -count - 1])


def staging(arrays):
    return [pltpu.VMEM(item.shape, item.dtype) for item in arrays] + [pltpu.SemaphoreType.DMA((len(arrays),))]


def rows_of(k, size):
    return pl.ds(pl.multiple_of(k * size, size), size)


def put_own(out, at, value, axis_size):
    width = value.shape[1] // axis_size
    me = lax.axis_index("tp")
    for piece in range(axis_size):
        @pl.when(me == piece)
        def _():
            out[at, :] = value[:, piece * width : (piece + 1) * width]


def attention_ffn_kernel(
    tp_devices, chunk, lag, group,
    *refs
):
    peers = greet_line(tp_devices)
    loads, refs = unstaged(refs, 9, [0, 1, 2, 3, 4, 8, 7, 5, 6])
    (heads_ref, w_out_ref, tokens_ref, live_ref, gain_ref, w_gate_ref, w_up_ref, w_down_ref, cot_ref,
     normed_ref, dboth_ref, hid_ref, own_ref, hidden_ref, pulled_ref, part, ups, downs, sems, dhid_ref) = refs
    rows, dim = tokens_ref.shape
    ffn = w_gate_ref.shape[1]
    gap = dboth_ref.shape[1] // 2
    per = group // chunk
    if gap > ffn:
        dboth_ref[...] = jnp.zeros_like(dboth_ref)
    if hid_ref.shape[1] > ffn:
        hid_ref[:, ffn // 128 * 128 :] = jnp.zeros((rows, hid_ref.shape[1] - ffn // 128 * 128), bf16)

    def attn_done(k, total):
        at = rows_of(k, chunk)
        now = tokens_ref[at, :].astype(f32) + live_ref[at, :] * total
        hidden_ref[at, :] = now.astype(bf16)
        scale = lax.rsqrt(jnp.mean(now * now, axis=-1, keepdims=True) + norm_eps)
        normed_ref[at, :] = (now * scale * gain_ref[...]).astype(bf16)
        put_own(own_ref, at, now, tp_devices)

    line = Line(tp_devices, part, ups, downs, None, sems, chunk, lag, True, attn_done)

    def begin(q, carry):
        at = rows_of(q, 128)
        part[at, :] = mm(heads_ref[at, :], w_out_ref[...]).astype(bf16)
        return carry
    loads[0].wait()
    loads[1].wait()
    begin(0, 0)
    meet(peers)
    line.begin(0, 128 // chunk)

    def rest(q, carry):
        begin(q, carry)
        line.begin(q * (128 // chunk), 128 // chunk)
        return carry
    lax.fori_loop(1, rows // 128, rest, 0)

    tile = 256
    full = ffn // tile
    feeds = -(-ffn // tile)
    items = feeds + dim // tile

    def feed(at, cols, up_cols):
        normed = normed_ref[at, :]
        gate = mm(normed, w_gate_ref[:, cols])
        up = mm(normed, w_up_ref[:, cols])
        sig = sigmoid(gate)
        act = gate * sig
        dhid = dhid_ref[at, cols].astype(f32)
        hid_ref[at, cols] = (act * up).astype(bf16)
        dboth_ref[at, cols] = (dhid * up * (sig * (1.0 + gate * (1.0 - sig)))).astype(bf16)
        dboth_ref[at, up_cols] = (dhid * act).astype(bf16)

    def item(q, w):
        at = rows_of(q, group)

        @pl.when(w < full)
        def _():
            start = pl.multiple_of(w * tile, tile)
            feed(at, pl.ds(start, tile), pl.ds(pl.multiple_of(gap + w * tile, 128), tile))

        if feeds > full:
            @pl.when(w == full)
            def _():
                feed(at, slice(full * tile, ffn), slice(gap + full * tile, gap + ffn))

        @pl.when((w >= feeds) & (w < items))
        def _():
            mine = rows_of(w - feeds, tile)
            total = mm(dboth_ref[at, 0:ffn], w_gate_ref[mine, :], 1, 1)
            total = total + mm(dboth_ref[at, gap : gap + ffn], w_up_ref[mine, :], 1, 1)
            pulled_ref[at, mine] = total.astype(bf16)

    first = max(line.last + per, rows // 64 + 1)
    each = -(-items // per)
    groups = rows // group

    for load in loads[2:]:
        load.wait()

    def lead(i, carry):
        line.step(i)
        at = rows_of(i - 1, 64)

        @pl.when((i >= 1) & (i <= rows // 64))
        def _():
            dhid_ref[at, :] = mm(cot_ref[at, :], w_down_ref[...], 1, 1).astype(bf16)
        return carry
    lax.fori_loop(0, first, lead, 0)

    def beside(i, carry):
        line.step(i)
        q, p = (i - first) // per, lax.rem(i - first, per)

        def work(w, carry):
            item(q, p * each + w)
            return carry
        lax.fori_loop(0, each, work, 0)
        return carry
    lax.fori_loop(first, first + per * (groups - 1), beside, 0)

    def tail(w, carry):
        item(groups - 1, w)
        return carry
    lax.fori_loop(0, items, tail, 0)
    line.end()


def attention_ffn(tp_devices, heads_out, w_out, tokens, live, gain, w_gate, w_up, w_down, cot, chunk=32, lag=2, group=256):
    rows, dim = tokens.shape
    ffn = w_gate.shape[1]
    width = dim // tp_devices
    inputs = (heads_out, w_out, tokens, live, gain.reshape(1, dim), w_gate, w_up, w_down, cot)
    vmem = pl.BlockSpec(memory_space=pltpu.VMEM)
    out_shape = [
        jax.ShapeDtypeStruct((rows, dim), bf16),
        jax.ShapeDtypeStruct((rows, 2 * ceil_to(ffn, 128)), bf16),
        jax.ShapeDtypeStruct((rows, ceil_to(ffn, 256)), bf16),
        jax.ShapeDtypeStruct((rows, width), f32),
        jax.ShapeDtypeStruct((rows, dim), bf16),
        jax.ShapeDtypeStruct((rows, dim), bf16),
    ]
    return pl.pallas_call(
        functools.partial(attention_ffn_kernel, tp_devices, chunk, lag, group),
        in_specs=[pl.BlockSpec(memory_space=pltpu.HBM)] * len(inputs),
        out_specs=[vmem] * len(out_shape),
        out_shape=out_shape,
        scratch_shapes=[pltpu.VMEM((rows, dim), bf16)]
        + Line.scratch(rows, dim, tp_devices, chunk, True)
        + [pltpu.VMEM((rows, ffn), bf16)]
        + staging(inputs),
        compiler_params=pltpu.CompilerParams(
            collective_id=3, has_side_effects=True, vmem_limit_bytes=62 << 20
        ),
        name="attention_ffn",
    )(*inputs)


def paced(flow, pace, tick):
    @pl.when(lax.rem(tick * pace[0], pace[1]) < pace[0])
    def _():
        flow.step(tick * pace[0] // pace[1])


def paced_steps(flow, pace):
    return -(-flow.steps * pace[1] // pace[0])


def ffn_back_kernel(seq_devices, tp_devices, jobs, hid_at, cot_at, unit, chunk, scatter_lag, line_lag, wait, pace, lefts, *refs):
    peers = greet_halving(seq_devices) + greet_line(tp_devices)
    loads, refs = unstaged(refs, lefts + 6, [lefts] + list(range(lefts)) + list(range(lefts + 1, lefts + 6)))

    def take(count):
        out = refs[:count]
        del refs[:count]
        return out

    bits = seq_devices.bit_length() - 1
    arrays = take(lefts)
    part, hidden_ref, live_ref, gain_ref, w_out_ref, w_down_ref = take(6)
    cot_ref = arrays[cot_at]
    outs = take(len(jobs))
    dattn_ref, done_ref, dheads_ref, dgain_ref, ffn_ref = take(5)
    held, *rest = take(1 + bits + 2)
    ups, downs, sems = take(3)
    rows, dim = part.shape

    def dnormed_done(k, total):
        at = rows_of(k, chunk)
        now = hidden_ref[at, :].astype(f32)
        scale = lax.rsqrt(jnp.mean(now * now, axis=-1, keepdims=True) + norm_eps)
        unit_rows = now * scale
        dgain_ref[...] += jnp.sum((total * unit_rows).reshape(-1, 8, dim), axis=0)
        scaled = total * gain_ref[...]
        grad = cot_ref[at, :].astype(f32) + scale * (
            scaled - unit_rows * jnp.mean(scaled * unit_rows, axis=-1, keepdims=True)
        )
        dattn_ref[at, :] = (live_ref[at, :] * grad).astype(bf16)
        put_own(done_ref, at, grad, tp_devices)

    line = Line(tp_devices, part, ups, downs, None, sems, chunk, line_lag, True, dnormed_done)
    dgain_ref[...] = jnp.zeros_like(dgain_ref)
    loads[lefts].wait()
    meet(peers)
    line.begin(0, line.chunks)
    for load in loads[:lefts]:
        load.wait()
    pairs = Scatter.turned(arrays, jobs, refs)
    scatter = Scatter(seq_devices, pairs, held, rest[:bits], outs, rest[bits], rest[bits + 1], unit, scatter_lag, 1, wait)
    for load in loads[lefts + 1 :]:
        load.wait()
    per = 128 // chunk

    def step(i, carry):
        paced(scatter, pace, i)
        line.step(i)
        done = i - line.last

        @pl.when((done >= 0) & (done < line.chunks) & (lax.rem(done + line.chunks, per) == per - 1))
        def _():
            at = rows_of(done // per, 128)
            dheads_ref[at, :] = mm(dattn_ref[at, :], w_out_ref[...], 1, 1)

        @pl.when((i < line.chunks) & (lax.rem(i, per) == 1))
        def _():
            at = rows_of(i // per, 128)
            ffn_ref[at, :] = mm(arrays[hid_at][at, 0 : w_down_ref.shape[0]], w_down_ref[...]).astype(bf16)
        return carry
    lax.fori_loop(0, max(paced_steps(scatter, pace), line.steps), step, 0)
    line.end()


def ffn_back(
    seq_devices, tp_devices, arrays, jobs, hid_at, cot_at, part, hidden, live, gain, w_out, w_down,
    unit=256, chunk=32, scatter_lag=4, line_lag=2, wait=5, pace=(1, 1),
):
    rows, dim = part.shape
    vmem = pl.BlockSpec(memory_space=pltpu.VMEM)
    out_shape = [jax.ShapeDtypeStruct((dim // seq_devices, size), bf16) for _, _, _, size in jobs]
    out_shape += [
        jax.ShapeDtypeStruct((rows, dim), bf16),
        jax.ShapeDtypeStruct((rows, dim // tp_devices), f32),
        jax.ShapeDtypeStruct((rows, w_out.shape[0]), f32),
        jax.ShapeDtypeStruct((8, dim), f32),
        jax.ShapeDtypeStruct((rows, dim), bf16),
    ]
    scratch = Scatter.scratch(seq_devices, dim, sum(size for _, _, _, size in jobs), unit)
    scratch += Line.scratch(rows, dim, tp_devices, chunk, True)
    scratch += Scatter.spaces(arrays, jobs)
    inputs = [*arrays, part, hidden, live, gain.reshape(1, dim), w_out, w_down]
    scratch += staging(inputs)
    return pl.pallas_call(
        functools.partial(
            ffn_back_kernel, seq_devices, tp_devices, jobs, hid_at, cot_at, unit, chunk, scatter_lag, line_lag, wait, pace, len(arrays)
        ),
        in_specs=[pl.BlockSpec(memory_space=pltpu.HBM)] * len(inputs),
        out_specs=[vmem] * len(out_shape),
        out_shape=out_shape,
        scratch_shapes=scratch,
        compiler_params=pltpu.CompilerParams(
            collective_id=4, has_side_effects=True, vmem_limit_bytes=62 << 20
        ),
        name="ffn_back",
    )(*inputs)


def remote(src, dst, send, recv, axis, device):
    return pltpu.make_async_remote_copy(
        src_ref=src, dst_ref=dst, send_sem=send, recv_sem=recv, device_id={axis: device}, device_id_type=MESH
    )


def delta_back_kernel(devices, taps, jobs, unit, scatter_lag, wait, count, *refs):
    peers = greet_axis("seq", devices)
    soon = [count + 10, count + 11, count + 12, count + 13, count + 6]
    later = list(range(count)) + [count + 9]
    rest_of_loads = [at for at in range(count + 14) if at not in soon + later]
    loads, refs = unstaged(refs, count + 14, soon + later + rest_of_loads)

    def take(number):
        out = refs[:number]
        del refs[:number]
        return out

    def arrived(which):
        for at in which:
            loads[at].wait()

    bits = devices.bit_length() - 1
    arrays = take(count)
    (proj_ref, halo_ref, conv_ref, beta_ref, slope_ref, tri_ref, keep_ref, fresh_ref, state_ref, moves_ref,
     dheads_ref, mixed_ref, gate_ref, gain_ref) = take(14)
    outs = take(len(jobs))
    dense_ref, dconv_ref, dbias_ref, dgain_ref = take(4)
    held, *rest = take(1 + bits + 2)
    (ext_ref, dext_ref, dmixed_ref, offset_in, offset_all, states, grads, edge_out, edge_in, last_rows, dbeta_ref,
     send_one, recv_one, send_two, recv_two, edge_sems) = take(16)
    _, seqs, length, width = proj_ref.shape
    pad = halo_ref.shape[2]
    heads = width // HEAD
    chains = seqs * heads
    me = lax.axis_index("seq")
    arrived(soon)
    scatter = Scatter(devices, Scatter.turns(arrays, jobs, refs), held, rest[:bits], outs, rest[bits], rest[bits + 1], unit, scatter_lag, 1, wait)

    def flow(first, last):
        def step(i, carry):
            scatter.step(i)
            return carry
        lax.fori_loop(first, last, step, 0)

    dconv_ref[...] = jnp.zeros_like(dconv_ref)
    dgain_ref[...] = jnp.zeros_like(dgain_ref)
    dbeta_ref[...] = jnp.zeros_like(dbeta_ref)
    dext_ref[...] = jnp.zeros_like(dext_ref)
    together = ext_ref.shape[0]
    groups = heads // together

    def lanes(h):
        return pl.ds(pl.multiple_of(h * HEAD, HEAD), HEAD)

    def head_back(it, carry):
        s = it // groups
        rows = rows_of(s, length)
        gain = gain_ref[...]
        for j in range(together):
            h = lax.rem(it, groups) * together + j
            lane = lanes(h)
            dheads = dheads_ref[rows, lane]
            mixed = mixed_ref[s, :, lane]
            gate = gate_ref[s, :, lane]
            sig = sigmoid(gate)
            act = gate * sig
            rstd = lax.rsqrt(jnp.mean(mixed * mixed, axis=-1, keepdims=True) + norm_eps)
            unit_out = mixed * rstd
            pulled = dheads * unit_out
            dgain_ref[...] += jnp.sum((pulled * act).reshape(-1, 8, HEAD), axis=0)
            dense_ref[rows, lanes(3 * heads + h)] = (pulled * gain * (sig * (1.0 + gate * (1.0 - sig)))).astype(bf16)
            dunit = dheads * gain * act
            dmixed = (rstd * (dunit - unit_out * jnp.mean(dunit * unit_out, axis=-1, keepdims=True))).astype(bf16)
            dmixed_ref[s, :, lane] = dmixed
            offset_in[s * heads + h] = mm(keep_ref[s, h, :, 0:HEAD], dmixed, 0, 0).astype(bf16)
        return carry

    def chain_maps(chain):
        return remote(offset_in.at[chain], offset_all.at[me], send_one.at[chain], recv_one.at[me], "seq", chain)

    lax.fori_loop(0, seqs * groups, head_back, 0)
    meet(peers)
    for chain in range(chains):
        @pl.when(me != chain)
        def _():
            chain_maps(chain).start()

        @pl.when(me == chain)
        def _():
            offset_all[chain] = offset_in[chain]
    arrived(later)
    Scatter.turn(arrays, jobs, refs)
    flow(0, 2)

    @pl.when(me < chains)
    def _():
        state = jnp.zeros((HEAD, HEAD), f32)
        for at in range(devices - 1, -1, -1):
            states[at] = state.astype(bf16)

            @pl.when(me != at)
            def _():
                remote(states.at[at], grads.at[me], send_two.at[at], recv_two.at[me], "seq", at).start()
                remote(offset_in.at[0], offset_all.at[at], send_one.at[0], recv_one.at[at], "seq", at).wait_recv()

            @pl.when(me == at)
            def _():
                grads[me] = states[at]
            state = state + mm(moves_ref[at], state, 0, 0) + offset_all[at].astype(f32)
        for at in range(devices):
            @pl.when(me != at)
            def _():
                remote(states.at[at], grads.at[0], send_two.at[at], recv_two.at[0], "seq", at).wait_send()
    flow(2, 4)
    for chain in range(chains):
        @pl.when(me != chain)
        def _():
            chain_maps(chain).wait_send()
            remote(states.at[0], grads.at[chain], send_two.at[0], recv_two.at[chain], "seq", chain).wait_recv()

    arrived(rest_of_loads)
    below, upto, _ = strict_lower(length)

    def column(ref, s, h):
        value = ref[s]
        at = lax.broadcasted_iota(jnp.int32, value.shape, 1)
        return jnp.sum(jnp.where(at == h, value, 0.0), axis=1, keepdims=True)

    def heads_at_once(s, hs):
        rows = rows_of(s, length)
        slots = range(len(hs))
        for slot, h in enumerate(hs):
            for part in range(3):
                ext_ref[slot, part, 0:pad, :] = halo_ref[part, s, :, lanes(h)].astype(f32)
                ext_ref[slot, part, pad : pad + length, :] = proj_ref[part, s, :, lanes(h)].astype(f32)

        def conv(slot, h, part):
            summed = None
            for tap in range(taps):
                term = (
                    conv_ref[part, tap : tap + 1, lanes(h)]
                    * ext_ref[slot, part, pl.ds(pad - taps + 1 + tap, length), :]
                )
                summed = term if summed is None else summed + term
            return summed

        def both(function, *lists):
            return [function(*items) for items in zip(*lists)]

        def normed(pre):
            act = pre * sigmoid(pre)
            scale = lax.rsqrt(jnp.sum(act * act, axis=-1, keepdims=True) + norm_eps)
            return act * scale

        queries = both(lambda slot, h: normed(conv(slot, h, 0)).astype(bf16), slots, hs)
        keys = both(lambda slot, h: normed(conv(slot, h, 1)).astype(bf16), slots, hs)
        states = [state_ref[s * heads + h] for h in hs]
        exits = [grads[s * heads + h] for h in hs]
        dmixeds = [dmixed_ref[s, :, lanes(h)] for h in hs]
        freshes = [fresh_ref[s, :, lanes(h)] for h in hs]
        betas = [column(beta_ref, s, h) for h in hs]
        scores = both(lambda q, k: jnp.where(upto, mm(q, k, 1, 1), 0.0).astype(bf16), queries, keys)
        dfresh = both(lambda p, d, k, g: (mm(p, d, 0, 0) + mm(k, g)).astype(bf16), scores, dmixeds, keys, exits)
        pulls = both(lambda h, d: mm(tri_ref[s, h], d, 0, 0), hs, dfresh)
        dscores = both(lambda d, f: jnp.where(upto, mm(d, f, 1, 1), 0.0).astype(bf16), dmixeds, freshes)
        dvalues = both(lambda beta, pulled: beta * pulled, betas, pulls)
        dtris = both(lambda pulled, f: jnp.where(below, -mm(pulled, f, 1, 1), 0.0), pulls, freshes)
        inners = both(lambda dtri, k: jnp.sum(dtri * mm(k, k, 1, 1), axis=-1, keepdims=True), dtris, keys)
        dinners = both(lambda beta, dtri: (beta * dtri).astype(bf16), betas, dtris)
        dqueries = both(lambda d, st, p, k: mm(d, st, 1, 1) + mm(p, k), dmixeds, states, dscores, keys)
        dkeys = both(
            lambda p, q, f, g, v, st: mm(p, q, 0, 0) + mm(f, g, 1, 1) - mm(v, st, 1, 1),
            dscores, queries, freshes, exits, dvalues, states,
        )
        dkeys = both(lambda d, g, k: d + mm(g, k) + mm(g, k, 0, 0), dkeys, dinners, keys)
        reads = both(mm, keys, states)
        at = lax.broadcasted_iota(jnp.int32, (length, HEAD), 1)
        for slot, h, pulled, read, inner, dquery, dkey, dvalue in zip(
            slots, hs, pulls, reads, inners, dqueries, dkeys, dvalues
        ):
            for part, dout in ((0, dquery), (1, dkey), (2, dvalue)):
                pre = conv(slot, h, part)
                sig = sigmoid(pre)
                act = pre * sig
                if part == 2:
                    dact = dout
                    missing = act.astype(bf16).astype(f32) - read
                    dbeta = jnp.sum(pulled * missing, axis=-1, keepdims=True) + inner
                    dbeta_ref[s] += jnp.where(at == h, dbeta * column(slope_ref, s, h), 0.0)
                else:
                    scale = lax.rsqrt(jnp.sum(act * act, axis=-1, keepdims=True) + norm_eps)
                    unit_act = act * scale
                    dact = scale * (dout - unit_act * jnp.sum(dout * unit_act, axis=-1, keepdims=True))
                dconv = dact * (sig * (1.0 + pre * (1.0 - sig)))
                dext_ref[slot, part, pad : pad + length, :] = dconv
                for tap in range(taps):
                    shifted = ext_ref[slot, part, pl.ds(pad - taps + 1 + tap, length), :]
                    dconv_ref[part, tap : tap + 1, lanes(h)] += jnp.sum(dconv * shifted, axis=0, keepdims=True)
                summed, edge = None, None
                for tap in range(taps):
                    weight = conv_ref[part, tap : tap + 1, lanes(h)]
                    term = weight * dext_ref[slot, part, pl.ds(pad + taps - 1 - tap, length), :]
                    before = weight * dext_ref[slot, part, pl.ds(taps - 1 - tap, pad), :]
                    summed = term if summed is None else summed + term
                    edge = before if edge is None else edge + before
                col = lanes(part * heads + h)
                dense_ref[rows, col] = summed.astype(bf16)
                edge_out[s, :, col] = edge
                last_rows[s, :, col] = summed[length - pad :, :]

    start = 4
    each = -(-(scatter.steps - start) // (seqs * groups + 1))

    def some_heads(it, carry):
        heads_at_once(it // groups, [lax.rem(it, groups) * together + j for j in range(together)])
        flow(start + it * each, start + (it + 1) * each)
        return carry
    lax.fori_loop(0, seqs * groups, some_heads, 0)

    def edge_copy(other):
        return remote(edge_out, edge_in, edge_sems.at[0], edge_sems.at[1], "seq", other)

    @pl.when(me > 0)
    def _():
        edge_copy(me - 1).start()
    dbias = jnp.zeros((1, HEAD), f32)
    for s in range(seqs):
        low = dbeta_ref[s].astype(bf16)
        dense_ref[s * length : (s + 1) * length, 4 * width : 4 * width + HEAD] = low
        dbias = dbias + jnp.sum(low.astype(f32), axis=0, keepdims=True)
    dbias_ref[...] = dbias
    spare = dense_ref.shape[1] - 4 * width - HEAD
    if spare:
        dense_ref[:, 4 * width + HEAD :] = jnp.zeros((seqs * length, spare), bf16)
    flow(start + seqs * groups * each, scatter.steps)

    @pl.when(me < devices - 1)
    def _():
        edge_copy(0).wait_recv()
        for s in range(seqs):
            dense_ref[(s + 1) * length - pad : (s + 1) * length, 0 : 3 * width] = (last_rows[s] + edge_in[s]).astype(bf16)

    @pl.when(me > 0)
    def _():
        edge_copy(0).wait_send()


def delta_back(devices, arrays, jobs, inputs, unit=256, scatter_lag=2, wait=3, at_once=4):
    dim = arrays[jobs[0][0]].shape[1]
    proj, halo, conv_weight = inputs[:3]
    _, seqs, length, width = proj.shape
    pad = halo.shape[2]
    heads = width // HEAD
    chains = seqs * heads
    taps = conv_weight.shape[1]
    square = (HEAD, HEAD)
    dma = pltpu.SemaphoreType.DMA
    vmem = pl.BlockSpec(memory_space=pltpu.VMEM)
    out_shape = [jax.ShapeDtypeStruct((dim // devices, size), bf16) for _, _, _, size in jobs]
    out_shape += [
        jax.ShapeDtypeStruct((seqs * length, ceil_to(4 * width + HEAD, unit)), bf16),
        jax.ShapeDtypeStruct(conv_weight.shape, f32),
        jax.ShapeDtypeStruct((1, HEAD), f32),
        jax.ShapeDtypeStruct((8, HEAD), f32),
    ]
    together = min(at_once, heads)
    scratch = Scatter.scratch(devices, dim, sum(size for _, _, _, size in jobs), unit)
    scratch += [
        pltpu.VMEM((together, 3, pad + length, HEAD), f32),
        pltpu.VMEM((together, 3, 2 * pad + length, HEAD), f32),
        pltpu.VMEM((seqs, length, width), bf16),
        pltpu.VMEM((chains,) + square, bf16),
        pltpu.VMEM((devices,) + square, bf16),
        pltpu.VMEM((devices,) + square, bf16),
        pltpu.VMEM((chains,) + square, bf16),
        pltpu.VMEM((seqs, pad, 3 * width), f32),
        pltpu.VMEM((seqs, pad, 3 * width), f32),
        pltpu.VMEM((seqs, pad, 3 * width), f32),
        pltpu.VMEM((seqs, length, HEAD), f32),
        dma((chains,)), dma((devices,)), dma((devices,)), dma((chains,)), dma((2,)),
    ]
    scratch += Scatter.spaces(arrays, jobs) + staging([*arrays, *inputs])
    return pl.pallas_call(
        functools.partial(delta_back_kernel, devices, taps, jobs, unit, scatter_lag, wait, len(arrays)),
        in_specs=[pl.BlockSpec(memory_space=pltpu.HBM)] * (len(arrays) + len(inputs)),
        out_specs=[vmem] * len(out_shape),
        out_shape=out_shape,
        scratch_shapes=scratch,
        compiler_params=pltpu.CompilerParams(
            collective_id=2, has_side_effects=True, vmem_limit_bytes=62 << 20
        ),
        name="delta_back",
    )(*arrays, *inputs)


def last_kernel(seq_devices, tp_devices, jobs, unit, chunk, scatter_lag, line_lag, wait, pace, count, late_rows, *refs):
    peers = greet_axis("seq", seq_devices) + greet_axis("tp", tp_devices)
    soon = [count, count + 1] + list(range(count + 11, count + 15))
    later = [at for at in range(count + 15) if at not in soon]
    loads, refs = unstaged(refs, count + 15, soon + later)

    def take(number):
        out = refs[:number]
        del refs[:number]
        return out

    bits = seq_devices.bit_length() - 1
    arrays = take(count)
    dense_ref, w_beta_ref, tokens_ref, rstd_ref, gain_all_ref, grad_ref = take(6)
    dconv_ref, dbias_ref, dffn_gain_ref, head_gain_ref, norms_ref = take(5)
    weights = take(4)
    outs = take(len(jobs))
    tokens_grad_ref, conv_out, bias_out, gain_out, ffn_gain_out, head_out = take(6)
    held, *rest = take(1 + bits + 2)
    part, ups, downs, line_sems = take(4)
    (scaled_ref, dgain_ref, dots, dots_in, early_in, late, late_in, total,
     early_sems, late_sems, dot_sems, both_sems, early_ref, both_out, gain_ref) = take(15)
    seq, tp = lax.axis_index("seq"), lax.axis_index("tp")
    rows, dim = part.shape
    width = weights[0].shape[1]
    own = dim // tp_devices
    heads = w_beta_ref.shape[0]
    dgain_ref[...] = jnp.zeros_like(dgain_ref)
    dots[...] = jnp.zeros_like(dots)
    late[...] = jnp.zeros_like(late)
    for at in soon:
        loads[at].wait()
    meet(peers)
    for at in later:
        loads[at].wait()

    parts, taps, _ = dconv_ref.shape
    conv_rows = parts * taps * (width // HEAD)
    slices = own // HEAD
    split = conv_rows + 8
    both = early_ref.shape[0] - split

    def conv_places():
        for p in range(parts):
            for tap in range(taps):
                for c in range(width // HEAD):
                    row = (p * taps + tap) * (width // HEAD) + c
                    yield row, (p, slice(tap, tap + 1), slice(c * HEAD, (c + 1) * HEAD))

    put_own(gain_ref, slice(0, 1), gain_all_ref[...], tp_devices)
    early_ref[...] = jnp.zeros_like(early_ref)
    for row, place in conv_places():
        early_ref[row : row + 1, :] = dconv_ref[place]
    early_ref[conv_rows : conv_rows + 1, :] = dbias_ref[...]
    ffn_gain_sum = jnp.sum(dffn_gain_ref[...], axis=0, keepdims=True)
    for piece in range(tp_devices):
        @pl.when(tp == piece)
        def _():
            for c in range(slices):
                low = piece * own + c * HEAD
                early_ref[split + c : split + c + 1, :] = ffn_gain_sum[:, low : low + HEAD]
    early_ref[split + slices : split + slices + 1, :] = jnp.sum(head_gain_ref[...], axis=0, keepdims=True)
    early_ref[split + slices + 1 : split + slices + 2, :] = norms_ref[0:1, :]

    def to_peers(src, slots, sems, axis, size):
        me = lax.axis_index(axis)
        return [
            remote(src, slots.at[turn], sems.at[0, turn], sems.at[1, turn], axis, lax.rem(me + turn, size))
            for turn in range(1, size)
        ]

    early_copies = to_peers(early_ref, early_in, early_sems, "seq", seq_devices)
    for copy in early_copies:
        copy.start()

    def done(k, value):
        at = rows_of(k, chunk)
        x = tokens_ref[at, :].astype(f32)
        unit_rows = x * rstd_ref[at, :]
        dgain_ref[...] += jnp.sum((value * unit_rows).reshape(-1, 8, own), axis=0)
        scaled = value * gain_ref[...]
        scaled_ref[at, :] = scaled
        dot = jnp.sum(scaled * x, axis=-1, keepdims=True)
        per = HEAD // chunk
        place = lax.broadcasted_iota(jnp.int32, (chunk, HEAD), 0) + lax.rem(k, per) * chunk
        lane = lax.broadcasted_iota(jnp.int32, (chunk, HEAD), 1)
        dots[pl.ds(k // per, 1), :] += jnp.sum(jnp.where(place == lane, dot, 0.0), axis=0, keepdims=True)

    pairs = Scatter.turned(arrays, jobs, refs)
    scatter = Scatter(seq_devices, pairs, held, rest[:bits], outs, rest[bits], rest[bits + 1], unit, scatter_lag, 1, wait)
    line = Line(tp_devices, part, ups, downs, None, line_sems, chunk, line_lag, False, done)
    per = HEAD // chunk
    groups = rows // HEAD
    part_rows = 256

    def step(i, carry):
        @pl.when(i < rows // part_rows)
        def _():
            at = rows_of(i, part_rows)
            value = mm(dense_ref[at, 4 * width : 4 * width + heads], w_beta_ref[...])
            for w in range(4):
                value = value + mm(dense_ref[at, w * width : (w + 1) * width], weights[w][...], 1, 1)
            part[at, :] = value.astype(bf16)
            line.begin(i * (part_rows // chunk), part_rows // chunk)
        paced(scatter, pace, i)
        line.step(i)
        for at, act in ((0, send_late), (gap, send_total), (2 * gap, finish_tokens)):
            pl.when(i == line.steps + at)(act)
        return carry

    late_copies = to_peers(late, late_in, late_sems, "seq", seq_devices)
    dot_copies = to_peers(dots, dots_in, dot_sems, "tp", tp_devices)
    both_copies = [
        remote(total, both_out.at[tp], both_sems.at[0, turn], both_sems.at[1, turn], "tp", lax.rem(tp + turn, tp_devices))
        for turn in range(1, tp_devices)
    ]
    gap = 4

    def send_late():
        dgain = jnp.sum(dgain_ref[...], axis=0, keepdims=True)
        for at in range(own // HEAD):
            late[at : at + 1, :] = dgain[:, at * HEAD : (at + 1) * HEAD]
        for copy in late_copies + dot_copies:
            copy.start()

    def send_total():
        for copy in early_copies + late_copies:
            copy.wait()
        early_total = early_ref[...]
        late_total = late[...]
        for turn in range(1, seq_devices):
            early_total = early_total + early_in[turn]
            late_total = late_total + late_in[turn]
        for row, place in conv_places():
            conv_out[place] = early_total[row : row + 1]
        bias_out[...] = early_total[conv_rows : conv_rows + 1]
        total[0:both, :] = early_total[split:]
        total[both:, :] = late_total
        both_out[tp] = total[...]
        for copy in both_copies:
            copy.start()

    def finish_tokens():
        for copy in dot_copies:
            copy.wait()
        dot_total = dots[...]
        for turn in range(1, tp_devices):
            dot_total = dot_total + dots_in[turn]
        dots[...] = dot_total / dim
        eye = lax.broadcasted_iota(jnp.int32, (HEAD, HEAD), 0) == lax.broadcasted_iota(jnp.int32, (HEAD, HEAD), 1)

        def finish(q, carry):
            at = rows_of(q, HEAD)
            dot = jnp.sum(jnp.where(eye, dots[pl.ds(q, 1), :], 0.0), axis=1, keepdims=True)
            scale = rstd_ref[at, :]
            x = tokens_ref[at, :].astype(f32)
            tokens_grad_ref[at, :] = grad_ref[at, :] + scale * scaled_ref[at, :] - x * (scale * scale * scale) * dot
            return carry
        lax.fori_loop(0, groups, finish, 0)

    lax.fori_loop(0, max(paced_steps(scatter, pace), line.steps + 2 * gap + 1), step, 0)
    line.end()
    for copy in both_copies:
        copy.wait()
    heads_total = jnp.zeros((2, HEAD), f32)
    for at in range(tp_devices):
        ffn_gain_out[at * slices : (at + 1) * slices, :] = both_out[at, 0:slices]
        gain_out[at * slices : (at + 1) * slices, :] = both_out[at, both : both + slices]
        heads_total = heads_total + both_out[at, slices : slices + 2]
    head_out[...] = heads_total


def last(
    seq_devices, tp_devices, arrays, jobs, dense, w_beta, tokens_own, rstd, gain, grad_own, small, sources,
    unit=256, chunk=32, scatter_lag=4, line_lag=2, wait=5, pace=(2, 3),
):
    dim = arrays[jobs[0][0]].shape[1]
    rows, own = tokens_own.shape
    width = sources[0].shape[1]
    late_rows = ceil_to(own // HEAD, 8)
    dot_rows = ceil_to(rows // HEAD, 8)
    dma = pltpu.SemaphoreType.DMA
    vmem, hbm = pl.BlockSpec(memory_space=pltpu.VMEM), pl.BlockSpec(memory_space=pltpu.HBM)
    out_shape = [jax.ShapeDtypeStruct((dim // seq_devices, size), bf16) for _, _, _, size in jobs]
    out_shape += [
        jax.ShapeDtypeStruct((rows, own), f32),
        jax.ShapeDtypeStruct(small[0].shape, f32),
        jax.ShapeDtypeStruct((1, HEAD), f32),
        jax.ShapeDtypeStruct((dim // HEAD, HEAD), f32),
        jax.ShapeDtypeStruct((dim // HEAD, HEAD), f32),
        jax.ShapeDtypeStruct((2, HEAD), f32),
    ]
    both = ceil_to(own // HEAD + 2, 8)
    early = small[0].size // HEAD + 8 + both
    scratch = Scatter.scratch(seq_devices, dim, sum(size for _, _, _, size in jobs), unit)
    scratch += [pltpu.VMEM((rows, dim), bf16)] + Line.scratch(rows, dim, tp_devices, chunk, False)
    scratch += [
        pltpu.VMEM((rows, own), f32),
        pltpu.VMEM((8, own), f32),
        pltpu.VMEM((dot_rows, HEAD), f32),
        pltpu.VMEM((tp_devices, dot_rows, HEAD), f32),
        pltpu.VMEM((seq_devices, early, HEAD), f32),
        pltpu.VMEM((late_rows, HEAD), f32),
        pltpu.VMEM((seq_devices, late_rows, HEAD), f32),
        pltpu.VMEM((both + late_rows, HEAD), f32),
        dma((2, seq_devices)), dma((2, seq_devices)), dma((2, tp_devices)), dma((2, tp_devices)),
        pltpu.VMEM((early, HEAD), f32),
        pltpu.VMEM((tp_devices, both + late_rows, HEAD), f32),
        pltpu.VMEM((1, own), f32),
    ]
    inputs = [*arrays, dense, w_beta, tokens_own, rstd, gain, grad_own, *small, *sources]
    scratch += Scatter.spaces(arrays, jobs) + staging(inputs)
    return pl.pallas_call(
        functools.partial(
            last_kernel, seq_devices, tp_devices, jobs, unit, chunk, scatter_lag, line_lag, wait, pace, len(arrays), late_rows
        ),
        in_specs=[hbm] * len(inputs),
        out_specs=[vmem] * len(out_shape),
        out_shape=out_shape,
        scratch_shapes=scratch,
        compiler_params=pltpu.CompilerParams(
            collective_id=5, has_side_effects=True, vmem_limit_bytes=62 << 20
        ),
        name="last_sums",
    )(*inputs)


def on_device(
    tokens,
    seq_lengths,
    norm_gain,
    w_query,
    w_key,
    w_value,
    w_gate,
    w_beta,
    beta_bias,
    conv_weight,
    out_gain,
    w_out,
    ffn_gain,
    w_ffn_gate,
    w_ffn_up,
    w_ffn_down,
    cotangent,
):
    seqs_here, local_len, model_dim = tokens.shape
    row_count = seqs_here * local_len
    heads_here = w_beta.shape[1]
    local_width = w_query.shape[1]
    halo_pad = 16
    seq_devices = lax.axis_size("seq")
    tp_devices = lax.axis_size("tp")
    slice_width = model_dim // lax.axis_size("tp")
    tokens_flat = tokens.reshape(row_count, model_dim)
    grad_low = cotangent.reshape(row_count, model_dim)
    normed_one, rstd_one, proj, halo, gate_pre, beta_val, slope, live_rows, tokens_own = first(
        seq_devices, tp_devices, tokens_flat, norm_gain, w_query, w_key, w_value, w_gate, w_beta.T, beta_bias, seq_lengths
    )
    proj_seq = proj.reshape(3, seqs_here, local_len, local_width)
    halo_rows = halo.reshape(3, seqs_here, halo_pad, local_width)
    beta_seq = beta_val.reshape(seqs_here, local_len, heads_here)
    slope = slope.reshape(seqs_here, local_len, heads_here)
    gate_seq = gate_pre.reshape(seqs_here, local_len, local_width)

    tri, keep, state_in, moves, norms, mixed, fresh, heads_seq = delta_forward(
        seq_devices, proj_seq, halo_rows, conv_weight, beta_seq, gate_seq, out_gain
    )
    heads_out = heads_seq.reshape(row_count, local_width)

    normed_two, dffn_both, ffn_hidden, hidden_own, hidden_low, dnormed_part_two = attention_ffn(
        tp_devices, heads_out, w_out, tokens_flat, live_rows, ffn_gain, w_ffn_gate, w_ffn_up, w_ffn_down, grad_low
    )
    ffn_width = w_ffn_gate.shape[1]
    ffn_pad = ffn_hidden.shape[1]
    early = min(768, ffn_pad - 256)
    dw_both, dw_down_early, dattn, grad_own, dheads, dffn_gain, ffn_part = ffn_back(
        seq_devices,
        tp_devices,
        [normed_two, grad_low, dffn_both, ffn_hidden],
        [(0, 2, 0, dffn_both.shape[1]), (1, 3, 0, early)],
        3,
        1,
        dnormed_part_two,
        hidden_low,
        live_rows,
        ffn_gain,
        w_out,
        w_ffn_down,
    )
    ffn_slice = lax.psum_scatter(ffn_part, "tp", scatter_dimension=1, tiled=True)

    dw_down, dw_out, dense, dconv, dbias, dgain = delta_back(
        seq_devices,
        [grad_low, ffn_hidden, dattn, heads_out],
        [(0, 1, early, ffn_pad - early), (2, 3, 0, local_width)],
        [
            proj_seq, halo_rows, conv_weight, beta_seq, slope, tri, keep, fresh, state_in, moves,
            dheads, mixed, gate_seq, out_gain.reshape(1, HEAD),
        ],
    )
    dense, ffn_slice = lax.optimization_barrier((dense, ffn_slice))
    dw_first, tokens_grad, conv_grad, bias_grad, gain_grad, ffn_gain_grad, head_total = last(
        seq_devices,
        tp_devices,
        [normed_one, dense],
        [(0, 1, 0, dense.shape[1])],
        dense,
        w_beta.T,
        tokens_own,
        rstd_one,
        norm_gain.reshape(1, model_dim),
        grad_own,
        [dconv, dbias, dffn_gain, dgain, norms],
        [w_query, w_key, w_value, w_gate],
    )
    out_tokens = (hidden_own + ffn_slice.astype(f32)).astype(bf16).reshape(seqs_here, local_len, slice_width)
    lw = local_width

    def wide(value):
        return value.astype(f32)

    return (
        out_tokens,
        tokens_grad.reshape(seqs_here, local_len, slice_width),
        gain_grad.reshape(model_dim),
        wide(dw_first[:, :lw]),
        wide(dw_first[:, lw : 2 * lw]),
        wide(dw_first[:, 2 * lw : 3 * lw]),
        wide(dw_first[:, 3 * lw : 4 * lw]),
        wide(dw_first[:, 4 * lw : 4 * lw + heads_here]),
        bias_grad[0, :heads_here],
        conv_grad,
        head_total[0],
        wide(dw_out.T),
        ffn_gain_grad.reshape(model_dim),
        wide(dw_both[:, :ffn_width]),
        wide(dw_both[:, dffn_both.shape[1] // 2 :][:, :ffn_width]),
        wide(jnp.concatenate([dw_down_early, dw_down], axis=1).T[:ffn_width]),
        head_total[1, 0] / (seqs_here * HEADS),
    )


def solution(mesh):
    in_specs = (
        P(None, "seq", None),
        P(),
        P(),
        P(None, "tp"),
        P(None, "tp"),
        P(None, "tp"),
        P(None, "tp"),
        P(None, "tp"),
        P("tp"),
        P(None, None, "tp"),
        P(),
        P("tp", None),
        P(),
        P(None, "tp"),
        P(None, "tp"),
        P("tp", None),
        P(None, "seq", None),
    )
    out_specs = (
        P(None, "seq", "tp"),
        P(None, "seq", "tp"),
        P(),
        P("seq", "tp"),
        P("seq", "tp"),
        P("seq", "tp"),
        P("seq", "tp"),
        P("seq", "tp"),
        P("tp"),
        P(None, None, "tp"),
        P(),
        P("tp", "seq"),
        P(),
        P("seq", "tp"),
        P("seq", "tp"),
        P("tp", "seq"),
        P(),
    )
    return jax.shard_map(
        on_device, mesh=mesh, in_specs=in_specs, out_specs=out_specs, check_vma=False
    )
```
